32 devices in a mesh: ctx: 8 (over z, x), head: 4 (over y, core).
Axes of the slice: x: 2, y: 2, z: 4, core: 2. Of those that a mesh axis runs over, the one named last changes fastest.
Arguments:
- tokens: float32 [4096, 2048], P('ctx', 'head'), may hold values from -6 to 6
- w_proj: float32 [2048, 2048], P(None, 'head'), may hold values from -0.125 to 0.125
- w_mix: float32 [2048, 36], P(None, 'head'), may hold values from -0.125 to 0.125
- conv_w: float32 [4, 1536], P(None, 'head'), may hold values from -3 to 3
- rates: float32 [4], P('head'), may hold values from 0.0001 to 0.05
- doc_start: int32 [4096], P('ctx'), may hold values 0 or 1
- norm_gain: float32 [512], P('head'), may hold values from 0.5 to 1.5
- w_out: float32 [512, 2048], P(None, 'head'), may hold values from -0.25 to 0.25
Outputs:
- output: float32 [4096, 2048], P('ctx', 'head')
The draws below stay inside these ranges and needn't reach their ends.
All inputs are finite; a program needn't handle non-finite values. No bound on the sum of `doc_start` on one device may be relied on, other than what follows from the above.
Results may differ from the reference program's by a relative error of at most 0.00021.
Values sent between devices are 32-bit elements; how exact they have to be, the bound alone decides.
No kernel may reach another device: no remote copies, remote signals or barrier semaphores. Data moves between devices by JAX's collectives and lax.ppermute only.
A program may use at most 64 MiB of HBM per device.

```python
import math
import jax
import jax.numpy as jnp
from jax import lax

D = 2048
DK = 128
KERNEL = 4
LEVELS = 7
TOK_DEV = 512
HEADS = 4
NMIX = 9
TOKENS = 4096
N_CTX = 8


def place_ends(values, stream_key, least, high):
    extent = values.shape
    spot = [jax.random.randint(jax.random.fold_in(stream_key, axis), (), 0, extent[axis]) for axis in range(len(extent))]
    values = values.at[tuple(spot)].set(least)
    longest = extent.index(max(extent))
    spot[longest] = (spot[longest] + 1) % extent[longest]
    return values.at[tuple(spot)].set(high)


def block_levels(key, shape, pieces, least, high):
    level = 1.0
    for dim, blocks in pieces:
        draws = jax.random.uniform(jax.random.fold_in(jax.random.fold_in(key, 6), dim), (blocks,), jnp.float32, least / len(pieces), high / len(pieces))
        level = level * jnp.repeat(jnp.exp(draws), shape[dim] // blocks).reshape((-1,) + (1,) * (len(shape) - 1 - dim))
    return level


def normal_values(stream_key, extent, scale, limit, pieces=(), kind=jnp.bfloat16):
    drawn = scale * jax.random.normal(stream_key, extent, jnp.float32)
    if pieces:
        drawn = drawn * block_levels(stream_key, extent, pieces, -0.22, 0.18)
    return jnp.clip(drawn, -limit, limit).astype(kind)


def setup_inputs(seed: int = 0) -> dict:
    arg_keys = jax.random.split(jax.random.key(seed), 9)
    tokens = normal_values(arg_keys[0], (TOKENS, D), 1.0, 6.0, ((0, 8), (1, 4)), jnp.float32)
    w_proj = normal_values(arg_keys[1], (D, HEADS * 4 * DK), D ** -0.5, 0.125, ((1, 4),), jnp.float32)
    w_mix = normal_values(arg_keys[2], (D, HEADS * NMIX), D ** -0.5, 0.125, ((1, 4),), jnp.float32)
    conv_w = normal_values(arg_keys[3], (KERNEL, HEADS * 3 * DK), 0.5, 3.0, ((1, 4),), jnp.float32)
    rates = jnp.clip(jnp.exp(math.log(0.05) - 6.214608 * jax.random.uniform(arg_keys[4], (HEADS,), jnp.float32) ** block_levels(arg_keys[4], (HEADS,), ((0, 4),), -0.2, 0.2)), 0.0001, 0.05)
    doc_start = place_ends((jax.random.randint(arg_keys[5], (TOKENS,), 0, 1024) < 1).astype(jnp.int32), jax.random.fold_in(arg_keys[5], 1), 0, 1)
    norm_gain = jnp.clip(1.0 + 0.1 * jax.random.normal(arg_keys[6], (HEADS * DK,), jnp.float32), 0.5, 1.5)
    w_out = normal_values(arg_keys[7], (HEADS * DK, D), (HEADS * DK) ** -0.5, 0.25, ((1, 4),), jnp.float32)
    return dict(tokens=tokens, w_proj=w_proj, w_mix=w_mix, conv_w=conv_w, rates=rates, doc_start=doc_start, norm_gain=norm_gain, w_out=w_out)


def combine_pairs(first_a, first_b, second_a, second_b):
    highest = lax.Precision.HIGHEST
    new_a = jnp.einsum('nij,njk->nik', first_a, second_a, precision=highest)
    new_b = jnp.einsum('nij,njk->nik', first_b, second_a, precision=highest) + second_b
    return (new_a, new_b)

def reference(tokens, w_proj, w_mix, conv_w, rates, doc_start, norm_gain, w_out):
    highest = lax.Precision.HIGHEST
    proj_heads = w_proj.reshape(D, HEADS, 4 * DK).transpose(1, 0, 2)
    mix_heads = w_mix.reshape(D, HEADS, NMIX).transpose(1, 0, 2)
    conv_heads = conv_w.reshape(KERNEL, HEADS, 3 * DK).transpose(1, 0, 2)
    gain_heads = norm_gain.reshape(HEADS, DK)
    out_heads = w_out.reshape(HEADS, DK, D)
    resets = doc_start.astype(jnp.float32)
    nbits = N_CTX.bit_length() - 1
    identity_d = jnp.eye(DK, dtype=jnp.float32)
    block_index = jnp.arange(N_CTX, dtype=jnp.int32)

    def one_head(accum, items):
        w_head, m_head, c_head, rate, gain, o_head = items
        projected = jnp.dot(tokens, w_head, precision=highest, preferred_element_type=jnp.float32)
        mixing = jnp.dot(tokens, m_head, precision=highest, preferred_element_type=jnp.float32)
        raw_qkv = projected[:, :3 * DK]
        gate_raw = projected[:, 3 * DK:]
        padded = jnp.concatenate([jnp.zeros((KERNEL - 1, 3 * DK), jnp.float32), raw_qkv], axis=0)
        convolved = jnp.zeros((TOKENS, 3 * DK), jnp.float32)
        for step in range(KERNEL):
            convolved = convolved + c_head[step][None, :] * padded[step:step + TOKENS]
        convolved = jax.nn.silu(convolved)
        query = convolved[:, :DK]
        keys = convolved[:, DK:2 * DK]
        values = convolved[:, 2 * DK:]
        query = query / jnp.sqrt(lax.optimization_barrier(jnp.sum(query * query, axis=1, keepdims=True)) + 1e-06)
        keys = keys / jnp.sqrt(lax.optimization_barrier(jnp.sum(keys * keys, axis=1, keepdims=True)) + 1e-06)
        beta = jax.nn.sigmoid(mixing[:, 0])
        log_decay = -rate * jax.nn.softplus(mixing[:, 1]) - 20.0 * resets
        level_weight = jax.nn.softplus(mixing[:, 2:])

        def blocked(arr):
            return arr.reshape((N_CTX, TOK_DEV) + arr.shape[1:]).swapaxes(0, 1)

        def token_step(state, inputs):
            trans, memory = state
            q_t, k_t, v_t, b_t, l_t = inputs
            a_t = jnp.exp(l_t)[:, None, None]
            trans_k = jnp.einsum('nij,nj->ni', trans, k_t, precision=highest)
            trans = a_t * (trans - b_t[:, None, None] * trans_k[:, :, None] * k_t[:, None, :])
            mem_k = jnp.einsum('nij,nj->ni', memory, k_t, precision=highest)
            memory = a_t * (memory - b_t[:, None, None] * mem_k[:, :, None] * k_t[:, None, :])
            memory = memory + b_t[:, None, None] * v_t[:, :, None] * k_t[:, None, :]
            carried = jnp.einsum('nij,nj->ni', trans, q_t, precision=highest)
            local = jnp.einsum('nij,nj->ni', memory, q_t, precision=highest)
            return ((trans, memory), (carried, local))
        start = (jnp.broadcast_to(identity_d, (N_CTX, DK, DK)), jnp.zeros((N_CTX, DK, DK), jnp.float32))
        (block_a, block_b), (carried, local) = lax.scan(token_step, start, (blocked(query), blocked(keys), blocked(values), blocked(beta), blocked(log_decay)))
        carried = carried.swapaxes(0, 1)
        local = local.swapaxes(0, 1)
        weights = level_weight.reshape(N_CTX, TOK_DEV, LEVELS)
        mixed = weights[:, :, 0:1] * local
        agg_a, agg_b = (block_a, block_b)
        carry_m = jnp.broadcast_to(identity_d, (N_CTX, DK, DK))
        for level in range(nbits):
            upper = block_index >> level & 1 == 1
            source = jnp.clip((block_index >> level) - 1, 0, None)
            seg_a = jnp.where(upper[:, None, None], agg_a[source], identity_d[None])
            seg_b = jnp.where(upper[:, None, None], agg_b[source], 0.0)
            level_state = jnp.einsum('nij,njk->nik', seg_b, carry_m, precision=highest)
            carry_m = jnp.einsum('nij,njk->nik', seg_a, carry_m, precision=highest)
            mixed = mixed + weights[:, :, level + 1:level + 2] * jnp.einsum('ntk,nvk->ntv', carried, level_state, precision=highest)
            agg_a, agg_b = combine_pairs(agg_a[0::2], agg_b[0::2], agg_a[1::2], agg_b[1::2])
        mixed = mixed.reshape(TOKENS, DK)
        scale = jnp.sqrt(lax.optimization_barrier(jnp.mean(mixed * mixed, axis=1, keepdims=True)) + 1e-05)
        normed = mixed / scale * gain[None, :] * jax.nn.silu(gate_raw)
        accum = accum + jnp.dot(normed, o_head, precision=highest, preferred_element_type=jnp.float32)
        return (accum, None)
    total, unused = lax.scan(one_head, jnp.zeros((TOKENS, D), jnp.float32), (proj_heads, mix_heads, conv_heads, rates, gain_heads, out_heads))
    return total
```

```python
import functools

import jax
import jax.numpy as jnp
from jax import lax
from jax.experimental import pallas as pl
from jax.experimental.pallas import tpu as pltpu
from jax.sharding import PartitionSpec as P

CHUNK = 128
F32 = jnp.float32
BF16 = jnp.bfloat16


def halves(value):
    high = value.astype(BF16)
    return high, (value - high.astype(F32)).astype(BF16)


def left_parts(value):
    return jnp.concatenate(halves(value), axis=1)


def right_parts(value):
    row = jnp.concatenate(halves(value), axis=1)
    return jnp.concatenate([row, row], axis=0)


def parts_dot(left, right):
    both = jnp.dot(left, right, preferred_element_type=F32)
    half = both.shape[1] // 2
    return both[:, :half] + both[:, half:]


def product(left, right):
    return parts_dot(left_parts(left), right_parts(right))


def softplus(value):
    return jnp.maximum(value, 0.0) + jnp.log1p(jnp.exp(-jnp.abs(value)))


def sigmoid(value):
    return 1.0 / (1.0 + jnp.exp(-value))


def unit_lower_inverse(lowers, row, col):
    size = lowers[0].shape[0]
    eye = jnp.where(row == col, 1.0, 0.0).astype(F32)
    inverses = [eye - jnp.where((row >> 1) == (col >> 1), lower, 0.0) for lower in lowers]
    lower_parts = [halves(lower) for lower in lowers]
    step = 1
    while 2 << (step - 1) < size:
        off = ((row >> (step + 1)) == (col >> (step + 1))) & ((row >> step) > (col >> step))
        lefts = [left_parts(inverse) for inverse in inverses]
        offs = [
            jnp.concatenate([jnp.where(off, part, jnp.zeros_like(part)) for part in parts], axis=1)
            for parts in lower_parts
        ]
        inner = [
            parts_dot(offdiag, right_parts(inverse)) for offdiag, inverse in zip(offs, inverses)
        ]
        inverses = [
            inverse - parts_dot(left, right_parts(value))
            for inverse, left, value in zip(inverses, lefts, inner)
        ]
        step += 1
    return inverses


def local_kernel(
    raw_ref, rim_ref, mix_ref, conv_ref, rate_ref, doc_ref,
    carried_ref, local_ref, weight_ref, pair_ref, padded,
):
    tok_rows = raw_ref.shape[0]
    width = raw_ref.shape[1] // 3
    taps = conv_ref.shape[0]
    rim = rim_ref.shape[0]
    chunks = tok_rows // CHUNK
    padded[0:rim, :] = rim_ref[...]
    padded[rim:, :] = raw_ref[...]
    row = lax.broadcasted_iota(jnp.int32, (CHUNK, CHUNK), 0)
    col = lax.broadcasted_iota(jnp.int32, (CHUNK, CHUNK), 1)
    lower = row >= col
    tri = jnp.where(lower, 1.0, 0.0).astype(F32)
    rate = rate_ref[0, 0]
    queries, keys, values, betas, grids, gammas, tails = [], [], [], [], [], [], []
    for part in range(chunks):
        base = part * CHUNK
        conv = conv_ref[0:1, :] * padded[base + rim - taps + 1 : base + rim - taps + 1 + CHUNK, :]
        for tap in range(1, taps):
            start = base + rim - taps + 1 + tap
            conv = conv + conv_ref[tap : tap + 1, :] * padded[start : start + CHUNK, :]
        conv = conv * sigmoid(conv)
        query = conv[:, :width]
        key = conv[:, width : 2 * width]
        query = query * lax.rsqrt(jnp.sum(query * query, axis=1, keepdims=True) + 1e-06)
        key = key * lax.rsqrt(jnp.sum(key * key, axis=1, keepdims=True) + 1e-06)
        queries.append(query)
        keys.append(key)
        values.append(conv[:, 2 * width :])
        mixing = mix_ref[base : base + CHUNK, :]
        plus = softplus(mixing)
        weight_ref[base : base + CHUNK, :] = plus
        betas.append(sigmoid(mixing[:, 0:1]))
        docs = jnp.transpose(jnp.broadcast_to(doc_ref[part : part + 1, :], (CHUNK, CHUNK)))
        steps = jnp.where(col == 1, -rate * plus, jnp.where(col == 0, docs, 0.0))
        sums = jnp.dot(tri, steps, precision=lax.Precision.HIGHEST, preferred_element_type=F32)
        across = jnp.transpose(sums)
        smooth, count = sums[:, 1:2], sums[:, 0:1]
        span = (smooth - across[1:2, :]) - 20.0 * (count - across[0:1, :])
        grids.append(jnp.exp(jnp.where(lower, span, -1e30)))
        gammas.append(jnp.exp(smooth - 20.0 * count))
        last = sums[CHUNK - 1 : CHUNK, :]
        tails.append(jnp.exp((last[:, 1:2] - smooth) - 20.0 * (last[:, 0:1] - count)))
    across_keys = [jnp.transpose(key) for key in keys]
    grams = [
        parts_dot(left_parts(jnp.concatenate([key, query], axis=0)), right_parts(across))
        for key, query, across in zip(keys, queries, across_keys)
    ]
    lowers = [
        jnp.where(row > col, beta * gram[:CHUNK], 0.0) for beta, gram in zip(betas, grams)
    ]
    inverses = unit_lower_inverse(lowers, row, col)
    states = None
    eye = jnp.where(row == col, 1.0, 0.0).astype(F32)
    for part in range(chunks):
        base = part * CHUNK
        inverse, beta, grid = inverses[part], betas[part], grids[part]
        factor_x = product(inverse, beta * keys[part])
        factor_y = product(grid * inverse, beta * values[part])
        left_keys = left_parts(across_keys[part])
        gamma, tail = gammas[part], tails[part]
        trans = gamma[CHUNK - 1 : CHUNK, :] * (eye - parts_dot(left_keys, right_parts(factor_x)))
        memory = parts_dot(left_keys, right_parts(tail * factor_y))
        overlap = grams[part][CHUNK:]
        carried = gamma * (
            queries[part] - product(jnp.where(lower, overlap, 0.0), factor_x)
        )
        local = product(grid * overlap, factor_y)
        if states is None:
            states = (memory, trans)
        else:
            left = left_parts(jnp.concatenate([carried, trans], axis=0))
            onto_s = parts_dot(left, right_parts(states[0]))
            onto_a = parts_dot(left, right_parts(states[1]))
            local = local + onto_s[:CHUNK]
            carried = onto_a[:CHUNK]
            states = (onto_s[CHUNK:] + memory, onto_a[CHUNK:])
        carried_ref[base : base + CHUNK, :] = carried
        local_ref[base : base + CHUNK, :] = local
    pair_ref[0] = states[1]
    pair_ref[1] = states[0]


def mix_kernel(carried_ref, local_ref, weight_ref, level_ref, gate_ref, gain_ref, normed_ref):
    levels = level_ref.shape[0]
    carried = left_parts(carried_ref[...])
    weights = weight_ref[...]
    mixed = weights[:, 2:3] * local_ref[...]
    for level in range(levels):
        mixed = mixed + weights[:, level + 3 : level + 4] * parts_dot(
            carried, right_parts(level_ref[level])
        )
    scale = lax.rsqrt(jnp.mean(mixed * mixed, axis=1, keepdims=True) + 1e-05)
    gate = gate_ref[...]
    normed_ref[...] = mixed * scale * gain_ref[...] * (gate * sigmoid(gate))


def vmem_call(kernel, outs, scratch, *args):
    spec = pl.BlockSpec(memory_space=pltpu.VMEM)
    return pl.pallas_call(
        kernel,
        out_shape=outs,
        in_specs=[spec] * len(args),
        out_specs=jax.tree.map(lambda unused: spec, outs),
        scratch_shapes=scratch,
        compiler_params=pltpu.CompilerParams(vmem_limit_bytes=40 << 20),
    )(*args)


def gather_head(value):
    count = lax.axis_size("head")
    me = lax.axis_index("head")
    siblings = [(source, source ^ 1) for source in range(count)]
    gathered = [(me, value)]
    for step in range(1, count // 2):
        pairs = [(source, (source + 2 * step) % count) for source in range(count)]
        gathered.append(((me + count - 2 * step) % count, lax.ppermute(value, "head", pairs)))
    for index, held in list(gathered):
        gathered.append((index ^ 1, lax.ppermute(held, "head", siblings)))
    return gathered


def gathered_dot(pieces, weight):
    total = 0.0
    for index, piece in pieces:
        depth = piece.shape[1]
        rows = lax.dynamic_slice_in_dim(weight, index * depth, depth, 0)
        total = total + jnp.dot(
            piece, rows, precision=lax.Precision.HIGH, preferred_element_type=F32
        )
    return total


def partner(value, axis, bit):
    pairs = [(source, source ^ (1 << bit)) for source in range(lax.axis_size(axis))]
    return lax.ppermute(value, axis, pairs)


def shards(tokens, w_proj, w_mix, conv_w, rates, doc_start, norm_gain, w_out):
    tok_rows = tokens.shape[0]
    width = w_proj.shape[1] // 4
    mixes = w_mix.shape[1]
    rim_rows = conv_w.shape[0] - 1
    weight = jnp.concatenate([w_proj, jnp.pad(w_mix, ((0, 0), (0, CHUNK - mixes)))], axis=1)
    raw = gathered_dot(gather_head(tokens), weight)
    raw_qkv = raw[:, : 3 * width]
    gate_raw = raw[:, 3 * width : 4 * width]
    mixing = raw[:, 4 * width :]
    blocks = lax.axis_size("ctx")
    rim = lax.ppermute(
        raw_qkv[tok_rows - 8 :], "ctx", [(source, source + 1) for source in range(blocks - 1)]
    )
    shape = jax.ShapeDtypeStruct((tok_rows, width), F32)
    carried, local, weights, pair = vmem_call(
        local_kernel,
        [shape, shape, jax.ShapeDtypeStruct((tok_rows, CHUNK), F32),
         jax.ShapeDtypeStruct((2, width, width), F32)],
        [pltpu.VMEM((tok_rows + 8, 3 * width), F32)],
        raw_qkv, rim, mixing, conv_w, rates[:, None],
        doc_start.astype(F32).reshape(tok_rows // CHUNK, CHUNK),
    )
    my_index = lax.axis_index("ctx")
    high = functools.partial(
        jnp.dot, precision=lax.Precision.HIGHEST, preferred_element_type=F32
    )
    group_a, group_s = pair[0], pair[1]
    identity = jnp.eye(width, dtype=F32)
    carry = identity
    level_states = []
    for level in range(blocks.bit_length() - 1):
        other_a, other_s = partner((group_a, group_s), "ctx", level)
        upper = my_index >> level & 1 == 1
        seg_a = jnp.where(upper, other_a, identity)
        seg_s = jnp.where(upper, other_s, 0.0)
        first_a = jnp.where(upper, other_a, group_a)
        first_s = jnp.where(upper, other_s, group_s)
        second_a = jnp.where(upper, group_a, other_a)
        second_s = jnp.where(upper, group_s, other_s)
        group_a = high(second_a, first_a)
        group_s = high(second_a, first_s) + second_s
        level_states.append(high(carry, seg_s))
        carry = high(carry, seg_a)
    normed = vmem_call(
        mix_kernel, shape, [],
        carried, local, weights, jnp.stack(level_states), gate_raw, norm_gain[None, :],
    )
    return gathered_dot(gather_head(normed), w_out)


def solution(mesh):
    placed = (
        P("ctx", "head"),
        P(None, "head"),
        P(None, "head"),
        P(None, "head"),
        P("head"),
        P("ctx"),
        P("head"),
        P(None, "head"),
    )
    return jax.shard_map(
        shards, mesh=mesh, in_specs=placed, out_specs=P("ctx", "head"), check_vma=False
    )
```

```python
import functools

import jax
import jax.numpy as jnp
from jax import lax
from jax.experimental import pallas as pl
from jax.experimental.pallas import tpu as pltpu
from jax.sharding import PartitionSpec as P

CHUNK = 128
RIM = 16
F32 = jnp.float32
BF16 = jnp.bfloat16


def halves(value):
    high = value.astype(BF16)
    return high, (value - high.astype(F32)).astype(BF16)


def left_parts(value):
    return jnp.concatenate(halves(value), axis=1)


def right_parts(value):
    row = jnp.concatenate(halves(value), axis=1)
    return jnp.concatenate([row, row], axis=0)


def parts_dot(left, right):
    both = jnp.dot(left, right, preferred_element_type=F32)
    half = both.shape[1] // 2
    return both[:, :half] + both[:, half:]


def product(left, right):
    return parts_dot(left_parts(left), right_parts(right))


def softplus(value):
    return jnp.maximum(value, 0.0) + jnp.log1p(jnp.exp(-jnp.abs(value)))


def sigmoid(value):
    return 1.0 / (1.0 + jnp.exp(-value))


def unit_lower_inverse(lowers, row, col):
    size = lowers[0].shape[0]
    eye = jnp.where(row == col, 1.0, 0.0).astype(F32)
    inverses = [eye - jnp.where((row >> 1) == (col >> 1), lower, 0.0) for lower in lowers]
    lower_parts = [halves(lower) for lower in lowers]
    step = 1
    while 2 << (step - 1) < size:
        off = ((row >> (step + 1)) == (col >> (step + 1))) & ((row >> step) > (col >> step))
        lefts = [left_parts(inverse) for inverse in inverses]
        offs = [
            jnp.concatenate([jnp.where(off, part, jnp.zeros_like(part)) for part in parts], axis=1)
            for parts in lower_parts
        ]
        inner = [
            parts_dot(offdiag, right_parts(inverse)) for offdiag, inverse in zip(offs, inverses)
        ]
        inverses = [
            inverse - parts_dot(left, right_parts(value))
            for inverse, left, value in zip(inverses, lefts, inner)
        ]
        step += 1
    return inverses


def chunk_pass(raw, conv_ref, rate, doc_ref, first_chunk, rim, width, state, outs):
    carried_ref, local_ref, weight_ref, gate_ref = outs
    taps = conv_ref.shape[0]
    chunks = carried_ref.shape[0] // CHUNK
    row = lax.broadcasted_iota(jnp.int32, (CHUNK, CHUNK), 0)
    col = lax.broadcasted_iota(jnp.int32, (CHUNK, CHUNK), 1)
    lower = row >= col
    tri = jnp.where(lower, 1.0, 0.0).astype(F32)
    eye = jnp.where(row == col, 1.0, 0.0).astype(F32)
    queries, keys, values, betas, grids, gammas, tails = [], [], [], [], [], [], []
    for part in range(chunks):
        base = part * CHUNK
        start = base + rim - taps + 1
        conv = conv_ref[0:1, :] * raw[start : start + CHUNK, : 3 * width]
        for tap in range(1, taps):
            conv = conv + conv_ref[tap : tap + 1, :] * raw[
                start + tap : start + tap + CHUNK, : 3 * width
            ]
        conv = conv * sigmoid(conv)
        query = conv[:, :width]
        key = conv[:, width : 2 * width]
        query = query * lax.rsqrt(jnp.sum(query * query, axis=1, keepdims=True) + 1e-06)
        key = key * lax.rsqrt(jnp.sum(key * key, axis=1, keepdims=True) + 1e-06)
        queries.append(query)
        keys.append(key)
        values.append(conv[:, 2 * width :])
        gate = raw[base + rim : base + rim + CHUNK, 3 * width : 4 * width]
        gate_ref[base : base + CHUNK, :] = gate * sigmoid(gate)
        mixing = raw[base + rim : base + rim + CHUNK, 4 * width :]
        plus = softplus(mixing)
        weight_ref[base : base + CHUNK, :] = plus
        betas.append(sigmoid(mixing[:, 0:1]))
        spot = first_chunk + part
        docs = jnp.transpose(jnp.broadcast_to(doc_ref[spot : spot + 1, :], (CHUNK, CHUNK)))
        steps = jnp.where(col == 1, -rate * plus, jnp.where(col == 0, docs, 0.0))
        sums = jnp.dot(tri, steps, precision=lax.Precision.HIGHEST, preferred_element_type=F32)
        across = jnp.transpose(sums)
        smooth, count = sums[:, 1:2], sums[:, 0:1]
        span = (smooth - across[1:2, :]) - 20.0 * (count - across[0:1, :])
        grids.append(jnp.exp(jnp.where(lower, span, -1e30)))
        gammas.append(jnp.exp(smooth - 20.0 * count))
        last = sums[CHUNK - 1 : CHUNK, :]
        tails.append(jnp.exp((last[:, 1:2] - smooth) - 20.0 * (last[:, 0:1] - count)))
    across_keys = [jnp.transpose(key) for key in keys]
    grams = [
        parts_dot(left_parts(jnp.concatenate([key, query], axis=0)), right_parts(across))
        for key, query, across in zip(keys, queries, across_keys)
    ]
    lowers = [
        jnp.where(row > col, beta * gram[:CHUNK], 0.0) for beta, gram in zip(betas, grams)
    ]
    inverses = unit_lower_inverse(lowers, row, col)
    for part in range(chunks):
        base = part * CHUNK
        inverse, beta, grid = inverses[part], betas[part], grids[part]
        factor_x = product(inverse, beta * keys[part])
        factor_y = product(grid * inverse, beta * values[part])
        left_keys = left_parts(across_keys[part])
        gamma, tail = gammas[part], tails[part]
        trans = gamma[CHUNK - 1 : CHUNK, :] * (eye - parts_dot(left_keys, right_parts(factor_x)))
        memory = parts_dot(left_keys, right_parts(tail * factor_y))
        overlap = grams[part][CHUNK:]
        carried = gamma * (
            queries[part] - product(jnp.where(lower, overlap, 0.0), factor_x)
        )
        local = product(grid * overlap, factor_y)
        if state is None:
            state = (trans, memory)
        else:
            left = left_parts(jnp.concatenate([trans, carried], axis=0))
            onto_a = parts_dot(left, right_parts(state[0]))
            onto_s = parts_dot(left, right_parts(state[1]))
            local = local + onto_s[CHUNK:]
            carried = onto_a[CHUNK:]
            state = (onto_a[:CHUNK], onto_s[:CHUNK] + memory)
        carried_ref[base : base + CHUNK, :] = carried
        local_ref[base : base + CHUNK, :] = local
    return state


def part_kernel(segments, width, first_chunk, *refs):
    sources = len(segments[0][2])
    arrays = 1 + max(spot for _, _, places in segments for spot, _ in places)
    index_ref, refs = refs[0], refs[1:]
    held, refs = refs[:arrays], refs[arrays:]
    weight_ref, conv_ref, rate_ref, doc_ref = refs[:4]
    refs = refs[4:]
    state = None
    if first_chunk:
        rim_ref, state_ref = refs[:2]
        refs = refs[2:]
    carried_ref, local_ref, plus_ref, gate_ref, pair_ref, last_ref, raw, high, low = refs
    depth = held[0].shape[1]
    columns = weight_ref.shape[1] // 2
    for start, rows, places in segments:
        for source in range(sources):
            spot, begin = places[source]
            piece = held[spot][begin : begin + rows, :]
            piece_high, piece_low = halves(piece)
            where = pl.ds(pl.multiple_of(index_ref[source] * depth, depth), depth)
            high[start : start + rows, where] = piece_high
            low[start : start + rows, where] = piece_low
    begin = segments[0][0]
    both = jnp.dot(high[begin:, :], weight_ref[...], preferred_element_type=F32)
    rest = jnp.dot(low[begin:, :], weight_ref[:, :columns], preferred_element_type=F32)
    raw[begin:, :] = (both[:, :columns] + both[:, columns:]) + rest
    if first_chunk:
        raw[:begin, : 3 * width] = rim_ref[...]
        state = (state_ref[0], state_ref[1])
    state = chunk_pass(
        raw, conv_ref, rate_ref[0, 0], doc_ref, first_chunk, RIM, width, state,
        (carried_ref, local_ref, plus_ref, gate_ref),
    )
    pair_ref[0] = state[0]
    pair_ref[1] = state[1]
    last_ref[...] = raw[raw.shape[0] - RIM :, : 3 * width]


def four_kernel(bits_ref, own_ref, one_ref, two_ref, three_ref, carry_ref, group_ref, level_ref, next_ref, pairs):
    low_bit, high_bit = bits_ref[0], bits_ref[1]
    place = 2 * high_bit + low_bit
    for mask, ref in enumerate((own_ref, one_ref, two_ref, three_ref)):
        pairs[place ^ mask] = ref[...]
    width = carry_ref.shape[0]
    joined = lambda spot: jnp.concatenate([pairs[spot, 0], pairs[spot, 1]], axis=1)
    onto_low = product(pairs[1, 0], joined(0))
    onto_high = product(pairs[3, 0], joined(2))
    low_a, low_s = onto_low[:, :width], onto_low[:, width:] + pairs[1, 1]
    high_a, high_s = onto_high[:, :width], onto_high[:, width:] + pairs[3, 1]
    onto = product(high_a, jnp.concatenate([low_a, low_s], axis=1))
    group_ref[0] = onto[:, :width]
    group_ref[1] = onto[:, width:] + high_s
    carry = carry_ref[...]
    first = product(carry, jnp.concatenate([one_ref[0], one_ref[1]], axis=1))
    set_low = jnp.broadcast_to(low_bit, (width, width)) == 1
    set_high = jnp.broadcast_to(high_bit, (width, width)) == 1
    level_ref[0] = jnp.where(set_low, first[:, width:], 0.0)
    carry = jnp.where(set_low, first[:, :width], carry)
    second = product(carry, jnp.concatenate([low_a, low_s], axis=1))
    level_ref[1] = jnp.where(set_high, second[:, width:], 0.0)
    next_ref[...] = jnp.where(set_high, second[:, :width], carry)


def mix_kernel(parts, stages, single, *refs):
    pieces = [refs[4 * part : 4 * part + 4] for part in range(parts)]
    refs = refs[4 * parts :]
    level_refs, refs = refs[:stages], refs[stages:]
    states = [ref[spot] for ref in level_refs for spot in range(ref.shape[0])]
    if single:
        carry_ref, seg_ref = refs[:2]
        refs = refs[2:]
        states.append(product(carry_ref[...], seg_ref[...]))
    gain_ref, normed_ref = refs
    states = [right_parts(state) for state in states]
    base = 0
    for carried_ref, local_ref, weight_ref, gate_ref in pieces:
        rows = carried_ref.shape[0]
        carried = left_parts(carried_ref[...])
        weights = weight_ref[...]
        mixed = weights[:, 2:3] * local_ref[...]
        for level, state in enumerate(states):
            mixed = mixed + weights[:, level + 3 : level + 4] * parts_dot(carried, state)
        scale = lax.rsqrt(jnp.mean(mixed * mixed, axis=1, keepdims=True) + 1e-05)
        normed_ref[base : base + rows, :] = mixed * scale * gain_ref[...] * gate_ref[...]
        base += rows


def out_kernel(pieces, added, index_ref, *refs):
    held, weight_ref, refs = refs[:pieces], refs[pieces], refs[pieces + 1 :]
    total = refs[0][...] if added else 0.0
    out_ref = refs[-1]
    columns = out_ref.shape[1]
    for source in range(pieces):
        depth = held[source].shape[1]
        rows = pl.ds(pl.multiple_of(index_ref[source] * depth, depth), depth)
        high, low = halves(held[source][...])
        both = jnp.dot(high, weight_ref[rows, :], preferred_element_type=F32)
        rest = jnp.dot(low, weight_ref[rows, :columns], preferred_element_type=F32)
        total = total + ((both[:, :columns] + both[:, columns:]) + rest)
    out_ref[...] = total


def vmem_call(kernel, outs, scratch, *args):
    spec = pl.BlockSpec(memory_space=pltpu.VMEM)
    small = pl.BlockSpec(memory_space=pltpu.SMEM)
    return pl.pallas_call(
        kernel,
        out_shape=outs,
        in_specs=[small if arg.dtype == jnp.int32 else spec for arg in args],
        out_specs=jax.tree.map(lambda unused: spec, outs),
        scratch_shapes=scratch,
        compiler_params=pltpu.CompilerParams(vmem_limit_bytes=44 << 20),
    )(*args)


def split_columns(weight):
    high = lax.reduce_precision(weight, 8, 7)
    return jnp.concatenate([high.astype(BF16), (weight - high).astype(BF16)], axis=1)


def to_sibling(value):
    count = lax.axis_size("head")
    return lax.ppermute(value, "head", [(source, source ^ 1) for source in range(count)])


def to_chips(value):
    count = lax.axis_size("head")
    return [
        lax.ppermute(
            value, "head", [(source, (source + 2 * step) % count) for source in range(count)]
        )
        for step in range(1, count // 2)
    ]


def after(value, earlier):
    return lax.optimization_barrier((value, earlier))


def shards(tokens, w_proj, w_mix, conv_w, rates, doc_start, norm_gain, w_out):
    tok_rows = tokens.shape[0]
    width = w_proj.shape[1] // 4
    features = w_proj.shape[0]
    heads, me = lax.axis_size("head"), lax.axis_index("head")
    blocks, my_index = lax.axis_size("ctx"), lax.axis_index("ctx")
    remote = [(me + heads - 2 * step) % heads for step in range(1, heads // 2)]
    order = [me, me ^ 1] + remote + [index ^ 1 for index in remote]
    index = jnp.stack(order).astype(jnp.int32)

    half = tok_rows // 2
    quarter = half // 2
    rim = lax.ppermute(
        tokens[tok_rows - RIM :], "ctx", [(source, source + 1) for source in range(blocks - 1)]
    )
    second = to_chips(tokens[quarter:half])
    extended = jnp.concatenate([rim, tokens], axis=0)
    beside = to_sibling(extended)
    first = to_chips(extended[: quarter + RIM])
    third_rows, second = after(tokens[half : half + quarter], second)
    third = to_chips(third_rows)
    second_on = [to_sibling(value) for value in second]
    fourth_rows, first = after(tokens[half + quarter :], first)
    fourth = to_chips(fourth_rows)
    first_on = [to_sibling(value) for value in first]
    third_on = [to_sibling(value) for value in third]
    fourth_on = [to_sibling(value) for value in fourth]

    weight = split_columns(
        jnp.concatenate([w_proj, jnp.pad(w_mix, ((0, 0), (0, CHUNK - w_mix.shape[1])))], axis=1)
    )
    docs = doc_start.astype(F32).reshape(tok_rows // CHUNK, CHUNK)

    def part(segments, arrays, rows, first_chunk, earlier):
        shape = jax.ShapeDtypeStruct((rows, width), F32)
        return vmem_call(
            functools.partial(part_kernel, segments, width, first_chunk),
            [shape, shape, jax.ShapeDtypeStruct((rows, CHUNK), F32), shape,
             jax.ShapeDtypeStruct((2, width, width), F32),
             jax.ShapeDtypeStruct((RIM, 3 * width), F32)],
            [pltpu.VMEM((RIM + rows, weight.shape[1] // 2), F32)]
            + [pltpu.VMEM((RIM + rows, features), BF16)] * 2,
            index, *arrays, weight, conv_w, rates[:, None], docs, *earlier,
        )

    count = heads - 2
    top = quarter + RIM
    arrays = [extended, beside, *first, *first_on, *second, *second_on]
    segments = [
        (0, top, [(0, 0), (1, 0)] + [(2 + spot, 0) for spot in range(count)]),
        (top, quarter, [(0, top), (1, top)] + [(2 + count + spot, 0) for spot in range(count)]),
    ]
    results = [part(segments, arrays, half, 0, ())]
    for turn, (moved, moved_on) in enumerate(((third, third_on), (fourth, fourth_on))):
        begin = RIM + half + turn * quarter
        segments = [(RIM, quarter, [(0, begin), (1, begin)] + [(2 + spot, 0) for spot in range(count)])]
        earlier = (results[-1][5], results[-1][4])
        arrays = [extended, beside, *moved, *moved_on]
        first_chunk = (half + turn * quarter) // CHUNK
        results.append(part(segments, arrays, quarter, first_chunk, earlier))

    pair = results[-1][4]
    carry = jnp.eye(width, dtype=F32)
    square = jax.ShapeDtypeStruct((width, width), F32)
    double = jax.ShapeDtypeStruct((2, width, width), F32)
    bits = blocks.bit_length() - 1
    levels = []
    for bit in range(0, bits - 1, 2):
        others = [
            lax.ppermute(
                pair, "ctx", [(source, source ^ (mask << bit)) for source in range(blocks)]
            )
            for mask in (1, 2, 3)
        ]
        flags = jnp.stack([my_index >> bit & 1, my_index >> (bit + 1) & 1]).astype(jnp.int32)
        pair, level, carry = vmem_call(
            four_kernel, [double, double, square], [pltpu.VMEM((4, 2, width, width), F32)],
            flags, pair, *others, carry,
        )
        levels.append(level)
    single = []
    if bits % 2:
        reach = blocks // 2
        single = [
            carry,
            lax.ppermute(pair[1], "ctx", [(source, source + reach) for source in range(reach)]),
        ]
    fields = [field for result in results for field in result[:4]]
    normed = vmem_call(
        functools.partial(mix_kernel, len(results), len(levels), bool(single)),
        jax.ShapeDtypeStruct((tok_rows, width), F32), [],
        *fields, *levels, *single, norm_gain[None, :],
    )
    own_weight = split_columns(w_out)
    out_shape = jax.ShapeDtypeStruct((tok_rows, w_out.shape[1]), F32)
    far = to_chips(normed)
    near = to_sibling(normed)
    far_on = [to_sibling(value) for value in far]
    total = vmem_call(
        functools.partial(out_kernel, 2, False), out_shape, [], index[:2], normed, near, own_weight
    )
    return vmem_call(
        functools.partial(out_kernel, 2 * len(far), True), out_shape, [],
        index[2:], *far, *far_on, own_weight, total,
    )


def solution(mesh):
    placed = (
        P("ctx", "head"),
        P(None, "head"),
        P(None, "head"),
        P(None, "head"),
        P("head"),
        P("ctx"),
        P("head"),
        P(None, "head"),
    )
    return jax.shard_map(
        shards, mesh=mesh, in_specs=placed, out_specs=P("ctx", "head"), check_vma=False
    )
```

```python
import functools

import jax
import jax.numpy as jnp
from jax import lax
from jax.experimental import pallas as pl
from jax.experimental.pallas import tpu as pltpu
from jax.sharding import PartitionSpec as P

CHUNK = 128
RIM = 16
F32 = jnp.float32
BF16 = jnp.bfloat16


def halves(value):
    high = value.astype(BF16)
    return high, (value - high.astype(F32)).astype(BF16)


def left_parts(value):
    return jnp.concatenate(halves(value), axis=1)


def right_parts(value):
    row = jnp.concatenate(halves(value), axis=1)
    return jnp.concatenate([row, row], axis=0)


def parts_dot(left, right):
    both = jnp.dot(left, right, preferred_element_type=F32)
    half = both.shape[1] // 2
    return both[:, :half] + both[:, half:]


def product(left, right):
    return parts_dot(left_parts(left), right_parts(right))


def softplus(value):
    return jnp.maximum(value, 0.0) + jnp.log1p(jnp.exp(-jnp.abs(value)))


def sigmoid(value):
    return 1.0 / (1.0 + jnp.exp(-value))


def unit_lower_inverse(lowers, row, col):
    size = lowers[0].shape[0]
    eye = jnp.where(row == col, 1.0, 0.0).astype(F32)
    inverses = [eye - jnp.where((row >> 1) == (col >> 1), lower, 0.0) for lower in lowers]
    lower_parts = [halves(lower) for lower in lowers]
    step = 1
    while 2 << (step - 1) < size:
        off = ((row >> (step + 1)) == (col >> (step + 1))) & ((row >> step) > (col >> step))
        lefts = [left_parts(inverse) for inverse in inverses]
        offs = [
            jnp.concatenate([jnp.where(off, part, jnp.zeros_like(part)) for part in parts], axis=1)
            for parts in lower_parts
        ]
        inner = [
            parts_dot(offdiag, right_parts(inverse)) for offdiag, inverse in zip(offs, inverses)
        ]
        inverses = [
            inverse - parts_dot(left, right_parts(value))
            for inverse, left, value in zip(inverses, lefts, inner)
        ]
        step += 1
    return inverses


def prepare_kernel(proj_ref, mix_ref, out_ref, weight_ref, own_ref):
    width = proj_ref.shape[1]
    columns = weight_ref.shape[1] // 2
    mixes = mix_ref.shape[0]
    for base in range(0, proj_ref.shape[0], CHUNK):
        rows = slice(base, base + CHUNK)
        high, low = halves(proj_ref[rows, :])
        weight_ref[rows, :width] = high
        weight_ref[rows, columns : columns + width] = low
        mixing = jnp.concatenate(
            [mix_ref[:, rows], jnp.zeros((CHUNK - mixes, CHUNK), F32)], axis=0
        )
        high, low = halves(jnp.transpose(mixing))
        weight_ref[rows, width:columns] = high
        weight_ref[rows, columns + width :] = low
    for base in range(0, out_ref.shape[0], CHUNK):
        rows = slice(base, base + CHUNK)
        own_ref[rows, :] = left_parts(out_ref[rows, :])


def add_products(total, pieces, index_ref, first, weight_ref):
    columns = weight_ref.shape[1] // 2
    for spot, piece in enumerate(pieces):
        depth = piece.shape[1]
        rows = pl.ds(pl.multiple_of(index_ref[first + spot] * depth, depth), depth)
        high, low = halves(piece)
        both = jnp.dot(high, weight_ref[rows, :], preferred_element_type=F32)
        rest = jnp.dot(low, weight_ref[rows, :columns], preferred_element_type=F32)
        part = (both[:, :columns] + both[:, columns:]) + rest
        total = part if total is None else total + part
    return total


def base_kernel(index_ref, own_ref, beside_ref, weight_ref, base_ref):
    half = own_ref.shape[0] // 2
    for rows in (slice(0, half), slice(half, 2 * half)):
        base_ref[rows, :] = add_products(
            None, [own_ref[rows, :], beside_ref[rows, :]], index_ref, 0, weight_ref
        )


def late_kernel(count, begin, index_ref, *refs):
    base_ref, weight_ref, raw_ref = refs[count:]
    raw_ref[...] = add_products(
        base_ref[begin:, :], [ref[...] for ref in refs[:count]], index_ref, 2, weight_ref
    )


def convolve(raw, start, conv_ref, columns):
    taps = conv_ref.shape[0]
    conv = 0.0
    for tap in range(taps):
        spot = start - taps + 1 + tap
        conv = conv + conv_ref[tap : tap + 1, columns] * raw[spot : spot + CHUNK, columns]
    return conv * sigmoid(conv)


def unit_rows(value):
    return value * lax.rsqrt(jnp.sum(value * value, axis=1, keepdims=True) + 1e-06)


def key_pass(raw, conv_ref, rate, doc_ref, first_chunk, outs, state):
    key_ref, x_ref, y_ref, grid_ref, gamma_ref, chunk_ref, pair_ref = outs
    width = key_ref.shape[1]
    chunks = key_ref.shape[0] // CHUNK
    row = lax.broadcasted_iota(jnp.int32, (CHUNK, CHUNK), 0)
    col = lax.broadcasted_iota(jnp.int32, (CHUNK, CHUNK), 1)
    lower = row >= col
    tri = jnp.where(lower, 1.0, 0.0).astype(F32)
    eye = jnp.where(row == col, 1.0, 0.0).astype(F32)
    keys, values, betas, grids, gammas, tails = [], [], [], [], [], []
    for part in range(chunks):
        start = RIM + part * CHUNK
        rows = slice(part * CHUNK, (part + 1) * CHUNK)
        keys.append(unit_rows(convolve(raw, start, conv_ref, slice(width, 2 * width))))
        values.append(convolve(raw, start, conv_ref, slice(2 * width, 3 * width)))
        mixing = raw[start : start + CHUNK, 4 * width :]
        betas.append(sigmoid(mixing[:, 0:1]))
        spot = first_chunk + part
        docs = jnp.transpose(jnp.broadcast_to(doc_ref[spot : spot + 1, :], (CHUNK, CHUNK)))
        steps = jnp.where(col == 1, -rate * softplus(mixing), jnp.where(col == 0, docs, 0.0))
        sums = jnp.dot(tri, steps, precision=lax.Precision.HIGHEST, preferred_element_type=F32)
        across = jnp.transpose(sums)
        smooth, count = sums[:, 1:2], sums[:, 0:1]
        span = (smooth - across[1:2, :]) - 20.0 * (count - across[0:1, :])
        grids.append(jnp.exp(jnp.where(lower, span, -1e30)))
        gammas.append(jnp.exp(smooth - 20.0 * count))
        last = sums[CHUNK - 1 : CHUNK, :]
        tails.append(jnp.exp((last[:, 1:2] - smooth) - 20.0 * (last[:, 0:1] - count)))
        key_ref[rows, :] = keys[part]
        grid_ref[rows, :] = grids[part]
        gamma_ref[rows, :] = jnp.broadcast_to(gammas[part], (CHUNK, width))
    across_keys = [jnp.transpose(key) for key in keys]
    grams = [
        parts_dot(left_parts(key), right_parts(across)) for key, across in zip(keys, across_keys)
    ]
    lowers = [jnp.where(row > col, beta * gram, 0.0) for beta, gram in zip(betas, grams)]
    inverses = unit_lower_inverse(lowers, row, col)
    states = []
    for part in range(chunks):
        rows = slice(part * CHUNK, (part + 1) * CHUNK)
        inverse, beta = inverses[part], betas[part]
        factor_x = product(inverse, beta * keys[part])
        factor_y = product(grids[part] * inverse, beta * values[part])
        x_ref[rows, :] = factor_x
        y_ref[rows, :] = factor_y
        onto = product(
            across_keys[part], jnp.concatenate([factor_x, tails[part] * factor_y], axis=1)
        )
        trans = gammas[part][CHUNK - 1 : CHUNK, :] * (eye - onto[:, :width])
        states.append((trans, onto[:, width:]))
        chunk_ref[part, 0] = trans
        chunk_ref[part, 1] = onto[:, width:]
    for part in range(1, chunks):
        states[0] = followed(states[0], states[part])
    total = states[0] if state is None else followed(states[0], state)
    pair_ref[0] = total[0]
    pair_ref[1] = total[1]


def followed(first, second):
    width = first[0].shape[0]
    onto = product(second[0], jnp.concatenate(first, axis=1))
    return onto[:, :width], onto[:, width:] + second[1]


def later_kernel(first_chunk, raw_ref, conv_ref, rate_ref, doc_ref, *outs):
    key_pass(raw_ref, conv_ref, rate_ref[0, 0], doc_ref, first_chunk, outs, None)


def earlier_kernel(count, index_ref, *refs):
    held, refs = refs[:count], refs[count:]
    base_ref, weight_ref, rim_ref, next_ref, state_ref, conv_ref, rate_ref, doc_ref, raw = refs[:9]
    rows = held[0].shape[0]
    raw[RIM : RIM + rows, :] = add_products(
        base_ref[:rows, :], [ref[...] for ref in held], index_ref, 2, weight_ref
    )
    raw[:RIM, : rim_ref.shape[1]] = rim_ref[...]
    raw[RIM + rows :, :] = next_ref[:RIM, :]
    key_pass(
        raw, conv_ref, rate_ref[0, 0], doc_ref, 0, refs[9:], (state_ref[0], state_ref[1])
    )


def query_kernel(pieces, *refs):
    fields = [refs[7 * piece : 7 * piece + 7] for piece in range(pieces)]
    conv_ref, carried_ref, local_ref, plus_ref, gate_ref = refs[7 * pieces :]
    width = carried_ref.shape[1]
    row = lax.broadcasted_iota(jnp.int32, (CHUNK, CHUNK), 0)
    col = lax.broadcasted_iota(jnp.int32, (CHUNK, CHUNK), 1)
    state = None
    base = 0
    for raw, key_ref, x_ref, y_ref, grid_ref, gamma_ref, chunk_ref in fields:
        for part in range(key_ref.shape[0] // CHUNK):
            start = RIM + part * CHUNK
            rows = slice(part * CHUNK, (part + 1) * CHUNK)
            out = slice(base, base + CHUNK)
            base += CHUNK
            query = unit_rows(convolve(raw, start, conv_ref, slice(0, width)))
            gate = raw[start : start + CHUNK, 3 * width : 4 * width]
            gate_ref[out, :] = gate * sigmoid(gate)
            plus_ref[out, :] = softplus(raw[start : start + CHUNK, 4 * width :])
            overlap = product(query, jnp.transpose(key_ref[rows, :]))
            carried = gamma_ref[rows, :] * (
                query - product(jnp.where(row >= col, overlap, 0.0), x_ref[rows, :])
            )
            local = product(grid_ref[rows, :] * overlap, y_ref[rows, :])
            trans, memory = chunk_ref[part, 0], chunk_ref[part, 1]
            if state is None:
                state = (trans, memory)
            else:
                onto = product(
                    jnp.concatenate([trans, carried], axis=0), jnp.concatenate(state, axis=1)
                )
                carried = onto[CHUNK:, :width]
                local = local + onto[CHUNK:, width:]
                state = (onto[:CHUNK, :width], onto[:CHUNK, width:] + memory)
            carried_ref[out, :] = carried
            local_ref[out, :] = local


def four_kernel(bits_ref, own_ref, one_ref, two_ref, three_ref, carry_ref, group_ref, level_ref, next_ref, pairs):
    low_bit, high_bit = bits_ref[0], bits_ref[1]
    place = 2 * high_bit + low_bit
    for mask, ref in enumerate((own_ref, one_ref, two_ref, three_ref)):
        pairs[place ^ mask] = ref[...]
    width = carry_ref.shape[0]
    joined = lambda spot: jnp.concatenate([pairs[spot, 0], pairs[spot, 1]], axis=1)
    onto_low = product(pairs[1, 0], joined(0))
    onto_high = product(pairs[3, 0], joined(2))
    low_a, low_s = onto_low[:, :width], onto_low[:, width:] + pairs[1, 1]
    high_a, high_s = onto_high[:, :width], onto_high[:, width:] + pairs[3, 1]
    onto = product(high_a, jnp.concatenate([low_a, low_s], axis=1))
    group_ref[0] = onto[:, :width]
    group_ref[1] = onto[:, width:] + high_s
    carry = carry_ref[...]
    first = product(carry, jnp.concatenate([one_ref[0], one_ref[1]], axis=1))
    set_low = jnp.broadcast_to(low_bit, (width, width)) == 1
    set_high = jnp.broadcast_to(high_bit, (width, width)) == 1
    level_ref[0] = jnp.where(set_low, first[:, width:], 0.0)
    carry = jnp.where(set_low, first[:, :width], carry)
    second = product(carry, jnp.concatenate([low_a, low_s], axis=1))
    level_ref[1] = jnp.where(set_high, second[:, width:], 0.0)
    next_ref[...] = jnp.where(set_high, second[:, :width], carry)


def mix_kernel(stages, single, carried_ref, local_ref, weight_ref, gate_ref, gain_ref, *refs):
    states = [ref[spot] for ref in refs[:stages] for spot in range(ref.shape[0])]
    if single:
        states.append(product(refs[stages][...], refs[stages + 1][...]))
    normed_ref = refs[-1]
    states = [right_parts(state) for state in states]
    carried = left_parts(carried_ref[...])
    weights = weight_ref[...]
    mixed = weights[:, 2:3] * local_ref[...]
    for level, state in enumerate(states):
        mixed = mixed + weights[:, level + 3 : level + 4] * parts_dot(carried, state)
    scale = lax.rsqrt(jnp.mean(mixed * mixed, axis=1, keepdims=True) + 1e-05)
    normed_ref[...] = mixed * scale * gain_ref[...] * gate_ref[...]


def out_kernel(pieces, first, index_ref, *refs):
    weight_ref = refs[pieces]
    total = refs[pieces + 1][...] if first else None
    refs[-1][...] = add_products(
        total, [ref[...] for ref in refs[:pieces]], index_ref, first, weight_ref
    )


def vmem_call(kernel, outs, scratch, cost, *args):
    spec = pl.BlockSpec(memory_space=pltpu.VMEM)
    small = pl.BlockSpec(memory_space=pltpu.SMEM)
    return pl.pallas_call(
        kernel,
        out_shape=outs,
        in_specs=[small if arg.dtype == jnp.int32 else spec for arg in args],
        out_specs=jax.tree.map(lambda unused: spec, outs),
        scratch_shapes=scratch,
        compiler_params=pltpu.CompilerParams(vmem_limit_bytes=40 << 20),
        cost_estimate=pl.CostEstimate(flops=int(cost * 1e9), bytes_accessed=1 << 20, transcendentals=0),
    )(*args)


def to_sibling(value):
    count = lax.axis_size("head")
    return lax.ppermute(value, "head", [(source, source ^ 1) for source in range(count)])


def to_chips(value):
    count = lax.axis_size("head")
    return [
        lax.ppermute(
            value, "head", [(source, (source + 2 * step) % count) for source in range(count)]
        )
        for step in range(1, count // 2)
    ]


def after(value, *earlier):
    return lax.optimization_barrier((value, *earlier))


def shards(tokens, w_proj, w_mix, conv_w, rates, doc_start, norm_gain, w_out):
    tok_rows, depth = tokens.shape
    width = w_proj.shape[1] // 4
    features = w_proj.shape[0]
    columns = 4 * width + CHUNK
    heads, me = lax.axis_size("head"), lax.axis_index("head")
    blocks, my_index = lax.axis_size("ctx"), lax.axis_index("ctx")
    remote = [(me + heads - 2 * step) % heads for step in range(1, heads // 2)]
    order = [me, me ^ 1] + remote + [index ^ 1 for index in remote]
    index = jnp.stack(order).astype(jnp.int32)
    count = heads - 2
    like = lambda *shape: jax.ShapeDtypeStruct(shape, F32)

    half = tok_rows // 2
    cut = half - RIM
    late = to_chips(tokens[cut:])
    beside = to_sibling(tokens)
    weight, own_weight = vmem_call(
        prepare_kernel,
        [jax.ShapeDtypeStruct((features, 2 * columns), BF16),
         jax.ShapeDtypeStruct((w_out.shape[0], 2 * w_out.shape[1]), BF16)],
        [], 3, w_proj, w_mix.T, w_out,
    )
    base = vmem_call(base_kernel, like(tok_rows, columns), [], 3, index, tokens, beside, weight)
    early_rows, base = after(tokens[:cut], base)
    early = to_chips(early_rows)
    late, base = after(late, base)
    late_on = [to_sibling(value) for value in late]
    raw_late = vmem_call(
        functools.partial(late_kernel, count, cut), like(tok_rows - cut, columns), [], 2,
        index, *late, *late_on, base, weight,
    )
    rim = lax.ppermute(
        raw_late[tok_rows - cut - RIM :, : 3 * width], "ctx",
        [(source, source + 1) for source in range(blocks - 1)],
    )
    docs = doc_start.astype(F32).reshape(tok_rows // CHUNK, CHUNK)
    rate = rates[:, None]
    outs = [like(half, width)] * 5 + [like(half // CHUNK, 2, width, width), like(2, width, width)]
    later = vmem_call(
        functools.partial(later_kernel, half // CHUNK), outs, [], 4, raw_late, conv_w, rate, docs
    )
    early, pair_late, rim = after(early, later[6], rim)
    early_on = [to_sibling(value) for value in early]
    raw_early, *earlier = vmem_call(
        functools.partial(earlier_kernel, count), [like(half + RIM, columns)] + outs, [], 5,
        index, *early, *early_on, base, weight, rim, raw_late, pair_late, conv_w, rate, docs,
    )

    pair = earlier[6]
    carry = jnp.eye(width, dtype=F32)
    bits = blocks.bit_length() - 1
    levels = []
    moved = None
    for bit in range(0, bits - 1, 2):
        others = [
            lax.ppermute(
                pair, "ctx", [(source, source ^ (mask << bit)) for source in range(blocks)]
            )
            for mask in (1, 2, 3)
        ]
        flags = jnp.stack([my_index >> bit & 1, my_index >> (bit + 1) & 1]).astype(jnp.int32)
        pair, level, carry = vmem_call(
            four_kernel, [like(2, width, width)] * 2 + [like(width, width)],
            [pltpu.VMEM((4, 2, width, width), F32)], 1,
            flags, pair, *others, carry,
        )
        levels.append(level)
    fields = vmem_call(
        functools.partial(query_kernel, 2), [like(tok_rows, width)] * 4, [], 5,
        raw_early, *earlier[:6], raw_late, *later[:6], conv_w,
    )
    single = []
    if bits % 2:
        reach = blocks // 2
        single = [
            carry,
            lax.ppermute(pair[1], "ctx", [(source, source + reach) for source in range(reach)]),
        ]
    normed = vmem_call(
        functools.partial(mix_kernel, len(levels), bool(single)), like(tok_rows, width), [], 1,
        *fields, norm_gain[None, :], *levels, *single,
    )
    far = to_chips(normed)
    near = to_sibling(normed)
    out_shape = like(tok_rows, w_out.shape[1])
    total = vmem_call(
        functools.partial(out_kernel, 2, 0), out_shape, [], 2, index, normed, near, own_weight
    )
    far, total = after(far, total)
    far_on = [to_sibling(value) for value in far]
    return vmem_call(
        functools.partial(out_kernel, count, 2), out_shape, [], 2,
        index, *far, *far_on, own_weight, total,
    )


def solution(mesh):
    placed = (
        P("ctx", "head"),
        P(None, "head"),
        P(None, "head"),
        P(None, "head"),
        P("head"),
        P("ctx"),
        P("head"),
        P(None, "head"),
    )
    return jax.shard_map(
        shards, mesh=mesh, in_specs=placed, out_specs=P("ctx", "head"), check_vma=False
    )
```

```python
import functools

import jax
import jax.numpy as jnp
from jax import lax
from jax.experimental import pallas as pl
from jax.experimental.pallas import tpu as pltpu
from jax.sharding import PartitionSpec as P

CHUNK = 128
RIM = 16
VMEM_GRANT = 8 << 20
F32 = jnp.float32
BF16 = jnp.bfloat16


def halves(value):
    high = value.astype(BF16)
    return high, (value - high.astype(F32)).astype(BF16)


def left_parts(value):
    return jnp.concatenate(halves(value), axis=1)


def right_parts(value):
    row = jnp.concatenate(halves(value), axis=1)
    return jnp.concatenate([row, row], axis=0)


def parts_dot(left, right):
    both = jnp.dot(left, right, preferred_element_type=F32)
    half = both.shape[1] // 2
    return both[:, :half] + both[:, half:]


def product(left, right):
    return parts_dot(left_parts(left), right_parts(right))


def softplus(value):
    return jnp.maximum(value, 0.0) + jnp.log1p(jnp.exp(-jnp.abs(value)))


def sigmoid(value):
    return 1.0 / (1.0 + jnp.exp(-value))


def unit_lower_inverse(lowers, row, col):
    size = lowers[0].shape[0]
    eye = jnp.where(row == col, 1.0, 0.0).astype(F32)
    inverses = [eye - jnp.where((row >> 1) == (col >> 1), lower, 0.0) for lower in lowers]
    lower_parts = [halves(lower) for lower in lowers]
    step = 1
    while 2 << (step - 1) < size:
        off = ((row >> (step + 1)) == (col >> (step + 1))) & ((row >> step) > (col >> step))
        lefts = [left_parts(inverse) for inverse in inverses]
        offs = [
            jnp.concatenate([jnp.where(off, part, jnp.zeros_like(part)) for part in parts], axis=1)
            for parts in lower_parts
        ]
        inner = [
            parts_dot(offdiag, right_parts(inverse)) for offdiag, inverse in zip(offs, inverses)
        ]
        inverses = [
            inverse - parts_dot(left, right_parts(value))
            for inverse, left, value in zip(inverses, lefts, inner)
        ]
        step += 1
    return inverses


def prepare_kernel(proj_ref, mix_ref, out_ref, weight_ref, own_ref):
    width = proj_ref.shape[1]
    columns = weight_ref.shape[1] // 2
    mixes = mix_ref.shape[0]
    for base in range(0, proj_ref.shape[0], CHUNK):
        rows = slice(base, base + CHUNK)
        high, low = halves(proj_ref[rows, :])
        weight_ref[rows, :width] = high
        weight_ref[rows, columns : columns + width] = low
        mixing = jnp.concatenate(
            [mix_ref[:, rows], jnp.zeros((CHUNK - mixes, CHUNK), F32)], axis=0
        )
        high, low = halves(jnp.transpose(mixing))
        weight_ref[rows, width:columns] = high
        weight_ref[rows, columns + width :] = low
    for base in range(0, out_ref.shape[0], CHUNK):
        rows = slice(base, base + CHUNK)
        own_ref[rows, :] = left_parts(out_ref[rows, :])


def add_products(total, pieces, index_ref, first, weight_ref):
    columns = weight_ref.shape[1] // 2
    for spot, piece in enumerate(pieces):
        depth = piece.shape[1]
        rows = pl.ds(pl.multiple_of(index_ref[first + spot] * depth, depth), depth)
        high, low = halves(piece)
        both = jnp.dot(high, weight_ref[rows, :], preferred_element_type=F32)
        rest = jnp.dot(low, weight_ref[rows, :columns], preferred_element_type=F32)
        part = (both[:, :columns] + both[:, columns:]) + rest
        total = part if total is None else total + part
    return total


def base_kernel(index_ref, own_ref, beside_ref, weight_ref, base_ref):
    half = own_ref.shape[0] // 2
    for rows in (slice(0, half), slice(half, 2 * half)):
        base_ref[rows, :] = add_products(
            None, [own_ref[rows, :], beside_ref[rows, :]], index_ref, 0, weight_ref
        )


def late_kernel(count, begin, index_ref, *refs):
    base_ref, weight_ref, raw_ref = refs[count:]
    raw_ref[...] = add_products(
        base_ref[begin:, :], [ref[...] for ref in refs[:count]], index_ref, 2, weight_ref
    )


def convolve(raw, start, conv_ref, columns):
    taps = conv_ref.shape[0]
    conv = 0.0
    for tap in range(taps):
        spot = start - taps + 1 + tap
        conv = conv + conv_ref[tap : tap + 1, columns] * raw[spot : spot + CHUNK, columns]
    return conv * sigmoid(conv)


def unit_rows(value):
    return value * lax.rsqrt(jnp.sum(value * value, axis=1, keepdims=True) + 1e-06)


def key_pass(raw, conv_ref, rate, doc_ref, first_chunk, outs, state):
    key_ref, x_ref, y_ref, grid_ref, gamma_ref, chunk_ref, pair_ref = outs
    width = key_ref.shape[1]
    chunks = key_ref.shape[0] // CHUNK
    row = lax.broadcasted_iota(jnp.int32, (CHUNK, CHUNK), 0)
    col = lax.broadcasted_iota(jnp.int32, (CHUNK, CHUNK), 1)
    lower = row >= col
    tri = jnp.where(lower, 1.0, 0.0).astype(F32)
    eye = jnp.where(row == col, 1.0, 0.0).astype(F32)
    keys, values, betas, grids, gammas, tails = [], [], [], [], [], []
    for part in range(chunks):
        start = RIM + part * CHUNK
        rows = slice(part * CHUNK, (part + 1) * CHUNK)
        keys.append(unit_rows(convolve(raw, start, conv_ref, slice(width, 2 * width))))
        values.append(convolve(raw, start, conv_ref, slice(2 * width, 3 * width)))
        mixing = raw[start : start + CHUNK, 4 * width :]
        betas.append(sigmoid(mixing[:, 0:1]))
        spot = first_chunk + part
        docs = jnp.transpose(jnp.broadcast_to(doc_ref[spot : spot + 1, :], (CHUNK, CHUNK)))
        steps = jnp.where(col == 1, -rate * softplus(mixing), jnp.where(col == 0, docs, 0.0))
        sums = jnp.dot(tri, steps, precision=lax.Precision.HIGHEST, preferred_element_type=F32)
        across = jnp.transpose(sums)
        smooth, count = sums[:, 1:2], sums[:, 0:1]
        span = (smooth - across[1:2, :]) - 20.0 * (count - across[0:1, :])
        grids.append(jnp.exp(jnp.where(lower, span, -1e30)))
        gammas.append(jnp.exp(smooth - 20.0 * count))
        last = sums[CHUNK - 1 : CHUNK, :]
        tails.append(jnp.exp((last[:, 1:2] - smooth) - 20.0 * (last[:, 0:1] - count)))
        key_ref[rows, :] = keys[part]
        grid_ref[rows, :] = grids[part]
        gamma_ref[rows, :] = jnp.broadcast_to(gammas[part], (CHUNK, width))
    across_keys = [jnp.transpose(key) for key in keys]
    grams = [
        parts_dot(left_parts(key), right_parts(across)) for key, across in zip(keys, across_keys)
    ]
    lowers = [jnp.where(row > col, beta * gram, 0.0) for beta, gram in zip(betas, grams)]
    inverses = unit_lower_inverse(lowers, row, col)
    states = []
    for part in range(chunks):
        rows = slice(part * CHUNK, (part + 1) * CHUNK)
        inverse, beta = inverses[part], betas[part]
        factor_x = product(inverse, beta * keys[part])
        factor_y = product(grids[part] * inverse, beta * values[part])
        x_ref[rows, :] = factor_x
        y_ref[rows, :] = factor_y
        onto = product(
            across_keys[part], jnp.concatenate([factor_x, tails[part] * factor_y], axis=1)
        )
        trans = gammas[part][CHUNK - 1 : CHUNK, :] * (eye - onto[:, :width])
        states.append((trans, onto[:, width:]))
        chunk_ref[part, 0] = trans
        chunk_ref[part, 1] = onto[:, width:]
    for part in range(1, chunks):
        states[0] = followed(states[0], states[part])
    total = states[0] if state is None else followed(states[0], state)
    pair_ref[0] = total[0]
    pair_ref[1] = total[1]


def followed(first, second):
    width = first[0].shape[0]
    onto = product(second[0], jnp.concatenate(first, axis=1))
    return onto[:, :width], onto[:, width:] + second[1]


def later_kernel(first_chunk, raw_ref, conv_ref, rate_ref, doc_ref, *outs):
    key_pass(raw_ref, conv_ref, rate_ref[0, 0], doc_ref, first_chunk, outs, None)


def earlier_kernel(count, index_ref, *refs):
    held, refs = refs[:count], refs[count:]
    base_ref, weight_ref, rim_ref, next_ref, state_ref, conv_ref, rate_ref, doc_ref, raw = refs[:9]
    rows = held[0].shape[0]
    raw[RIM : RIM + rows, :] = add_products(
        base_ref[:rows, :], [ref[...] for ref in held], index_ref, 2, weight_ref
    )
    raw[:RIM, : rim_ref.shape[1]] = rim_ref[...]
    raw[RIM + rows :, :] = next_ref[:RIM, :]
    key_pass(
        raw, conv_ref, rate_ref[0, 0], doc_ref, 0, refs[9:], (state_ref[0], state_ref[1])
    )


def query_kernel(pieces, *refs):
    fields = [refs[7 * piece : 7 * piece + 7] for piece in range(pieces)]
    conv_ref, carried_ref, local_ref, plus_ref, gate_ref = refs[7 * pieces :]
    width = carried_ref.shape[1]
    row = lax.broadcasted_iota(jnp.int32, (CHUNK, CHUNK), 0)
    col = lax.broadcasted_iota(jnp.int32, (CHUNK, CHUNK), 1)
    state = None
    base = 0
    for raw, key_ref, x_ref, y_ref, grid_ref, gamma_ref, chunk_ref in fields:
        for part in range(key_ref.shape[0] // CHUNK):
            start = RIM + part * CHUNK
            rows = slice(part * CHUNK, (part + 1) * CHUNK)
            out = slice(base, base + CHUNK)
            base += CHUNK
            query = unit_rows(convolve(raw, start, conv_ref, slice(0, width)))
            gate = raw[start : start + CHUNK, 3 * width : 4 * width]
            gate_ref[out, :] = gate * sigmoid(gate)
            plus_ref[out, :] = softplus(raw[start : start + CHUNK, 4 * width :])
            overlap = product(query, jnp.transpose(key_ref[rows, :]))
            carried = gamma_ref[rows, :] * (
                query - product(jnp.where(row >= col, overlap, 0.0), x_ref[rows, :])
            )
            local = product(grid_ref[rows, :] * overlap, y_ref[rows, :])
            trans, memory = chunk_ref[part, 0], chunk_ref[part, 1]
            if state is None:
                state = (trans, memory)
            else:
                onto = product(
                    jnp.concatenate([trans, carried], axis=0), jnp.concatenate(state, axis=1)
                )
                carried = onto[CHUNK:, :width]
                local = local + onto[CHUNK:, width:]
                state = (onto[:CHUNK, :width], onto[:CHUNK, width:] + memory)
            carried_ref[out, :] = carried
            local_ref[out, :] = local


def four_kernel(bits_ref, own_ref, one_ref, two_ref, three_ref, carry_ref, group_ref, level_ref, next_ref, pairs):
    low_bit, high_bit = bits_ref[0], bits_ref[1]
    place = 2 * high_bit + low_bit
    for mask, ref in enumerate((own_ref, one_ref, two_ref, three_ref)):
        pairs[place ^ mask] = ref[...]
    width = carry_ref.shape[0]
    joined = lambda spot: jnp.concatenate([pairs[spot, 0], pairs[spot, 1]], axis=1)
    onto_low = product(pairs[1, 0], joined(0))
    onto_high = product(pairs[3, 0], joined(2))
    low_a, low_s = onto_low[:, :width], onto_low[:, width:] + pairs[1, 1]
    high_a, high_s = onto_high[:, :width], onto_high[:, width:] + pairs[3, 1]
    onto = product(high_a, jnp.concatenate([low_a, low_s], axis=1))
    group_ref[0] = onto[:, :width]
    group_ref[1] = onto[:, width:] + high_s
    carry = carry_ref[...]
    first = product(carry, jnp.concatenate([one_ref[0], one_ref[1]], axis=1))
    set_low = jnp.broadcast_to(low_bit, (width, width)) == 1
    set_high = jnp.broadcast_to(high_bit, (width, width)) == 1
    level_ref[0] = jnp.where(set_low, first[:, width:], 0.0)
    carry = jnp.where(set_low, first[:, :width], carry)
    second = product(carry, jnp.concatenate([low_a, low_s], axis=1))
    level_ref[1] = jnp.where(set_high, second[:, width:], 0.0)
    next_ref[...] = jnp.where(set_high, second[:, :width], carry)


def mix_kernel(stages, single, carried_ref, local_ref, weight_ref, gate_ref, gain_ref, *refs):
    states = [ref[spot] for ref in refs[:stages] for spot in range(ref.shape[0])]
    if single:
        states.append(product(refs[stages][...], refs[stages + 1][...]))
    normed_ref = refs[-1]
    states = [right_parts(state) for state in states]
    carried = left_parts(carried_ref[...])
    weights = weight_ref[...]
    mixed = weights[:, 2:3] * local_ref[...]
    for level, state in enumerate(states):
        mixed = mixed + weights[:, level + 3 : level + 4] * parts_dot(carried, state)
    scale = lax.rsqrt(jnp.mean(mixed * mixed, axis=1, keepdims=True) + 1e-05)
    normed_ref[...] = mixed * scale * gain_ref[...] * gate_ref[...]


def out_kernel(pieces, first, index_ref, *refs):
    weight_ref = refs[pieces]
    out_ref = refs[-1]
    columns = out_ref.shape[1]
    weights = []
    for spot in range(pieces):
        depth = refs[spot].shape[1]
        rows = pl.ds(pl.multiple_of(index_ref[first + spot] * depth, depth), depth)
        weights.append(weight_ref[rows, :])
    weight = jnp.concatenate(weights, axis=0)
    for base in range(0, out_ref.shape[0], CHUNK):
        rows = slice(base, base + CHUNK)
        parts = [halves(ref[rows, :]) for ref in refs[:pieces]]
        high, low = (jnp.concatenate(part, axis=1) for part in zip(*parts))
        both = jnp.dot(high, weight, preferred_element_type=F32)
        rest = jnp.dot(low, weight[:, :columns], preferred_element_type=F32)
        part = (both[:, :columns] + both[:, columns:]) + rest
        out_ref[rows, :] = refs[pieces + 1][rows, :] + part if first else part


def vmem_call(kernel, outs, scratch, cost, *args):
    spec = pl.BlockSpec(memory_space=pltpu.VMEM)
    small = pl.BlockSpec(memory_space=pltpu.SMEM)
    return pl.pallas_call(
        kernel,
        out_shape=outs,
        in_specs=[small if arg.dtype == jnp.int32 else spec for arg in args],
        out_specs=jax.tree.map(lambda unused: spec, outs),
        scratch_shapes=scratch,
        compiler_params=pltpu.CompilerParams(vmem_limit_bytes=VMEM_GRANT),
        cost_estimate=pl.CostEstimate(flops=int(cost * 1e9), bytes_accessed=1 << 20, transcendentals=0),
    )(*args)


def to_sibling(value):
    count = lax.axis_size("head")
    return lax.ppermute(value, "head", [(source, source ^ 1) for source in range(count)])


def to_chips(value):
    count = lax.axis_size("head")
    return [
        lax.ppermute(
            value, "head", [(source, (source + 2 * step) % count) for source in range(count)]
        )
        for step in range(1, count // 2)
    ]


def after(value, *earlier):
    return lax.optimization_barrier((value, *earlier))


def shards(tokens, w_proj, w_mix, conv_w, rates, doc_start, norm_gain, w_out):
    tok_rows, depth = tokens.shape
    width = w_proj.shape[1] // 4
    features = w_proj.shape[0]
    columns = 4 * width + CHUNK
    heads, me = lax.axis_size("head"), lax.axis_index("head")
    blocks, my_index = lax.axis_size("ctx"), lax.axis_index("ctx")
    remote = [(me + heads - 2 * step) % heads for step in range(1, heads // 2)]
    order = [me, me ^ 1] + remote + [index ^ 1 for index in remote]
    index = jnp.stack(order).astype(jnp.int32)
    count = heads - 2
    like = lambda *shape: jax.ShapeDtypeStruct(shape, F32)

    half = tok_rows // 2
    cut = half - RIM
    late = to_chips(tokens[cut:])
    beside = to_sibling(tokens)
    weight, own_weight = vmem_call(
        prepare_kernel,
        [jax.ShapeDtypeStruct((features, 2 * columns), BF16),
         jax.ShapeDtypeStruct((w_out.shape[0], 2 * w_out.shape[1]), BF16)],
        [], 3, w_proj, w_mix.T, w_out,
    )
    base = vmem_call(base_kernel, like(tok_rows, columns), [], 3, index, tokens, beside, weight)
    early_rows, base = after(tokens[:cut], base)
    early = to_chips(early_rows)
    late, base = after(late, base)
    late_on = [to_sibling(value) for value in late]
    raw_late = vmem_call(
        functools.partial(late_kernel, count, cut), like(tok_rows - cut, columns), [], 2,
        index, *late, *late_on, base, weight,
    )
    rim = lax.ppermute(
        raw_late[tok_rows - cut - RIM :, : 3 * width], "ctx",
        [(source, source + 1) for source in range(blocks - 1)],
    )
    docs = doc_start.astype(F32).reshape(tok_rows // CHUNK, CHUNK)
    rate = rates[:, None]
    outs = [like(half, width)] * 5 + [like(half // CHUNK, 2, width, width), like(2, width, width)]
    later = vmem_call(
        functools.partial(later_kernel, half // CHUNK), outs, [], 4, raw_late, conv_w, rate, docs
    )
    early, pair_late, rim = after(early, later[6], rim)
    early_on = [to_sibling(value) for value in early]
    raw_early, *earlier = vmem_call(
        functools.partial(earlier_kernel, count), [like(half + RIM, columns)] + outs, [], 5,
        index, *early, *early_on, base, weight, rim, raw_late, pair_late, conv_w, rate, docs,
    )

    pair = earlier[6]
    carry = jnp.eye(width, dtype=F32)
    bits = blocks.bit_length() - 1
    levels = []
    moved = None
    for bit in range(0, bits - 1, 2):
        others = [
            lax.ppermute(
                pair, "ctx", [(source, source ^ (mask << bit)) for source in range(blocks)]
            )
            for mask in (1, 2, 3)
        ]
        flags = jnp.stack([my_index >> bit & 1, my_index >> (bit + 1) & 1]).astype(jnp.int32)
        pair, level, carry = vmem_call(
            four_kernel, [like(2, width, width)] * 2 + [like(width, width)],
            [pltpu.VMEM((4, 2, width, width), F32)], 1,
            flags, pair, *others, carry,
        )
        levels.append(level)
    fields = vmem_call(
        functools.partial(query_kernel, 2), [like(tok_rows, width)] * 4, [], 5,
        raw_early, *earlier[:6], raw_late, *later[:6], conv_w,
    )
    single = []
    if bits % 2:
        reach = blocks // 2
        single = [
            carry,
            lax.ppermute(pair[1], "ctx", [(source, source + reach) for source in range(reach)]),
        ]
    normed = vmem_call(
        functools.partial(mix_kernel, len(levels), bool(single)), like(tok_rows, width), [], 1,
        *fields, norm_gain[None, :], *levels, *single,
    )
    far = to_chips(normed)
    near = to_sibling(normed)
    out_shape = like(tok_rows, w_out.shape[1])
    total = vmem_call(
        functools.partial(out_kernel, 2, 0), out_shape, [], 2, index, normed, near, own_weight
    )
    far, total = after(far, total)
    far_on = [to_sibling(value) for value in far]
    return vmem_call(
        functools.partial(out_kernel, count, 2), out_shape, [], 2,
        index, *far, *far_on, own_weight, total,
    )


def solution(mesh):
    placed = (
        P("ctx", "head"),
        P(None, "head"),
        P(None, "head"),
        P(None, "head"),
        P("head"),
        P("ctx"),
        P("head"),
        P(None, "head"),
    )
    return jax.shard_map(
        shards, mesh=mesh, in_specs=placed, out_specs=P("ctx", "head"), check_vma=False
    )
```

```python
import functools

import jax
import jax.numpy as jnp
from jax import lax
from jax.experimental import pallas as pl
from jax.experimental.pallas import tpu as pltpu
from jax.sharding import PartitionSpec as P

CHUNK = 128
RIM = 16
VMEM_GRANT = 16 << 20
F32 = jnp.float32
BF16 = jnp.bfloat16


def halves(value):
    high = value.astype(BF16)
    return high, (value - high.astype(F32)).astype(BF16)


def left_parts(value):
    return jnp.concatenate(halves(value), axis=1)


def right_parts(value):
    row = jnp.concatenate(halves(value), axis=1)
    return jnp.concatenate([row, row], axis=0)


def parts_dot(left, right):
    both = jnp.dot(left, right, preferred_element_type=F32)
    half = both.shape[1] // 2
    return both[:, :half] + both[:, half:]


def product(left, right):
    return parts_dot(left_parts(left), right_parts(right))


def softplus(value):
    return jnp.maximum(value, 0.0) + jnp.log1p(jnp.exp(-jnp.abs(value)))


def sigmoid(value):
    return 1.0 / (1.0 + jnp.exp(-value))


def unit_lower_inverse(lowers, row, col):
    size = lowers[0].shape[0]
    eye = jnp.where(row == col, 1.0, 0.0).astype(F32)
    inverses = [eye - jnp.where((row >> 1) == (col >> 1), lower, 0.0) for lower in lowers]
    lower_parts = [halves(lower) for lower in lowers]
    step = 1
    while 2 << (step - 1) < size:
        off = ((row >> (step + 1)) == (col >> (step + 1))) & ((row >> step) > (col >> step))
        lefts = [left_parts(inverse) for inverse in inverses]
        offs = [
            jnp.concatenate([jnp.where(off, part, jnp.zeros_like(part)) for part in parts], axis=1)
            for parts in lower_parts
        ]
        inner = [
            parts_dot(offdiag, right_parts(inverse)) for offdiag, inverse in zip(offs, inverses)
        ]
        inverses = [
            inverse - parts_dot(left, right_parts(value))
            for inverse, left, value in zip(inverses, lefts, inner)
        ]
        step += 1
    return inverses


def add_products(total, pieces, weight_ref, first):
    columns = weight_ref.shape[1] // 2
    for spot, piece in enumerate(pieces):
        depth = piece.shape[1]
        rows = slice((first + spot) * depth, (first + spot + 1) * depth)
        high, low = halves(piece)
        both = jnp.dot(high, weight_ref[rows, :], preferred_element_type=F32)
        rest = jnp.dot(low, weight_ref[rows, :columns], preferred_element_type=F32)
        part = (both[:, :columns] + both[:, columns:]) + rest
        total = part if total is None else total + part
    return total


def base_kernel(
    index_ref, own_ref, beside_ref, mix_ref, proj_ref,
    state_ref, query_ref, far_state_ref, far_query_ref, early_ref,
    held, near_state, near_query, sems,
):
    sources, depth, across = held.shape
    width = across // 4
    copies = []
    for source in range(sources):
        rows = pl.ds(pl.multiple_of(index_ref[source] * depth, depth), depth)
        copies.append(pltpu.make_async_copy(proj_ref.at[rows, :], held.at[source], sems.at[source]))
        copies[-1].start()
    early_ref[...] = own_ref[: early_ref.shape[0], :]
    mixes = mix_ref.shape[0]

    def split(source, state_out, query_out, base):
        copies[source].wait()
        lanes = pl.ds(pl.multiple_of(index_ref[source] * depth, depth), depth)
        for begin in range(0, depth, CHUNK):
            rows = slice(begin, begin + CHUNK)
            out = slice(base + begin, base + begin + CHUNK)
            value = held[source, rows, :]
            mixing = mix_ref[:, lanes][:, rows]
            mixing = jnp.concatenate([mixing, jnp.zeros((CHUNK - mixes, CHUNK), F32)], axis=0)
            state = jnp.concatenate([value[:, width : 3 * width], jnp.transpose(mixing)], axis=1)
            query = jnp.concatenate([value[:, :width], value[:, 3 * width :]], axis=1)
            state_out[out, :] = left_parts(state)
            query_out[out, :] = left_parts(query)

    for source in range(2):
        split(source, near_state, near_query, source * depth)
    half = own_ref.shape[0] // 2
    for rows in (slice(0, half), slice(half, 2 * half)):
        pieces = [own_ref[rows, :], beside_ref[rows, :]]
        state_ref[rows, :] = add_products(None, pieces, near_state, 0)
        query_ref[rows, :] = add_products(None, pieces, near_query, 0)
    for source in range(2, sources):
        split(source, far_state_ref, far_query_ref, (source - 2) * depth)


def late_kernel(count, begin, *refs):
    base_state, base_query, far_state, far_query, state_ref, query_ref, rim_ref = refs[count:]
    pieces = [ref[...] for ref in refs[:count]]
    width = base_query.shape[1] // 2
    state_ref[...] = add_products(base_state[begin:, :], pieces, far_state, 0)
    query_ref[...] = add_products(base_query[begin:, :], pieces, far_query, 0)
    last = state_ref.shape[0] - RIM
    rim_ref[:, :width] = query_ref[last:, :width]
    rim_ref[:, width:] = state_ref[last:, : 2 * width]


def partial_kernel(count, *refs):
    base_state, far_state, out_ref = refs[count:]
    out_ref[...] = add_products(
        base_state[: out_ref.shape[0], :], [ref[...] for ref in refs[:count]], far_state, 0
    )


def convolve(raw, start, columns, conv_ref, taps_at):
    taps = conv_ref.shape[0]
    conv = 0.0
    for tap in range(taps):
        spot = start - taps + 1 + tap
        conv = conv + conv_ref[tap : tap + 1, taps_at] * raw[spot : spot + CHUNK, columns]
    return conv * sigmoid(conv)


def unit_rows(value):
    return value * lax.rsqrt(jnp.sum(value * value, axis=1, keepdims=True) + 1e-06)


def key_pass(raw, conv_ref, rate, doc_ref, first_chunk, outs, state):
    key_ref, x_ref, y_ref, grid_ref, gamma_ref, plus_ref, chunk_ref, pair_ref = outs
    width = key_ref.shape[1]
    chunks = key_ref.shape[0] // CHUNK
    row = lax.broadcasted_iota(jnp.int32, (CHUNK, CHUNK), 0)
    col = lax.broadcasted_iota(jnp.int32, (CHUNK, CHUNK), 1)
    lower = row >= col
    tri = jnp.where(lower, 1.0, 0.0).astype(F32)
    eye = jnp.where(row == col, 1.0, 0.0).astype(F32)
    keys, values, betas, grids, gammas, tails = [], [], [], [], [], []
    for part in range(chunks):
        start = RIM + part * CHUNK
        rows = slice(part * CHUNK, (part + 1) * CHUNK)
        middle, last = slice(width, 2 * width), slice(2 * width, 3 * width)
        keys.append(unit_rows(convolve(raw, start, slice(0, width), conv_ref, middle)))
        values.append(convolve(raw, start, middle, conv_ref, last))
        mixing = raw[start : start + CHUNK, last]
        plus = softplus(mixing)
        plus_ref[rows, :] = plus
        betas.append(sigmoid(mixing[:, 0:1]))
        spot = first_chunk + part
        docs = jnp.transpose(jnp.broadcast_to(doc_ref[spot : spot + 1, :], (CHUNK, CHUNK)))
        steps = jnp.where(col == 1, -rate * plus, jnp.where(col == 0, docs, 0.0))
        sums = jnp.dot(tri, steps, precision=lax.Precision.HIGHEST, preferred_element_type=F32)
        across = jnp.transpose(sums)
        smooth, count = sums[:, 1:2], sums[:, 0:1]
        span = (smooth - across[1:2, :]) - 20.0 * (count - across[0:1, :])
        grids.append(jnp.exp(jnp.where(lower, span, -1e30)))
        gammas.append(jnp.exp(smooth - 20.0 * count))
        last = sums[CHUNK - 1 : CHUNK, :]
        tails.append(jnp.exp((last[:, 1:2] - smooth) - 20.0 * (last[:, 0:1] - count)))
        key_ref[rows, :] = keys[part]
        grid_ref[rows, :] = grids[part]
        gamma_ref[rows, :] = jnp.broadcast_to(gammas[part], (CHUNK, width))
    across_keys = [jnp.transpose(key) for key in keys]
    grams = [
        parts_dot(left_parts(key), right_parts(across)) for key, across in zip(keys, across_keys)
    ]
    lowers = [jnp.where(row > col, beta * gram, 0.0) for beta, gram in zip(betas, grams)]
    inverses = unit_lower_inverse(lowers, row, col)
    states = []
    for part in range(chunks):
        rows = slice(part * CHUNK, (part + 1) * CHUNK)
        inverse, beta = inverses[part], betas[part]
        factor_x = product(inverse, beta * keys[part])
        factor_y = product(grids[part] * inverse, beta * values[part])
        x_ref[rows, :] = factor_x
        y_ref[rows, :] = factor_y
        onto = product(
            across_keys[part], jnp.concatenate([factor_x, tails[part] * factor_y], axis=1)
        )
        trans = gammas[part][CHUNK - 1 : CHUNK, :] * (eye - onto[:, :width])
        states.append((trans, onto[:, width:]))
        chunk_ref[part, 0] = trans
        chunk_ref[part, 1] = onto[:, width:]
    for part in range(1, chunks):
        states[0] = followed(states[0], states[part])
    total = states[0] if state is None else followed(states[0], state)
    pair_ref[0] = total[0]
    pair_ref[1] = total[1]


def followed(first, second):
    width = first[0].shape[0]
    onto = product(second[0], jnp.concatenate(first, axis=1))
    return onto[:, :width], onto[:, width:] + second[1]


def later_kernel(first_chunk, raw_ref, conv_ref, rate_ref, doc_ref, *outs):
    key_pass(raw_ref, conv_ref, rate_ref[0, 0], doc_ref, first_chunk, outs, None)


def earlier_kernel(first, count, *refs):
    held, refs = refs[:count], refs[count:]
    part_ref, far_ref, rim_ref, next_ref, state_ref, conv_ref, rate_ref, doc_ref = refs[:8]
    outs, raw = refs[8:-1], refs[-1]
    rows, width = part_ref.shape[0], state_ref.shape[1]
    raw[RIM : RIM + rows, :] = add_products(
        part_ref[...], [ref[...] for ref in held], far_ref, first
    )
    raw[:RIM, : 2 * width] = rim_ref[:, width:]
    raw[RIM + rows :, :] = next_ref[:RIM, :]
    key_pass(raw, conv_ref, rate_ref[0, 0], doc_ref, 0, outs, (state_ref[0], state_ref[1]))


def query_kernel(count, *refs):
    held, refs = refs[:count], refs[count:]
    base_ref, far_ref, rim_ref, next_ref, conv_ref = refs[:5]
    fields = [(refs[5:11], 0), (refs[11:17], 1)]
    carried_ref, local_ref, gate_ref, raw = refs[17:]
    width = carried_ref.shape[1]
    rows = held[0].shape[0]
    raw[RIM : RIM + rows, :] = add_products(
        base_ref[:rows, :], [ref[...] for ref in held], far_ref, 0
    )
    raw[:RIM, :width] = rim_ref[:, :width]
    raw[RIM + rows :, :] = next_ref[:RIM, :]
    row = lax.broadcasted_iota(jnp.int32, (CHUNK, CHUNK), 0)
    col = lax.broadcasted_iota(jnp.int32, (CHUNK, CHUNK), 1)
    state = None
    base = 0
    for (key_ref, x_ref, y_ref, grid_ref, gamma_ref, chunk_ref), later in fields:
        source = next_ref if later else raw
        for part in range(key_ref.shape[0] // CHUNK):
            start = RIM + part * CHUNK
            rows = slice(part * CHUNK, (part + 1) * CHUNK)
            out = slice(base, base + CHUNK)
            base += CHUNK
            columns = slice(0, width)
            query = unit_rows(convolve(source, start, columns, conv_ref, columns))
            gate = source[start : start + CHUNK, width:]
            gate_ref[out, :] = gate * sigmoid(gate)
            overlap = product(query, jnp.transpose(key_ref[rows, :]))
            carried = gamma_ref[rows, :] * (
                query - product(jnp.where(row >= col, overlap, 0.0), x_ref[rows, :])
            )
            local = product(grid_ref[rows, :] * overlap, y_ref[rows, :])
            trans, memory = chunk_ref[part, 0], chunk_ref[part, 1]
            if state is None:
                state = (trans, memory)
            else:
                onto = product(
                    jnp.concatenate([trans, carried], axis=0), jnp.concatenate(state, axis=1)
                )
                carried = onto[CHUNK:, :width]
                local = local + onto[CHUNK:, width:]
                state = (onto[:CHUNK, :width], onto[:CHUNK, width:] + memory)
            carried_ref[out, :] = carried
            local_ref[out, :] = local


def four_kernel(bits_ref, own_ref, one_ref, two_ref, three_ref, carry_ref, group_ref, level_ref, next_ref, pairs):
    low_bit, high_bit = bits_ref[0], bits_ref[1]
    place = 2 * high_bit + low_bit
    for mask, ref in enumerate((own_ref, one_ref, two_ref, three_ref)):
        pairs[place ^ mask] = ref[...]
    width = carry_ref.shape[0]
    joined = lambda spot: jnp.concatenate([pairs[spot, 0], pairs[spot, 1]], axis=1)
    onto_low = product(pairs[1, 0], joined(0))
    onto_high = product(pairs[3, 0], joined(2))
    low_a, low_s = onto_low[:, :width], onto_low[:, width:] + pairs[1, 1]
    high_a, high_s = onto_high[:, :width], onto_high[:, width:] + pairs[3, 1]
    onto = product(high_a, jnp.concatenate([low_a, low_s], axis=1))
    group_ref[0] = onto[:, :width]
    group_ref[1] = onto[:, width:] + high_s
    carry = carry_ref[...]
    first = product(carry, jnp.concatenate([one_ref[0], one_ref[1]], axis=1))
    set_low = jnp.broadcast_to(low_bit, (width, width)) == 1
    set_high = jnp.broadcast_to(high_bit, (width, width)) == 1
    level_ref[0] = jnp.where(set_low, first[:, width:], 0.0)
    carry = jnp.where(set_low, first[:, :width], carry)
    second = product(carry, jnp.concatenate([low_a, low_s], axis=1))
    level_ref[1] = jnp.where(set_high, second[:, width:], 0.0)
    next_ref[...] = jnp.where(set_high, second[:, :width], carry)


def mix_kernel(stages, single, carried_ref, local_ref, gate_ref, low_ref, high_ref, gain_ref, *refs):
    states = [ref[spot] for ref in refs[:stages] for spot in range(ref.shape[0])]
    if single:
        states.append(product(refs[stages][...], refs[stages + 1][...]))
    normed_ref = refs[-1]
    states = [right_parts(state) for state in states]
    carried = left_parts(carried_ref[...])
    weights = jnp.concatenate([low_ref[...], high_ref[...]], axis=0)
    mixed = weights[:, 2:3] * local_ref[...]
    for level, state in enumerate(states):
        mixed = mixed + weights[:, level + 3 : level + 4] * parts_dot(carried, state)
    scale = lax.rsqrt(jnp.mean(mixed * mixed, axis=1, keepdims=True) + 1e-05)
    normed_ref[...] = mixed * scale * gain_ref[...] * gate_ref[...]


def out_kernel(pieces, first, index_ref, *refs):
    weight_ref = refs[pieces]
    parts = []
    for spot in range(pieces):
        depth = refs[spot].shape[1]
        rows = pl.ds(pl.multiple_of(index_ref[first + spot] * depth, depth), depth)
        parts.append(weight_ref[rows, :])
    weight = left_parts(jnp.concatenate(parts, axis=0))
    columns = weight.shape[1] // 2

    def block(rows):
        parts = [halves(ref[rows, :]) for ref in refs[:pieces]]
        high, low = (jnp.concatenate(part, axis=1) for part in zip(*parts))
        both = jnp.dot(high, weight, preferred_element_type=F32)
        rest = jnp.dot(low, weight[:, :columns], preferred_element_type=F32)
        return (both[:, :columns] + both[:, columns:]) + rest

    blocks = [slice(base, base + CHUNK) for base in range(0, refs[0].shape[0], CHUNK)]
    if not first:
        for rows in blocks:
            refs[-1][rows, :] = block(rows)
        return
    total_ref, out_ref, held, sems = refs[pieces + 1 :]
    copies = []
    for spot, rows in enumerate(blocks):
        held[rows, :] = total_ref[rows, :] + block(rows)
        copies.append(pltpu.make_async_copy(held.at[rows, :], out_ref.at[rows, :], sems.at[spot]))
        copies[-1].start()
    for copy in copies:
        copy.wait()


def vmem_call(kernel, outs, scratch, cost, *args, any_in=(), any_out=False):
    spec = pl.BlockSpec(memory_space=pltpu.VMEM)
    small = pl.BlockSpec(memory_space=pltpu.SMEM)
    free = pl.BlockSpec(memory_space=pl.ANY)
    return pl.pallas_call(
        kernel,
        out_shape=outs,
        in_specs=[
            free if spot in any_in else small if arg.dtype == jnp.int32 else spec
            for spot, arg in enumerate(args)
        ],
        out_specs=jax.tree.map(lambda unused: free if any_out else spec, outs),
        scratch_shapes=scratch,
        compiler_params=pltpu.CompilerParams(vmem_limit_bytes=VMEM_GRANT),
        cost_estimate=pl.CostEstimate(flops=int(cost * 1e9), bytes_accessed=1 << 20, transcendentals=0),
    )(*args)


def to_sibling(value):
    count = lax.axis_size("head")
    return lax.ppermute(value, "head", [(source, source ^ 1) for source in range(count)])


def to_chips(value):
    count = lax.axis_size("head")
    return [
        lax.ppermute(
            value, "head", [(source, (source + 2 * step) % count) for source in range(count)]
        )
        for step in range(1, count // 2)
    ]


def after(value, *earlier):
    return lax.optimization_barrier((value, *earlier))


def shards(tokens, w_proj, w_mix, conv_w, rates, doc_start, norm_gain, w_out):
    tok_rows, depth = tokens.shape
    width = w_proj.shape[1] // 4
    state_columns, query_columns = 2 * width + CHUNK, 2 * width
    heads, me = lax.axis_size("head"), lax.axis_index("head")
    blocks, my_index = lax.axis_size("ctx"), lax.axis_index("ctx")
    remote = [(me + heads - 2 * step) % heads for step in range(1, heads // 2)]
    order = [me, me ^ 1] + remote + [index ^ 1 for index in remote]
    index = jnp.stack(order).astype(jnp.int32)
    count = heads - 2
    like = lambda *shape: jax.ShapeDtypeStruct(shape, F32)
    parts = lambda *shape: jax.ShapeDtypeStruct(shape, BF16)

    half = tok_rows // 2
    cut = half - RIM
    late = to_chips(tokens[cut:])
    beside = to_sibling(tokens)
    base_state, base_query, far_state, far_query, early_rows = vmem_call(
        base_kernel,
        [like(tok_rows, state_columns), like(tok_rows, query_columns),
         parts(count * depth, 2 * state_columns), parts(count * depth, 2 * query_columns),
         like(cut, depth)],
        [pltpu.VMEM((heads, depth, 4 * width), F32),
         pltpu.VMEM((2 * depth, 2 * state_columns), BF16),
         pltpu.VMEM((2 * depth, 2 * query_columns), BF16),
         pltpu.SemaphoreType.DMA((heads,))],
        3, index, tokens, beside, w_mix.T, w_proj, any_in=(4,),
    )
    early = to_chips(early_rows)
    late, far_state = after(late, far_state)
    late_on = [to_sibling(value) for value in late]
    late_state, late_query, rim = vmem_call(
        functools.partial(late_kernel, count, cut),
        [like(tok_rows - cut, state_columns), like(tok_rows - cut, query_columns),
         like(RIM, 3 * width)],
        [], 2, *late, *late_on, base_state, base_query, far_state, far_query,
    )
    rim = lax.ppermute(rim, "ctx", [(source, source + 1) for source in range(blocks - 1)])
    docs = doc_start.astype(F32).reshape(tok_rows // CHUNK, CHUNK)
    rate = rates[:, None]
    outs = [like(half, width)] * 6 + [like(half // CHUNK, 2, width, width), like(2, width, width)]
    later = vmem_call(
        functools.partial(later_kernel, half // CHUNK), outs, [], 4, late_state, conv_w, rate, docs
    )
    early, pair_late, rim = after(early, later[7], rim)
    early_on = [to_sibling(value) for value in early]
    partial = vmem_call(
        functools.partial(partial_kernel, len(early)), like(cut, state_columns), [], 1,
        *early, base_state, far_state,
    )
    earlier = vmem_call(
        functools.partial(earlier_kernel, len(early), len(early)), outs,
        [pltpu.VMEM((half + RIM, state_columns), F32)], 5,
        *early_on, partial, far_state, rim, late_state, pair_late, conv_w, rate, docs,
    )

    pair = earlier[7]
    carry = jnp.eye(width, dtype=F32)
    bits = blocks.bit_length() - 1
    levels = []
    for bit in range(0, bits - 1, 2):
        others = [
            lax.ppermute(
                pair, "ctx", [(source, source ^ (mask << bit)) for source in range(blocks)]
            )
            for mask in (1, 2, 3)
        ]
        flags = jnp.stack([my_index >> bit & 1, my_index >> (bit + 1) & 1]).astype(jnp.int32)
        pair, level, carry = vmem_call(
            four_kernel, [like(2, width, width)] * 2 + [like(width, width)],
            [pltpu.VMEM((4, 2, width, width), F32)], 1,
            flags, pair, *others, carry,
        )
        levels.append(level)
    fields = vmem_call(
        functools.partial(query_kernel, count), [like(tok_rows, width)] * 3,
        [pltpu.VMEM((half + RIM, query_columns), F32)], 5,
        *early, *early_on, base_query, far_query, rim, late_query, conv_w,
        *earlier[:5], earlier[6], *later[:5], later[6],
    )
    single = []
    if bits % 2:
        reach = blocks // 2
        single = [
            carry,
            lax.ppermute(pair[1], "ctx", [(source, source + reach) for source in range(reach)]),
        ]
    normed = vmem_call(
        functools.partial(mix_kernel, len(levels), bool(single)), like(tok_rows, width), [], 1,
        *fields, earlier[5], later[5], norm_gain[None, :], *levels, *single,
    )
    far = to_chips(normed)
    near = to_sibling(normed)
    out_shape = like(tok_rows, w_out.shape[1])
    total = vmem_call(
        functools.partial(out_kernel, 2, 0), out_shape, [], 2, index, normed, near, w_out
    )
    far, total = after(far, total)
    far_on = [to_sibling(value) for value in far]
    return vmem_call(
        functools.partial(out_kernel, count, 2), out_shape,
        [pltpu.VMEM(out_shape.shape, F32), pltpu.SemaphoreType.DMA((tok_rows // CHUNK,))], 2,
        index, *far, *far_on, w_out, total, any_out=True,
    )


def solution(mesh):
    placed = (
        P("ctx", "head"),
        P(None, "head"),
        P(None, "head"),
        P(None, "head"),
        P("head"),
        P("ctx"),
        P("head"),
        P(None, "head"),
    )
    return jax.shard_map(
        shards, mesh=mesh, in_specs=placed, out_specs=P("ctx", "head"), check_vma=False
    )
```

```python
import functools

import jax
import jax.numpy as jnp
from jax import lax
from jax.experimental import pallas as pl
from jax.experimental.pallas import tpu as pltpu
from jax.sharding import PartitionSpec as P

CHUNK = 128
RIM = 16
VMEM_GRANT = 16 << 20
F32 = jnp.float32
BF16 = jnp.bfloat16


def halves(value):
    high = value.astype(BF16)
    return high, (value - high.astype(F32)).astype(BF16)


def left_parts(value):
    return jnp.concatenate(halves(value), axis=1)


def right_parts(value):
    row = jnp.concatenate(halves(value), axis=1)
    return jnp.concatenate([row, row], axis=0)


def parts_dot(left, right):
    both = jnp.dot(left, right, preferred_element_type=F32)
    half = both.shape[1] // 2
    return both[:, :half] + both[:, half:]


def product(left, right):
    return parts_dot(left_parts(left), right_parts(right))


def softplus(value):
    return jnp.maximum(value, 0.0) + jnp.log1p(jnp.exp(-jnp.abs(value)))


def sigmoid(value):
    return 1.0 / (1.0 + jnp.exp(-value))


def unit_lower_inverse(lowers, row, col):
    size = lowers[0].shape[0]
    eye = jnp.where(row == col, 1.0, 0.0).astype(F32)
    inverses = [eye - jnp.where((row >> 1) == (col >> 1), lower, 0.0) for lower in lowers]
    lower_parts = [halves(lower) for lower in lowers]
    step = 1
    while 2 << (step - 1) < size:
        off = ((row >> (step + 1)) == (col >> (step + 1))) & ((row >> step) > (col >> step))
        lefts = [left_parts(inverse) for inverse in inverses]
        offs = [
            jnp.concatenate([jnp.where(off, part, jnp.zeros_like(part)) for part in parts], axis=1)
            for parts in lower_parts
        ]
        inner = [
            parts_dot(offdiag, right_parts(inverse)) for offdiag, inverse in zip(offs, inverses)
        ]
        inverses = [
            inverse - parts_dot(left, right_parts(value))
            for inverse, left, value in zip(inverses, lefts, inner)
        ]
        step += 1
    return inverses


def add_products(total, pieces, weight_ref, first):
    columns = weight_ref.shape[1] // 2
    for spot, piece in enumerate(pieces):
        depth = piece.shape[1]
        rows = slice((first + spot) * depth, (first + spot + 1) * depth)
        high, low = halves(piece)
        both = jnp.dot(high, weight_ref[rows, :], preferred_element_type=F32)
        rest = jnp.dot(low, weight_ref[rows, :columns], preferred_element_type=F32)
        part = (both[:, :columns] + both[:, columns:]) + rest
        total = part if total is None else total + part
    return total


def base_kernel(
    index_ref, own_ref, beside_ref, mix_ref, proj_ref,
    state_ref, query_ref, far_state_ref, far_query_ref, early_ref,
    held, near_state, near_query, sems,
):
    sources, depth, across = held.shape
    width = across // 4
    copies = []
    for source in range(sources):
        rows = pl.ds(pl.multiple_of(index_ref[source] * depth, depth), depth)
        copies.append(pltpu.make_async_copy(proj_ref.at[rows, :], held.at[source], sems.at[source]))
        copies[-1].start()
    early_ref[...] = own_ref[: early_ref.shape[0], :]
    mixes = mix_ref.shape[0]

    def split(source, state_out, query_out, base):
        copies[source].wait()
        lanes = pl.ds(pl.multiple_of(index_ref[source] * depth, depth), depth)
        for begin in range(0, depth, CHUNK):
            rows = slice(begin, begin + CHUNK)
            out = slice(base + begin, base + begin + CHUNK)
            value = held[source, rows, :]
            mixing = mix_ref[:, lanes][:, rows]
            mixing = jnp.concatenate([mixing, jnp.zeros((CHUNK - mixes, CHUNK), F32)], axis=0)
            state = jnp.concatenate([value[:, width : 3 * width], jnp.transpose(mixing)], axis=1)
            query = jnp.concatenate([value[:, :width], value[:, 3 * width :]], axis=1)
            state_out[out, :] = left_parts(state)
            query_out[out, :] = left_parts(query)

    for source in range(2):
        split(source, near_state, near_query, source * depth)
    half = own_ref.shape[0] // 2
    for rows in (slice(0, half), slice(half, 2 * half)):
        pieces = [own_ref[rows, :], beside_ref[rows, :]]
        state_ref[rows, :] = add_products(None, pieces, near_state, 0)
        query_ref[rows, :] = add_products(None, pieces, near_query, 0)
    for source in range(2, sources):
        split(source, far_state_ref, far_query_ref, (source - 2) * depth)


def late_kernel(count, begin, *refs):
    base_state, base_query, far_state, far_query, state_ref, query_ref, rim_ref = refs[count:]
    pieces = [ref[...] for ref in refs[:count]]
    width = base_query.shape[1] // 2
    state_ref[...] = add_products(base_state[begin:, :], pieces, far_state, 0)
    query_ref[...] = add_products(base_query[begin:, :], pieces, far_query, 0)
    last = state_ref.shape[0] - RIM
    rim_ref[:, :width] = query_ref[last:, :width]
    rim_ref[:, width:] = state_ref[last:, : 2 * width]


def partial_kernel(count, *refs):
    base_state, far_state, out_ref = refs[count:]
    out_ref[...] = add_products(
        base_state[: out_ref.shape[0], :], [ref[...] for ref in refs[:count]], far_state, 0
    )


def convolve(raw, start, columns, conv_ref, taps_at):
    taps = conv_ref.shape[0]
    conv = 0.0
    for tap in range(taps):
        spot = start - taps + 1 + tap
        conv = conv + conv_ref[tap : tap + 1, taps_at] * raw[spot : spot + CHUNK, columns]
    return conv * sigmoid(conv)


def unit_rows(value):
    return value * lax.rsqrt(jnp.sum(value * value, axis=1, keepdims=True) + 1e-06)


def key_pass(raw, conv_ref, rate, doc_ref, first_chunk, outs, state):
    key_ref, x_ref, y_ref, grid_ref, gamma_ref, plus_ref, chunk_ref, pair_ref = outs
    width = key_ref.shape[1]
    chunks = key_ref.shape[0] // CHUNK
    row = lax.broadcasted_iota(jnp.int32, (CHUNK, CHUNK), 0)
    col = lax.broadcasted_iota(jnp.int32, (CHUNK, CHUNK), 1)
    lower = row >= col
    tri = jnp.where(lower, 1.0, 0.0).astype(F32)
    eye = jnp.where(row == col, 1.0, 0.0).astype(F32)
    keys, values, betas, grids, gammas, tails = [], [], [], [], [], []
    for part in range(chunks):
        start = RIM + part * CHUNK
        rows = slice(part * CHUNK, (part + 1) * CHUNK)
        middle, last = slice(width, 2 * width), slice(2 * width, 3 * width)
        keys.append(unit_rows(convolve(raw, start, slice(0, width), conv_ref, middle)))
        values.append(convolve(raw, start, middle, conv_ref, last))
        mixing = raw[start : start + CHUNK, last]
        plus = softplus(mixing)
        plus_ref[rows, :] = plus
        betas.append(sigmoid(mixing[:, 0:1]))
        spot = first_chunk + part
        docs = jnp.broadcast_to(doc_ref[spot : spot + 1, :].astype(F32), (CHUNK, CHUNK))
        docs = jnp.transpose(docs)
        steps = jnp.where(col == 1, -rate * plus, jnp.where(col == 0, docs, 0.0))
        sums = jnp.dot(tri, steps, precision=lax.Precision.HIGHEST, preferred_element_type=F32)
        across = jnp.transpose(sums)
        smooth, count = sums[:, 1:2], sums[:, 0:1]
        span = (smooth - across[1:2, :]) - 20.0 * (count - across[0:1, :])
        grids.append(jnp.exp(jnp.where(lower, span, -1e30)))
        gammas.append(jnp.exp(smooth - 20.0 * count))
        last = sums[CHUNK - 1 : CHUNK, :]
        tails.append(jnp.exp((last[:, 1:2] - smooth) - 20.0 * (last[:, 0:1] - count)))
        key_ref[rows, :] = keys[part]
        grid_ref[rows, :] = grids[part]
        gamma_ref[rows, :] = jnp.broadcast_to(gammas[part], (CHUNK, width))
    across_keys = [jnp.transpose(key) for key in keys]
    grams = [
        parts_dot(left_parts(key), right_parts(across)) for key, across in zip(keys, across_keys)
    ]
    lowers = [jnp.where(row > col, beta * gram, 0.0) for beta, gram in zip(betas, grams)]
    inverses = unit_lower_inverse(lowers, row, col)
    states = []
    for part in range(chunks):
        rows = slice(part * CHUNK, (part + 1) * CHUNK)
        inverse, beta = inverses[part], betas[part]
        factor_x = product(inverse, beta * keys[part])
        factor_y = product(grids[part] * inverse, beta * values[part])
        x_ref[rows, :] = factor_x
        y_ref[rows, :] = factor_y
        onto = product(
            across_keys[part], jnp.concatenate([factor_x, tails[part] * factor_y], axis=1)
        )
        trans = gammas[part][CHUNK - 1 : CHUNK, :] * (eye - onto[:, :width])
        states.append((trans, onto[:, width:]))
        chunk_ref[part, 0] = trans
        chunk_ref[part, 1] = onto[:, width:]
    for part in range(1, chunks):
        states[0] = followed(states[0], states[part])
    total = states[0] if state is None else followed(states[0], state)
    pair_ref[0] = total[0]
    pair_ref[1] = total[1]


def followed(first, second):
    width = first[0].shape[0]
    onto = product(second[0], jnp.concatenate(first, axis=1))
    return onto[:, :width], onto[:, width:] + second[1]


def later_kernel(first_chunk, raw_ref, conv_ref, rate_ref, doc_ref, *outs):
    key_pass(raw_ref, conv_ref, rate_ref[0, 0], doc_ref, first_chunk, outs, None)


def earlier_kernel(first, count, *refs):
    held, refs = refs[:count], refs[count:]
    part_ref, far_ref, rim_ref, next_ref, state_ref, conv_ref, rate_ref, doc_ref = refs[:8]
    outs, raw = refs[8:-1], refs[-1]
    rows, width = part_ref.shape[0], state_ref.shape[1]
    raw[RIM : RIM + rows, :] = add_products(
        part_ref[...], [ref[...] for ref in held], far_ref, first
    )
    raw[:RIM, : 2 * width] = rim_ref[:, width:]
    raw[RIM + rows :, :] = next_ref[:RIM, :]
    key_pass(raw, conv_ref, rate_ref[0, 0], doc_ref, 0, outs, (state_ref[0], state_ref[1]))


def query_kernel(count, *refs):
    held, refs = refs[:count], refs[count:]
    base_ref, far_ref, rim_ref, next_ref, conv_ref = refs[:5]
    fields = [(refs[5:11], 0), (refs[11:17], 1)]
    carried_ref, local_ref, gate_ref, raw = refs[17:]
    width = carried_ref.shape[1]
    rows = held[0].shape[0]
    raw[RIM : RIM + rows, :] = add_products(
        base_ref[:rows, :], [ref[...] for ref in held], far_ref, 0
    )
    raw[:RIM, :width] = rim_ref[:, :width]
    raw[RIM + rows :, :] = next_ref[:RIM, :]
    row = lax.broadcasted_iota(jnp.int32, (CHUNK, CHUNK), 0)
    col = lax.broadcasted_iota(jnp.int32, (CHUNK, CHUNK), 1)
    state = None
    base = 0
    for (key_ref, x_ref, y_ref, grid_ref, gamma_ref, chunk_ref), later in fields:
        source = next_ref if later else raw
        for part in range(key_ref.shape[0] // CHUNK):
            start = RIM + part * CHUNK
            rows = slice(part * CHUNK, (part + 1) * CHUNK)
            out = slice(base, base + CHUNK)
            base += CHUNK
            columns = slice(0, width)
            query = unit_rows(convolve(source, start, columns, conv_ref, columns))
            gate = source[start : start + CHUNK, width:]
            gate_ref[out, :] = gate * sigmoid(gate)
            overlap = product(query, jnp.transpose(key_ref[rows, :]))
            carried = gamma_ref[rows, :] * (
                query - product(jnp.where(row >= col, overlap, 0.0), x_ref[rows, :])
            )
            local = product(grid_ref[rows, :] * overlap, y_ref[rows, :])
            trans, memory = chunk_ref[part, 0], chunk_ref[part, 1]
            if state is None:
                state = (trans, memory)
            else:
                onto = product(
                    jnp.concatenate([trans, carried], axis=0), jnp.concatenate(state, axis=1)
                )
                carried = onto[CHUNK:, :width]
                local = local + onto[CHUNK:, width:]
                state = (onto[:CHUNK, :width], onto[:CHUNK, width:] + memory)
            carried_ref[out, :] = carried
            local_ref[out, :] = local


def four_kernel(first_bit, carried, last, bits_ref, own_ref, one_ref, two_ref, three_ref, *refs):
    group_ref, level_ref, next_ref, pairs = refs[-4:]
    low_bit, high_bit = bits_ref[first_bit], bits_ref[first_bit + 1]
    place = 2 * high_bit + low_bit
    for mask, ref in enumerate((own_ref, one_ref, two_ref, three_ref)):
        pairs[place ^ mask] = ref[...]
    width = next_ref.shape[0]
    joined = lambda spot: jnp.concatenate([pairs[spot, 0], pairs[spot, 1]], axis=1)
    onto_low = product(pairs[1, 0], joined(0))
    onto_high = product(pairs[3, 0], joined(2))
    low_a, low_s = onto_low[:, :width], onto_low[:, width:] + pairs[1, 1]
    high_a, high_s = onto_high[:, :width], onto_high[:, width:] + pairs[3, 1]
    if last:
        group_ref[...] = product(high_a, low_s) + high_s
    else:
        onto = product(high_a, jnp.concatenate([low_a, low_s], axis=1))
        group_ref[0] = onto[:, :width]
        group_ref[1] = onto[:, width:] + high_s
    set_low = jnp.broadcast_to(low_bit, (width, width)) == 1
    set_high = jnp.broadcast_to(high_bit, (width, width)) == 1
    if carried:
        carry = refs[0][...]
        first = product(carry, jnp.concatenate([one_ref[0], one_ref[1]], axis=1))
        first_a, first_s = first[:, :width], first[:, width:]
    else:
        row = lax.broadcasted_iota(jnp.int32, (width, width), 0)
        col = lax.broadcasted_iota(jnp.int32, (width, width), 1)
        carry = jnp.where(row == col, 1.0, 0.0).astype(F32)
        first_a, first_s = one_ref[0], one_ref[1]
    level_ref[0] = jnp.where(set_low, first_s, 0.0)
    carry = jnp.where(set_low, first_a, carry)
    second = product(carry, jnp.concatenate([low_a, low_s], axis=1))
    level_ref[1] = jnp.where(set_high, second[:, width:], 0.0)
    next_ref[...] = jnp.where(set_high, second[:, :width], carry)


def mix_kernel(stages, single, carried_ref, local_ref, gate_ref, low_ref, high_ref, gain_ref, *refs):
    states = [ref[spot] for ref in refs[:stages] for spot in range(ref.shape[0])]
    if single:
        states.append(product(refs[stages][...], refs[stages + 1][...]))
    normed_ref = refs[-1]
    states = [right_parts(state) for state in states]
    carried = left_parts(carried_ref[...])
    weights = jnp.concatenate([low_ref[...], high_ref[...]], axis=0)
    mixed = weights[:, 2:3] * local_ref[...]
    for level, state in enumerate(states):
        mixed = mixed + weights[:, level + 3 : level + 4] * parts_dot(carried, state)
    scale = lax.rsqrt(jnp.mean(mixed * mixed, axis=1, keepdims=True) + 1e-05)
    normed_ref[...] = mixed * scale * gain_ref[...] * gate_ref[...]


def out_kernel(pieces, first, index_ref, *refs):
    weight_ref = refs[pieces]
    parts = []
    for spot in range(pieces):
        depth = refs[spot].shape[1]
        rows = pl.ds(pl.multiple_of(index_ref[first + spot] * depth, depth), depth)
        parts.append(weight_ref[rows, :])
    weight = left_parts(jnp.concatenate(parts, axis=0))
    columns = weight.shape[1] // 2

    def block(rows):
        parts = [halves(ref[rows, :]) for ref in refs[:pieces]]
        high, low = (jnp.concatenate(part, axis=1) for part in zip(*parts))
        both = jnp.dot(high, weight, preferred_element_type=F32)
        rest = jnp.dot(low, weight[:, :columns], preferred_element_type=F32)
        return (both[:, :columns] + both[:, columns:]) + rest

    blocks = [slice(base, base + CHUNK) for base in range(0, refs[0].shape[0], CHUNK)]
    if not first:
        for rows in blocks:
            refs[-1][rows, :] = block(rows)
        return
    total_ref, out_ref, held, sems = refs[pieces + 1 :]
    copies = []
    for spot, rows in enumerate(blocks):
        held[rows, :] = total_ref[rows, :] + block(rows)
        copies.append(pltpu.make_async_copy(held.at[rows, :], out_ref.at[rows, :], sems.at[spot]))
        copies[-1].start()
    for copy in copies:
        copy.wait()


def vmem_call(kernel, outs, scratch, cost, *args, any_in=(), any_out=False):
    spec = pl.BlockSpec(memory_space=pltpu.VMEM)
    small = pl.BlockSpec(memory_space=pltpu.SMEM)
    free = pl.BlockSpec(memory_space=pl.ANY)
    return pl.pallas_call(
        kernel,
        out_shape=outs,
        in_specs=[
            free if spot in any_in else small if arg.dtype == jnp.int32 and arg.ndim == 1 else spec
            for spot, arg in enumerate(args)
        ],
        out_specs=jax.tree.map(lambda unused: free if any_out else spec, outs),
        scratch_shapes=scratch,
        compiler_params=pltpu.CompilerParams(vmem_limit_bytes=VMEM_GRANT),
        cost_estimate=pl.CostEstimate(flops=int(cost * 1e9), bytes_accessed=1 << 20, transcendentals=0),
    )(*args)


def to_sibling(value):
    count = lax.axis_size("head")
    return lax.ppermute(value, "head", [(source, source ^ 1) for source in range(count)])


def to_chips(value):
    count = lax.axis_size("head")
    return [
        lax.ppermute(
            value, "head", [(source, (source + 2 * step) % count) for source in range(count)]
        )
        for step in range(1, count // 2)
    ]


def after(value, *earlier):
    return lax.optimization_barrier((value, *earlier))


def shards(tokens, w_proj, w_mix, conv_w, rates, doc_start, norm_gain, w_out):
    tok_rows, depth = tokens.shape
    width = w_proj.shape[1] // 4
    state_columns, query_columns = 2 * width + CHUNK, 2 * width
    heads, me = lax.axis_size("head"), lax.axis_index("head")
    blocks, my_index = lax.axis_size("ctx"), lax.axis_index("ctx")
    remote = [(me + heads - 2 * step) % heads for step in range(1, heads // 2)]
    order = [me, me ^ 1] + remote + [index ^ 1 for index in remote]
    bits = blocks.bit_length() - 1
    flags = [my_index >> bit & 1 for bit in range(bits)]
    index = jnp.stack(order + flags).astype(jnp.int32)
    count = heads - 2
    like = lambda *shape: jax.ShapeDtypeStruct(shape, F32)
    parts = lambda *shape: jax.ShapeDtypeStruct(shape, BF16)

    half = tok_rows // 2
    cut = half - RIM
    late = to_chips(tokens[cut:])
    beside = to_sibling(tokens)
    base_state, base_query, far_state, far_query, early_rows = vmem_call(
        base_kernel,
        [like(tok_rows, state_columns), like(tok_rows, query_columns),
         parts(count * depth, 2 * state_columns), parts(count * depth, 2 * query_columns),
         like(cut, depth)],
        [pltpu.VMEM((heads, depth, 4 * width), F32),
         pltpu.VMEM((2 * depth, 2 * state_columns), BF16),
         pltpu.VMEM((2 * depth, 2 * query_columns), BF16),
         pltpu.SemaphoreType.DMA((heads,))],
        3, index, tokens, beside, w_mix.T, w_proj, any_in=(4,),
    )
    early = to_chips(early_rows)
    late, far_state = after(late, far_state)
    late_on = [to_sibling(value) for value in late]
    late_state, late_query, rim = vmem_call(
        functools.partial(late_kernel, count, cut),
        [like(tok_rows - cut, state_columns), like(tok_rows - cut, query_columns),
         like(RIM, 3 * width)],
        [], 0.5, *late, *late_on, base_state, base_query, far_state, far_query,
    )
    rim = lax.ppermute(rim, "ctx", [(source, source + 1) for source in range(blocks - 1)])
    docs = doc_start.reshape(tok_rows // CHUNK, CHUNK)
    rate = rates[:, None]
    outs = [like(half, width)] * 6 + [like(half // CHUNK, 2, width, width), like(2, width, width)]
    later = vmem_call(
        functools.partial(later_kernel, half // CHUNK), outs, [], 0.5, late_state, conv_w, rate, docs
    )
    early, pair_late, rim = after(early, later[7], rim)
    early_on = [to_sibling(value) for value in early]
    partial = vmem_call(
        functools.partial(partial_kernel, len(early)), like(cut, state_columns), [], 1,
        *early, base_state, far_state,
    )
    earlier = vmem_call(
        functools.partial(earlier_kernel, len(early), len(early)), outs,
        [pltpu.VMEM((half + RIM, state_columns), F32)], 5,
        *early_on, partial, far_state, rim, late_state, pair_late, conv_w, rate, docs,
    )

    pair = earlier[7]
    carry = ()
    levels = []
    for bit in range(0, bits - 1, 2):
        others = [
            lax.ppermute(
                pair, "ctx", [(source, source ^ (mask << bit)) for source in range(blocks)]
            )
            for mask in (1, 2, 3)
        ]
        last = bit + 2 >= bits - 1 and bits % 2
        group = [like(width, width)] if last else [like(2, width, width)]
        pair, level, *carry = vmem_call(
            functools.partial(four_kernel, heads + bit, bool(carry), last),
            group + [like(2, width, width), like(width, width)],
            [pltpu.VMEM((4, 2, width, width), F32)], 1,
            index, pair, *others, *carry,
        )
        levels.append(level)
    fields = vmem_call(
        functools.partial(query_kernel, count), [like(tok_rows, width)] * 3,
        [pltpu.VMEM((half + RIM, query_columns), F32)], 5,
        *early, *early_on, base_query, far_query, rim, late_query, conv_w,
        *earlier[:5], earlier[6], *later[:5], later[6],
    )
    single = []
    if bits % 2:
        reach = blocks // 2
        single = [
            *(carry or [jnp.eye(width, dtype=F32)]),
            lax.ppermute(
                pair if carry else pair[1],
                "ctx", [(source, source + reach) for source in range(reach)],
            ),
        ]
    normed = vmem_call(
        functools.partial(mix_kernel, len(levels), bool(single)), like(tok_rows, width), [], 1,
        *fields, earlier[5], later[5], norm_gain[None, :], *levels, *single,
    )
    far = to_chips(normed)
    near = to_sibling(normed)
    out_shape = like(tok_rows, w_out.shape[1])
    total = vmem_call(
        functools.partial(out_kernel, 2, 0), out_shape, [], 2, index, normed, near, w_out
    )
    far, total = after(far, total)
    far_on = [to_sibling(value) for value in far]
    return vmem_call(
        functools.partial(out_kernel, count, 2), out_shape,
        [pltpu.VMEM(out_shape.shape, F32), pltpu.SemaphoreType.DMA((tok_rows // CHUNK,))], 2,
        index, *far, *far_on, w_out, total, any_out=True,
    )


def solution(mesh):
    placed = (
        P("ctx", "head"),
        P(None, "head"),
        P(None, "head"),
        P(None, "head"),
        P("head"),
        P("ctx"),
        P("head"),
        P(None, "head"),
    )
    return jax.shard_map(
        shards, mesh=mesh, in_specs=placed, out_specs=P("ctx", "head"), check_vma=False
    )
```

```python
import functools

import jax
import jax.numpy as jnp
from jax import lax
from jax.experimental import pallas as pl
from jax.experimental.pallas import tpu as pltpu
from jax.sharding import PartitionSpec as P

CHUNK = 128
RIM = 16
VMEM_GRANT = 16 << 20
F32 = jnp.float32
BF16 = jnp.bfloat16


def halves(value):
    high = value.astype(BF16)
    return high, (value - high.astype(F32)).astype(BF16)


def left_parts(value):
    return jnp.concatenate(halves(value), axis=1)


def right_parts(value):
    row = jnp.concatenate(halves(value), axis=1)
    return jnp.concatenate([row, row], axis=0)


def parts_dot(left, right):
    both = jnp.dot(left, right, preferred_element_type=F32)
    half = both.shape[1] // 2
    return both[:, :half] + both[:, half:]


def product(left, right):
    return parts_dot(left_parts(left), right_parts(right))


def softplus(value):
    return jnp.maximum(value, 0.0) + jnp.log1p(jnp.exp(-jnp.abs(value)))


def sigmoid(value):
    return 1.0 / (1.0 + jnp.exp(-value))


def unit_lower_inverse(lowers, row, col):
    size = lowers[0].shape[0]
    eye = jnp.where(row == col, 1.0, 0.0).astype(F32)
    inverses = [eye - jnp.where((row >> 1) == (col >> 1), lower, 0.0) for lower in lowers]
    lower_parts = [halves(lower) for lower in lowers]
    step = 1
    while 1 << step < size:
        off = ((row >> (step + 2)) == (col >> (step + 2))) & ((row >> step) > (col >> step))
        offs = [
            jnp.concatenate([jnp.where(off, part, jnp.zeros_like(part)) for part in parts], axis=1)
            for parts in lower_parts
        ]
        onto = [parts_dot(left, right_parts(inverse)) for left, inverse in zip(offs, inverses)]
        rights = [right_parts(value) for value in onto]
        squares = [parts_dot(left_parts(value), right) for value, right in zip(onto, rights)]
        firsts = [
            inverse - parts_dot(left_parts(inverse), right)
            for inverse, right in zip(inverses, rights)
        ]
        inverses = [first + product(first, square) for first, square in zip(firsts, squares)]
        step += 2
    return inverses


def add_products(total, pieces, weight_ref, first):
    columns = weight_ref.shape[1] // 2
    for spot, piece in enumerate(pieces):
        depth = piece.shape[1]
        rows = slice((first + spot) * depth, (first + spot + 1) * depth)
        high, low = halves(piece)
        both = jnp.dot(high, weight_ref[rows, :], preferred_element_type=F32)
        rest = jnp.dot(low, weight_ref[rows, :columns], preferred_element_type=F32)
        part = (both[:, :columns] + both[:, columns:]) + rest
        total = part if total is None else total + part
    return total


def base_kernel(
    index_ref, own_ref, beside_ref, mix_ref, proj_ref,
    state_ref, query_ref, far_state_ref, far_query_ref,
    held, near_state, near_query, sems,
):
    sources, depth, across = held.shape
    width = across // 4
    copies = []
    for source in range(sources):
        rows = pl.ds(pl.multiple_of(index_ref[source] * depth, depth), depth)
        copies.append(pltpu.make_async_copy(proj_ref.at[rows, :], held.at[source], sems.at[source]))
        copies[-1].start()
    mixes = mix_ref.shape[0]

    def split(source, state_out, query_out, base):
        copies[source].wait()
        lanes = pl.ds(pl.multiple_of(index_ref[source] * depth, depth), depth)
        for begin in range(0, depth, CHUNK):
            rows = slice(begin, begin + CHUNK)
            out = slice(base + begin, base + begin + CHUNK)
            value = held[source, rows, :]
            mixing = mix_ref[:, lanes][:, rows]
            mixing = jnp.concatenate([mixing, jnp.zeros((CHUNK - mixes, CHUNK), F32)], axis=0)
            state = jnp.concatenate([value[:, width : 3 * width], jnp.transpose(mixing)], axis=1)
            query = jnp.concatenate([value[:, :width], value[:, 3 * width :]], axis=1)
            state_out[out, :] = left_parts(state)
            query_out[out, :] = left_parts(query)

    for source in range(2):
        split(source, near_state, near_query, source * depth)
    half = own_ref.shape[0] // 2
    for rows in (slice(0, half), slice(half, 2 * half)):
        pieces = [own_ref[rows, :], beside_ref[rows, :]]
        state_ref[rows, :] = add_products(None, pieces, near_state, 0)
        query_ref[rows, :] = add_products(None, pieces, near_query, 0)
    for source in range(2, sources):
        split(source, far_state_ref, far_query_ref, (source - 2) * depth)


def late_kernel(count, begin, *refs):
    base_state, base_query, far_state, far_query, state_ref, query_ref, rim_ref = refs[count:]
    pieces = [ref[...] for ref in refs[:count]]
    width = base_query.shape[1] // 2
    state_ref[...] = add_products(base_state[begin:, :], pieces, far_state, 0)
    query_ref[...] = add_products(base_query[begin:, :], pieces, far_query, 0)
    last = state_ref.shape[0] - RIM
    rim_ref[:, :width] = query_ref[last:, :width]
    rim_ref[:, width:] = state_ref[last:, : 2 * width]


def partial_kernel(count, *refs):
    base_state, far_state, out_ref = refs[count:]
    out_ref[...] = add_products(
        base_state[: out_ref.shape[0], :], [ref[...] for ref in refs[:count]], far_state, 0
    )


def convolve(raw, start, columns, conv_ref, taps_at):
    taps = conv_ref.shape[0]
    conv = 0.0
    for tap in range(taps):
        spot = start - taps + 1 + tap
        conv = conv + conv_ref[tap : tap + 1, taps_at] * raw[spot : spot + CHUNK, columns]
    return conv * sigmoid(conv)


def unit_rows(value):
    return value * lax.rsqrt(jnp.sum(value * value, axis=1, keepdims=True) + 1e-06)


def key_pass(raw, conv_ref, rate, doc_ref, first_chunk, outs, state):
    key_ref, x_ref, y_ref, grid_ref, gamma_ref, plus_ref, chunk_ref, pair_ref = outs
    width = key_ref.shape[1]
    chunks = key_ref.shape[0] // CHUNK
    row = lax.broadcasted_iota(jnp.int32, (CHUNK, CHUNK), 0)
    col = lax.broadcasted_iota(jnp.int32, (CHUNK, CHUNK), 1)
    lower = row >= col
    tri = jnp.where(lower, 1.0, 0.0).astype(F32)
    eye = jnp.where(row == col, 1.0, 0.0).astype(F32)
    keys, values, betas, grids, gammas, tails = [], [], [], [], [], []
    for part in range(chunks):
        start = RIM + part * CHUNK
        rows = slice(part * CHUNK, (part + 1) * CHUNK)
        middle, last = slice(width, 2 * width), slice(2 * width, 3 * width)
        keys.append(unit_rows(convolve(raw, start, slice(0, width), conv_ref, middle)))
        values.append(convolve(raw, start, middle, conv_ref, last))
        mixing = raw[start : start + CHUNK, last]
        plus = softplus(mixing)
        plus_ref[rows, :] = plus
        betas.append(sigmoid(mixing[:, 0:1]))
        spot = first_chunk + part
        docs = jnp.broadcast_to(doc_ref[spot : spot + 1, :].astype(F32), (CHUNK, CHUNK))
        docs = jnp.transpose(docs)
        steps = jnp.where(col == 1, -rate * plus, jnp.where(col == 0, docs, 0.0))
        sums = jnp.dot(tri, steps, precision=lax.Precision.HIGHEST, preferred_element_type=F32)
        across = jnp.transpose(sums)
        smooth, count = sums[:, 1:2], sums[:, 0:1]
        span = (smooth - across[1:2, :]) - 20.0 * (count - across[0:1, :])
        grids.append(jnp.exp(jnp.where(lower, span, -1e30)))
        gammas.append(jnp.exp(smooth - 20.0 * count))
        last = sums[CHUNK - 1 : CHUNK, :]
        tails.append(jnp.exp((last[:, 1:2] - smooth) - 20.0 * (last[:, 0:1] - count)))
        key_ref[rows, :] = keys[part]
        grid_ref[rows, :] = grids[part]
        gamma_ref[rows, :] = jnp.broadcast_to(gammas[part], (CHUNK, width))
    across_keys = [jnp.transpose(key) for key in keys]
    grams = [
        parts_dot(left_parts(key), right_parts(across)) for key, across in zip(keys, across_keys)
    ]
    lowers = [jnp.where(row > col, beta * gram, 0.0) for beta, gram in zip(betas, grams)]
    inverses = unit_lower_inverse(lowers, row, col)
    states = []
    for part in range(chunks):
        rows = slice(part * CHUNK, (part + 1) * CHUNK)
        inverse, beta = inverses[part], betas[part]
        factor_x = product(inverse, beta * keys[part])
        factor_y = product(grids[part] * inverse, beta * values[part])
        x_ref[rows, :] = factor_x
        y_ref[rows, :] = factor_y
        onto = product(
            across_keys[part], jnp.concatenate([factor_x, tails[part] * factor_y], axis=1)
        )
        trans = gammas[part][CHUNK - 1 : CHUNK, :] * (eye - onto[:, :width])
        states.append((trans, onto[:, width:]))
        chunk_ref[part, 0] = trans
        chunk_ref[part, 1] = onto[:, width:]
    if state is not None:
        states.append(state)
    while len(states) > 1:
        joined = [followed(*states[at : at + 2]) for at in range(0, len(states) - 1, 2)]
        states = joined + states[2 * len(joined) :]
    pair_ref[0] = states[0][0]
    pair_ref[1] = states[0][1]


def followed(first, second):
    width = first[0].shape[0]
    onto = product(second[0], jnp.concatenate(first, axis=1))
    return onto[:, :width], onto[:, width:] + second[1]


def later_kernel(first_chunk, raw_ref, conv_ref, rate_ref, doc_ref, *outs):
    key_pass(raw_ref, conv_ref, rate_ref[0, 0], doc_ref, first_chunk, outs, None)


def earlier_kernel(first, count, *refs):
    held, refs = refs[:count], refs[count:]
    part_ref, far_ref, rim_ref, next_ref, state_ref, conv_ref, rate_ref, doc_ref = refs[:8]
    outs, raw = refs[8:-1], refs[-1]
    rows, width = part_ref.shape[0], state_ref.shape[1]
    raw[RIM : RIM + rows, :] = add_products(
        part_ref[...], [ref[...] for ref in held], far_ref, first
    )
    raw[:RIM, : 2 * width] = rim_ref[:, width:]
    raw[RIM + rows :, :] = next_ref[:RIM, :]
    key_pass(raw, conv_ref, rate_ref[0, 0], doc_ref, 0, outs, (state_ref[0], state_ref[1]))


def query_kernel(count, *refs):
    held, refs = refs[:count], refs[count:]
    base_ref, far_ref, rim_ref, next_ref, conv_ref = refs[:5]
    fields = [(refs[5:11], 0), (refs[11:17], 1)]
    carried_ref, local_ref, gate_ref, raw = refs[17:]
    width = carried_ref.shape[1]
    rows = held[0].shape[0]
    raw[RIM : RIM + rows, :] = add_products(
        base_ref[:rows, :], [ref[...] for ref in held], far_ref, 0
    )
    raw[:RIM, :width] = rim_ref[:, :width]
    raw[RIM + rows :, :] = next_ref[:RIM, :]
    row = lax.broadcasted_iota(jnp.int32, (CHUNK, CHUNK), 0)
    col = lax.broadcasted_iota(jnp.int32, (CHUNK, CHUNK), 1)
    state = None
    base = 0
    for (key_ref, x_ref, y_ref, grid_ref, gamma_ref, chunk_ref), later in fields:
        source = next_ref if later else raw
        for part in range(key_ref.shape[0] // CHUNK):
            start = RIM + part * CHUNK
            rows = slice(part * CHUNK, (part + 1) * CHUNK)
            out = slice(base, base + CHUNK)
            base += CHUNK
            columns = slice(0, width)
            query = unit_rows(convolve(source, start, columns, conv_ref, columns))
            gate = source[start : start + CHUNK, width:]
            gate_ref[out, :] = gate * sigmoid(gate)
            overlap = product(query, jnp.transpose(key_ref[rows, :]))
            carried = gamma_ref[rows, :] * (
                query - product(jnp.where(row >= col, overlap, 0.0), x_ref[rows, :])
            )
            local = product(grid_ref[rows, :] * overlap, y_ref[rows, :])
            trans, memory = chunk_ref[part, 0], chunk_ref[part, 1]
            if state is None:
                state = (trans, memory)
            else:
                onto = product(
                    jnp.concatenate([trans, carried], axis=0), jnp.concatenate(state, axis=1)
                )
                carried = onto[CHUNK:, :width]
                local = local + onto[CHUNK:, width:]
                state = (onto[:CHUNK, :width], onto[:CHUNK, width:] + memory)
            carried_ref[out, :] = carried
            local_ref[out, :] = local


def four_kernel(first_bit, carried, last, bits_ref, own_ref, one_ref, two_ref, three_ref, *refs):
    group_ref, level_ref, next_ref, pairs = refs[-4:]
    low_bit, high_bit = bits_ref[first_bit], bits_ref[first_bit + 1]
    place = 2 * high_bit + low_bit
    for mask, ref in enumerate((own_ref, one_ref, two_ref, three_ref)):
        pairs[place ^ mask] = ref[...]
    width = next_ref.shape[0]
    joined = lambda spot: jnp.concatenate([pairs[spot, 0], pairs[spot, 1]], axis=1)
    onto_low = product(pairs[1, 0], joined(0))
    onto_high = product(pairs[3, 0], joined(2))
    low_a, low_s = onto_low[:, :width], onto_low[:, width:] + pairs[1, 1]
    high_a, high_s = onto_high[:, :width], onto_high[:, width:] + pairs[3, 1]
    if last:
        group_ref[...] = product(high_a, low_s) + high_s
    else:
        onto = product(high_a, jnp.concatenate([low_a, low_s], axis=1))
        group_ref[0] = onto[:, :width]
        group_ref[1] = onto[:, width:] + high_s
    set_low = jnp.broadcast_to(low_bit, (width, width)) == 1
    set_high = jnp.broadcast_to(high_bit, (width, width)) == 1
    if carried:
        carry = refs[0][...]
        first = product(carry, jnp.concatenate([one_ref[0], one_ref[1]], axis=1))
        first_a, first_s = first[:, :width], first[:, width:]
    else:
        row = lax.broadcasted_iota(jnp.int32, (width, width), 0)
        col = lax.broadcasted_iota(jnp.int32, (width, width), 1)
        carry = jnp.where(row == col, 1.0, 0.0).astype(F32)
        first_a, first_s = one_ref[0], one_ref[1]
    level_ref[0] = jnp.where(set_low, first_s, 0.0)
    carry = jnp.where(set_low, first_a, carry)
    second = product(carry, jnp.concatenate([low_a, low_s], axis=1))
    level_ref[1] = jnp.where(set_high, second[:, width:], 0.0)
    next_ref[...] = jnp.where(set_high, second[:, :width], carry)


def mix_kernel(stages, single, carried_ref, local_ref, gate_ref, low_ref, high_ref, gain_ref, *refs):
    states = [ref[spot] for ref in refs[:stages] for spot in range(ref.shape[0])]
    if single:
        states.append(product(refs[stages][...], refs[stages + 1][...]))
    normed_ref = refs[-1]
    states = [right_parts(state) for state in states]
    carried = left_parts(carried_ref[...])
    weights = jnp.concatenate([low_ref[...], high_ref[...]], axis=0)
    mixed = weights[:, 2:3] * local_ref[...]
    for level, state in enumerate(states):
        mixed = mixed + weights[:, level + 3 : level + 4] * parts_dot(carried, state)
    scale = lax.rsqrt(jnp.mean(mixed * mixed, axis=1, keepdims=True) + 1e-05)
    normed_ref[...] = mixed * scale * gain_ref[...] * gate_ref[...]


def out_kernel(pieces, first, last, index_ref, *refs):
    weight_ref = refs[pieces]
    parts = []
    for spot in range(pieces):
        depth = refs[spot].shape[1]
        rows = pl.ds(pl.multiple_of(index_ref[first + spot] * depth, depth), depth)
        parts.append(weight_ref[rows, :])
    weight = left_parts(jnp.concatenate(parts, axis=0))
    columns = weight.shape[1] // 2

    def block(rows):
        parts = [halves(ref[rows, :]) for ref in refs[:pieces]]
        high, low = (jnp.concatenate(part, axis=1) for part in zip(*parts))
        both = jnp.dot(high, weight, preferred_element_type=F32)
        rest = jnp.dot(low, weight[:, :columns], preferred_element_type=F32)
        return (both[:, :columns] + both[:, columns:]) + rest

    blocks = [slice(base, base + CHUNK) for base in range(0, refs[0].shape[0], CHUNK)]
    if not last:
        for rows in blocks:
            part = block(rows)
            refs[-1][rows, :] = refs[pieces + 1][rows, :] + part if first else part
        return
    total_ref, out_ref, held, sems = refs[pieces + 1 :]
    copies = []
    for spot, rows in enumerate(blocks):
        held[rows, :] = total_ref[rows, :] + block(rows)
        copies.append(pltpu.make_async_copy(held.at[rows, :], out_ref.at[rows, :], sems.at[spot]))
        copies[-1].start()
    for copy in copies:
        copy.wait()


def vmem_call(kernel, outs, scratch, cost, *args, any_in=(), any_out=False):
    spec = pl.BlockSpec(memory_space=pltpu.VMEM)
    small = pl.BlockSpec(memory_space=pltpu.SMEM)
    free = pl.BlockSpec(memory_space=pl.ANY)
    return pl.pallas_call(
        kernel,
        out_shape=outs,
        in_specs=[
            free if spot in any_in else small if arg.dtype == jnp.int32 and arg.ndim == 1 else spec
            for spot, arg in enumerate(args)
        ],
        out_specs=jax.tree.map(lambda unused: free if any_out else spec, outs),
        scratch_shapes=scratch,
        compiler_params=pltpu.CompilerParams(vmem_limit_bytes=VMEM_GRANT),
        cost_estimate=pl.CostEstimate(flops=int(cost * 1e9), bytes_accessed=1 << 20, transcendentals=0),
    )(*args)


def to_sibling(value):
    count = lax.axis_size("head")
    return lax.ppermute(value, "head", [(source, source ^ 1) for source in range(count)])


def to_chips(value):
    count = lax.axis_size("head")
    return [
        lax.ppermute(
            value, "head", [(source, (source + 2 * step) % count) for source in range(count)]
        )
        for step in range(1, count // 2)
    ]


def after(value, *earlier):
    return lax.optimization_barrier((value, *earlier))


def shards(tokens, w_proj, w_mix, conv_w, rates, doc_start, norm_gain, w_out):
    tok_rows, depth = tokens.shape
    width = w_proj.shape[1] // 4
    state_columns, query_columns = 2 * width + CHUNK, 2 * width
    heads, me = lax.axis_size("head"), lax.axis_index("head")
    blocks, my_index = lax.axis_size("ctx"), lax.axis_index("ctx")
    remote = [(me + heads - 2 * step) % heads for step in range(1, heads // 2)]
    order = [me, me ^ 1] + remote + [index ^ 1 for index in remote]
    bits = blocks.bit_length() - 1
    flags = [my_index >> bit & 1 for bit in range(bits)]
    index = jnp.stack(order + flags).astype(jnp.int32)
    count = heads - 2
    like = lambda *shape: jax.ShapeDtypeStruct(shape, F32)
    parts = lambda *shape: jax.ShapeDtypeStruct(shape, BF16)

    first = tok_rows - CHUNK
    cut = first - RIM
    late_rows, early_rows = after(tokens[cut:], tokens)
    late = to_chips(late_rows)
    early = to_chips(early_rows[:cut])
    beside = to_sibling(tokens)
    base_state, base_query, far_state, far_query = vmem_call(
        base_kernel,
        [like(tok_rows, state_columns), like(tok_rows, query_columns),
         parts(count * depth, 2 * state_columns), parts(count * depth, 2 * query_columns)],
        [pltpu.VMEM((heads, depth, 4 * width), F32),
         pltpu.VMEM((2 * depth, 2 * state_columns), BF16),
         pltpu.VMEM((2 * depth, 2 * query_columns), BF16),
         pltpu.SemaphoreType.DMA((heads,))],
        3, index, tokens, beside, w_mix.T, w_proj, any_in=(4,),
    )
    late, far_state = after(late, far_state)
    late_on = [to_sibling(value) for value in late]
    late_state, late_query, rim = vmem_call(
        functools.partial(late_kernel, count, cut),
        [like(tok_rows - cut, state_columns), like(tok_rows - cut, query_columns),
         like(RIM, 3 * width)],
        [], 0.5, *late, *late_on, base_state, base_query, far_state, far_query,
    )
    rim = lax.ppermute(rim, "ctx", [(source, source + 1) for source in range(blocks - 1)])
    docs = doc_start.reshape(tok_rows // CHUNK, CHUNK)
    rate = rates[:, None]

    def outs(rows):
        chunks = like(rows // CHUNK, 2, width, width)
        return [like(rows, width)] * 6 + [chunks, like(2, width, width)]

    later = vmem_call(
        functools.partial(later_kernel, first // CHUNK), outs(tok_rows - first), [], 0.5,
        late_state, conv_w, rate, docs,
    )
    early, pair_late, rim = after(early, later[7], rim)
    early_on = [to_sibling(value) for value in early]
    partial = vmem_call(
        functools.partial(partial_kernel, len(early)), like(cut, state_columns), [], 1,
        *early, base_state, far_state,
    )
    earlier = vmem_call(
        functools.partial(earlier_kernel, len(early), len(early)), outs(first),
        [pltpu.VMEM((first + RIM, state_columns), F32)], 5,
        *early_on, partial, far_state, rim, late_state, pair_late, conv_w, rate, docs,
    )

    pair = earlier[7]
    carry = ()
    levels = []
    for bit in range(0, bits - 1, 2):
        others = [
            lax.ppermute(
                pair, "ctx", [(source, source ^ (mask << bit)) for source in range(blocks)]
            )
            for mask in (1, 2, 3)
        ]
        last = bit + 2 >= bits - 1 and bits % 2
        group = [like(width, width)] if last else [like(2, width, width)]
        pair, level, *carry = vmem_call(
            functools.partial(four_kernel, heads + bit, bool(carry), last),
            group + [like(2, width, width), like(width, width)],
            [pltpu.VMEM((4, 2, width, width), F32)], 1,
            index, pair, *others, *carry,
        )
        levels.append(level)
    fields = vmem_call(
        functools.partial(query_kernel, count), [like(tok_rows, width)] * 3,
        [pltpu.VMEM((first + RIM, query_columns), F32)], 5,
        *early, *early_on, base_query, far_query, rim, late_query, conv_w,
        *earlier[:5], earlier[6], *later[:5], later[6],
    )
    single = []
    if bits % 2:
        reach = blocks // 2
        single = [
            *(carry or [jnp.eye(width, dtype=F32)]),
            lax.ppermute(
                pair if carry else pair[1],
                "ctx", [(source, source + reach) for source in range(reach)],
            ),
        ]
    normed = vmem_call(
        functools.partial(mix_kernel, len(levels), bool(single)), like(tok_rows, width), [], 1,
        *fields, earlier[5], later[5], norm_gain[None, :], *levels, *single,
    )
    far = to_chips(normed)
    near = to_sibling(normed)
    out_shape = like(tok_rows, w_out.shape[1])
    total = vmem_call(
        functools.partial(out_kernel, 2, 0, False), out_shape, [], 2, index, normed, near, w_out
    )
    far, total = after(far, total)
    far_on = [to_sibling(value) for value in far]
    total = vmem_call(
        functools.partial(out_kernel, len(far), 2, False), out_shape, [], 1,
        index, *far, w_out, total,
    )
    return vmem_call(
        functools.partial(out_kernel, len(far), 2 + len(far), True), out_shape,
        [pltpu.VMEM(out_shape.shape, F32), pltpu.SemaphoreType.DMA((tok_rows // CHUNK,))], 1,
        index, *far_on, w_out, total, any_out=True,
    )


def solution(mesh):
    placed = (
        P("ctx", "head"),
        P(None, "head"),
        P(None, "head"),
        P(None, "head"),
        P("head"),
        P("ctx"),
        P("head"),
        P(None, "head"),
    )
    return jax.shard_map(
        shards, mesh=mesh, in_specs=placed, out_specs=P("ctx", "head"), check_vma=False
    )
```

```python
import functools

import jax
import jax.numpy as jnp
from jax import lax
from jax.experimental import pallas as pl
from jax.experimental.pallas import tpu as pltpu
from jax.sharding import PartitionSpec as P

CHUNK = 128
RIM = 16
VMEM_GRANT = 16 << 20
F32 = jnp.float32
BF16 = jnp.bfloat16


def halves(value):
    high = value.astype(BF16)
    return high, (value - high.astype(F32)).astype(BF16)


def left_parts(value):
    return jnp.concatenate(halves(value), axis=1)


def right_parts(value):
    row = jnp.concatenate(halves(value), axis=1)
    return jnp.concatenate([row, row], axis=0)


def parts_dot(left, right):
    both = jnp.dot(left, right, preferred_element_type=F32)
    half = both.shape[1] // 2
    return both[:, :half] + both[:, half:]


def product(left, right):
    return parts_dot(left_parts(left), right_parts(right))


def softplus(value):
    return jnp.maximum(value, 0.0) + jnp.log1p(jnp.exp(-jnp.abs(value)))


def sigmoid(value):
    return 1.0 / (1.0 + jnp.exp(-value))


def unit_lower_inverse(lowers, row, col):
    size = lowers[0].shape[0]
    eye = jnp.where(row == col, 1.0, 0.0).astype(F32)
    inverses = [eye - jnp.where((row >> 1) == (col >> 1), lower, 0.0) for lower in lowers]
    lower_parts = [halves(lower) for lower in lowers]
    step = 1
    while 1 << step < size:
        off = ((row >> (step + 2)) == (col >> (step + 2))) & ((row >> step) > (col >> step))
        offs = [
            jnp.concatenate([jnp.where(off, part, jnp.zeros_like(part)) for part in parts], axis=1)
            for parts in lower_parts
        ]
        onto = [parts_dot(left, right_parts(inverse)) for left, inverse in zip(offs, inverses)]
        rights = [right_parts(value) for value in onto]
        squares = [parts_dot(left_parts(value), right) for value, right in zip(onto, rights)]
        firsts = [
            inverse - parts_dot(left_parts(inverse), right)
            for inverse, right in zip(inverses, rights)
        ]
        inverses = [first + product(first, square) for first, square in zip(firsts, squares)]
        step += 2
    return inverses


def add_products(total, pieces, weight_ref, first):
    columns = weight_ref.shape[1] // 2
    for spot, piece in enumerate(pieces):
        depth = piece.shape[1]
        rows = slice((first + spot) * depth, (first + spot + 1) * depth)
        high, low = halves(piece)
        both = jnp.dot(high, weight_ref[rows, :], preferred_element_type=F32)
        rest = jnp.dot(low, weight_ref[rows, :columns], preferred_element_type=F32)
        part = (both[:, :columns] + both[:, columns:]) + rest
        total = part if total is None else total + part
    return total


def base_kernel(
    index_ref, own_ref, beside_ref, mix_ref, proj_ref,
    state_ref, query_ref, far_state_ref, far_query_ref,
    held, near_state, near_query, sems,
):
    sources, depth, across = held.shape
    width = across // 4
    copies = []
    for source in range(sources):
        rows = pl.ds(pl.multiple_of(index_ref[source] * depth, depth), depth)
        copies.append(pltpu.make_async_copy(proj_ref.at[rows, :], held.at[source], sems.at[source]))
        copies[-1].start()
    mixes = mix_ref.shape[0]

    def split(source, state_out, query_out, base):
        copies[source].wait()
        lanes = pl.ds(pl.multiple_of(index_ref[source] * depth, depth), depth)
        for begin in range(0, depth, CHUNK):
            rows = slice(begin, begin + CHUNK)
            out = slice(base + begin, base + begin + CHUNK)
            value = held[source, rows, :]
            mixing = mix_ref[:, lanes][:, rows]
            mixing = jnp.concatenate([mixing, jnp.zeros((CHUNK - mixes, CHUNK), F32)], axis=0)
            state = jnp.concatenate([value[:, width : 3 * width], jnp.transpose(mixing)], axis=1)
            query = jnp.concatenate([value[:, :width], value[:, 3 * width :]], axis=1)
            state_out[out, :] = left_parts(state)
            query_out[out, :] = left_parts(query)

    for source in range(2):
        split(source, near_state, near_query, source * depth)
    half = own_ref.shape[0] // 2
    for rows in (slice(0, half), slice(half, 2 * half)):
        pieces = [own_ref[rows, :], beside_ref[rows, :]]
        state_ref[rows, :] = add_products(None, pieces, near_state, 0)
        query_ref[rows, :] = add_products(None, pieces, near_query, 0)
    for source in range(2, sources):
        split(source, far_state_ref, far_query_ref, (source - 2) * depth)


def late_kernel(count, segments, *refs):
    begin = segments[0].start
    held, refs = refs[: count * len(segments)], refs[count * len(segments) :]
    base_state, base_query, far_state, far_query, state_ref, query_ref, rim_ref = refs
    width = base_query.shape[1] // 2
    for turn, rows in enumerate(segments):
        pieces = [ref[...] for ref in held[turn * count : (turn + 1) * count]]
        out = slice(rows.start - begin, rows.stop - begin)
        state_ref[out, :] = add_products(base_state[rows, :], pieces, far_state, 0)
        query_ref[out, :] = add_products(base_query[rows, :], pieces, far_query, 0)
    last = state_ref.shape[0] - RIM
    rim_ref[:, :width] = query_ref[last:, :width]
    rim_ref[:, width:] = state_ref[last:, : 2 * width]


def partial_kernel(count, *refs):
    base_state, far_state, out_ref = refs[count:]
    out_ref[...] = add_products(
        base_state[: out_ref.shape[0], :], [ref[...] for ref in refs[:count]], far_state, 0
    )


def convolve(raw, start, columns, conv_ref, taps_at):
    taps = conv_ref.shape[0]
    conv = 0.0
    for tap in range(taps):
        spot = start - taps + 1 + tap
        conv = conv + conv_ref[tap : tap + 1, taps_at] * raw[spot : spot + CHUNK, columns]
    return conv * sigmoid(conv)


def unit_rows(value):
    return value * lax.rsqrt(jnp.sum(value * value, axis=1, keepdims=True) + 1e-06)


def key_pass(raw, conv_ref, rate, doc_ref, first_chunk, outs, state):
    key_ref, x_ref, y_ref, grid_ref, gamma_ref, plus_ref, chunk_ref, pair_ref = outs
    width = key_ref.shape[1]
    chunks = key_ref.shape[0] // CHUNK
    row = lax.broadcasted_iota(jnp.int32, (CHUNK, CHUNK), 0)
    col = lax.broadcasted_iota(jnp.int32, (CHUNK, CHUNK), 1)
    lower = row >= col
    tri = jnp.where(lower, 1.0, 0.0).astype(F32)
    eye = jnp.where(row == col, 1.0, 0.0).astype(F32)
    keys, values, betas, grids, gammas, tails = [], [], [], [], [], []
    for part in range(chunks):
        start = RIM + part * CHUNK
        rows = slice(part * CHUNK, (part + 1) * CHUNK)
        middle, last = slice(width, 2 * width), slice(2 * width, 3 * width)
        keys.append(unit_rows(convolve(raw, start, slice(0, width), conv_ref, middle)))
        values.append(convolve(raw, start, middle, conv_ref, last))
        mixing = raw[start : start + CHUNK, last]
        plus = softplus(mixing)
        plus_ref[rows, :] = plus
        betas.append(sigmoid(mixing[:, 0:1]))
        spot = first_chunk + part
        docs = jnp.broadcast_to(doc_ref[spot : spot + 1, :].astype(F32), (CHUNK, CHUNK))
        docs = jnp.transpose(docs)
        steps = jnp.where(col == 1, -rate * plus, jnp.where(col == 0, docs, 0.0))
        sums = jnp.dot(tri, steps, precision=lax.Precision.HIGHEST, preferred_element_type=F32)
        across = jnp.transpose(sums)
        smooth, count = sums[:, 1:2], sums[:, 0:1]
        span = (smooth - across[1:2, :]) - 20.0 * (count - across[0:1, :])
        grids.append(jnp.exp(jnp.where(lower, span, -1e30)))
        gammas.append(jnp.exp(smooth - 20.0 * count))
        last = sums[CHUNK - 1 : CHUNK, :]
        tails.append(jnp.exp((last[:, 1:2] - smooth) - 20.0 * (last[:, 0:1] - count)))
        key_ref[rows, :] = keys[part]
        grid_ref[rows, :] = grids[part]
        gamma_ref[rows, :] = jnp.broadcast_to(gammas[part], (CHUNK, width))
    across_keys = [jnp.transpose(key) for key in keys]
    grams = [
        parts_dot(left_parts(key), right_parts(across)) for key, across in zip(keys, across_keys)
    ]
    lowers = [jnp.where(row > col, beta * gram, 0.0) for beta, gram in zip(betas, grams)]
    inverses = unit_lower_inverse(lowers, row, col)
    states = []
    for part in range(chunks):
        rows = slice(part * CHUNK, (part + 1) * CHUNK)
        inverse, beta = inverses[part], betas[part]
        factor_x = product(inverse, beta * keys[part])
        factor_y = product(grids[part] * inverse, beta * values[part])
        x_ref[rows, :] = factor_x
        y_ref[rows, :] = factor_y
        onto = product(
            across_keys[part], jnp.concatenate([factor_x, tails[part] * factor_y], axis=1)
        )
        trans = gammas[part][CHUNK - 1 : CHUNK, :] * (eye - onto[:, :width])
        states.append((trans, onto[:, width:]))
        chunk_ref[part, 0] = trans
        chunk_ref[part, 1] = onto[:, width:]
    if state is not None:
        states.append(state)
    while len(states) > 1:
        joined = [followed(*states[at : at + 2]) for at in range(0, len(states) - 1, 2)]
        states = joined + states[2 * len(joined) :]
    pair_ref[0] = states[0][0]
    pair_ref[1] = states[0][1]


def followed(first, second):
    width = first[0].shape[0]
    onto = product(second[0], jnp.concatenate(first, axis=1))
    return onto[:, :width], onto[:, width:] + second[1]


def later_kernel(first_chunk, raw_ref, conv_ref, rate_ref, doc_ref, *outs):
    key_pass(raw_ref, conv_ref, rate_ref[0, 0], doc_ref, first_chunk, outs, None)


def earlier_kernel(first, count, *refs):
    held, refs = refs[:count], refs[count:]
    part_ref, far_ref, rim_ref, next_ref, state_ref, conv_ref, rate_ref, doc_ref = refs[:8]
    outs, raw = refs[8:-1], refs[-1]
    rows, width = part_ref.shape[0], state_ref.shape[1]
    raw[RIM : RIM + rows, :] = add_products(
        part_ref[...], [ref[...] for ref in held], far_ref, first
    )
    raw[:RIM, : 2 * width] = rim_ref[:, width:]
    raw[RIM + rows :, :] = next_ref[:RIM, :]
    key_pass(raw, conv_ref, rate_ref[0, 0], doc_ref, 0, outs, (state_ref[0], state_ref[1]))


def query_kernel(count, *refs):
    held, refs = refs[:count], refs[count:]
    base_ref, far_ref, rim_ref, next_ref, conv_ref = refs[:5]
    fields = [(refs[5:11], 0), (refs[11:17], 1)]
    carried_ref, local_ref, gate_ref, raw = refs[17:]
    width = carried_ref.shape[1]
    rows = held[0].shape[0]
    raw[RIM : RIM + rows, :] = add_products(
        base_ref[:rows, :], [ref[...] for ref in held], far_ref, 0
    )
    raw[:RIM, :width] = rim_ref[:, :width]
    raw[RIM + rows :, :] = next_ref[:RIM, :]
    row = lax.broadcasted_iota(jnp.int32, (CHUNK, CHUNK), 0)
    col = lax.broadcasted_iota(jnp.int32, (CHUNK, CHUNK), 1)
    state = None
    base = 0
    for (key_ref, x_ref, y_ref, grid_ref, gamma_ref, chunk_ref), later in fields:
        source = next_ref if later else raw
        for part in range(key_ref.shape[0] // CHUNK):
            start = RIM + part * CHUNK
            rows = slice(part * CHUNK, (part + 1) * CHUNK)
            out = slice(base, base + CHUNK)
            base += CHUNK
            columns = slice(0, width)
            query = unit_rows(convolve(source, start, columns, conv_ref, columns))
            gate = source[start : start + CHUNK, width:]
            gate_ref[out, :] = gate * sigmoid(gate)
            overlap = product(query, jnp.transpose(key_ref[rows, :]))
            carried = gamma_ref[rows, :] * (
                query - product(jnp.where(row >= col, overlap, 0.0), x_ref[rows, :])
            )
            local = product(grid_ref[rows, :] * overlap, y_ref[rows, :])
            trans, memory = chunk_ref[part, 0], chunk_ref[part, 1]
            if state is None:
                state = (trans, memory)
            else:
                onto = product(
                    jnp.concatenate([trans, carried], axis=0), jnp.concatenate(state, axis=1)
                )
                carried = onto[CHUNK:, :width]
                local = local + onto[CHUNK:, width:]
                state = (onto[:CHUNK, :width], onto[:CHUNK, width:] + memory)
            carried_ref[out, :] = carried
            local_ref[out, :] = local


def four_kernel(first_bit, carried, last, bits_ref, own_ref, one_ref, two_ref, three_ref, *refs):
    group_ref, level_ref, next_ref, pairs = refs[-4:]
    low_bit, high_bit = bits_ref[first_bit], bits_ref[first_bit + 1]
    place = 2 * high_bit + low_bit
    for mask, ref in enumerate((own_ref, one_ref, two_ref, three_ref)):
        pairs[place ^ mask] = ref[...]
    width = next_ref.shape[0]
    joined = lambda spot: jnp.concatenate([pairs[spot, 0], pairs[spot, 1]], axis=1)
    onto_low = product(pairs[1, 0], joined(0))
    onto_high = product(pairs[3, 0], joined(2))
    low_a, low_s = onto_low[:, :width], onto_low[:, width:] + pairs[1, 1]
    high_a, high_s = onto_high[:, :width], onto_high[:, width:] + pairs[3, 1]
    if last:
        group_ref[...] = product(high_a, low_s) + high_s
    else:
        onto = product(high_a, jnp.concatenate([low_a, low_s], axis=1))
        group_ref[0] = onto[:, :width]
        group_ref[1] = onto[:, width:] + high_s
    set_low = jnp.broadcast_to(low_bit, (width, width)) == 1
    set_high = jnp.broadcast_to(high_bit, (width, width)) == 1
    if carried:
        carry = refs[0][...]
        first = product(carry, jnp.concatenate([one_ref[0], one_ref[1]], axis=1))
        first_a, first_s = first[:, :width], first[:, width:]
    else:
        row = lax.broadcasted_iota(jnp.int32, (width, width), 0)
        col = lax.broadcasted_iota(jnp.int32, (width, width), 1)
        carry = jnp.where(row == col, 1.0, 0.0).astype(F32)
        first_a, first_s = one_ref[0], one_ref[1]
    level_ref[0] = jnp.where(set_low, first_s, 0.0)
    carry = jnp.where(set_low, first_a, carry)
    second = product(carry, jnp.concatenate([low_a, low_s], axis=1))
    level_ref[1] = jnp.where(set_high, second[:, width:], 0.0)
    next_ref[...] = jnp.where(set_high, second[:, :width], carry)


def mix_kernel(stages, single, carried_ref, local_ref, gate_ref, low_ref, high_ref, gain_ref, *refs):
    states = [ref[spot] for ref in refs[:stages] for spot in range(ref.shape[0])]
    if single:
        states.append(product(refs[stages][...], refs[stages + 1][...]))
    normed_ref = refs[-1]
    states = [right_parts(state) for state in states]
    carried = left_parts(carried_ref[...])
    weights = jnp.concatenate([low_ref[...], high_ref[...]], axis=0)
    mixed = weights[:, 2:3] * local_ref[...]
    for level, state in enumerate(states):
        mixed = mixed + weights[:, level + 3 : level + 4] * parts_dot(carried, state)
    scale = lax.rsqrt(jnp.mean(mixed * mixed, axis=1, keepdims=True) + 1e-05)
    normed_ref[...] = mixed * scale * gain_ref[...] * gate_ref[...]


def out_kernel(pieces, first, last, index_ref, *refs):
    weight_ref = refs[pieces]
    parts = []
    for spot in range(pieces):
        depth = refs[spot].shape[1]
        rows = pl.ds(pl.multiple_of(index_ref[first + spot] * depth, depth), depth)
        parts.append(weight_ref[rows, :])
    weight = left_parts(jnp.concatenate(parts, axis=0))
    columns = weight.shape[1] // 2

    def block(rows):
        parts = [halves(ref[rows, :]) for ref in refs[:pieces]]
        high, low = (jnp.concatenate(part, axis=1) for part in zip(*parts))
        both = jnp.dot(high, weight, preferred_element_type=F32)
        rest = jnp.dot(low, weight[:, :columns], preferred_element_type=F32)
        return (both[:, :columns] + both[:, columns:]) + rest

    blocks = [slice(base, base + CHUNK) for base in range(0, refs[0].shape[0], CHUNK)]
    if not last:
        for rows in blocks:
            part = block(rows)
            refs[-1][rows, :] = refs[pieces + 1][rows, :] + part if first else part
        return
    total_ref, out_ref, held, sems = refs[pieces + 1 :]
    copies = []
    for spot, rows in enumerate(blocks):
        held[rows, :] = total_ref[rows, :] + block(rows)
        copies.append(pltpu.make_async_copy(held.at[rows, :], out_ref.at[rows, :], sems.at[spot]))
        copies[-1].start()
    for copy in copies:
        copy.wait()


def vmem_call(kernel, outs, scratch, cost, *args, any_in=(), any_out=False):
    spec = pl.BlockSpec(memory_space=pltpu.VMEM)
    small = pl.BlockSpec(memory_space=pltpu.SMEM)
    free = pl.BlockSpec(memory_space=pl.ANY)
    return pl.pallas_call(
        kernel,
        out_shape=outs,
        in_specs=[
            free if spot in any_in else small if arg.dtype == jnp.int32 and arg.ndim == 1 else spec
            for spot, arg in enumerate(args)
        ],
        out_specs=jax.tree.map(lambda unused: free if any_out else spec, outs),
        scratch_shapes=scratch,
        compiler_params=pltpu.CompilerParams(vmem_limit_bytes=VMEM_GRANT),
        cost_estimate=pl.CostEstimate(flops=int(cost * 1e9), bytes_accessed=1 << 20, transcendentals=0),
    )(*args)


def to_sibling(value):
    count = lax.axis_size("head")
    return lax.ppermute(value, "head", [(source, source ^ 1) for source in range(count)])


def to_chips(value):
    count = lax.axis_size("head")
    return [
        lax.ppermute(
            value, "head", [(source, (source + 2 * step) % count) for source in range(count)]
        )
        for step in range(1, count // 2)
    ]


def after(value, *earlier):
    return lax.optimization_barrier((value, *earlier))


def shards(tokens, w_proj, w_mix, conv_w, rates, doc_start, norm_gain, w_out):
    tok_rows, depth = tokens.shape
    width = w_proj.shape[1] // 4
    state_columns, query_columns = 2 * width + CHUNK, 2 * width
    heads, me = lax.axis_size("head"), lax.axis_index("head")
    blocks, my_index = lax.axis_size("ctx"), lax.axis_index("ctx")
    remote = [(me + heads - 2 * step) % heads for step in range(1, heads // 2)]
    order = [me, me ^ 1] + remote + [index ^ 1 for index in remote]
    bits = blocks.bit_length() - 1
    flags = [my_index >> bit & 1 for bit in range(bits)]
    index = jnp.stack(order + flags).astype(jnp.int32)
    count = heads - 2
    like = lambda *shape: jax.ShapeDtypeStruct(shape, F32)
    parts = lambda *shape: jax.ShapeDtypeStruct(shape, BF16)

    first = tok_rows // 2
    cut = first - RIM
    middle = tok_rows - CHUNK - RIM
    segments = (slice(cut, middle), slice(middle, tok_rows))
    late = [to_chips(tokens[rows]) for rows in segments]
    beside = to_sibling(tokens)
    early_rows, beside = after(tokens, beside)
    early = to_chips(early_rows[:cut])
    base_state, base_query, far_state, far_query = vmem_call(
        base_kernel,
        [like(tok_rows, state_columns), like(tok_rows, query_columns),
         parts(count * depth, 2 * state_columns), parts(count * depth, 2 * query_columns)],
        [pltpu.VMEM((heads, depth, 4 * width), F32),
         pltpu.VMEM((2 * depth, 2 * state_columns), BF16),
         pltpu.VMEM((2 * depth, 2 * query_columns), BF16),
         pltpu.SemaphoreType.DMA((heads,))],
        3, index, tokens, beside, w_mix.T, w_proj, any_in=(4,),
    )
    late, far_state = after(late, far_state)
    late_on = [[to_sibling(value) for value in values] for values in late]
    arrived = [value for pair in zip(late, late_on) for values in pair for value in values]
    late_state, late_query, rim = vmem_call(
        functools.partial(late_kernel, count, segments),
        [like(tok_rows - cut, state_columns), like(tok_rows - cut, query_columns),
         like(RIM, 3 * width)],
        [], 0.5, *arrived, base_state, base_query, far_state, far_query,
    )
    rim = lax.ppermute(rim, "ctx", [(source, source + 1) for source in range(blocks - 1)])
    docs = doc_start.reshape(tok_rows // CHUNK, CHUNK)
    rate = rates[:, None]

    def outs(rows):
        chunks = like(rows // CHUNK, 2, width, width)
        return [like(rows, width)] * 6 + [chunks, like(2, width, width)]

    later = vmem_call(
        functools.partial(later_kernel, first // CHUNK), outs(tok_rows - first), [], 0.5,
        late_state, conv_w, rate, docs,
    )
    early, pair_late, rim = after(early, later[7], rim)
    early_on = [to_sibling(value) for value in early]
    partial = vmem_call(
        functools.partial(partial_kernel, len(early)), like(cut, state_columns), [], 1,
        *early, base_state, far_state,
    )
    earlier = vmem_call(
        functools.partial(earlier_kernel, len(early), len(early)), outs(first),
        [pltpu.VMEM((first + RIM, state_columns), F32)], 5,
        *early_on, partial, far_state, rim, late_state, pair_late, conv_w, rate, docs,
    )

    pair = earlier[7]
    carry = ()
    levels = []
    for bit in range(0, bits - 1, 2):
        others = [
            lax.ppermute(
                pair, "ctx", [(source, source ^ (mask << bit)) for source in range(blocks)]
            )
            for mask in (1, 2, 3)
        ]
        last = bit + 2 >= bits - 1 and bits % 2
        group = [like(width, width)] if last else [like(2, width, width)]
        pair, level, *carry = vmem_call(
            functools.partial(four_kernel, heads + bit, bool(carry), last),
            group + [like(2, width, width), like(width, width)],
            [pltpu.VMEM((4, 2, width, width), F32)], 1,
            index, pair, *others, *carry,
        )
        levels.append(level)
    fields = vmem_call(
        functools.partial(query_kernel, count), [like(tok_rows, width)] * 3,
        [pltpu.VMEM((first + RIM, query_columns), F32)], 5,
        *early, *early_on, base_query, far_query, rim, late_query, conv_w,
        *earlier[:5], earlier[6], *later[:5], later[6],
    )
    single = []
    if bits % 2:
        reach = blocks // 2
        single = [
            *(carry or [jnp.eye(width, dtype=F32)]),
            lax.ppermute(
                pair if carry else pair[1],
                "ctx", [(source, source + reach) for source in range(reach)],
            ),
        ]
    normed = vmem_call(
        functools.partial(mix_kernel, len(levels), bool(single)), like(tok_rows, width), [], 1,
        *fields, earlier[5], later[5], norm_gain[None, :], *levels, *single,
    )
    far = to_chips(normed)
    near = to_sibling(normed)
    out_shape = like(tok_rows, w_out.shape[1])
    total = vmem_call(
        functools.partial(out_kernel, 2, 0, False), out_shape, [], 2, index, normed, near, w_out
    )
    far, total = after(far, total)
    far_on = [to_sibling(value) for value in far]
    total = vmem_call(
        functools.partial(out_kernel, len(far), 2, False), out_shape, [], 1,
        index, *far, w_out, total,
    )
    return vmem_call(
        functools.partial(out_kernel, len(far), 2 + len(far), True), out_shape,
        [pltpu.VMEM(out_shape.shape, F32), pltpu.SemaphoreType.DMA((tok_rows // CHUNK,))], 1,
        index, *far_on, w_out, total, any_out=True,
    )


def solution(mesh):
    placed = (
        P("ctx", "head"),
        P(None, "head"),
        P(None, "head"),
        P(None, "head"),
        P("head"),
        P("ctx"),
        P("head"),
        P(None, "head"),
    )
    return jax.shard_map(
        shards, mesh=mesh, in_specs=placed, out_specs=P("ctx", "head"), check_vma=False
    )
```

```python
import functools

import jax
import jax.numpy as jnp
from jax import lax
from jax.experimental import pallas as pl
from jax.experimental.pallas import tpu as pltpu
from jax.sharding import PartitionSpec as P

CHUNK = 128
RIM = 16
VMEM_GRANT = 16 << 20
F32 = jnp.float32
BF16 = jnp.bfloat16


def halves(value):
    high = value.astype(BF16)
    return high, (value - high.astype(F32)).astype(BF16)


def left_parts(value):
    return jnp.concatenate(halves(value), axis=1)


def right_parts(value):
    row = jnp.concatenate(halves(value), axis=1)
    return jnp.concatenate([row, row], axis=0)


def parts_dot(left, right):
    both = jnp.dot(left, right, preferred_element_type=F32)
    half = both.shape[1] // 2
    return both[:, :half] + both[:, half:]


def product(left, right):
    return parts_dot(left_parts(left), right_parts(right))


def softplus(value):
    return jnp.maximum(value, 0.0) + jnp.log1p(jnp.exp(-jnp.abs(value)))


def sigmoid(value):
    return 1.0 / (1.0 + jnp.exp(-value))


def unit_lower_inverse(lowers, row, col):
    size = lowers[0].shape[0]
    eye = jnp.where(row == col, 1.0, 0.0).astype(F32)
    inverses = [eye - jnp.where((row >> 1) == (col >> 1), lower, 0.0) for lower in lowers]
    lower_parts = [halves(lower) for lower in lowers]
    step = 1
    while 1 << step < size:
        off = ((row >> (step + 2)) == (col >> (step + 2))) & ((row >> step) > (col >> step))
        offs = [
            jnp.concatenate([jnp.where(off, part, jnp.zeros_like(part)) for part in parts], axis=1)
            for parts in lower_parts
        ]
        onto = [parts_dot(left, right_parts(inverse)) for left, inverse in zip(offs, inverses)]
        rights = [right_parts(value) for value in onto]
        squares = [parts_dot(left_parts(value), right) for value, right in zip(onto, rights)]
        firsts = [
            inverse - parts_dot(left_parts(inverse), right)
            for inverse, right in zip(inverses, rights)
        ]
        inverses = [first + product(first, square) for first, square in zip(firsts, squares)]
        step += 2
    return inverses


def add_products(total, pieces, weight_ref, first):
    columns = weight_ref.shape[1] // 2
    for spot, piece in enumerate(pieces):
        depth = piece.shape[1]
        rows = slice((first + spot) * depth, (first + spot + 1) * depth)
        high, low = halves(piece)
        both = jnp.dot(high, weight_ref[rows, :], preferred_element_type=F32)
        rest = jnp.dot(low, weight_ref[rows, :columns], preferred_element_type=F32)
        part = (both[:, :columns] + both[:, columns:]) + rest
        total = part if total is None else total + part
    return total


def base_kernel(
    index_ref, own_ref, beside_ref, mix_ref, proj_ref,
    state_ref, query_ref, far_state_ref, far_query_ref,
    held, near_state, near_query, sems,
):
    sources, depth, across = held.shape
    width = across // 4
    copies = []
    for source in range(sources):
        rows = pl.ds(pl.multiple_of(index_ref[source] * depth, depth), depth)
        copies.append(pltpu.make_async_copy(proj_ref.at[rows, :], held.at[source], sems.at[source]))
        copies[-1].start()
    mixes = mix_ref.shape[0]

    def split(source, state_out, query_out, base):
        copies[source].wait()
        lanes = pl.ds(pl.multiple_of(index_ref[source] * depth, depth), depth)
        for begin in range(0, depth, CHUNK):
            rows = slice(begin, begin + CHUNK)
            out = slice(base + begin, base + begin + CHUNK)
            value = held[source, rows, :]
            mixing = mix_ref[:, lanes][:, rows]
            mixing = jnp.concatenate([mixing, jnp.zeros((CHUNK - mixes, CHUNK), F32)], axis=0)
            state = jnp.concatenate([value[:, width : 3 * width], jnp.transpose(mixing)], axis=1)
            query = jnp.concatenate([value[:, :width], value[:, 3 * width :]], axis=1)
            state_out[out, :] = left_parts(state)
            query_out[out, :] = left_parts(query)

    for source in range(2):
        split(source, near_state, near_query, source * depth)
    half = own_ref.shape[0] // 2
    for rows in (slice(0, half), slice(half, 2 * half)):
        pieces = [own_ref[rows, :], beside_ref[rows, :]]
        state_ref[rows, :] = add_products(None, pieces, near_state, 0)
        query_ref[rows, :] = add_products(None, pieces, near_query, 0)
    for source in range(2, sources):
        split(source, far_state_ref, far_query_ref, (source - 2) * depth)


def late_kernel(count, segments, *refs):
    begin = segments[0].start
    held, refs = refs[: count * len(segments)], refs[count * len(segments) :]
    base_state, base_query, far_state, far_query, state_ref, query_ref, rim_ref = refs
    width = base_query.shape[1] // 2
    for turn, rows in enumerate(segments):
        pieces = [ref[...] for ref in held[turn * count : (turn + 1) * count]]
        out = slice(rows.start - begin, rows.stop - begin)
        state_ref[out, :] = add_products(base_state[rows, :], pieces, far_state, 0)
        query_ref[out, :] = add_products(base_query[rows, :], pieces, far_query, 0)
    last = state_ref.shape[0] - RIM
    rim_ref[:, :width] = query_ref[last:, :width]
    rim_ref[:, width:] = state_ref[last:, : 2 * width]


def partial_kernel(count, *refs):
    base_state, far_state, out_ref = refs[count:]
    out_ref[...] = add_products(
        base_state[: out_ref.shape[0], :], [ref[...] for ref in refs[:count]], far_state, 0
    )


def convolve(raw, start, columns, conv_ref, taps_at):
    taps = conv_ref.shape[0]
    conv = 0.0
    for tap in range(taps):
        spot = start - taps + 1 + tap
        conv = conv + conv_ref[tap : tap + 1, taps_at] * raw[spot : spot + CHUNK, columns]
    return conv * sigmoid(conv)


def unit_rows(value):
    return value * lax.rsqrt(jnp.sum(value * value, axis=1, keepdims=True) + 1e-06)


def key_pass(raw, conv_ref, rate, doc_ref, first_chunk, outs, state):
    key_ref, x_ref, y_ref, grid_ref, gamma_ref, plus_ref, chunk_ref, pair_ref = outs
    width = key_ref.shape[1]
    chunks = key_ref.shape[0] // CHUNK
    row = lax.broadcasted_iota(jnp.int32, (CHUNK, CHUNK), 0)
    col = lax.broadcasted_iota(jnp.int32, (CHUNK, CHUNK), 1)
    lower = row >= col
    tri = jnp.where(lower, 1.0, 0.0).astype(F32)
    eye = jnp.where(row == col, 1.0, 0.0).astype(F32)
    keys, values, betas, grids, gammas, tails = [], [], [], [], [], []
    for part in range(chunks):
        start = RIM + part * CHUNK
        rows = slice(part * CHUNK, (part + 1) * CHUNK)
        middle, last = slice(width, 2 * width), slice(2 * width, 3 * width)
        keys.append(unit_rows(convolve(raw, start, slice(0, width), conv_ref, middle)))
        values.append(convolve(raw, start, middle, conv_ref, last))
        mixing = raw[start : start + CHUNK, last]
        plus = softplus(mixing)
        plus_ref[rows, :] = plus
        betas.append(sigmoid(mixing[:, 0:1]))
        spot = first_chunk + part
        docs = jnp.broadcast_to(doc_ref[spot : spot + 1, :].astype(F32), (CHUNK, CHUNK))
        docs = jnp.transpose(docs)
        steps = jnp.where(col == 1, -rate * plus, jnp.where(col == 0, docs, 0.0))
        sums = jnp.dot(tri, steps, precision=lax.Precision.HIGHEST, preferred_element_type=F32)
        across = jnp.transpose(sums)
        smooth, count = sums[:, 1:2], sums[:, 0:1]
        span = (smooth - across[1:2, :]) - 20.0 * (count - across[0:1, :])
        grids.append(jnp.exp(jnp.where(lower, span, -1e30)))
        gammas.append(jnp.exp(smooth - 20.0 * count))
        last = sums[CHUNK - 1 : CHUNK, :]
        tails.append(jnp.exp((last[:, 1:2] - smooth) - 20.0 * (last[:, 0:1] - count)))
        key_ref[rows, :] = keys[part]
        grid_ref[rows, :] = grids[part]
        gamma_ref[rows, :] = jnp.broadcast_to(gammas[part], (CHUNK, width))
    across_keys = [jnp.transpose(key) for key in keys]
    grams = [
        parts_dot(left_parts(key), right_parts(across)) for key, across in zip(keys, across_keys)
    ]
    lowers = [jnp.where(row > col, beta * gram, 0.0) for beta, gram in zip(betas, grams)]
    inverses = unit_lower_inverse(lowers, row, col)
    states = []
    for part in range(chunks):
        rows = slice(part * CHUNK, (part + 1) * CHUNK)
        inverse, beta = inverses[part], betas[part]
        factor_x = product(inverse, beta * keys[part])
        factor_y = product(grids[part] * inverse, beta * values[part])
        x_ref[rows, :] = factor_x
        y_ref[rows, :] = factor_y
        onto = product(
            across_keys[part], jnp.concatenate([factor_x, tails[part] * factor_y], axis=1)
        )
        trans = gammas[part][CHUNK - 1 : CHUNK, :] * (eye - onto[:, :width])
        states.append((trans, onto[:, width:]))
        chunk_ref[part, 0] = trans
        chunk_ref[part, 1] = onto[:, width:]
    if state is not None:
        states.append(state)
    while len(states) > 1:
        joined = [followed(*states[at : at + 2]) for at in range(0, len(states) - 1, 2)]
        states = joined + states[2 * len(joined) :]
    pair_ref[0] = states[0][0]
    pair_ref[1] = states[0][1]


def followed(first, second):
    width = first[0].shape[0]
    onto = product(second[0], jnp.concatenate(first, axis=1))
    return onto[:, :width], onto[:, width:] + second[1]


def later_kernel(first_chunk, raw_ref, conv_ref, rate_ref, doc_ref, *outs):
    key_pass(raw_ref, conv_ref, rate_ref[0, 0], doc_ref, first_chunk, outs, None)


def earlier_kernel(first, count, *refs):
    held, refs = refs[:count], refs[count:]
    part_ref, far_ref, rim_ref, next_ref, state_ref, conv_ref, rate_ref, doc_ref = refs[:8]
    outs, raw = refs[8:-1], refs[-1]
    rows, width = part_ref.shape[0], state_ref.shape[1]
    raw[RIM : RIM + rows, :] = add_products(
        part_ref[...], [ref[...] for ref in held], far_ref, first
    )
    raw[:RIM, : 2 * width] = rim_ref[:, width:]
    raw[RIM + rows :, :] = next_ref[:RIM, :]
    key_pass(raw, conv_ref, rate_ref[0, 0], doc_ref, 0, outs, (state_ref[0], state_ref[1]))


def query_kernel(count, *refs):
    held, refs = refs[:count], refs[count:]
    base_ref, far_ref, rim_ref, next_ref, conv_ref = refs[:5]
    fields = [(refs[5:11], 0), (refs[11:17], 1)]
    carried_ref, local_ref, gate_ref, raw = refs[17:]
    width = carried_ref.shape[1]
    rows = held[0].shape[0]
    raw[RIM : RIM + rows, :] = add_products(
        base_ref[:rows, :], [ref[...] for ref in held], far_ref, 0
    )
    raw[:RIM, :width] = rim_ref[:, :width]
    raw[RIM + rows :, :] = next_ref[:RIM, :]
    row = lax.broadcasted_iota(jnp.int32, (CHUNK, CHUNK), 0)
    col = lax.broadcasted_iota(jnp.int32, (CHUNK, CHUNK), 1)
    state = None
    base = 0
    for (key_ref, x_ref, y_ref, grid_ref, gamma_ref, chunk_ref), later in fields:
        source = next_ref if later else raw
        for part in range(key_ref.shape[0] // CHUNK):
            start = RIM + part * CHUNK
            rows = slice(part * CHUNK, (part + 1) * CHUNK)
            out = slice(base, base + CHUNK)
            base += CHUNK
            columns = slice(0, width)
            query = unit_rows(convolve(source, start, columns, conv_ref, columns))
            gate = source[start : start + CHUNK, width:]
            gate_ref[out, :] = gate * sigmoid(gate)
            overlap = product(query, jnp.transpose(key_ref[rows, :]))
            carried = gamma_ref[rows, :] * (
                query - product(jnp.where(row >= col, overlap, 0.0), x_ref[rows, :])
            )
            local = product(grid_ref[rows, :] * overlap, y_ref[rows, :])
            trans, memory = chunk_ref[part, 0], chunk_ref[part, 1]
            if state is None:
                state = (trans, memory)
            else:
                onto = product(
                    jnp.concatenate([trans, carried], axis=0), jnp.concatenate(state, axis=1)
                )
                carried = onto[CHUNK:, :width]
                local = local + onto[CHUNK:, width:]
                state = (onto[:CHUNK, :width], onto[:CHUNK, width:] + memory)
            carried_ref[out, :] = carried
            local_ref[out, :] = local


def four_kernel(first_bit, carried, last, bits_ref, own_ref, one_ref, two_ref, three_ref, *refs):
    group_ref, level_ref, next_ref, pairs = refs[-4:]
    low_bit, high_bit = bits_ref[first_bit], bits_ref[first_bit + 1]
    place = 2 * high_bit + low_bit
    for mask, ref in enumerate((own_ref, one_ref, two_ref, three_ref)):
        pairs[place ^ mask] = ref[...]
    width = next_ref.shape[0]
    joined = lambda spot: jnp.concatenate([pairs[spot, 0], pairs[spot, 1]], axis=1)
    onto_low = product(pairs[1, 0], joined(0))
    onto_high = product(pairs[3, 0], joined(2))
    low_a, low_s = onto_low[:, :width], onto_low[:, width:] + pairs[1, 1]
    high_a, high_s = onto_high[:, :width], onto_high[:, width:] + pairs[3, 1]
    if last:
        group_ref[...] = product(high_a, low_s) + high_s
    else:
        onto = product(high_a, jnp.concatenate([low_a, low_s], axis=1))
        group_ref[0] = onto[:, :width]
        group_ref[1] = onto[:, width:] + high_s
    set_low = jnp.broadcast_to(low_bit, (width, width)) == 1
    set_high = jnp.broadcast_to(high_bit, (width, width)) == 1
    if carried:
        carry = refs[0][...]
        first = product(carry, jnp.concatenate([one_ref[0], one_ref[1]], axis=1))
        first_a, first_s = first[:, :width], first[:, width:]
    else:
        row = lax.broadcasted_iota(jnp.int32, (width, width), 0)
        col = lax.broadcasted_iota(jnp.int32, (width, width), 1)
        carry = jnp.where(row == col, 1.0, 0.0).astype(F32)
        first_a, first_s = one_ref[0], one_ref[1]
    level_ref[0] = jnp.where(set_low, first_s, 0.0)
    carry = jnp.where(set_low, first_a, carry)
    second = product(carry, jnp.concatenate([low_a, low_s], axis=1))
    level_ref[1] = jnp.where(set_high, second[:, width:], 0.0)
    next_ref[...] = jnp.where(set_high, second[:, :width], carry)


def mix_kernel(stages, single, bits_ref, carried_ref, local_ref, gate_ref, low_ref, high_ref, gain_ref, *refs):
    states = [ref[spot] for ref in refs[:stages] for spot in range(ref.shape[0])]
    if single:
        carry_ref, other_ref = refs[stages : stages + 2]
        upper = jnp.broadcast_to(bits_ref[single], other_ref.shape) == 1
        states.append(product(carry_ref[...], jnp.where(upper, other_ref[...], 0.0)))
    outs = refs[stages + (2 if single else 0) :]
    states = [right_parts(state) for state in states]
    carried = left_parts(carried_ref[...])
    weights = jnp.concatenate([low_ref[...], high_ref[...]], axis=0)
    mixed = weights[:, 2:3] * local_ref[...]
    for level, state in enumerate(states):
        mixed = mixed + weights[:, level + 3 : level + 4] * parts_dot(carried, state)
    scale = lax.rsqrt(jnp.mean(mixed * mixed, axis=1, keepdims=True) + 1e-05)
    normed = mixed * scale * gain_ref[...] * gate_ref[...]
    outs[0][...] = normed
    base = 0
    for out in outs[1:]:
        out[...] = normed[base : base + out.shape[0]]
        base += out.shape[0]


def block_product(pieces, weight, rows):
    parts = [halves(ref[rows, :]) for ref in pieces]
    high, low = (jnp.concatenate(part, axis=1) for part in zip(*parts))
    columns = weight.shape[1] // 2
    both = jnp.dot(high, weight, preferred_element_type=F32)
    rest = jnp.dot(low, weight[:, :columns], preferred_element_type=F32)
    return (both[:, :columns] + both[:, columns:]) + rest


def source_rows(index_ref, first, pieces, weight_ref):
    parts = []
    for spot, piece in enumerate(pieces):
        depth = piece.shape[1]
        rows = pl.ds(pl.multiple_of(index_ref[first + spot] * depth, depth), depth)
        parts.append(weight_ref[rows, :])
    return left_parts(jnp.concatenate(parts, axis=0))


def row_blocks(rows):
    return [slice(base, base + CHUNK) for base in range(0, rows, CHUNK)]


def near_kernel(index_ref, own_ref, near_ref, weight_ref, low_ref, high_ref):
    weight = source_rows(index_ref, 0, [own_ref, near_ref], weight_ref)
    half = low_ref.shape[0]
    for rows in row_blocks(half):
        low_ref[rows, :] = block_product([own_ref, near_ref], weight, rows)
        later = slice(half + rows.start, half + rows.stop)
        high_ref[rows, :] = block_product([own_ref, near_ref], weight, later)


def far_kernel(count, first, index_ref, *refs):
    held, (weight_ref, total_ref, out_ref) = refs[:-3], refs[-3:]
    weight = source_rows(index_ref, first, held[:count], weight_ref)
    base = 0
    for at in range(0, len(held), count):
        pieces = held[at : at + count]
        for rows in row_blocks(pieces[0].shape[0]):
            out = slice(base + rows.start, base + rows.stop)
            out_ref[out, :] = total_ref[out, :] + block_product(pieces, weight, rows)
        base += pieces[0].shape[0]


def last_kernel(count, first, index_ref, *refs):
    pieces = refs[:count]
    weight_ref, ready_ref, total_ref, out_ref, held, sems = refs[count:]
    half = ready_ref.shape[0]
    copies = [pltpu.make_async_copy(ready_ref, out_ref.at[:half, :], sems.at[0])]
    copies[0].start()
    weight = source_rows(index_ref, first, pieces, weight_ref)
    for spot, rows in enumerate(row_blocks(total_ref.shape[0])):
        held[rows, :] = total_ref[rows, :] + block_product(pieces, weight, rows)
        out = slice(half + rows.start, half + rows.stop)
        copies.append(
            pltpu.make_async_copy(held.at[rows, :], out_ref.at[out, :], sems.at[spot + 1])
        )
        copies[-1].start()
    for copy in copies:
        copy.wait()


def vmem_call(kernel, outs, scratch, cost, *args, any_in=(), any_out=False):
    spec = pl.BlockSpec(memory_space=pltpu.VMEM)
    small = pl.BlockSpec(memory_space=pltpu.SMEM)
    free = pl.BlockSpec(memory_space=pl.ANY)
    return pl.pallas_call(
        kernel,
        out_shape=outs,
        in_specs=[
            free if spot in any_in else small if arg.dtype == jnp.int32 and arg.ndim == 1 else spec
            for spot, arg in enumerate(args)
        ],
        out_specs=jax.tree.map(lambda unused: free if any_out else spec, outs),
        scratch_shapes=scratch,
        compiler_params=pltpu.CompilerParams(vmem_limit_bytes=VMEM_GRANT),
        cost_estimate=pl.CostEstimate(flops=int(cost * 1e9), bytes_accessed=1 << 20, transcendentals=0),
    )(*args)


def to_sibling(value):
    count = lax.axis_size("head")
    return lax.ppermute(value, "head", [(source, source ^ 1) for source in range(count)])


def to_chips(value):
    count = lax.axis_size("head")
    return [
        lax.ppermute(
            value, "head", [(source, (source + 2 * step) % count) for source in range(count)]
        )
        for step in range(1, count // 2)
    ]


def after(value, *earlier):
    return lax.optimization_barrier((value, *earlier))


def shards(tokens, w_proj, w_mix, conv_w, rates, doc_start, norm_gain, w_out):
    tok_rows, depth = tokens.shape
    width = w_proj.shape[1] // 4
    state_columns, query_columns = 2 * width + CHUNK, 2 * width
    heads, me = lax.axis_size("head"), lax.axis_index("head")
    blocks, my_index = lax.axis_size("ctx"), lax.axis_index("ctx")
    remote = [(me + heads - 2 * step) % heads for step in range(1, heads // 2)]
    order = [me, me ^ 1] + remote + [index ^ 1 for index in remote]
    bits = blocks.bit_length() - 1
    flags = [my_index >> bit & 1 for bit in range(bits)]
    index = jnp.stack(order + flags).astype(jnp.int32)
    count = heads - 2
    like = lambda *shape: jax.ShapeDtypeStruct(shape, F32)
    parts = lambda *shape: jax.ShapeDtypeStruct(shape, BF16)

    first = tok_rows // 2
    cut = first - RIM
    middle = tok_rows - CHUNK - RIM
    segments = (slice(cut, middle), slice(middle, tok_rows))
    late = [to_chips(tokens[rows]) for rows in segments]
    beside = to_sibling(tokens)
    early_rows, beside = after(tokens, beside)
    early = to_chips(early_rows[:cut])
    base_state, base_query, far_state, far_query = vmem_call(
        base_kernel,
        [like(tok_rows, state_columns), like(tok_rows, query_columns),
         parts(count * depth, 2 * state_columns), parts(count * depth, 2 * query_columns)],
        [pltpu.VMEM((heads, depth, 4 * width), F32),
         pltpu.VMEM((2 * depth, 2 * state_columns), BF16),
         pltpu.VMEM((2 * depth, 2 * query_columns), BF16),
         pltpu.SemaphoreType.DMA((heads,))],
        3, index, tokens, beside, w_mix.T, w_proj, any_in=(4,),
    )
    late, far_state = after(late, far_state)
    late_on = [[to_sibling(value) for value in values] for values in late]
    arrived = [value for pair in zip(late, late_on) for values in pair for value in values]
    late_state, late_query, rim = vmem_call(
        functools.partial(late_kernel, count, segments),
        [like(tok_rows - cut, state_columns), like(tok_rows - cut, query_columns),
         like(RIM, 3 * width)],
        [], 0.5, *arrived, base_state, base_query, far_state, far_query,
    )
    rim = lax.ppermute(rim, "ctx", [(source, source + 1) for source in range(blocks - 1)])
    docs = doc_start.reshape(tok_rows // CHUNK, CHUNK)
    rate = rates[:, None]

    def outs(rows):
        chunks = like(rows // CHUNK, 2, width, width)
        return [like(rows, width)] * 6 + [chunks, like(2, width, width)]

    later = vmem_call(
        functools.partial(later_kernel, first // CHUNK), outs(tok_rows - first), [], 0.5,
        late_state, conv_w, rate, docs,
    )
    early, pair_late, rim = after(early, later[7], rim)
    early_on = [to_sibling(value) for value in early]
    partial = vmem_call(
        functools.partial(partial_kernel, len(early)), like(cut, state_columns), [], 1,
        *early, base_state, far_state,
    )
    earlier = vmem_call(
        functools.partial(earlier_kernel, len(early), len(early)), outs(first),
        [pltpu.VMEM((first + RIM, state_columns), F32)], 5,
        *early_on, partial, far_state, rim, late_state, pair_late, conv_w, rate, docs,
    )

    pair = earlier[7]
    carry = ()
    levels = []
    for bit in range(0, bits - 1, 2):
        others = [
            lax.ppermute(
                pair, "ctx", [(source, source ^ (mask << bit)) for source in range(blocks)]
            )
            for mask in (1, 2, 3)
        ]
        last = bit + 2 >= bits - 1 and bits % 2
        group = [like(width, width)] if last else [like(2, width, width)]
        pair, level, *carry = vmem_call(
            functools.partial(four_kernel, heads + bit, bool(carry), last),
            group + [like(2, width, width), like(width, width)],
            [pltpu.VMEM((4, 2, width, width), F32)], 1,
            index, pair, *others, *carry,
        )
        levels.append(level)
    fields = vmem_call(
        functools.partial(query_kernel, count), [like(tok_rows, width)] * 3,
        [pltpu.VMEM((first + RIM, query_columns), F32)], 5,
        *early, *early_on, base_query, far_query, rim, late_query, conv_w,
        *earlier[:5], earlier[6], *later[:5], later[6],
    )
    single = []
    if bits % 2:
        reach = blocks // 2
        single = [
            *(carry or [jnp.eye(width, dtype=F32)]),
            lax.ppermute(
                pair if carry else pair[1],
                "ctx", [(source, source ^ reach) for source in range(blocks)],
            ),
        ]
    half = tok_rows // 2
    normed, *lows, high = vmem_call(
        functools.partial(mix_kernel, len(levels), heads + bits - 1 if single else 0),
        [like(tok_rows, width)] + [like(half // 2, width)] * 2 + [like(half, width)], [], 1,
        index, *fields, earlier[5], later[5], norm_gain[None, :], *levels, *single,
    )
    columns = w_out.shape[1]
    near = to_sibling(normed)
    far_lows = [to_chips(low) for low in lows]
    high, near = after(high, near)
    far_high = to_chips(high)
    total_low, total_high = vmem_call(
        near_kernel, [like(half, columns)] * 2, [], 2, index, normed, near, w_out
    )
    far_lows, total_low = after(far_lows, total_low)
    far_lows_on = [[to_sibling(value) for value in values] for values in far_lows]
    arrived = [value for pair in zip(far_lows, far_lows_on) for values in pair for value in values]
    total_low = vmem_call(
        functools.partial(far_kernel, count, 2), like(half, columns), [], 0.01,
        index, *arrived, w_out, total_low,
    )
    far_high, total_low = after(far_high, total_low)
    far_high_on = [to_sibling(value) for value in far_high]
    total_high = vmem_call(
        functools.partial(far_kernel, len(far_high), 2), like(half, columns), [], 1,
        index, *far_high, w_out, total_high,
    )
    return vmem_call(
        functools.partial(last_kernel, len(far_high), 2 + len(far_high)), like(tok_rows, columns),
        [pltpu.VMEM((half, columns), F32), pltpu.SemaphoreType.DMA((half // CHUNK + 1,))], 1,
        index, *far_high_on, w_out, total_low, total_high, any_out=True,
    )


def solution(mesh):
    placed = (
        P("ctx", "head"),
        P(None, "head"),
        P(None, "head"),
        P(None, "head"),
        P("head"),
        P("ctx"),
        P("head"),
        P(None, "head"),
    )
    return jax.shard_map(
        shards, mesh=mesh, in_specs=placed, out_specs=P("ctx", "head"), check_vma=False
    )
```

```python
import functools

import jax
import jax.numpy as jnp
from jax import lax
from jax.experimental import pallas as pl
from jax.experimental.pallas import tpu as pltpu
from jax.sharding import PartitionSpec as P

CHUNK = 128
RIM = 16
VMEM_GRANT = 16 << 20
F32 = jnp.float32
BF16 = jnp.bfloat16


def halves(value):
    high = value.astype(BF16)
    return high, (value - high.astype(F32)).astype(BF16)


def left_parts(value):
    return jnp.concatenate(halves(value), axis=1)


def right_parts(value):
    row = jnp.concatenate(halves(value), axis=1)
    return jnp.concatenate([row, row], axis=0)


def parts_dot(left, right):
    both = jnp.dot(left, right, preferred_element_type=F32)
    half = both.shape[1] // 2
    return both[:, :half] + both[:, half:]


def product(left, right):
    return parts_dot(left_parts(left), right_parts(right))


def softplus(value):
    return jnp.maximum(value, 0.0) + jnp.log1p(jnp.exp(-jnp.abs(value)))


def sigmoid(value):
    return 1.0 / (1.0 + jnp.exp(-value))


def unit_lower_inverse(lowers, row, col):
    size = lowers[0].shape[0]
    eye = jnp.where(row == col, 1.0, 0.0).astype(F32)
    inverses = [eye - jnp.where((row >> 1) == (col >> 1), lower, 0.0) for lower in lowers]
    lower_parts = [halves(lower) for lower in lowers]
    step = 1
    while 1 << step < size:
        off = ((row >> (step + 2)) == (col >> (step + 2))) & ((row >> step) > (col >> step))
        offs = [
            jnp.concatenate([jnp.where(off, part, jnp.zeros_like(part)) for part in parts], axis=1)
            for parts in lower_parts
        ]
        onto = [parts_dot(left, right_parts(inverse)) for left, inverse in zip(offs, inverses)]
        rights = [right_parts(value) for value in onto]
        squares = [parts_dot(left_parts(value), right) for value, right in zip(onto, rights)]
        firsts = [
            inverse - parts_dot(left_parts(inverse), right)
            for inverse, right in zip(inverses, rights)
        ]
        inverses = [first + product(first, square) for first, square in zip(firsts, squares)]
        step += 2
    return inverses


def add_products(total, pieces, weight_ref, first):
    columns = weight_ref.shape[1] // 2
    for spot, piece in enumerate(pieces):
        depth = piece.shape[1]
        rows = slice((first + spot) * depth, (first + spot + 1) * depth)
        high, low = halves(piece)
        both = jnp.dot(high, weight_ref[rows, :], preferred_element_type=F32)
        rest = jnp.dot(low, weight_ref[rows, :columns], preferred_element_type=F32)
        part = (both[:, :columns] + both[:, columns:]) + rest
        total = part if total is None else total + part
    return total


def base_kernel(
    index_ref, own_ref, beside_ref, mix_ref, proj_ref,
    state_ref, query_ref, far_state_ref, far_query_ref, flag_ref,
    held, near_state, near_query, sems,
):
    sources, depth, across = held.shape
    width = across // 4
    copies = []
    for source in range(sources):
        rows = pl.ds(pl.multiple_of(index_ref[source] * depth, depth), depth)
        copies.append(pltpu.make_async_copy(proj_ref.at[rows, :], held.at[source], sems.at[source]))
        copies[-1].start()
    for bit in range(flag_ref.shape[0]):
        flag_ref[bit : bit + 1, :] = jnp.broadcast_to(index_ref[sources + bit], (1, CHUNK))
    mixes = mix_ref.shape[0]

    def split(source, state_out, query_out, base):
        copies[source].wait()
        lanes = pl.ds(pl.multiple_of(index_ref[source] * depth, depth), depth)
        for begin in range(0, depth, CHUNK):
            rows = slice(begin, begin + CHUNK)
            out = slice(base + begin, base + begin + CHUNK)
            value = held[source, rows, :]
            mixing = mix_ref[:, lanes][:, rows]
            mixing = jnp.concatenate([mixing, jnp.zeros((CHUNK - mixes, CHUNK), F32)], axis=0)
            state = jnp.concatenate([value[:, width : 3 * width], jnp.transpose(mixing)], axis=1)
            query = jnp.concatenate([value[:, :width], value[:, 3 * width :]], axis=1)
            state_out[out, :] = left_parts(state)
            query_out[out, :] = left_parts(query)

    for source in range(2):
        split(source, near_state, near_query, source * depth)
    half = own_ref.shape[0] // 2
    for rows in (slice(0, half), slice(half, 2 * half)):
        pieces = [own_ref[rows, :], beside_ref[rows, :]]
        state_ref[rows, :] = add_products(None, pieces, near_state, 0)
        query_ref[rows, :] = add_products(None, pieces, near_query, 0)
    for source in range(2, sources):
        split(source, far_state_ref, far_query_ref, (source - 2) * depth)


def late_kernel(count, segments, *refs):
    begin = segments[0].start
    held, refs = refs[: count * len(segments)], refs[count * len(segments) :]
    base_state, base_query, far_state, far_query, state_ref, query_ref, rim_ref = refs
    width = base_query.shape[1] // 2
    for turn, rows in enumerate(segments):
        pieces = [ref[...] for ref in held[turn * count : (turn + 1) * count]]
        out = slice(rows.start - begin, rows.stop - begin)
        state_ref[out, :] = add_products(base_state[rows, :], pieces, far_state, 0)
        query_ref[out, :] = add_products(base_query[rows, :], pieces, far_query, 0)
    last = state_ref.shape[0] - RIM
    rim_ref[:, :width] = query_ref[last:, :width]
    rim_ref[:, width:] = state_ref[last:, : 2 * width]


def partial_kernel(count, *refs):
    base_state, far_state, out_ref = refs[count:]
    out_ref[...] = add_products(
        base_state[: out_ref.shape[0], :], [ref[...] for ref in refs[:count]], far_state, 0
    )


def convolve(raw, start, columns, conv_ref, taps_at):
    taps = conv_ref.shape[0]
    conv = 0.0
    for tap in range(taps):
        spot = start - taps + 1 + tap
        conv = conv + conv_ref[tap : tap + 1, taps_at] * raw[spot : spot + CHUNK, columns]
    return conv * sigmoid(conv)


def unit_rows(value):
    return value * lax.rsqrt(jnp.sum(value * value, axis=1, keepdims=True) + 1e-06)


def key_pass(raw, conv_ref, rate, doc_ref, first_chunk, outs, state):
    key_ref, x_ref, y_ref, grid_ref, gamma_ref, plus_ref, chunk_ref, pair_ref = outs
    width = key_ref.shape[1]
    chunks = key_ref.shape[0] // CHUNK
    row = lax.broadcasted_iota(jnp.int32, (CHUNK, CHUNK), 0)
    col = lax.broadcasted_iota(jnp.int32, (CHUNK, CHUNK), 1)
    lower = row >= col
    tri = jnp.where(lower, 1.0, 0.0).astype(F32)
    eye = jnp.where(row == col, 1.0, 0.0).astype(F32)
    keys, values, betas, grids, gammas, tails = [], [], [], [], [], []
    for part in range(chunks):
        start = RIM + part * CHUNK
        rows = slice(part * CHUNK, (part + 1) * CHUNK)
        middle, last = slice(width, 2 * width), slice(2 * width, 3 * width)
        keys.append(unit_rows(convolve(raw, start, slice(0, width), conv_ref, middle)))
        values.append(convolve(raw, start, middle, conv_ref, last))
        mixing = raw[start : start + CHUNK, last]
        plus = softplus(mixing)
        plus_ref[rows, :] = plus
        betas.append(sigmoid(mixing[:, 0:1]))
        spot = first_chunk + part
        docs = jnp.broadcast_to(doc_ref[spot : spot + 1, :].astype(F32), (CHUNK, CHUNK))
        docs = jnp.transpose(docs)
        steps = jnp.where(col == 1, -rate * plus, jnp.where(col == 0, docs, 0.0))
        sums = jnp.dot(tri, steps, precision=lax.Precision.HIGHEST, preferred_element_type=F32)
        across = jnp.transpose(sums)
        smooth, count = sums[:, 1:2], sums[:, 0:1]
        span = (smooth - across[1:2, :]) - 20.0 * (count - across[0:1, :])
        grids.append(jnp.exp(jnp.where(lower, span, -1e30)))
        gammas.append(jnp.exp(smooth - 20.0 * count))
        last = sums[CHUNK - 1 : CHUNK, :]
        tails.append(jnp.exp((last[:, 1:2] - smooth) - 20.0 * (last[:, 0:1] - count)))
        key_ref[rows, :] = keys[part]
        grid_ref[rows, :] = grids[part]
        gamma_ref[rows, :] = jnp.broadcast_to(gammas[part], (CHUNK, width))
    across_keys = [jnp.transpose(key) for key in keys]
    grams = [
        parts_dot(left_parts(key), right_parts(across)) for key, across in zip(keys, across_keys)
    ]
    lowers = [jnp.where(row > col, beta * gram, 0.0) for beta, gram in zip(betas, grams)]
    inverses = unit_lower_inverse(lowers, row, col)
    states = []
    for part in range(chunks):
        rows = slice(part * CHUNK, (part + 1) * CHUNK)
        inverse, beta = inverses[part], betas[part]
        factor_x = product(inverse, beta * keys[part])
        factor_y = product(grids[part] * inverse, beta * values[part])
        x_ref[rows, :] = factor_x
        y_ref[rows, :] = factor_y
        onto = product(
            across_keys[part], jnp.concatenate([factor_x, tails[part] * factor_y], axis=1)
        )
        trans = gammas[part][CHUNK - 1 : CHUNK, :] * (eye - onto[:, :width])
        states.append((trans, onto[:, width:]))
        chunk_ref[part, 0] = trans
        chunk_ref[part, 1] = onto[:, width:]
    if state is not None:
        states.append(state)
    while len(states) > 1:
        joined = [followed(*states[at : at + 2]) for at in range(0, len(states) - 1, 2)]
        states = joined + states[2 * len(joined) :]
    pair_ref[0] = states[0][0]
    pair_ref[1] = states[0][1]


def followed(first, second):
    width = first[0].shape[0]
    onto = product(second[0], jnp.concatenate(first, axis=1))
    return onto[:, :width], onto[:, width:] + second[1]


def later_kernel(first_chunk, raw_ref, conv_ref, rate_ref, doc_ref, *outs):
    key_pass(raw_ref, conv_ref, rate_ref[0, 0], doc_ref, first_chunk, outs, None)


def earlier_kernel(first, count, *refs):
    held, refs = refs[:count], refs[count:]
    part_ref, far_ref, rim_ref, next_ref, state_ref, conv_ref, rate_ref, doc_ref = refs[:8]
    outs, raw = refs[8:-1], refs[-1]
    rows, width = part_ref.shape[0], state_ref.shape[1]
    raw[RIM : RIM + rows, :] = add_products(
        part_ref[...], [ref[...] for ref in held], far_ref, first
    )
    raw[:RIM, : 2 * width] = rim_ref[:, width:]
    raw[RIM + rows :, :] = next_ref[:RIM, :]
    key_pass(raw, conv_ref, rate_ref[0, 0], doc_ref, 0, outs, (state_ref[0], state_ref[1]))


def query_kernel(count, *refs):
    held, refs = refs[:count], refs[count:]
    base_ref, far_ref, rim_ref, next_ref, conv_ref = refs[:5]
    fields = [(refs[5:11], 0), (refs[11:17], 1)]
    carried_ref, local_ref, gate_ref, raw = refs[17:]
    width = carried_ref.shape[1]
    rows = held[0].shape[0]
    raw[RIM : RIM + rows, :] = add_products(
        base_ref[:rows, :], [ref[...] for ref in held], far_ref, 0
    )
    raw[:RIM, :width] = rim_ref[:, :width]
    raw[RIM + rows :, :] = next_ref[:RIM, :]
    row = lax.broadcasted_iota(jnp.int32, (CHUNK, CHUNK), 0)
    col = lax.broadcasted_iota(jnp.int32, (CHUNK, CHUNK), 1)
    state = None
    base = 0
    for (key_ref, x_ref, y_ref, grid_ref, gamma_ref, chunk_ref), later in fields:
        source = next_ref if later else raw
        for part in range(key_ref.shape[0] // CHUNK):
            start = RIM + part * CHUNK
            rows = slice(part * CHUNK, (part + 1) * CHUNK)
            out = slice(base, base + CHUNK)
            base += CHUNK
            columns = slice(0, width)
            query = unit_rows(convolve(source, start, columns, conv_ref, columns))
            gate = source[start : start + CHUNK, width:]
            gate_ref[out, :] = gate * sigmoid(gate)
            overlap = product(query, jnp.transpose(key_ref[rows, :]))
            carried = gamma_ref[rows, :] * (
                query - product(jnp.where(row >= col, overlap, 0.0), x_ref[rows, :])
            )
            local = product(grid_ref[rows, :] * overlap, y_ref[rows, :])
            trans, memory = chunk_ref[part, 0], chunk_ref[part, 1]
            if state is None:
                state = (trans, memory)
            else:
                onto = product(
                    jnp.concatenate([trans, carried], axis=0), jnp.concatenate(state, axis=1)
                )
                carried = onto[CHUNK:, :width]
                local = local + onto[CHUNK:, width:]
                state = (onto[:CHUNK, :width], onto[:CHUNK, width:] + memory)
            carried_ref[out, :] = carried
            local_ref[out, :] = local


def four_kernel(bit, carried, last, flag_ref, own_ref, one_ref, two_ref, three_ref, *refs):
    group_ref, level_ref, next_ref = refs[-3:]
    width = next_ref.shape[0]
    flag = lambda at: jnp.broadcast_to(flag_ref[at : at + 1, :], (width, width)) == 1
    set_low, set_high = flag(bit), flag(bit + 1)
    held = (own_ref, one_ref, two_ref, three_ref)

    def placed(part):
        by_low = [jnp.where(set_low, held[at ^ 1][part], held[at][part]) for at in range(4)]
        return [jnp.where(set_high, by_low[at ^ 2], by_low[at]) for at in range(4)]

    trans, memory = placed(0), placed(1)
    joined = lambda at: jnp.concatenate([trans[at], memory[at]], axis=1)
    onto_low = product(trans[1], joined(0))
    onto_high = product(trans[3], joined(2))
    low_a, low_s = onto_low[:, :width], onto_low[:, width:] + memory[1]
    high_a, high_s = onto_high[:, :width], onto_high[:, width:] + memory[3]
    if last:
        group_ref[...] = product(high_a, low_s) + high_s
    else:
        onto = product(high_a, jnp.concatenate([low_a, low_s], axis=1))
        group_ref[0] = onto[:, :width]
        group_ref[1] = onto[:, width:] + high_s
    if carried:
        carry = refs[0][...]
        first = product(carry, jnp.concatenate([one_ref[0], one_ref[1]], axis=1))
        first_a, first_s = first[:, :width], first[:, width:]
    else:
        row = lax.broadcasted_iota(jnp.int32, (width, width), 0)
        col = lax.broadcasted_iota(jnp.int32, (width, width), 1)
        carry = jnp.where(row == col, 1.0, 0.0).astype(F32)
        first_a, first_s = one_ref[0], one_ref[1]
    level_ref[0] = jnp.where(set_low, first_s, 0.0)
    carry = jnp.where(set_low, first_a, carry)
    second = product(carry, jnp.concatenate([low_a, low_s], axis=1))
    level_ref[1] = jnp.where(set_high, second[:, width:], 0.0)
    carry = jnp.where(set_high, second[:, :width], carry)
    next_ref[...] = jnp.where(flag(bit + 2), carry, 0.0) if last else carry


def mix_kernel(stages, single, carried_ref, local_ref, gate_ref, low_ref, high_ref, gain_ref, *refs):
    states = [ref[spot] for ref in refs[:stages] for spot in range(ref.shape[0])]
    if single:
        states.append(product(refs[stages][...], refs[stages + 1][...]))
    outs = refs[stages + (2 if single else 0) :]
    states = [right_parts(state) for state in states]
    carried = left_parts(carried_ref[...])
    weights = jnp.concatenate([low_ref[...], high_ref[...]], axis=0)
    mixed = weights[:, 2:3] * local_ref[...]
    for level, state in enumerate(states):
        mixed = mixed + weights[:, level + 3 : level + 4] * parts_dot(carried, state)
    scale = lax.rsqrt(jnp.mean(mixed * mixed, axis=1, keepdims=True) + 1e-05)
    normed = mixed * scale * gain_ref[...] * gate_ref[...]
    outs[0][...] = normed
    base = 0
    for out in outs[1:]:
        out[...] = normed[base : base + out.shape[0]]
        base += out.shape[0]


def block_product(pieces, weight, rows):
    parts = [halves(ref[rows, :]) for ref in pieces]
    high, low = (jnp.concatenate(part, axis=1) for part in zip(*parts))
    columns = weight.shape[1] // 2
    both = jnp.dot(high, weight, preferred_element_type=F32)
    rest = jnp.dot(low, weight[:, :columns], preferred_element_type=F32)
    return (both[:, :columns] + both[:, columns:]) + rest


def order_kernel(sources, index_ref, weight_ref, out_ref):
    depth = weight_ref.shape[0] // sources
    for source in range(sources):
        rows = pl.ds(pl.multiple_of(index_ref[source] * depth, depth), depth)
        out_ref[source * depth : (source + 1) * depth, :] = left_parts(weight_ref[rows, :])


def source_rows(first, pieces, weight_ref):
    depth = pieces[0].shape[1]
    return weight_ref[first * depth : (first + len(pieces)) * depth, :]


def row_blocks(rows):
    return [slice(base, base + CHUNK) for base in range(0, rows, CHUNK)]


def near_kernel(own_ref, near_ref, weight_ref, low_ref, high_ref):
    weight = source_rows(0, [own_ref, near_ref], weight_ref)
    half = low_ref.shape[0]
    for rows in row_blocks(half):
        low_ref[rows, :] = block_product([own_ref, near_ref], weight, rows)
        later = slice(half + rows.start, half + rows.stop)
        high_ref[rows, :] = block_product([own_ref, near_ref], weight, later)


def far_kernel(count, first, *refs):
    held, (weight_ref, total_ref, out_ref) = refs[:-3], refs[-3:]
    weight = source_rows(first, held[:count], weight_ref)
    base = 0
    for at in range(0, len(held), count):
        pieces = held[at : at + count]
        for rows in row_blocks(pieces[0].shape[0]):
            out = slice(base + rows.start, base + rows.stop)
            out_ref[out, :] = total_ref[out, :] + block_product(pieces, weight, rows)
        base += pieces[0].shape[0]


def last_kernel(count, first, *refs):
    pieces = refs[:count]
    weight_ref, ready_ref, total_ref, out_ref, held, sems = refs[count:]
    half = ready_ref.shape[0]
    copies = [pltpu.make_async_copy(ready_ref, out_ref.at[:half, :], sems.at[0])]
    copies[0].start()
    weight = source_rows(first, pieces, weight_ref)
    for spot, rows in enumerate(row_blocks(total_ref.shape[0])):
        held[rows, :] = total_ref[rows, :] + block_product(pieces, weight, rows)
        out = slice(half + rows.start, half + rows.stop)
        copies.append(
            pltpu.make_async_copy(held.at[rows, :], out_ref.at[out, :], sems.at[spot + 1])
        )
        copies[-1].start()
    for copy in copies:
        copy.wait()


def vmem_call(kernel, outs, scratch, cost, *args, any_in=(), any_out=False):
    spec = pl.BlockSpec(memory_space=pltpu.VMEM)
    small = pl.BlockSpec(memory_space=pltpu.SMEM)
    free = pl.BlockSpec(memory_space=pl.ANY)
    return pl.pallas_call(
        kernel,
        out_shape=outs,
        in_specs=[
            free if spot in any_in else small if arg.dtype == jnp.int32 and arg.ndim == 1 else spec
            for spot, arg in enumerate(args)
        ],
        out_specs=jax.tree.map(lambda unused: free if any_out else spec, outs),
        scratch_shapes=scratch,
        compiler_params=pltpu.CompilerParams(vmem_limit_bytes=VMEM_GRANT),
        cost_estimate=pl.CostEstimate(flops=int(cost * 1e9), bytes_accessed=1 << 20, transcendentals=0),
    )(*args)


def to_sibling(value):
    count = lax.axis_size("head")
    return lax.ppermute(value, "head", [(source, source ^ 1) for source in range(count)])


def to_chips(value):
    count = lax.axis_size("head")
    return [
        lax.ppermute(
            value, "head", [(source, (source + 2 * step) % count) for source in range(count)]
        )
        for step in range(1, count // 2)
    ]


def after(value, *earlier):
    return lax.optimization_barrier((value, *earlier))


def shards(tokens, w_proj, w_mix, conv_w, rates, doc_start, norm_gain, w_out):
    tok_rows, depth = tokens.shape
    width = w_proj.shape[1] // 4
    state_columns, query_columns = 2 * width + CHUNK, 2 * width
    heads, me = lax.axis_size("head"), lax.axis_index("head")
    blocks, my_index = lax.axis_size("ctx"), lax.axis_index("ctx")
    remote = [(me + heads - 2 * step) % heads for step in range(1, heads // 2)]
    order = [me, me ^ 1] + remote + [index ^ 1 for index in remote]
    bits = blocks.bit_length() - 1
    index = jnp.stack(order + [my_index >> bit & 1 for bit in range(bits)]).astype(jnp.int32)
    count = heads - 2
    like = lambda *shape: jax.ShapeDtypeStruct(shape, F32)
    parts = lambda *shape: jax.ShapeDtypeStruct(shape, BF16)

    first = tok_rows // 2
    cut = first - RIM
    middle = tok_rows - CHUNK - RIM
    segments = (slice(cut, middle), slice(middle, tok_rows))
    late = [to_chips(tokens[rows]) for rows in segments]
    beside = to_sibling(tokens)
    early_rows, beside = after(tokens, beside)
    early = to_chips(early_rows[:cut])
    base_state, base_query, far_state, far_query, flags = vmem_call(
        base_kernel,
        [like(tok_rows, state_columns), like(tok_rows, query_columns),
         parts(count * depth, 2 * state_columns), parts(count * depth, 2 * query_columns),
         jax.ShapeDtypeStruct((bits, CHUNK), jnp.int32)],
        [pltpu.VMEM((heads, depth, 4 * width), F32),
         pltpu.VMEM((2 * depth, 2 * state_columns), BF16),
         pltpu.VMEM((2 * depth, 2 * query_columns), BF16),
         pltpu.SemaphoreType.DMA((heads,))],
        3, index, tokens, beside, w_mix.T, w_proj, any_in=(4,),
    )
    late, far_state = after(late, far_state)
    late_on = [[to_sibling(value) for value in values] for values in late]
    arrived = [value for pair in zip(late, late_on) for values in pair for value in values]
    late_state, late_query, rim = vmem_call(
        functools.partial(late_kernel, count, segments),
        [like(tok_rows - cut, state_columns), like(tok_rows - cut, query_columns),
         like(RIM, 3 * width)],
        [], 0.5, *arrived, base_state, base_query, far_state, far_query,
    )
    rim = lax.ppermute(rim, "ctx", [(source, source + 1) for source in range(blocks - 1)])
    docs = doc_start.reshape(tok_rows // CHUNK, CHUNK)
    rate = rates[:, None]

    def outs(rows):
        chunks = like(rows // CHUNK, 2, width, width)
        return [like(rows, width)] * 6 + [chunks, like(2, width, width)]

    later = vmem_call(
        functools.partial(later_kernel, first // CHUNK), outs(tok_rows - first), [], 0.5,
        late_state, conv_w, rate, docs,
    )
    early, pair_late, rim = after(early, later[7], rim)
    early_on = [to_sibling(value) for value in early]
    partial = vmem_call(
        functools.partial(partial_kernel, len(early)), like(cut, state_columns), [], 1,
        *early, base_state, far_state,
    )
    earlier = vmem_call(
        functools.partial(earlier_kernel, len(early), len(early)), outs(first),
        [pltpu.VMEM((first + RIM, state_columns), F32)], 5,
        *early_on, partial, far_state, rim, late_state, pair_late, conv_w, rate, docs,
    )

    pair = earlier[7]
    fields = vmem_call(
        functools.partial(query_kernel, count), [like(tok_rows, width)] * 3,
        [pltpu.VMEM((first + RIM, query_columns), F32)], 5,
        *early, *early_on, base_query, far_query, rim, late_query, conv_w,
        *earlier[:5], earlier[6], *later[:5], later[6],
    )
    own_weight = vmem_call(
        functools.partial(order_kernel, heads), parts(w_out.shape[0], 2 * w_out.shape[1]), [], 1,
        index, w_out,
    )
    carry = ()
    levels = []
    for bit in range(0, bits - 1, 2):
        others = [
            lax.ppermute(
                pair, "ctx", [(source, source ^ (mask << bit)) for source in range(blocks)]
            )
            for mask in (1, 2, 3)
        ]
        if not bit:
            others[0], *fields, own_weight = after(others[0], *fields, own_weight)
        last = bit + 2 >= bits - 1 and bits % 2
        group = [like(width, width)] if last else [like(2, width, width)]
        pair, level, *carry = vmem_call(
            functools.partial(four_kernel, bit, bool(carry), last),
            group + [like(2, width, width), like(width, width)], [], 1,
            flags, pair, *others, *carry,
        )
        levels.append(level)
    single = []
    if bits % 2:
        reach = blocks // 2
        single = [
            *(carry or [jnp.where(my_index >= reach, jnp.eye(width, dtype=F32), 0.0)]),
            lax.ppermute(
                pair if carry else pair[1],
                "ctx", [(source, source ^ reach) for source in range(blocks)],
            ),
        ]
    half = tok_rows // 2
    normed, *lows, high = vmem_call(
        functools.partial(mix_kernel, len(levels), bool(single)),
        [like(tok_rows, width)] + [like(half // 2, width)] * 2 + [like(half, width)], [], 1,
        *fields, earlier[5], later[5], norm_gain[None, :], *levels, *single,
    )
    columns = w_out.shape[1]
    near = to_sibling(normed)
    far_lows = [to_chips(low) for low in lows]
    high, near = after(high, near)
    far_high = to_chips(high)
    total_low, total_high = vmem_call(
        near_kernel, [like(half, columns)] * 2, [], 2, normed, near, own_weight
    )
    far_lows, total_low = after(far_lows, total_low)
    far_lows_on = [[to_sibling(value) for value in values] for values in far_lows]
    arrived = [value for pair in zip(far_lows, far_lows_on) for values in pair for value in values]
    total_low = vmem_call(
        functools.partial(far_kernel, count, 2), like(half, columns), [], 0.01,
        *arrived, own_weight, total_low,
    )
    far_high, total_low = after(far_high, total_low)
    far_high_on = [to_sibling(value) for value in far_high]
    total_high = vmem_call(
        functools.partial(far_kernel, len(far_high), 2), like(half, columns), [], 1,
        *far_high, own_weight, total_high,
    )
    return vmem_call(
        functools.partial(last_kernel, len(far_high), 2 + len(far_high)), like(tok_rows, columns),
        [pltpu.VMEM((half, columns), F32), pltpu.SemaphoreType.DMA((half // CHUNK + 1,))], 1,
        *far_high_on, own_weight, total_low, total_high, any_out=True,
    )


def solution(mesh):
    placed = (
        P("ctx", "head"),
        P(None, "head"),
        P(None, "head"),
        P(None, "head"),
        P("head"),
        P("ctx"),
        P("head"),
        P(None, "head"),
    )
    return jax.shard_map(
        shards, mesh=mesh, in_specs=placed, out_specs=P("ctx", "head"), check_vma=False
    )
```

```python
import functools

import jax
import jax.numpy as jnp
from jax import lax
from jax.experimental import pallas as pl
from jax.experimental.pallas import tpu as pltpu
from jax.sharding import PartitionSpec as P

CHUNK = 128
RIM = 16
VMEM_GRANT = 16 << 20
F32 = jnp.float32
BF16 = jnp.bfloat16


def halves(value):
    high = value.astype(BF16)
    return high, (value - high.astype(F32)).astype(BF16)


def left_parts(value):
    return jnp.concatenate(halves(value), axis=1)


def right_parts(value):
    row = jnp.concatenate(halves(value), axis=1)
    return jnp.concatenate([row, row], axis=0)


def parts_dot(left, right):
    both = jnp.dot(left, right, preferred_element_type=F32)
    half = both.shape[1] // 2
    return both[:, :half] + both[:, half:]


def product(left, right):
    return parts_dot(left_parts(left), right_parts(right))


def softplus(value):
    return jnp.maximum(value, 0.0) + jnp.log1p(jnp.exp(-jnp.abs(value)))


def sigmoid(value):
    return 1.0 / (1.0 + jnp.exp(-value))


def unit_lower_inverse(lowers, row, col):
    size = lowers[0].shape[0]
    eye = jnp.where(row == col, 1.0, 0.0).astype(F32)
    inverses = [eye - jnp.where((row >> 1) == (col >> 1), lower, 0.0) for lower in lowers]
    lower_parts = [halves(lower) for lower in lowers]
    step = 1
    while 1 << step < size:
        off = ((row >> (step + 2)) == (col >> (step + 2))) & ((row >> step) > (col >> step))
        offs = [
            jnp.concatenate([jnp.where(off, part, jnp.zeros_like(part)) for part in parts], axis=1)
            for parts in lower_parts
        ]
        onto = [parts_dot(left, right_parts(inverse)) for left, inverse in zip(offs, inverses)]
        rights = [right_parts(value) for value in onto]
        squares = [parts_dot(left_parts(value), right) for value, right in zip(onto, rights)]
        firsts = [
            inverse - parts_dot(left_parts(inverse), right)
            for inverse, right in zip(inverses, rights)
        ]
        inverses = [first + product(first, square) for first, square in zip(firsts, squares)]
        step += 2
    return inverses


def add_products(total, pieces, weight_ref, first):
    columns = weight_ref.shape[1] // 2
    for spot, piece in enumerate(pieces):
        depth = piece.shape[1]
        rows = slice((first + spot) * depth, (first + spot + 1) * depth)
        high, low = halves(piece)
        both = jnp.dot(high, weight_ref[rows, :], preferred_element_type=F32)
        rest = jnp.dot(low, weight_ref[rows, :columns], preferred_element_type=F32)
        part = (both[:, :columns] + both[:, columns:]) + rest
        total = part if total is None else total + part
    return total


def base_kernel(
    index_ref, own_ref, beside_ref, mix_ref, proj_ref,
    state_ref, query_ref, far_state_ref, far_query_ref, flag_ref,
    held, near_state, near_query, sems,
):
    sources, depth, across = held.shape
    width = across // 4
    copies = []
    for source in range(sources):
        rows = pl.ds(pl.multiple_of(index_ref[source] * depth, depth), depth)
        copies.append(pltpu.make_async_copy(proj_ref.at[rows, :], held.at[source], sems.at[source]))
        copies[-1].start()
    for bit in range(flag_ref.shape[0]):
        flag_ref[bit : bit + 1, :] = jnp.broadcast_to(index_ref[sources + bit], (1, CHUNK))
    mixes = mix_ref.shape[0]

    def split(source, state_out, query_out, base):
        copies[source].wait()
        lanes = pl.ds(pl.multiple_of(index_ref[source] * depth, depth), depth)
        for begin in range(0, depth, CHUNK):
            rows = slice(begin, begin + CHUNK)
            out = slice(base + begin, base + begin + CHUNK)
            value = held[source, rows, :]
            mixing = mix_ref[:, lanes][:, rows]
            mixing = jnp.concatenate([mixing, jnp.zeros((CHUNK - mixes, CHUNK), F32)], axis=0)
            state = jnp.concatenate([value[:, width : 3 * width], jnp.transpose(mixing)], axis=1)
            query = jnp.concatenate([value[:, :width], value[:, 3 * width :]], axis=1)
            state_out[out, :] = left_parts(state)
            query_out[out, :] = left_parts(query)

    for source in range(2):
        split(source, near_state, near_query, source * depth)
    half = own_ref.shape[0] // 2
    for rows in (slice(0, half), slice(half, 2 * half)):
        pieces = [own_ref[rows, :], beside_ref[rows, :]]
        state_ref[rows, :] = add_products(None, pieces, near_state, 0)
        query_ref[rows, :] = add_products(None, pieces, near_query, 0)
    for source in range(2, sources):
        split(source, far_state_ref, far_query_ref, (source - 2) * depth)


def late_kernel(count, segments, *refs):
    begin = segments[0].start
    held, refs = refs[: count * len(segments)], refs[count * len(segments) :]
    base_state, base_query, far_state, far_query, state_ref, query_ref, rim_ref = refs
    width = base_query.shape[1] // 2
    for turn, rows in enumerate(segments):
        pieces = [ref[...] for ref in held[turn * count : (turn + 1) * count]]
        out = slice(rows.start - begin, rows.stop - begin)
        state_ref[out, :] = add_products(base_state[rows, :], pieces, far_state, 0)
        query_ref[out, :] = add_products(base_query[rows, :], pieces, far_query, 0)
    last = state_ref.shape[0] - RIM
    rim_ref[:, :width] = query_ref[last:, :width]
    rim_ref[:, width:] = state_ref[last:, : 2 * width]


def partial_kernel(count, *refs):
    base_state, far_state, out_ref = refs[count:]
    out_ref[...] = add_products(
        base_state[: out_ref.shape[0], :], [ref[...] for ref in refs[:count]], far_state, 0
    )


def convolve(raw, start, columns, conv_ref, taps_at):
    taps = conv_ref.shape[0]
    conv = 0.0
    for tap in range(taps):
        spot = start - taps + 1 + tap
        conv = conv + conv_ref[tap : tap + 1, taps_at] * raw[spot : spot + CHUNK, columns]
    return conv * sigmoid(conv)


def unit_rows(value):
    return value * lax.rsqrt(jnp.sum(value * value, axis=1, keepdims=True) + 1e-06)


def key_pass(raw, conv_ref, rate, doc_ref, first_chunk, outs, state):
    key_ref, x_ref, y_ref, grid_ref, gamma_ref, plus_ref, chunk_ref, pair_ref = outs
    width = key_ref.shape[1]
    chunks = key_ref.shape[0] // CHUNK
    row = lax.broadcasted_iota(jnp.int32, (CHUNK, CHUNK), 0)
    col = lax.broadcasted_iota(jnp.int32, (CHUNK, CHUNK), 1)
    lower = row >= col
    tri = jnp.where(lower, 1.0, 0.0).astype(F32)
    eye = jnp.where(row == col, 1.0, 0.0).astype(F32)
    keys, values, betas, grids, gammas, tails = [], [], [], [], [], []
    for part in range(chunks):
        start = RIM + part * CHUNK
        rows = slice(part * CHUNK, (part + 1) * CHUNK)
        middle, last = slice(width, 2 * width), slice(2 * width, 3 * width)
        keys.append(unit_rows(convolve(raw, start, slice(0, width), conv_ref, middle)))
        values.append(convolve(raw, start, middle, conv_ref, last))
        mixing = raw[start : start + CHUNK, last]
        plus = softplus(mixing)
        plus_ref[rows, :] = plus
        betas.append(sigmoid(mixing[:, 0:1]))
        spot = first_chunk + part
        docs = jnp.broadcast_to(doc_ref[spot : spot + 1, :].astype(F32), (CHUNK, CHUNK))
        docs = jnp.transpose(docs)
        steps = jnp.where(col == 1, -rate * plus, jnp.where(col == 0, docs, 0.0))
        sums = jnp.dot(tri, steps, precision=lax.Precision.HIGHEST, preferred_element_type=F32)
        across = jnp.transpose(sums)
        smooth, count = sums[:, 1:2], sums[:, 0:1]
        span = (smooth - across[1:2, :]) - 20.0 * (count - across[0:1, :])
        grids.append(jnp.exp(jnp.where(lower, span, -1e30)))
        gammas.append(jnp.exp(smooth - 20.0 * count))
        last = sums[CHUNK - 1 : CHUNK, :]
        tails.append(jnp.exp((last[:, 1:2] - smooth) - 20.0 * (last[:, 0:1] - count)))
        key_ref[rows, :] = keys[part]
        grid_ref[rows, :] = grids[part]
        gamma_ref[rows, :] = jnp.broadcast_to(gammas[part], (CHUNK, width))
    across_keys = [jnp.transpose(key) for key in keys]
    grams = [
        parts_dot(left_parts(key), right_parts(across)) for key, across in zip(keys, across_keys)
    ]
    lowers = [jnp.where(row > col, beta * gram, 0.0) for beta, gram in zip(betas, grams)]
    inverses = unit_lower_inverse(lowers, row, col)
    states = []
    for part in range(chunks):
        rows = slice(part * CHUNK, (part + 1) * CHUNK)
        inverse, beta = inverses[part], betas[part]
        factor_x = product(inverse, beta * keys[part])
        factor_y = product(grids[part] * inverse, beta * values[part])
        x_ref[rows, :] = factor_x
        y_ref[rows, :] = factor_y
        onto = product(
            across_keys[part], jnp.concatenate([factor_x, tails[part] * factor_y], axis=1)
        )
        trans = gammas[part][CHUNK - 1 : CHUNK, :] * (eye - onto[:, :width])
        states.append((trans, onto[:, width:]))
        chunk_ref[part, 0] = trans
        chunk_ref[part, 1] = onto[:, width:]
    if state is not None:
        states.append(state)
    while len(states) > 1:
        joined = [followed(*states[at : at + 2]) for at in range(0, len(states) - 1, 2)]
        states = joined + states[2 * len(joined) :]
    pair_ref[0] = states[0][0]
    pair_ref[1] = states[0][1]


def followed(first, second):
    width = first[0].shape[0]
    onto = product(second[0], jnp.concatenate(first, axis=1))
    return onto[:, :width], onto[:, width:] + second[1]


def later_kernel(first_chunk, raw_ref, conv_ref, rate_ref, doc_ref, *outs):
    key_pass(raw_ref, conv_ref, rate_ref[0, 0], doc_ref, first_chunk, outs, None)


def earlier_kernel(first, count, *refs):
    held, refs = refs[:count], refs[count:]
    part_ref, far_ref, rim_ref, next_ref, state_ref, conv_ref, rate_ref, doc_ref = refs[:8]
    outs, raw = refs[8:-1], refs[-1]
    rows, width = part_ref.shape[0], state_ref.shape[1]
    raw[RIM : RIM + rows, :] = add_products(
        part_ref[...], [ref[...] for ref in held], far_ref, first
    )
    raw[:RIM, : 2 * width] = rim_ref[:, width:]
    raw[RIM + rows :, :] = next_ref[:RIM, :]
    key_pass(raw, conv_ref, rate_ref[0, 0], doc_ref, 0, outs, (state_ref[0], state_ref[1]))


def query_kernel(count, *refs):
    held, refs = refs[:count], refs[count:]
    base_ref, far_ref, rim_ref, next_ref, conv_ref = refs[:5]
    fields = [(refs[5:11], 0), (refs[11:17], 1)]
    carried_ref, local_ref, gate_ref, raw = refs[17:]
    width = carried_ref.shape[1]
    rows = held[0].shape[0]
    raw[RIM : RIM + rows, :] = add_products(
        base_ref[:rows, :], [ref[...] for ref in held], far_ref, 0
    )
    raw[:RIM, :width] = rim_ref[:, :width]
    raw[RIM + rows :, :] = next_ref[:RIM, :]
    row = lax.broadcasted_iota(jnp.int32, (CHUNK, CHUNK), 0)
    col = lax.broadcasted_iota(jnp.int32, (CHUNK, CHUNK), 1)
    state = None
    base = 0
    for (key_ref, x_ref, y_ref, grid_ref, gamma_ref, chunk_ref), later in fields:
        source = next_ref if later else raw
        for part in range(key_ref.shape[0] // CHUNK):
            start = RIM + part * CHUNK
            rows = slice(part * CHUNK, (part + 1) * CHUNK)
            out = slice(base, base + CHUNK)
            base += CHUNK
            columns = slice(0, width)
            query = unit_rows(convolve(source, start, columns, conv_ref, columns))
            gate = source[start : start + CHUNK, width:]
            gate_ref[out, :] = gate * sigmoid(gate)
            overlap = product(query, jnp.transpose(key_ref[rows, :]))
            carried = gamma_ref[rows, :] * (
                query - product(jnp.where(row >= col, overlap, 0.0), x_ref[rows, :])
            )
            local = product(grid_ref[rows, :] * overlap, y_ref[rows, :])
            trans, memory = chunk_ref[part, 0], chunk_ref[part, 1]
            if state is None:
                state = (trans, memory)
            else:
                onto = product(
                    jnp.concatenate([trans, carried], axis=0), jnp.concatenate(state, axis=1)
                )
                carried = onto[CHUNK:, :width]
                local = local + onto[CHUNK:, width:]
                state = (onto[:CHUNK, :width], onto[:CHUNK, width:] + memory)
            carried_ref[out, :] = carried
            local_ref[out, :] = local


def four_kernel(bit, carried, last, flag_ref, four_ref, *refs):
    group_ref, level_ref, next_ref = refs[-3:]
    width = next_ref.shape[0]
    flag = lambda at: jnp.broadcast_to(flag_ref[at : at + 1, :], (width, width)) == 1
    set_low, set_high = flag(bit), flag(bit + 1)
    trans = [four_ref[2 * at] for at in range(4)]
    memory = [four_ref[2 * at + 1] for at in range(4)]
    one_a, one_s = (jnp.where(set_high, part[2], part[0]) for part in (trans, memory))
    joined = lambda at: jnp.concatenate([trans[at], memory[at]], axis=1)
    onto_low = product(trans[1], joined(0))
    onto_high = product(trans[3], joined(2))
    low_a, low_s = onto_low[:, :width], onto_low[:, width:] + memory[1]
    high_a, high_s = onto_high[:, :width], onto_high[:, width:] + memory[3]
    if last:
        group_ref[...] = product(high_a, low_s) + high_s
    else:
        onto = product(high_a, jnp.concatenate([low_a, low_s], axis=1))
        group_ref[0] = onto[:, :width]
        group_ref[1] = onto[:, width:] + high_s
    if carried:
        carry = refs[0][...]
        first = product(carry, jnp.concatenate([one_a, one_s], axis=1))
        first_a, first_s = first[:, :width], first[:, width:]
    else:
        row = lax.broadcasted_iota(jnp.int32, (width, width), 0)
        col = lax.broadcasted_iota(jnp.int32, (width, width), 1)
        carry = jnp.where(row == col, 1.0, 0.0).astype(F32)
        first_a, first_s = one_a, one_s
    level_ref[0] = jnp.where(set_low, first_s, 0.0)
    carry = jnp.where(set_low, first_a, carry)
    second = product(carry, jnp.concatenate([low_a, low_s], axis=1))
    level_ref[1] = jnp.where(set_high, second[:, width:], 0.0)
    carry = jnp.where(set_high, second[:, :width], carry)
    next_ref[...] = jnp.where(flag(bit + 2), carry, 0.0) if last else carry


def mix_kernel(stages, single, carried_ref, local_ref, gate_ref, low_ref, high_ref, gain_ref, *refs):
    states = [ref[spot] for ref in refs[:stages] for spot in range(ref.shape[0])]
    if single:
        states.append(product(refs[stages][...], refs[stages + 1][...]))
    outs = refs[stages + (2 if single else 0) :]
    states = [right_parts(state) for state in states]
    carried = left_parts(carried_ref[...])
    weights = jnp.concatenate([low_ref[...], high_ref[...]], axis=0)
    mixed = weights[:, 2:3] * local_ref[...]
    for level, state in enumerate(states):
        mixed = mixed + weights[:, level + 3 : level + 4] * parts_dot(carried, state)
    scale = lax.rsqrt(jnp.mean(mixed * mixed, axis=1, keepdims=True) + 1e-05)
    normed = mixed * scale * gain_ref[...] * gate_ref[...]
    outs[0][...] = normed
    base = 0
    for out in outs[1:]:
        out[...] = normed[base : base + out.shape[0]]
        base += out.shape[0]


def block_product(pieces, weight, rows):
    parts = [halves(ref[rows, :]) for ref in pieces]
    high, low = (jnp.concatenate(part, axis=1) for part in zip(*parts))
    columns = weight.shape[1] // 2
    both = jnp.dot(high, weight, preferred_element_type=F32)
    rest = jnp.dot(low, weight[:, :columns], preferred_element_type=F32)
    return (both[:, :columns] + both[:, columns:]) + rest


def order_kernel(sources, index_ref, weight_ref, out_ref):
    depth = weight_ref.shape[0] // sources
    for source in range(sources):
        rows = pl.ds(pl.multiple_of(index_ref[source] * depth, depth), depth)
        out_ref[source * depth : (source + 1) * depth, :] = left_parts(weight_ref[rows, :])


def source_rows(first, pieces, weight_ref):
    depth = pieces[0].shape[1]
    return weight_ref[first * depth : (first + len(pieces)) * depth, :]


def row_blocks(rows):
    return [slice(base, base + CHUNK) for base in range(0, rows, CHUNK)]


def near_kernel(own_ref, near_ref, weight_ref, low_ref, high_ref):
    weight = source_rows(0, [own_ref, near_ref], weight_ref)
    half = low_ref.shape[0]
    for rows in row_blocks(half):
        low_ref[rows, :] = block_product([own_ref, near_ref], weight, rows)
        later = slice(half + rows.start, half + rows.stop)
        high_ref[rows, :] = block_product([own_ref, near_ref], weight, later)


def far_kernel(count, first, *refs):
    held, (weight_ref, total_ref, out_ref) = refs[:-3], refs[-3:]
    weight = source_rows(first, held[:count], weight_ref)
    base = 0
    for at in range(0, len(held), count):
        pieces = held[at : at + count]
        for rows in row_blocks(pieces[0].shape[0]):
            out = slice(base + rows.start, base + rows.stop)
            out_ref[out, :] = total_ref[out, :] + block_product(pieces, weight, rows)
        base += pieces[0].shape[0]


def last_kernel(count, first, *refs):
    pieces = refs[:count]
    weight_ref, ready_ref, total_ref, out_ref, held, sems = refs[count:]
    half = ready_ref.shape[0]
    copies = [pltpu.make_async_copy(ready_ref, out_ref.at[:half, :], sems.at[0])]
    copies[0].start()
    weight = source_rows(first, pieces, weight_ref)
    for spot, rows in enumerate(row_blocks(total_ref.shape[0])):
        held[rows, :] = total_ref[rows, :] + block_product(pieces, weight, rows)
        out = slice(half + rows.start, half + rows.stop)
        copies.append(
            pltpu.make_async_copy(held.at[rows, :], out_ref.at[out, :], sems.at[spot + 1])
        )
        copies[-1].start()
    for copy in copies:
        copy.wait()


def vmem_call(kernel, outs, scratch, cost, *args, any_in=(), any_out=False):
    spec = pl.BlockSpec(memory_space=pltpu.VMEM)
    small = pl.BlockSpec(memory_space=pltpu.SMEM)
    free = pl.BlockSpec(memory_space=pl.ANY)
    return pl.pallas_call(
        kernel,
        out_shape=outs,
        in_specs=[
            free if spot in any_in else small if arg.dtype == jnp.int32 and arg.ndim == 1 else spec
            for spot, arg in enumerate(args)
        ],
        out_specs=jax.tree.map(lambda unused: free if any_out else spec, outs),
        scratch_shapes=scratch,
        compiler_params=pltpu.CompilerParams(vmem_limit_bytes=VMEM_GRANT),
        cost_estimate=pl.CostEstimate(flops=int(cost * 1e9), bytes_accessed=1 << 20, transcendentals=0),
    )(*args)


def to_sibling(value):
    count = lax.axis_size("head")
    return lax.ppermute(value, "head", [(source, source ^ 1) for source in range(count)])


def to_chips(value):
    count = lax.axis_size("head")
    return [
        lax.ppermute(
            value, "head", [(source, (source + 2 * step) % count) for source in range(count)]
        )
        for step in range(1, count // 2)
    ]


def after(value, *earlier):
    return lax.optimization_barrier((value, *earlier))


def shards(tokens, w_proj, w_mix, conv_w, rates, doc_start, norm_gain, w_out):
    tok_rows, depth = tokens.shape
    width = w_proj.shape[1] // 4
    state_columns, query_columns = 2 * width + CHUNK, 2 * width
    heads, me = lax.axis_size("head"), lax.axis_index("head")
    blocks, my_index = lax.axis_size("ctx"), lax.axis_index("ctx")
    remote = [(me + heads - 2 * step) % heads for step in range(1, heads // 2)]
    order = [me, me ^ 1] + remote + [index ^ 1 for index in remote]
    bits = blocks.bit_length() - 1
    index = jnp.stack(order + [my_index >> bit & 1 for bit in range(bits)]).astype(jnp.int32)
    count = heads - 2
    like = lambda *shape: jax.ShapeDtypeStruct(shape, F32)
    parts = lambda *shape: jax.ShapeDtypeStruct(shape, BF16)

    first = tok_rows // 2
    cut = first - RIM
    middle = tok_rows - CHUNK - RIM
    segments = (slice(cut, middle), slice(middle, tok_rows))
    late = [to_chips(tokens[rows]) for rows in segments]
    beside = to_sibling(tokens)
    early_rows, beside = after(tokens, beside)
    early = to_chips(early_rows[:cut])
    base_state, base_query, far_state, far_query, flags = vmem_call(
        base_kernel,
        [like(tok_rows, state_columns), like(tok_rows, query_columns),
         parts(count * depth, 2 * state_columns), parts(count * depth, 2 * query_columns),
         jax.ShapeDtypeStruct((bits, CHUNK), jnp.int32)],
        [pltpu.VMEM((heads, depth, 4 * width), F32),
         pltpu.VMEM((2 * depth, 2 * state_columns), BF16),
         pltpu.VMEM((2 * depth, 2 * query_columns), BF16),
         pltpu.SemaphoreType.DMA((heads,))],
        3, index, tokens, beside, w_mix.T, w_proj, any_in=(4,),
    )
    late, far_state = after(late, far_state)
    late_on = [[to_sibling(value) for value in values] for values in late]
    arrived = [value for pair in zip(late, late_on) for values in pair for value in values]
    late_state, late_query, rim = vmem_call(
        functools.partial(late_kernel, count, segments),
        [like(tok_rows - cut, state_columns), like(tok_rows - cut, query_columns),
         like(RIM, 3 * width)],
        [], 0.5, *arrived, base_state, base_query, far_state, far_query,
    )
    rim = lax.ppermute(rim, "ctx", [(source, source + 1) for source in range(blocks - 1)])
    docs = doc_start.reshape(tok_rows // CHUNK, CHUNK)
    rate = rates[:, None]

    def outs(rows):
        chunks = like(rows // CHUNK, 2, width, width)
        return [like(rows, width)] * 6 + [chunks, like(2, width, width)]

    later = vmem_call(
        functools.partial(later_kernel, first // CHUNK), outs(tok_rows - first), [], 0.5,
        late_state, conv_w, rate, docs,
    )
    early, pair_late, rim = after(early, later[7], rim)
    early_on = [to_sibling(value) for value in early]
    partial = vmem_call(
        functools.partial(partial_kernel, len(early)), like(cut, state_columns), [], 1,
        *early, base_state, far_state,
    )
    earlier = vmem_call(
        functools.partial(earlier_kernel, len(early), len(early)), outs(first),
        [pltpu.VMEM((first + RIM, state_columns), F32)], 5,
        *early_on, partial, far_state, rim, late_state, pair_late, conv_w, rate, docs,
    )

    pair = earlier[7]
    fields = vmem_call(
        functools.partial(query_kernel, count), [like(tok_rows, width)] * 3,
        [pltpu.VMEM((first + RIM, query_columns), F32)], 5,
        *early, *early_on, base_query, far_query, rim, late_query, conv_w,
        *earlier[:5], earlier[6], *later[:5], later[6],
    )
    own_weight = vmem_call(
        functools.partial(order_kernel, heads), parts(w_out.shape[0], 2 * w_out.shape[1]), [], 1,
        index, w_out,
    )
    carry = ()
    levels = []
    for bit in range(0, bits - 1, 2):
        groups = [
            [base + (at << bit) for at in range(4)]
            for base in range(blocks)
            if not base >> bit & 3
        ]
        four = lax.all_gather(pair, "ctx", axis_index_groups=groups, tiled=True)
        if not bit:
            four, *fields, own_weight = after(four, *fields, own_weight)
        last = bit + 2 >= bits - 1 and bits % 2
        group = [like(width, width)] if last else [like(2, width, width)]
        pair, level, *carry = vmem_call(
            functools.partial(four_kernel, bit, bool(carry), last),
            group + [like(2, width, width), like(width, width)], [], 1,
            flags, four, *carry,
        )
        levels.append(level)
    single = []
    if bits % 2:
        reach = blocks // 2
        single = [
            *(carry or [jnp.where(my_index >= reach, jnp.eye(width, dtype=F32), 0.0)]),
            lax.ppermute(
                pair if carry else pair[1],
                "ctx", [(source, source ^ reach) for source in range(blocks)],
            ),
        ]
    half = tok_rows // 2
    normed, *lows, high = vmem_call(
        functools.partial(mix_kernel, len(levels), bool(single)),
        [like(tok_rows, width)] + [like(half // 2, width)] * 2 + [like(half, width)], [], 1,
        *fields, earlier[5], later[5], norm_gain[None, :], *levels, *single,
    )
    columns = w_out.shape[1]
    near = to_sibling(normed)
    far_lows = [to_chips(low) for low in lows]
    high, near = after(high, near)
    far_high = to_chips(high)
    total_low, total_high = vmem_call(
        near_kernel, [like(half, columns)] * 2, [], 2, normed, near, own_weight
    )
    far_lows, total_low = after(far_lows, total_low)
    far_lows_on = [[to_sibling(value) for value in values] for values in far_lows]
    arrived = [value for pair in zip(far_lows, far_lows_on) for values in pair for value in values]
    total_low = vmem_call(
        functools.partial(far_kernel, count, 2), like(half, columns), [], 0.01,
        *arrived, own_weight, total_low,
    )
    far_high, total_low = after(far_high, total_low)
    far_high_on = [to_sibling(value) for value in far_high]
    total_high = vmem_call(
        functools.partial(far_kernel, len(far_high), 2), like(half, columns), [], 1,
        *far_high, own_weight, total_high,
    )
    return vmem_call(
        functools.partial(last_kernel, len(far_high), 2 + len(far_high)), like(tok_rows, columns),
        [pltpu.VMEM((half, columns), F32), pltpu.SemaphoreType.DMA((half // CHUNK + 1,))], 1,
        *far_high_on, own_weight, total_low, total_high, any_out=True,
    )


def solution(mesh):
    placed = (
        P("ctx", "head"),
        P(None, "head"),
        P(None, "head"),
        P(None, "head"),
        P("head"),
        P("ctx"),
        P("head"),
        P(None, "head"),
    )
    return jax.shard_map(
        shards, mesh=mesh, in_specs=placed, out_specs=P("ctx", "head"), check_vma=False
    )
```

```python
import functools

import jax
import jax.numpy as jnp
from jax import lax
from jax.experimental import pallas as pl
from jax.experimental.pallas import tpu as pltpu
from jax.sharding import PartitionSpec as P

CHUNK = 128
RIM = 16
VMEM_GRANT = 16 << 20
F32 = jnp.float32
BF16 = jnp.bfloat16


def halves(value):
    high = value.astype(BF16)
    return high, (value - high.astype(F32)).astype(BF16)


def left_parts(value):
    return jnp.concatenate(halves(value), axis=1)


def right_parts(value):
    return jnp.concatenate(halves(value), axis=1)


def parts_dot(left, right):
    depth, half = right.shape[0], right.shape[1] // 2
    both = jnp.dot(left[:, :depth], right, preferred_element_type=F32)
    rest = jnp.dot(left[:, depth:], right[:, :half], preferred_element_type=F32)
    return (both[:, :half] + both[:, half:]) + rest


def product(left, right):
    return parts_dot(left_parts(left), right_parts(right))


def softplus(value):
    return jnp.maximum(value, 0.0) + jnp.log1p(jnp.exp(-jnp.abs(value)))


def sigmoid(value):
    return 1.0 / (1.0 + jnp.exp(-value))


def unit_lower_inverse(lowers, row, col):
    size = lowers[0].shape[0]
    eye = jnp.where(row == col, 1.0, 0.0).astype(F32)
    inverses = [eye - jnp.where((row >> 1) == (col >> 1), lower, 0.0) for lower in lowers]
    lower_parts = [halves(lower) for lower in lowers]
    step = 1
    while 1 << step < size:
        off = ((row >> (step + 2)) == (col >> (step + 2))) & ((row >> step) > (col >> step))
        offs = [
            jnp.concatenate([jnp.where(off, part, jnp.zeros_like(part)) for part in parts], axis=1)
            for parts in lower_parts
        ]
        onto = [parts_dot(left, right_parts(inverse)) for left, inverse in zip(offs, inverses)]
        rights = [right_parts(value) for value in onto]
        squares = [parts_dot(left_parts(value), right) for value, right in zip(onto, rights)]
        firsts = [
            inverse - parts_dot(left_parts(inverse), right)
            for inverse, right in zip(inverses, rights)
        ]
        inverses = [first + product(first, square) for first, square in zip(firsts, squares)]
        step += 2
    return inverses


def add_products(total, pieces, weight_ref, first):
    columns = weight_ref.shape[1] // 2
    for spot, piece in enumerate(pieces):
        depth = piece.shape[1]
        rows = slice((first + spot) * depth, (first + spot + 1) * depth)
        high, low = halves(piece)
        both = jnp.dot(high, weight_ref[rows, :], preferred_element_type=F32)
        rest = jnp.dot(low, weight_ref[rows, :columns], preferred_element_type=F32)
        part = (both[:, :columns] + both[:, columns:]) + rest
        total = part if total is None else total + part
    return total


def base_kernel(
    index_ref, own_ref, beside_ref, mix_ref, proj_ref,
    state_ref, query_ref, far_state_ref, far_query_ref, flag_ref,
    held, near_state, near_query, sems,
):
    sources, depth, across = held.shape
    width = across // 4
    copies = []
    for source in range(sources):
        rows = pl.ds(pl.multiple_of(index_ref[source] * depth, depth), depth)
        copies.append(pltpu.make_async_copy(proj_ref.at[rows, :], held.at[source], sems.at[source]))
        copies[-1].start()
    for bit in range(flag_ref.shape[0]):
        flag_ref[bit : bit + 1, :] = jnp.broadcast_to(index_ref[sources + bit], (1, CHUNK))
    mixes = mix_ref.shape[0]

    def split(source, state_out, query_out, base):
        copies[source].wait()
        lanes = pl.ds(pl.multiple_of(index_ref[source] * depth, depth), depth)
        for begin in range(0, depth, CHUNK):
            rows = slice(begin, begin + CHUNK)
            out = slice(base + begin, base + begin + CHUNK)
            value = held[source, rows, :]
            mixing = mix_ref[:, lanes][:, rows]
            mixing = jnp.concatenate([mixing, jnp.zeros((CHUNK - mixes, CHUNK), F32)], axis=0)
            state = jnp.concatenate([value[:, width : 3 * width], jnp.transpose(mixing)], axis=1)
            query = jnp.concatenate([value[:, :width], value[:, 3 * width :]], axis=1)
            state_out[out, :] = left_parts(state)
            query_out[out, :] = left_parts(query)

    for source in range(2):
        split(source, near_state, near_query, source * depth)
    half = own_ref.shape[0] // 2
    for rows in (slice(0, half), slice(half, 2 * half)):
        pieces = [own_ref[rows, :], beside_ref[rows, :]]
        state_ref[rows, :] = add_products(None, pieces, near_state, 0)
        query_ref[rows, :] = add_products(None, pieces, near_query, 0)
    for source in range(2, sources):
        split(source, far_state_ref, far_query_ref, (source - 2) * depth)


def late_kernel(count, segments, *refs):
    begin = segments[0].start
    held, refs = refs[: count * len(segments)], refs[count * len(segments) :]
    base_state, base_query, far_state, far_query, state_ref, query_ref, rim_ref = refs
    width = base_query.shape[1] // 2
    for turn, rows in enumerate(segments):
        pieces = [ref[...] for ref in held[turn * count : (turn + 1) * count]]
        out = slice(rows.start - begin, rows.stop - begin)
        state_ref[out, :] = add_products(base_state[rows, :], pieces, far_state, 0)
        query_ref[out, :] = add_products(base_query[rows, :], pieces, far_query, 0)
    last = state_ref.shape[0] - RIM
    rim_ref[:, :width] = query_ref[last:, :width]
    rim_ref[:, width:] = state_ref[last:, : 2 * width]


def partial_kernel(count, *refs):
    base_state, far_state, out_ref = refs[count:]
    out_ref[...] = add_products(
        base_state[: out_ref.shape[0], :], [ref[...] for ref in refs[:count]], far_state, 0
    )


def convolve(raw, start, columns, conv_ref, taps_at):
    taps = conv_ref.shape[0]
    conv = 0.0
    for tap in range(taps):
        spot = start - taps + 1 + tap
        conv = conv + conv_ref[tap : tap + 1, taps_at] * raw[spot : spot + CHUNK, columns]
    return conv * sigmoid(conv)


def unit_rows(value):
    return value * lax.rsqrt(jnp.sum(value * value, axis=1, keepdims=True) + 1e-06)


def key_pass(raw, conv_ref, rate, doc_ref, first_chunk, outs, state):
    key_ref, x_ref, y_ref, grid_ref, gamma_ref, plus_ref, chunk_ref, pair_ref = outs
    width = key_ref.shape[1]
    chunks = key_ref.shape[0] // CHUNK
    row = lax.broadcasted_iota(jnp.int32, (CHUNK, CHUNK), 0)
    col = lax.broadcasted_iota(jnp.int32, (CHUNK, CHUNK), 1)
    lower = row >= col
    tri = jnp.where(lower, 1.0, 0.0).astype(F32)
    eye = jnp.where(row == col, 1.0, 0.0).astype(F32)
    keys, values, betas, grids, gammas, tails = [], [], [], [], [], []
    for part in range(chunks):
        start = RIM + part * CHUNK
        rows = slice(part * CHUNK, (part + 1) * CHUNK)
        middle, last = slice(width, 2 * width), slice(2 * width, 3 * width)
        keys.append(unit_rows(convolve(raw, start, slice(0, width), conv_ref, middle)))
        values.append(convolve(raw, start, middle, conv_ref, last))
        mixing = raw[start : start + CHUNK, last]
        plus = softplus(mixing)
        plus_ref[rows, :] = plus
        betas.append(sigmoid(mixing[:, 0:1]))
        spot = first_chunk + part
        docs = jnp.broadcast_to(doc_ref[spot : spot + 1, :].astype(F32), (CHUNK, CHUNK))
        docs = jnp.transpose(docs)
        steps = jnp.where(col == 1, -rate * plus, jnp.where(col == 0, docs, 0.0))
        sums = jnp.dot(tri, steps, precision=lax.Precision.HIGHEST, preferred_element_type=F32)
        across = jnp.transpose(sums)
        smooth, count = sums[:, 1:2], sums[:, 0:1]
        span = (smooth - across[1:2, :]) - 20.0 * (count - across[0:1, :])
        grids.append(jnp.exp(jnp.where(lower, span, -1e30)))
        gammas.append(jnp.exp(smooth - 20.0 * count))
        last = sums[CHUNK - 1 : CHUNK, :]
        tails.append(jnp.exp((last[:, 1:2] - smooth) - 20.0 * (last[:, 0:1] - count)))
        key_ref[rows, :] = keys[part]
        grid_ref[rows, :] = grids[part]
        gamma_ref[rows, :] = jnp.broadcast_to(gammas[part], (CHUNK, width))
    across_keys = [jnp.transpose(key) for key in keys]
    grams = [
        parts_dot(left_parts(key), right_parts(across)) for key, across in zip(keys, across_keys)
    ]
    lowers = [jnp.where(row > col, beta * gram, 0.0) for beta, gram in zip(betas, grams)]
    inverses = unit_lower_inverse(lowers, row, col)
    states = []
    for part in range(chunks):
        rows = slice(part * CHUNK, (part + 1) * CHUNK)
        inverse, beta = inverses[part], betas[part]
        factor_x = product(inverse, beta * keys[part])
        factor_y = product(grids[part] * inverse, beta * values[part])
        x_ref[rows, :] = factor_x
        y_ref[rows, :] = factor_y
        onto = product(
            across_keys[part], jnp.concatenate([factor_x, tails[part] * factor_y], axis=1)
        )
        trans = gammas[part][CHUNK - 1 : CHUNK, :] * (eye - onto[:, :width])
        states.append((trans, onto[:, width:]))
        chunk_ref[part, 0] = trans
        chunk_ref[part, 1] = onto[:, width:]
    if state is not None:
        states.append(state)
    while len(states) > 1:
        joined = [followed(*states[at : at + 2]) for at in range(0, len(states) - 1, 2)]
        states = joined + states[2 * len(joined) :]
    pair_ref[0] = states[0][0]
    pair_ref[1] = states[0][1]


def followed(first, second):
    width = first[0].shape[0]
    onto = product(second[0], jnp.concatenate(first, axis=1))
    return onto[:, :width], onto[:, width:] + second[1]


def later_kernel(first_chunk, raw_ref, conv_ref, rate_ref, doc_ref, *outs):
    key_pass(raw_ref, conv_ref, rate_ref[0, 0], doc_ref, first_chunk, outs, None)


def earlier_kernel(first, count, *refs):
    held, refs = refs[:count], refs[count:]
    part_ref, far_ref, rim_ref, next_ref, state_ref, conv_ref, rate_ref, doc_ref = refs[:8]
    outs, raw = refs[8:-1], refs[-1]
    rows, width = part_ref.shape[0], state_ref.shape[1]
    raw[RIM : RIM + rows, :] = add_products(
        part_ref[...], [ref[...] for ref in held], far_ref, first
    )
    raw[:RIM, : 2 * width] = rim_ref[:, width:]
    raw[RIM + rows :, :] = next_ref[:RIM, :]
    key_pass(raw, conv_ref, rate_ref[0, 0], doc_ref, 0, outs, (state_ref[0], state_ref[1]))


def query_kernel(count, *refs):
    held, refs = refs[:count], refs[count:]
    base_ref, far_ref, rim_ref, next_ref, conv_ref = refs[:5]
    fields = [(refs[5:11], 0), (refs[11:17], 1)]
    carried_ref, local_ref, gate_ref, raw = refs[17:]
    width = carried_ref.shape[1]
    rows = held[0].shape[0]
    raw[RIM : RIM + rows, :] = add_products(
        base_ref[:rows, :], [ref[...] for ref in held], far_ref, 0
    )
    raw[:RIM, :width] = rim_ref[:, :width]
    raw[RIM + rows :, :] = next_ref[:RIM, :]
    row = lax.broadcasted_iota(jnp.int32, (CHUNK, CHUNK), 0)
    col = lax.broadcasted_iota(jnp.int32, (CHUNK, CHUNK), 1)
    state = None
    base = 0
    for (key_ref, x_ref, y_ref, grid_ref, gamma_ref, chunk_ref), later in fields:
        source = next_ref if later else raw
        for part in range(key_ref.shape[0] // CHUNK):
            start = RIM + part * CHUNK
            rows = slice(part * CHUNK, (part + 1) * CHUNK)
            out = slice(base, base + CHUNK)
            base += CHUNK
            columns = slice(0, width)
            query = unit_rows(convolve(source, start, columns, conv_ref, columns))
            gate = source[start : start + CHUNK, width:]
            gate_ref[out, :] = gate * sigmoid(gate)
            overlap = product(query, jnp.transpose(key_ref[rows, :]))
            carried = gamma_ref[rows, :] * (
                query - product(jnp.where(row >= col, overlap, 0.0), x_ref[rows, :])
            )
            local = product(grid_ref[rows, :] * overlap, y_ref[rows, :])
            trans, memory = chunk_ref[part, 0], chunk_ref[part, 1]
            if state is None:
                state = (trans, memory)
            else:
                onto = product(
                    jnp.concatenate([trans, carried], axis=0), jnp.concatenate(state, axis=1)
                )
                carried = onto[CHUNK:, :width]
                local = local + onto[CHUNK:, width:]
                state = (onto[:CHUNK, :width], onto[:CHUNK, width:] + memory)
            carried_ref[out, :] = carried
            local_ref[out, :] = local


def four_kernel(bit, carried, last, flag_ref, own_ref, one_ref, two_ref, three_ref, *refs):
    group_ref, level_ref, next_ref = refs[-3:]
    width = next_ref.shape[0]
    flag = lambda at: jnp.broadcast_to(flag_ref[at : at + 1, :], (width, width)) == 1
    set_low, set_high = flag(bit), flag(bit + 1)
    held = (own_ref, one_ref, two_ref, three_ref)

    def placed(part):
        by_low = [jnp.where(set_low, held[at ^ 1][part], held[at][part]) for at in range(4)]
        return [jnp.where(set_high, by_low[at ^ 2], by_low[at]) for at in range(4)]

    trans, memory = placed(0), placed(1)
    joined = lambda at: jnp.concatenate([trans[at], memory[at]], axis=1)
    onto_low = product(trans[1], joined(0))
    onto_high = product(trans[3], joined(2))
    low_a, low_s = onto_low[:, :width], onto_low[:, width:] + memory[1]
    high_a, high_s = onto_high[:, :width], onto_high[:, width:] + memory[3]
    if last:
        group_ref[...] = product(high_a, low_s) + high_s
    else:
        onto = product(high_a, jnp.concatenate([low_a, low_s], axis=1))
        group_ref[0] = onto[:, :width]
        group_ref[1] = onto[:, width:] + high_s
    if carried:
        carry = refs[0][...]
        first = product(carry, jnp.concatenate([one_ref[0], one_ref[1]], axis=1))
        first_a, first_s = first[:, :width], first[:, width:]
    else:
        row = lax.broadcasted_iota(jnp.int32, (width, width), 0)
        col = lax.broadcasted_iota(jnp.int32, (width, width), 1)
        carry = jnp.where(row == col, 1.0, 0.0).astype(F32)
        first_a, first_s = one_ref[0], one_ref[1]
    level_ref[0] = jnp.where(set_low, first_s, 0.0)
    carry = jnp.where(set_low, first_a, carry)
    second = product(carry, jnp.concatenate([low_a, low_s], axis=1))
    level_ref[1] = jnp.where(set_high, second[:, width:], 0.0)
    carry = jnp.where(set_high, second[:, :width], carry)
    next_ref[...] = jnp.where(flag(bit + 2), carry, 0.0) if last else carry


def mix_kernel(stages, single, carried_ref, local_ref, gate_ref, low_ref, high_ref, gain_ref, *refs):
    states = [ref[spot] for ref in refs[:stages] for spot in range(ref.shape[0])]
    if single:
        states.append(product(refs[stages][...], refs[stages + 1][...]))
    outs = refs[stages + (2 if single else 0) :]
    states = [right_parts(state) for state in states]
    carried = left_parts(carried_ref[...])
    weights = jnp.concatenate([low_ref[...], high_ref[...]], axis=0)
    mixed = weights[:, 2:3] * local_ref[...]
    for level, state in enumerate(states):
        mixed = mixed + weights[:, level + 3 : level + 4] * parts_dot(carried, state)
    scale = lax.rsqrt(jnp.mean(mixed * mixed, axis=1, keepdims=True) + 1e-05)
    normed = mixed * scale * gain_ref[...] * gate_ref[...]
    outs[0][...] = normed
    base = 0
    for out in outs[1:]:
        out[...] = normed[base : base + out.shape[0]]
        base += out.shape[0]


def block_product(pieces, weight, rows):
    parts = [halves(ref[rows, :]) for ref in pieces]
    high, low = (jnp.concatenate(part, axis=1) for part in zip(*parts))
    columns = weight.shape[1] // 2
    both = jnp.dot(high, weight, preferred_element_type=F32)
    rest = jnp.dot(low, weight[:, :columns], preferred_element_type=F32)
    return (both[:, :columns] + both[:, columns:]) + rest


def order_kernel(sources, index_ref, weight_ref, out_ref):
    depth = weight_ref.shape[0] // sources
    for source in range(sources):
        rows = pl.ds(pl.multiple_of(index_ref[source] * depth, depth), depth)
        out_ref[source * depth : (source + 1) * depth, :] = left_parts(weight_ref[rows, :])


def source_rows(first, pieces, weight_ref):
    depth = pieces[0].shape[1]
    return weight_ref[first * depth : (first + len(pieces)) * depth, :]


def row_blocks(rows):
    return [slice(base, base + CHUNK) for base in range(0, rows, CHUNK)]


def near_kernel(own_ref, near_ref, weight_ref, low_ref, high_ref):
    weight = source_rows(0, [own_ref, near_ref], weight_ref)
    half = low_ref.shape[0]
    for rows in row_blocks(half):
        low_ref[rows, :] = block_product([own_ref, near_ref], weight, rows)
        later = slice(half + rows.start, half + rows.stop)
        high_ref[rows, :] = block_product([own_ref, near_ref], weight, later)


def far_kernel(count, first, *refs):
    held, (weight_ref, total_ref, out_ref) = refs[:-3], refs[-3:]
    weight = source_rows(first, held[:count], weight_ref)
    base = 0
    for at in range(0, len(held), count):
        pieces = held[at : at + count]
        for rows in row_blocks(pieces[0].shape[0]):
            out = slice(base + rows.start, base + rows.stop)
            out_ref[out, :] = total_ref[out, :] + block_product(pieces, weight, rows)
        base += pieces[0].shape[0]


def last_kernel(count, first, *refs):
    pieces = refs[:count]
    weight_ref, ready_ref, total_ref, out_ref, held, sems = refs[count:]
    half = ready_ref.shape[0]
    copies = [pltpu.make_async_copy(ready_ref, out_ref.at[:half, :], sems.at[0])]
    copies[0].start()
    weight = source_rows(first, pieces, weight_ref)
    for spot, rows in enumerate(row_blocks(total_ref.shape[0])):
        held[rows, :] = total_ref[rows, :] + block_product(pieces, weight, rows)
        out = slice(half + rows.start, half + rows.stop)
        copies.append(
            pltpu.make_async_copy(held.at[rows, :], out_ref.at[out, :], sems.at[spot + 1])
        )
        copies[-1].start()
    for copy in copies:
        copy.wait()


def vmem_call(kernel, outs, scratch, cost, *args, any_in=(), any_out=False):
    spec = pl.BlockSpec(memory_space=pltpu.VMEM)
    small = pl.BlockSpec(memory_space=pltpu.SMEM)
    free = pl.BlockSpec(memory_space=pl.ANY)
    return pl.pallas_call(
        kernel,
        out_shape=outs,
        in_specs=[
            free if spot in any_in else small if arg.dtype == jnp.int32 and arg.ndim == 1 else spec
            for spot, arg in enumerate(args)
        ],
        out_specs=jax.tree.map(lambda unused: free if any_out else spec, outs),
        scratch_shapes=scratch,
        compiler_params=pltpu.CompilerParams(vmem_limit_bytes=VMEM_GRANT),
        cost_estimate=pl.CostEstimate(flops=int(cost * 1e9), bytes_accessed=1 << 20, transcendentals=0),
    )(*args)


def to_sibling(value):
    count = lax.axis_size("head")
    return lax.ppermute(value, "head", [(source, source ^ 1) for source in range(count)])


def to_chips(value):
    count = lax.axis_size("head")
    return [
        lax.ppermute(
            value, "head", [(source, (source + 2 * step) % count) for source in range(count)]
        )
        for step in range(1, count // 2)
    ]


def after(value, *earlier):
    return lax.optimization_barrier((value, *earlier))


def shards(tokens, w_proj, w_mix, conv_w, rates, doc_start, norm_gain, w_out):
    tok_rows, depth = tokens.shape
    width = w_proj.shape[1] // 4
    state_columns, query_columns = 2 * width + CHUNK, 2 * width
    heads, me = lax.axis_size("head"), lax.axis_index("head")
    blocks, my_index = lax.axis_size("ctx"), lax.axis_index("ctx")
    remote = [(me + heads - 2 * step) % heads for step in range(1, heads // 2)]
    order = [me, me ^ 1] + remote + [index ^ 1 for index in remote]
    bits = blocks.bit_length() - 1
    index = jnp.stack(order + [my_index >> bit & 1 for bit in range(bits)]).astype(jnp.int32)
    count = heads - 2
    like = lambda *shape: jax.ShapeDtypeStruct(shape, F32)
    parts = lambda *shape: jax.ShapeDtypeStruct(shape, BF16)

    first = tok_rows // 2
    cut = first - RIM
    middle = tok_rows - CHUNK - RIM
    segments = (slice(cut, middle), slice(middle, tok_rows))
    late = [to_chips(tokens[rows]) for rows in segments]
    beside = to_sibling(tokens)
    early_rows, beside = after(tokens, beside)
    early = to_chips(early_rows[:cut])
    base_state, base_query, far_state, far_query, flags = vmem_call(
        base_kernel,
        [like(tok_rows, state_columns), like(tok_rows, query_columns),
         parts(count * depth, 2 * state_columns), parts(count * depth, 2 * query_columns),
         jax.ShapeDtypeStruct((bits, CHUNK), jnp.int32)],
        [pltpu.VMEM((heads, depth, 4 * width), F32),
         pltpu.VMEM((2 * depth, 2 * state_columns), BF16),
         pltpu.VMEM((2 * depth, 2 * query_columns), BF16),
         pltpu.SemaphoreType.DMA((heads,))],
        3, index, tokens, beside, w_mix.T, w_proj, any_in=(4,),
    )
    late, far_state = after(late, far_state)
    late_on = [[to_sibling(value) for value in values] for values in late]
    arrived = [value for pair in zip(late, late_on) for values in pair for value in values]
    late_state, late_query, rim = vmem_call(
        functools.partial(late_kernel, count, segments),
        [like(tok_rows - cut, state_columns), like(tok_rows - cut, query_columns),
         like(RIM, 3 * width)],
        [], 0.5, *arrived, base_state, base_query, far_state, far_query,
    )
    rim = lax.ppermute(rim, "ctx", [(source, source + 1) for source in range(blocks - 1)])
    docs = doc_start.reshape(tok_rows // CHUNK, CHUNK)
    rate = rates[:, None]

    def outs(rows):
        chunks = like(rows // CHUNK, 2, width, width)
        return [like(rows, width)] * 6 + [chunks, like(2, width, width)]

    later = vmem_call(
        functools.partial(later_kernel, first // CHUNK), outs(tok_rows - first), [], 0.5,
        late_state, conv_w, rate, docs,
    )
    early, pair_late, rim = after(early, later[7], rim)
    early_on = [to_sibling(value) for value in early]
    partial = vmem_call(
        functools.partial(partial_kernel, len(early)), like(cut, state_columns), [], 1,
        *early, base_state, far_state,
    )
    earlier = vmem_call(
        functools.partial(earlier_kernel, len(early), len(early)), outs(first),
        [pltpu.VMEM((first + RIM, state_columns), F32)], 5,
        *early_on, partial, far_state, rim, late_state, pair_late, conv_w, rate, docs,
    )

    pair = earlier[7]
    fields = vmem_call(
        functools.partial(query_kernel, count), [like(tok_rows, width)] * 3,
        [pltpu.VMEM((first + RIM, query_columns), F32)], 5,
        *early, *early_on, base_query, far_query, rim, late_query, conv_w,
        *earlier[:5], earlier[6], *later[:5], later[6],
    )
    own_weight = vmem_call(
        functools.partial(order_kernel, heads), parts(w_out.shape[0], 2 * w_out.shape[1]), [], 1,
        index, w_out,
    )
    carry = ()
    levels = []
    for bit in range(0, bits - 1, 2):
        others = [
            lax.ppermute(
                pair, "ctx", [(source, source ^ (mask << bit)) for source in range(blocks)]
            )
            for mask in (1, 2, 3)
        ]
        if not bit:
            others[0], *fields, own_weight = after(others[0], *fields, own_weight)
        last = bit + 2 >= bits - 1 and bits % 2
        group = [like(width, width)] if last else [like(2, width, width)]
        pair, level, *carry = vmem_call(
            functools.partial(four_kernel, bit, bool(carry), last),
            group + [like(2, width, width), like(width, width)], [], 1,
            flags, pair, *others, *carry,
        )
        levels.append(level)
    single = []
    if bits % 2:
        reach = blocks // 2
        single = [
            *(carry or [jnp.where(my_index >= reach, jnp.eye(width, dtype=F32), 0.0)]),
            lax.ppermute(
                pair if carry else pair[1],
                "ctx", [(source, source ^ reach) for source in range(blocks)],
            ),
        ]
    half = tok_rows // 2
    normed, *lows, high = vmem_call(
        functools.partial(mix_kernel, len(levels), bool(single)),
        [like(tok_rows, width)] + [like(half // 2, width)] * 2 + [like(half, width)], [], 1,
        *fields, earlier[5], later[5], norm_gain[None, :], *levels, *single,
    )
    columns = w_out.shape[1]
    near = to_sibling(normed)
    far_lows = [to_chips(low) for low in lows]
    high, near = after(high, near)
    far_high = to_chips(high)
    total_low, total_high = vmem_call(
        near_kernel, [like(half, columns)] * 2, [], 2, normed, near, own_weight
    )
    far_lows, total_low = after(far_lows, total_low)
    far_lows_on = [[to_sibling(value) for value in values] for values in far_lows]
    arrived = [value for pair in zip(far_lows, far_lows_on) for values in pair for value in values]
    total_low = vmem_call(
        functools.partial(far_kernel, count, 2), like(half, columns), [], 0.01,
        *arrived, own_weight, total_low,
    )
    far_high, total_low = after(far_high, total_low)
    far_high_on = [to_sibling(value) for value in far_high]
    total_high = vmem_call(
        functools.partial(far_kernel, len(far_high), 2), like(half, columns), [], 1,
        *far_high, own_weight, total_high,
    )
    return vmem_call(
        functools.partial(last_kernel, len(far_high), 2 + len(far_high)), like(tok_rows, columns),
        [pltpu.VMEM((half, columns), F32), pltpu.SemaphoreType.DMA((half // CHUNK + 1,))], 1,
        *far_high_on, own_weight, total_low, total_high, any_out=True,
    )


def solution(mesh):
    placed = (
        P("ctx", "head"),
        P(None, "head"),
        P(None, "head"),
        P(None, "head"),
        P("head"),
        P("ctx"),
        P("head"),
        P(None, "head"),
    )
    return jax.shard_map(
        shards, mesh=mesh, in_specs=placed, out_specs=P("ctx", "head"), check_vma=False
    )
```

```python
import functools

import jax
import jax.numpy as jnp
from jax import lax
from jax.experimental import pallas as pl
from jax.experimental.pallas import tpu as pltpu
from jax.sharding import PartitionSpec as P

CHUNK = 128
RIM = 16
VMEM_GRANT = 16 << 20
F32 = jnp.float32
BF16 = jnp.bfloat16


def halves(value):
    high = value.astype(BF16)
    return high, (value - high.astype(F32)).astype(BF16)


def left_parts(value):
    return jnp.concatenate(halves(value), axis=1)


def right_parts(value):
    row = jnp.concatenate(halves(value), axis=1)
    return jnp.concatenate([row, row], axis=0)


def parts_dot(left, right):
    both = jnp.dot(left, right, preferred_element_type=F32)
    half = both.shape[1] // 2
    return both[:, :half] + both[:, half:]


def product(left, right):
    return parts_dot(left_parts(left), right_parts(right))


def softplus(value):
    return jnp.maximum(value, 0.0) + jnp.log1p(jnp.exp(-jnp.abs(value)))


def sigmoid(value):
    return 1.0 / (1.0 + jnp.exp(-value))


def unit_lower_inverse(lowers, row, col):
    size = lowers[0].shape[0]
    eye = jnp.where(row == col, 1.0, 0.0).astype(F32)
    inverses = [eye - jnp.where((row >> 1) == (col >> 1), lower, 0.0) for lower in lowers]
    lower_parts = [halves(lower) for lower in lowers]
    step = 1
    while 1 << step < size:
        off = ((row >> (step + 2)) == (col >> (step + 2))) & ((row >> step) > (col >> step))
        offs = [
            jnp.concatenate([jnp.where(off, part, jnp.zeros_like(part)) for part in parts], axis=1)
            for parts in lower_parts
        ]
        onto = [parts_dot(left, right_parts(inverse)) for left, inverse in zip(offs, inverses)]
        rights = [right_parts(value) for value in onto]
        squares = [parts_dot(left_parts(value), right) for value, right in zip(onto, rights)]
        firsts = [
            inverse - parts_dot(left_parts(inverse), right)
            for inverse, right in zip(inverses, rights)
        ]
        inverses = [first + product(first, square) for first, square in zip(firsts, squares)]
        step += 2
    return inverses


def add_products(total, pieces, weight_ref, first):
    columns = weight_ref.shape[1] // 2
    for spot, piece in enumerate(pieces):
        depth = piece.shape[1]
        rows = slice((first + spot) * depth, (first + spot + 1) * depth)
        high, low = halves(piece)
        both = jnp.dot(high, weight_ref[rows, :], preferred_element_type=F32)
        rest = jnp.dot(low, weight_ref[rows, :columns], preferred_element_type=F32)
        part = (both[:, :columns] + both[:, columns:]) + rest
        total = part if total is None else total + part
    return total


def base_kernel(
    index_ref, own_ref, beside_ref, mix_ref, proj_ref,
    state_ref, query_ref, far_state_ref, far_query_ref, flag_ref,
    held, near_state, near_query, sems,
):
    sources, depth, across = held.shape
    width = across // 4
    copies = []
    for source in range(sources):
        rows = pl.ds(pl.multiple_of(index_ref[source] * depth, depth), depth)
        copies.append(pltpu.make_async_copy(proj_ref.at[rows, :], held.at[source], sems.at[source]))
        copies[-1].start()
    for bit in range(flag_ref.shape[0]):
        flag_ref[bit : bit + 1, :] = jnp.broadcast_to(index_ref[sources + bit], (1, CHUNK))
    mixes = mix_ref.shape[0]

    def split(source, state_out, query_out, base):
        copies[source].wait()
        lanes = pl.ds(pl.multiple_of(index_ref[source] * depth, depth), depth)
        for begin in range(0, depth, CHUNK):
            rows = slice(begin, begin + CHUNK)
            out = slice(base + begin, base + begin + CHUNK)
            value = held[source, rows, :]
            mixing = mix_ref[:, lanes][:, rows]
            mixing = jnp.concatenate([mixing, jnp.zeros((CHUNK - mixes, CHUNK), F32)], axis=0)
            state = jnp.concatenate([value[:, width : 3 * width], jnp.transpose(mixing)], axis=1)
            query = jnp.concatenate([value[:, :width], value[:, 3 * width :]], axis=1)
            state_out[out, :] = left_parts(state)
            query_out[out, :] = left_parts(query)

    for source in range(2):
        split(source, near_state, near_query, source * depth)
    half = own_ref.shape[0] // 2
    for rows in (slice(0, half), slice(half, 2 * half)):
        pieces = [own_ref[rows, :], beside_ref[rows, :]]
        state_ref[rows, :] = add_products(None, pieces, near_state, 0)
        query_ref[rows, :] = add_products(None, pieces, near_query, 0)
    for source in range(2, sources):
        split(source, far_state_ref, far_query_ref, (source - 2) * depth)


def late_kernel(count, segments, *refs):
    begin = segments[0].start
    held, refs = refs[: count * len(segments)], refs[count * len(segments) :]
    base_state, base_query, far_state, far_query, state_ref, query_ref, rim_ref = refs
    width = base_query.shape[1] // 2
    for turn, rows in enumerate(segments):
        pieces = [ref[...] for ref in held[turn * count : (turn + 1) * count]]
        out = slice(rows.start - begin, rows.stop - begin)
        state_ref[out, :] = add_products(base_state[rows, :], pieces, far_state, 0)
        query_ref[out, :] = add_products(base_query[rows, :], pieces, far_query, 0)
    last = state_ref.shape[0] - RIM
    rim_ref[:, :width] = query_ref[last:, :width]
    rim_ref[:, width:] = state_ref[last:, : 2 * width]


def partial_kernel(count, *refs):
    base_state, far_state, out_ref = refs[count:]
    out_ref[...] = add_products(
        base_state[: out_ref.shape[0], :], [ref[...] for ref in refs[:count]], far_state, 0
    )


def convolve(raw, start, columns, conv_ref, taps_at):
    taps = conv_ref.shape[0]
    conv = 0.0
    for tap in range(taps):
        spot = start - taps + 1 + tap
        conv = conv + conv_ref[tap : tap + 1, taps_at] * raw[spot : spot + CHUNK, columns]
    return conv * sigmoid(conv)


def unit_rows(value):
    return value * lax.rsqrt(jnp.sum(value * value, axis=1, keepdims=True) + 1e-06)


def key_pass(raw, conv_ref, rate, doc_ref, first_chunk, outs, state):
    key_ref, x_ref, y_ref, grid_ref, gamma_ref, plus_ref, chunk_ref, pair_ref = outs
    width = key_ref.shape[1]
    chunks = key_ref.shape[0] // CHUNK
    row = lax.broadcasted_iota(jnp.int32, (CHUNK, CHUNK), 0)
    col = lax.broadcasted_iota(jnp.int32, (CHUNK, CHUNK), 1)
    lower = row >= col
    tri = jnp.where(lower, 1.0, 0.0).astype(F32)
    eye = jnp.where(row == col, 1.0, 0.0).astype(F32)
    keys, values, betas, grids, gammas, tails = [], [], [], [], [], []
    for part in range(chunks):
        start = RIM + part * CHUNK
        rows = slice(part * CHUNK, (part + 1) * CHUNK)
        middle, last = slice(width, 2 * width), slice(2 * width, 3 * width)
        keys.append(unit_rows(convolve(raw, start, slice(0, width), conv_ref, middle)))
        values.append(convolve(raw, start, middle, conv_ref, last))
        mixing = raw[start : start + CHUNK, last]
        plus = softplus(mixing)
        plus_ref[rows, :] = plus
        betas.append(sigmoid(mixing[:, 0:1]))
        spot = first_chunk + part
        docs = jnp.broadcast_to(doc_ref[spot : spot + 1, :].astype(F32), (CHUNK, CHUNK))
        docs = jnp.transpose(docs)
        steps = jnp.where(col == 1, -rate * plus, jnp.where(col == 0, docs, 0.0))
        sums = jnp.dot(tri, steps, precision=lax.Precision.HIGHEST, preferred_element_type=F32)
        across = jnp.transpose(sums)
        smooth, count = sums[:, 1:2], sums[:, 0:1]
        span = (smooth - across[1:2, :]) - 20.0 * (count - across[0:1, :])
        grids.append(jnp.exp(jnp.where(lower, span, -1e30)))
        gammas.append(jnp.exp(smooth - 20.0 * count))
        last = sums[CHUNK - 1 : CHUNK, :]
        tails.append(jnp.exp((last[:, 1:2] - smooth) - 20.0 * (last[:, 0:1] - count)))
        key_ref[rows, :] = keys[part]
        grid_ref[rows, :] = grids[part]
        gamma_ref[rows, :] = jnp.broadcast_to(gammas[part], (CHUNK, width))
    across_keys = [jnp.transpose(key) for key in keys]
    grams = [
        parts_dot(left_parts(key), right_parts(across)) for key, across in zip(keys, across_keys)
    ]
    lowers = [jnp.where(row > col, beta * gram, 0.0) for beta, gram in zip(betas, grams)]
    inverses = unit_lower_inverse(lowers, row, col)
    states = []
    if state is not None:
        later_keys = product(state[0], across_keys[-1])
    for part in range(chunks):
        rows = slice(part * CHUNK, (part + 1) * CHUNK)
        inverse, beta = inverses[part], betas[part]
        factor_x = product(inverse, beta * keys[part])
        factor_y = product(grids[part] * inverse, beta * values[part])
        x_ref[rows, :] = factor_x
        y_ref[rows, :] = factor_y
        factors = jnp.concatenate([factor_x, tails[part] * factor_y], axis=1)
        onto = product(across_keys[part], factors)
        if state is not None and part == chunks - 1:
            behind = product(later_keys, factors)
        trans = gammas[part][CHUNK - 1 : CHUNK, :] * (eye - onto[:, :width])
        states.append((trans, onto[:, width:]))
        chunk_ref[part, 0] = trans
        chunk_ref[part, 1] = onto[:, width:]
    if state is not None:
        decay = gammas[-1][CHUNK - 1 : CHUNK, :]
        states[-1] = (decay * (state[0] - behind[:, :width]), behind[:, width:] + state[1])
    while len(states) > 1:
        joined = [followed(*states[at : at + 2]) for at in range(0, len(states) - 1, 2)]
        states = joined + states[2 * len(joined) :]
    pair_ref[0] = states[0][0]
    pair_ref[1] = states[0][1]


def followed(first, second):
    width = first[0].shape[0]
    onto = product(second[0], jnp.concatenate(first, axis=1))
    return onto[:, :width], onto[:, width:] + second[1]


def later_kernel(first_chunk, raw_ref, conv_ref, rate_ref, doc_ref, *outs):
    key_pass(raw_ref, conv_ref, rate_ref[0, 0], doc_ref, first_chunk, outs, None)


def earlier_kernel(first, count, *refs):
    held, refs = refs[:count], refs[count:]
    part_ref, far_ref, rim_ref, next_ref, state_ref, conv_ref, rate_ref, doc_ref = refs[:8]
    outs, raw = refs[8:-1], refs[-1]
    rows, width = part_ref.shape[0], state_ref.shape[1]
    raw[RIM : RIM + rows, :] = add_products(
        part_ref[...], [ref[...] for ref in held], far_ref, first
    )
    raw[:RIM, : 2 * width] = rim_ref[:, width:]
    raw[RIM + rows :, :] = next_ref[:RIM, :]
    key_pass(raw, conv_ref, rate_ref[0, 0], doc_ref, 0, outs, (state_ref[0], state_ref[1]))


def query_kernel(count, *refs):
    held, refs = refs[:count], refs[count:]
    base_ref, far_ref, rim_ref, next_ref, conv_ref = refs[:5]
    fields = [(refs[5:11], 0), (refs[11:17], 1)]
    carried_ref, local_ref, gate_ref, raw = refs[17:]
    width = carried_ref.shape[1]
    rows = held[0].shape[0]
    raw[RIM : RIM + rows, :] = add_products(
        base_ref[:rows, :], [ref[...] for ref in held], far_ref, 0
    )
    raw[:RIM, :width] = rim_ref[:, :width]
    raw[RIM + rows :, :] = next_ref[:RIM, :]
    row = lax.broadcasted_iota(jnp.int32, (CHUNK, CHUNK), 0)
    col = lax.broadcasted_iota(jnp.int32, (CHUNK, CHUNK), 1)
    state = None
    base = 0
    for (key_ref, x_ref, y_ref, grid_ref, gamma_ref, chunk_ref), later in fields:
        source = next_ref if later else raw
        for part in range(key_ref.shape[0] // CHUNK):
            start = RIM + part * CHUNK
            rows = slice(part * CHUNK, (part + 1) * CHUNK)
            out = slice(base, base + CHUNK)
            base += CHUNK
            columns = slice(0, width)
            query = unit_rows(convolve(source, start, columns, conv_ref, columns))
            gate = source[start : start + CHUNK, width:]
            gate_ref[out, :] = gate * sigmoid(gate)
            overlap = product(query, jnp.transpose(key_ref[rows, :]))
            carried = gamma_ref[rows, :] * (
                query - product(jnp.where(row >= col, overlap, 0.0), x_ref[rows, :])
            )
            local = product(grid_ref[rows, :] * overlap, y_ref[rows, :])
            trans, memory = chunk_ref[part, 0], chunk_ref[part, 1]
            if state is None:
                state = (trans, memory)
            else:
                onto = product(
                    jnp.concatenate([trans, carried], axis=0), jnp.concatenate(state, axis=1)
                )
                carried = onto[CHUNK:, :width]
                local = local + onto[CHUNK:, width:]
                state = (onto[:CHUNK, :width], onto[:CHUNK, width:] + memory)
            carried_ref[out, :] = carried
            local_ref[out, :] = local


def four_kernel(bit, carried, last, flag_ref, own_ref, one_ref, two_ref, three_ref, *refs):
    group_ref, level_ref, next_ref = refs[-3:]
    width = next_ref.shape[0]
    flag = lambda at: jnp.broadcast_to(flag_ref[at : at + 1, :], (width, width)) == 1
    set_low, set_high = flag(bit), flag(bit + 1)
    held = (own_ref, one_ref, two_ref, three_ref)

    def placed(part):
        by_low = [jnp.where(set_low, held[at ^ 1][part], held[at][part]) for at in range(4)]
        return [jnp.where(set_high, by_low[at ^ 2], by_low[at]) for at in range(4)]

    trans, memory = placed(0), placed(1)
    joined = lambda at: jnp.concatenate([trans[at], memory[at]], axis=1)
    onto_low = product(trans[1], joined(0))
    onto_high = product(trans[3], joined(2))
    low_a, low_s = onto_low[:, :width], onto_low[:, width:] + memory[1]
    high_a, high_s = onto_high[:, :width], onto_high[:, width:] + memory[3]
    if last:
        group_ref[...] = product(high_a, low_s) + high_s
    else:
        onto = product(high_a, jnp.concatenate([low_a, low_s], axis=1))
        group_ref[0] = onto[:, :width]
        group_ref[1] = onto[:, width:] + high_s
    if carried:
        carry = refs[0][...]
        first = product(carry, jnp.concatenate([one_ref[0], one_ref[1]], axis=1))
        first_a, first_s = first[:, :width], first[:, width:]
    else:
        row = lax.broadcasted_iota(jnp.int32, (width, width), 0)
        col = lax.broadcasted_iota(jnp.int32, (width, width), 1)
        carry = jnp.where(row == col, 1.0, 0.0).astype(F32)
        first_a, first_s = one_ref[0], one_ref[1]
    level_ref[0] = jnp.where(set_low, first_s, 0.0)
    carry = jnp.where(set_low, first_a, carry)
    second = product(carry, jnp.concatenate([low_a, low_s], axis=1))
    level_ref[1] = jnp.where(set_high, second[:, width:], 0.0)
    carry = jnp.where(set_high, second[:, :width], carry)
    next_ref[...] = jnp.where(flag(bit + 2), carry, 0.0) if last else carry


def mix_kernel(stages, single, carried_ref, local_ref, gate_ref, low_ref, high_ref, gain_ref, *refs):
    states = [ref[spot] for ref in refs[:stages] for spot in range(ref.shape[0])]
    if single:
        states.append(product(refs[stages][...], refs[stages + 1][...]))
    outs = refs[stages + (2 if single else 0) :]
    states = [right_parts(state) for state in states]
    carried = left_parts(carried_ref[...])
    weights = jnp.concatenate([low_ref[...], high_ref[...]], axis=0)
    mixed = weights[:, 2:3] * local_ref[...]
    for level, state in enumerate(states):
        mixed = mixed + weights[:, level + 3 : level + 4] * parts_dot(carried, state)
    scale = lax.rsqrt(jnp.mean(mixed * mixed, axis=1, keepdims=True) + 1e-05)
    normed = mixed * scale * gain_ref[...] * gate_ref[...]
    outs[0][...] = normed
    base = 0
    for out in outs[1:]:
        out[...] = normed[base : base + out.shape[0]]
        base += out.shape[0]


def block_product(pieces, weight, rows):
    parts = [halves(ref[rows, :]) for ref in pieces]
    high, low = (jnp.concatenate(part, axis=1) for part in zip(*parts))
    columns = weight.shape[1] // 2
    both = jnp.dot(high, weight, preferred_element_type=F32)
    rest = jnp.dot(low, weight[:, :columns], preferred_element_type=F32)
    return (both[:, :columns] + both[:, columns:]) + rest


def order_kernel(sources, index_ref, weight_ref, out_ref):
    depth = weight_ref.shape[0] // sources
    for source in range(sources):
        rows = pl.ds(pl.multiple_of(index_ref[source] * depth, depth), depth)
        out_ref[source * depth : (source + 1) * depth, :] = left_parts(weight_ref[rows, :])


def source_rows(first, pieces, weight_ref):
    depth = pieces[0].shape[1]
    return weight_ref[first * depth : (first + len(pieces)) * depth, :]


def row_blocks(rows):
    return [slice(base, base + CHUNK) for base in range(0, rows, CHUNK)]


def near_kernel(own_ref, near_ref, weight_ref, low_ref, high_ref):
    weight = source_rows(0, [own_ref, near_ref], weight_ref)
    half = low_ref.shape[0]
    for rows in row_blocks(half):
        low_ref[rows, :] = block_product([own_ref, near_ref], weight, rows)
        later = slice(half + rows.start, half + rows.stop)
        high_ref[rows, :] = block_product([own_ref, near_ref], weight, later)


def far_kernel(count, first, *refs):
    held, (weight_ref, total_ref, out_ref) = refs[:-3], refs[-3:]
    weight = source_rows(first, held[:count], weight_ref)
    base = 0
    for at in range(0, len(held), count):
        pieces = held[at : at + count]
        for rows in row_blocks(pieces[0].shape[0]):
            out = slice(base + rows.start, base + rows.stop)
            out_ref[out, :] = total_ref[out, :] + block_product(pieces, weight, rows)
        base += pieces[0].shape[0]


def flush_kernel(count, first, *refs):
    pieces = refs[:count]
    weight_ref, ready_ref, total_ref, out_ref, next_ref, sem = refs[count:]
    half = ready_ref.shape[0]
    copy = pltpu.make_async_copy(ready_ref, out_ref.at[:half, :], sem)
    copy.start()
    weight = source_rows(first, pieces, weight_ref)
    for rows in row_blocks(half):
        next_ref[rows, :] = total_ref[rows, :] + block_product(pieces, weight, rows)
    copy.wait()


def last_kernel(count, first, *refs):
    pieces = refs[:count]
    weight_ref, total_ref, begun_ref, out_ref, held, sems = refs[count:]
    half = total_ref.shape[0]
    copies = []
    weight = source_rows(first, pieces, weight_ref)
    for spot, rows in enumerate(row_blocks(half)):
        held[rows, :] = total_ref[rows, :] + block_product(pieces, weight, rows)
        out = slice(half + rows.start, half + rows.stop)
        copies.append(
            pltpu.make_async_copy(held.at[rows, :], out_ref.at[out, :], sems.at[spot])
        )
        copies[-1].start()
    for copy in copies:
        copy.wait()


def vmem_call(kernel, outs, scratch, cost, *args, any_in=(), any_out=(), aliases=()):
    spec = pl.BlockSpec(memory_space=pltpu.VMEM)
    small = pl.BlockSpec(memory_space=pltpu.SMEM)
    free = pl.BlockSpec(memory_space=pl.ANY)
    return pl.pallas_call(
        kernel,
        out_shape=outs,
        in_specs=[
            free if spot in any_in else small if arg.dtype == jnp.int32 and arg.ndim == 1 else spec
            for spot, arg in enumerate(args)
        ],
        out_specs=[free if spot in any_out else spec for spot in range(len(outs))]
        if isinstance(outs, list)
        else (free if any_out else spec),
        input_output_aliases=dict(aliases),
        scratch_shapes=scratch,
        compiler_params=pltpu.CompilerParams(vmem_limit_bytes=VMEM_GRANT),
        cost_estimate=pl.CostEstimate(flops=int(cost * 1e9), bytes_accessed=1 << 20, transcendentals=0),
    )(*args)


def to_sibling(value):
    count = lax.axis_size("head")
    return lax.ppermute(value, "head", [(source, source ^ 1) for source in range(count)])


def to_chips(value):
    count = lax.axis_size("head")
    return [
        lax.ppermute(
            value, "head", [(source, (source + 2 * step) % count) for source in range(count)]
        )
        for step in range(1, count // 2)
    ]


def after(value, *earlier):
    return lax.optimization_barrier((value, *earlier))


def shards(tokens, w_proj, w_mix, conv_w, rates, doc_start, norm_gain, w_out):
    tok_rows, depth = tokens.shape
    width = w_proj.shape[1] // 4
    state_columns, query_columns = 2 * width + CHUNK, 2 * width
    heads, me = lax.axis_size("head"), lax.axis_index("head")
    blocks, my_index = lax.axis_size("ctx"), lax.axis_index("ctx")
    remote = [(me + heads - 2 * step) % heads for step in range(1, heads // 2)]
    order = [me, me ^ 1] + remote + [index ^ 1 for index in remote]
    bits = blocks.bit_length() - 1
    index = jnp.stack(order + [my_index >> bit & 1 for bit in range(bits)]).astype(jnp.int32)
    count = heads - 2
    like = lambda *shape: jax.ShapeDtypeStruct(shape, F32)
    parts = lambda *shape: jax.ShapeDtypeStruct(shape, BF16)

    first = tok_rows // 2
    cut = first - RIM
    middle = tok_rows - CHUNK - RIM
    segments = (slice(cut, middle), slice(middle, tok_rows))
    late = [to_chips(tokens[rows]) for rows in segments]
    beside = to_sibling(tokens)
    early_rows, beside = after(tokens, beside)
    early = to_chips(early_rows[:cut])
    base_state, base_query, far_state, far_query, flags = vmem_call(
        base_kernel,
        [like(tok_rows, state_columns), like(tok_rows, query_columns),
         parts(count * depth, 2 * state_columns), parts(count * depth, 2 * query_columns),
         jax.ShapeDtypeStruct((bits, CHUNK), jnp.int32)],
        [pltpu.VMEM((heads, depth, 4 * width), F32),
         pltpu.VMEM((2 * depth, 2 * state_columns), BF16),
         pltpu.VMEM((2 * depth, 2 * query_columns), BF16),
         pltpu.SemaphoreType.DMA((heads,))],
        3, index, tokens, beside, w_mix.T, w_proj, any_in=(4,),
    )
    late, far_state = after(late, far_state)
    late_on = [[to_sibling(value) for value in values] for values in late]
    arrived = [value for pair in zip(late, late_on) for values in pair for value in values]
    late_state, late_query, rim = vmem_call(
        functools.partial(late_kernel, count, segments),
        [like(tok_rows - cut, state_columns), like(tok_rows - cut, query_columns),
         like(RIM, 3 * width)],
        [], 0.5, *arrived, base_state, base_query, far_state, far_query,
    )
    rim = lax.ppermute(rim, "ctx", [(source, source + 1) for source in range(blocks - 1)])
    docs = doc_start.reshape(tok_rows // CHUNK, CHUNK)
    rate = rates[:, None]

    def outs(rows):
        chunks = like(rows // CHUNK, 2, width, width)
        return [like(rows, width)] * 6 + [chunks, like(2, width, width)]

    later = vmem_call(
        functools.partial(later_kernel, first // CHUNK), outs(tok_rows - first), [], 0.5,
        late_state, conv_w, rate, docs,
    )
    early, pair_late, rim = after(early, later[7], rim)
    early_on = [to_sibling(value) for value in early]
    partial = vmem_call(
        functools.partial(partial_kernel, len(early)), like(cut, state_columns), [], 1,
        *early, base_state, far_state,
    )
    earlier = vmem_call(
        functools.partial(earlier_kernel, len(early), len(early)), outs(first),
        [pltpu.VMEM((first + RIM, state_columns), F32)], 5,
        *early_on, partial, far_state, rim, late_state, pair_late, conv_w, rate, docs,
    )

    pair = earlier[7]
    fields = vmem_call(
        functools.partial(query_kernel, count), [like(tok_rows, width)] * 3,
        [pltpu.VMEM((first + RIM, query_columns), F32)], 5,
        *early, *early_on, base_query, far_query, rim, late_query, conv_w,
        *earlier[:5], earlier[6], *later[:5], later[6],
    )
    own_weight = vmem_call(
        functools.partial(order_kernel, heads), parts(w_out.shape[0], 2 * w_out.shape[1]), [], 1,
        index, w_out,
    )
    carry = ()
    levels = []
    for bit in range(0, bits - 1, 2):
        others = [
            lax.ppermute(
                pair, "ctx", [(source, source ^ (mask << bit)) for source in range(blocks)]
            )
            for mask in (1, 2, 3)
        ]
        if not bit:
            others[0], *fields, own_weight = after(others[0], *fields, own_weight)
        last = bit + 2 >= bits - 1 and bits % 2
        group = [like(width, width)] if last else [like(2, width, width)]
        pair, level, *carry = vmem_call(
            functools.partial(four_kernel, bit, bool(carry), last),
            group + [like(2, width, width), like(width, width)], [], 1,
            flags, pair, *others, *carry,
        )
        levels.append(level)
    single = []
    if bits % 2:
        reach = blocks // 2
        single = [
            *(carry or [jnp.where(my_index >= reach, jnp.eye(width, dtype=F32), 0.0)]),
            lax.ppermute(
                pair if carry else pair[1],
                "ctx", [(source, source ^ reach) for source in range(blocks)],
            ),
        ]
    half = tok_rows // 2
    normed, *lows, high = vmem_call(
        functools.partial(mix_kernel, len(levels), bool(single)),
        [like(tok_rows, width)] + [like(half // 2, width)] * 2 + [like(half, width)], [], 1,
        *fields, earlier[5], later[5], norm_gain[None, :], *levels, *single,
    )
    columns = w_out.shape[1]
    near = to_sibling(normed)
    far_lows = [to_chips(low) for low in lows]
    high, near = after(high, near)
    far_high = to_chips(high)
    total_low, total_high = vmem_call(
        near_kernel, [like(half, columns)] * 2, [], 2, normed, near, own_weight
    )
    far_lows, total_low = after(far_lows, total_low)
    far_lows_on = [[to_sibling(value) for value in values] for values in far_lows]
    arrived = [value for pair in zip(far_lows, far_lows_on) for values in pair for value in values]
    total_low = vmem_call(
        functools.partial(far_kernel, count, 2), like(half, columns), [], 0.01,
        *arrived, own_weight, total_low,
    )
    far_high, total_low = after(far_high, total_low)
    far_high_on = [to_sibling(value) for value in far_high]
    whole = like(tok_rows, columns)
    begun, total_high = vmem_call(
        functools.partial(flush_kernel, len(far_high), 2), [whole, like(half, columns)],
        [pltpu.SemaphoreType.DMA], 1,
        *far_high, own_weight, total_low, total_high, any_out=(0,),
    )
    args = [*far_high_on, own_weight, total_high, begun]
    last = len(args) - 1
    return vmem_call(
        functools.partial(last_kernel, len(far_high), 2 + len(far_high)), whole,
        [pltpu.VMEM((half, columns), F32), pltpu.SemaphoreType.DMA((half // CHUNK,))], 1,
        *args, any_in=(last,), any_out=True, aliases=((last, 0),),
    )


def solution(mesh):
    placed = (
        P("ctx", "head"),
        P(None, "head"),
        P(None, "head"),
        P(None, "head"),
        P("head"),
        P("ctx"),
        P("head"),
        P(None, "head"),
    )
    return jax.shard_map(
        shards, mesh=mesh, in_specs=placed, out_specs=P("ctx", "head"), check_vma=False
    )
```

```python
import functools

import jax
import jax.numpy as jnp
from jax import lax
from jax.experimental import pallas as pl
from jax.experimental.pallas import tpu as pltpu
from jax.sharding import PartitionSpec as P

CHUNK = 128
RIM = 16
VMEM_GRANT = 16 << 20
F32 = jnp.float32
BF16 = jnp.bfloat16


def halves(value):
    high = value.astype(BF16)
    return high, (value - high.astype(F32)).astype(BF16)


def left_parts(value):
    return jnp.concatenate(halves(value), axis=1)


def right_parts(value):
    row = jnp.concatenate(halves(value), axis=1)
    return jnp.concatenate([row, row], axis=0)


def parts_dot(left, right):
    both = jnp.dot(left, right, preferred_element_type=F32)
    half = both.shape[1] // 2
    return both[:, :half] + both[:, half:]


def product(left, right):
    return parts_dot(left_parts(left), right_parts(right))


def softplus(value):
    return jnp.maximum(value, 0.0) + jnp.log1p(jnp.exp(-jnp.abs(value)))


def sigmoid(value):
    return 1.0 / (1.0 + jnp.exp(-value))


def unit_lower_inverse(lowers, row, col):
    size = lowers[0].shape[0]
    eye = jnp.where(row == col, 1.0, 0.0).astype(F32)
    inverses = [eye - jnp.where((row >> 1) == (col >> 1), lower, 0.0) for lower in lowers]
    lower_parts = [halves(lower) for lower in lowers]
    step = 1
    while 1 << step < size:
        off = ((row >> (step + 2)) == (col >> (step + 2))) & ((row >> step) > (col >> step))
        offs = [
            jnp.concatenate([jnp.where(off, part, jnp.zeros_like(part)) for part in parts], axis=1)
            for parts in lower_parts
        ]
        onto = [parts_dot(left, right_parts(inverse)) for left, inverse in zip(offs, inverses)]
        rights = [right_parts(value) for value in onto]
        squares = [parts_dot(left_parts(value), right) for value, right in zip(onto, rights)]
        firsts = [
            inverse - parts_dot(left_parts(inverse), right)
            for inverse, right in zip(inverses, rights)
        ]
        inverses = [first + product(first, square) for first, square in zip(firsts, squares)]
        step += 2
    return inverses


def add_products(total, pieces, weight_ref, first):
    columns = weight_ref.shape[1] // 2
    for spot, piece in enumerate(pieces):
        depth = piece.shape[1]
        rows = slice((first + spot) * depth, (first + spot + 1) * depth)
        high, low = halves(piece)
        both = jnp.dot(high, weight_ref[rows, :], preferred_element_type=F32)
        rest = jnp.dot(low, weight_ref[rows, :columns], preferred_element_type=F32)
        part = (both[:, :columns] + both[:, columns:]) + rest
        total = part if total is None else total + part
    return total


def base_kernel(
    index_ref, own_ref, beside_ref, mix_ref, proj_ref,
    state_ref, query_ref, far_state_ref, far_query_ref, flag_ref,
    held, near_state, near_query, sems,
):
    sources, depth, across = held.shape
    width = across // 4
    copies = []
    for source in range(sources):
        rows = pl.ds(pl.multiple_of(index_ref[source] * depth, depth), depth)
        copies.append(pltpu.make_async_copy(proj_ref.at[rows, :], held.at[source], sems.at[source]))
        copies[-1].start()
    for bit in range(flag_ref.shape[0]):
        flag_ref[bit : bit + 1, :] = jnp.broadcast_to(index_ref[sources + bit], (1, CHUNK))
    mixes = mix_ref.shape[0]

    def split(source, state_out, query_out, base):
        copies[source].wait()
        lanes = pl.ds(pl.multiple_of(index_ref[source] * depth, depth), depth)
        for begin in range(0, depth, CHUNK):
            rows = slice(begin, begin + CHUNK)
            out = slice(base + begin, base + begin + CHUNK)
            value = held[source, rows, :]
            mixing = mix_ref[:, lanes][:, rows]
            mixing = jnp.concatenate([mixing, jnp.zeros((CHUNK - mixes, CHUNK), F32)], axis=0)
            state = jnp.concatenate([value[:, width : 3 * width], jnp.transpose(mixing)], axis=1)
            query = jnp.concatenate([value[:, :width], value[:, 3 * width :]], axis=1)
            state_out[out, :] = left_parts(state)
            query_out[out, :] = left_parts(query)

    for source in range(2):
        split(source, near_state, near_query, source * depth)
    half = own_ref.shape[0] // 2
    for rows in (slice(0, half), slice(half, 2 * half)):
        pieces = [own_ref[rows, :], beside_ref[rows, :]]
        state_ref[rows, :] = add_products(None, pieces, near_state, 0)
        query_ref[rows, :] = add_products(None, pieces, near_query, 0)
    for source in range(2, sources):
        split(source, far_state_ref, far_query_ref, (source - 2) * depth)


def late_kernel(count, segments, *refs):
    begin = segments[0].start
    held, refs = refs[: count * len(segments)], refs[count * len(segments) :]
    base_state, base_query, far_state, far_query, state_ref, query_ref, rim_ref = refs
    width = base_query.shape[1] // 2
    for turn, rows in enumerate(segments):
        pieces = [ref[...] for ref in held[turn * count : (turn + 1) * count]]
        out = slice(rows.start - begin, rows.stop - begin)
        state_ref[out, :] = add_products(base_state[rows, :], pieces, far_state, 0)
        query_ref[out, :] = add_products(base_query[rows, :], pieces, far_query, 0)
    last = state_ref.shape[0] - RIM
    rim_ref[:, :width] = query_ref[last:, :width]
    rim_ref[:, width:] = state_ref[last:, : 2 * width]


def partial_kernel(count, *refs):
    base_state, far_state, out_ref = refs[count:]
    out_ref[...] = add_products(
        base_state[: out_ref.shape[0], :], [ref[...] for ref in refs[:count]], far_state, 0
    )


def convolve(raw, start, columns, conv_ref, taps_at):
    taps = conv_ref.shape[0]
    conv = 0.0
    for tap in range(taps):
        spot = start - taps + 1 + tap
        conv = conv + conv_ref[tap : tap + 1, taps_at] * raw[spot : spot + CHUNK, columns]
    return conv * sigmoid(conv)


def unit_rows(value):
    return value * lax.rsqrt(jnp.sum(value * value, axis=1, keepdims=True) + 1e-06)


def key_pass(raw, conv_ref, rate, doc_ref, first_chunk, outs, state):
    key_ref, x_ref, y_ref, grid_ref, gamma_ref, plus_ref, chunk_ref, pair_ref = outs
    width = key_ref.shape[1]
    chunks = key_ref.shape[0] // CHUNK
    row = lax.broadcasted_iota(jnp.int32, (CHUNK, CHUNK), 0)
    col = lax.broadcasted_iota(jnp.int32, (CHUNK, CHUNK), 1)
    lower = row >= col
    tri = jnp.where(lower, 1.0, 0.0).astype(F32)
    eye = jnp.where(row == col, 1.0, 0.0).astype(F32)
    keys, values, betas, grids, gammas, tails = [], [], [], [], [], []
    for part in range(chunks):
        start = RIM + part * CHUNK
        rows = slice(part * CHUNK, (part + 1) * CHUNK)
        middle, last = slice(width, 2 * width), slice(2 * width, 3 * width)
        keys.append(unit_rows(convolve(raw, start, slice(0, width), conv_ref, middle)))
        values.append(convolve(raw, start, middle, conv_ref, last))
        mixing = raw[start : start + CHUNK, last]
        plus = softplus(mixing)
        plus_ref[rows, :] = plus
        betas.append(sigmoid(mixing[:, 0:1]))
        spot = first_chunk + part
        docs = jnp.broadcast_to(doc_ref[spot : spot + 1, :].astype(F32), (CHUNK, CHUNK))
        docs = jnp.transpose(docs)
        steps = jnp.where(col == 1, -rate * plus, jnp.where(col == 0, docs, 0.0))
        sums = jnp.dot(tri, steps, precision=lax.Precision.HIGHEST, preferred_element_type=F32)
        across = jnp.transpose(sums)
        smooth, count = sums[:, 1:2], sums[:, 0:1]
        span = (smooth - across[1:2, :]) - 20.0 * (count - across[0:1, :])
        grids.append(jnp.exp(jnp.where(lower, span, -1e30)))
        gammas.append(jnp.exp(smooth - 20.0 * count))
        last = sums[CHUNK - 1 : CHUNK, :]
        tails.append(jnp.exp((last[:, 1:2] - smooth) - 20.0 * (last[:, 0:1] - count)))
        key_ref[rows, :] = keys[part]
        grid_ref[rows, :] = grids[part]
        gamma_ref[rows, :] = jnp.broadcast_to(gammas[part], (CHUNK, width))
    across_keys = [jnp.transpose(key) for key in keys]
    grams = [
        parts_dot(left_parts(key), right_parts(across)) for key, across in zip(keys, across_keys)
    ]
    lowers = [jnp.where(row > col, beta * gram, 0.0) for beta, gram in zip(betas, grams)]
    inverses = unit_lower_inverse(lowers, row, col)
    states = []
    if state is not None:
        later_keys = product(state[0], across_keys[-1])
    for part in range(chunks):
        rows = slice(part * CHUNK, (part + 1) * CHUNK)
        inverse, beta = inverses[part], betas[part]
        factor_x = product(inverse, beta * keys[part])
        factor_y = product(grids[part] * inverse, beta * values[part])
        x_ref[rows, :] = factor_x
        y_ref[rows, :] = factor_y
        factors = jnp.concatenate([factor_x, tails[part] * factor_y], axis=1)
        onto = product(across_keys[part], factors)
        if state is not None and part == chunks - 1:
            behind = product(later_keys, factors)
        trans = gammas[part][CHUNK - 1 : CHUNK, :] * (eye - onto[:, :width])
        states.append((trans, onto[:, width:]))
        chunk_ref[part, 0] = trans
        chunk_ref[part, 1] = onto[:, width:]
    if state is not None:
        decay = gammas[-1][CHUNK - 1 : CHUNK, :]
        states[-1] = (decay * (state[0] - behind[:, :width]), behind[:, width:] + state[1])
    while len(states) > 1:
        joined = [followed(*states[at : at + 2]) for at in range(0, len(states) - 1, 2)]
        states = joined + states[2 * len(joined) :]
    pair_ref[0] = states[0][0]
    pair_ref[1] = states[0][1]


def followed(first, second):
    width = first[0].shape[0]
    onto = product(second[0], jnp.concatenate(first, axis=1))
    return onto[:, :width], onto[:, width:] + second[1]


def later_kernel(first_chunk, raw_ref, conv_ref, rate_ref, doc_ref, *outs):
    key_pass(raw_ref, conv_ref, rate_ref[0, 0], doc_ref, first_chunk, outs, None)


def earlier_kernel(first, count, *refs):
    held, refs = refs[:count], refs[count:]
    part_ref, far_ref, rim_ref, next_ref, state_ref, conv_ref, rate_ref, doc_ref = refs[:8]
    outs, raw = refs[8:-1], refs[-1]
    rows, width = part_ref.shape[0], state_ref.shape[1]
    raw[RIM : RIM + rows, :] = add_products(
        part_ref[...], [ref[...] for ref in held], far_ref, first
    )
    raw[:RIM, : 2 * width] = rim_ref[:, width:]
    raw[RIM + rows :, :] = next_ref[:RIM, :]
    key_pass(raw, conv_ref, rate_ref[0, 0], doc_ref, 0, outs, (state_ref[0], state_ref[1]))


def query_kernel(count, *refs):
    held, refs = refs[:count], refs[count:]
    base_ref, far_ref, rim_ref, next_ref, conv_ref = refs[:5]
    fields = [(refs[5:11], 0), (refs[11:17], 1)]
    carried_ref, local_ref, gate_ref, raw = refs[17:]
    width = carried_ref.shape[1]
    rows = held[0].shape[0]
    raw[RIM : RIM + rows, :] = add_products(
        base_ref[:rows, :], [ref[...] for ref in held], far_ref, 0
    )
    raw[:RIM, :width] = rim_ref[:, :width]
    raw[RIM + rows :, :] = next_ref[:RIM, :]
    row = lax.broadcasted_iota(jnp.int32, (CHUNK, CHUNK), 0)
    col = lax.broadcasted_iota(jnp.int32, (CHUNK, CHUNK), 1)
    state = None
    base = 0
    for (key_ref, x_ref, y_ref, grid_ref, gamma_ref, chunk_ref), later in fields:
        source = next_ref if later else raw
        for part in range(key_ref.shape[0] // CHUNK):
            start = RIM + part * CHUNK
            rows = slice(part * CHUNK, (part + 1) * CHUNK)
            out = slice(base, base + CHUNK)
            base += CHUNK
            columns = slice(0, width)
            query = unit_rows(convolve(source, start, columns, conv_ref, columns))
            gate = source[start : start + CHUNK, width:]
            gate_ref[out, :] = gate * sigmoid(gate)
            overlap = product(query, jnp.transpose(key_ref[rows, :]))
            carried = gamma_ref[rows, :] * (
                query - product(jnp.where(row >= col, overlap, 0.0), x_ref[rows, :])
            )
            local = product(grid_ref[rows, :] * overlap, y_ref[rows, :])
            trans, memory = chunk_ref[part, 0], chunk_ref[part, 1]
            if state is None:
                state = (trans, memory)
            else:
                onto = product(
                    jnp.concatenate([trans, carried], axis=0), jnp.concatenate(state, axis=1)
                )
                carried = onto[CHUNK:, :width]
                local = local + onto[CHUNK:, width:]
                state = (onto[:CHUNK, :width], onto[:CHUNK, width:] + memory)
            carried_ref[out, :] = carried
            local_ref[out, :] = local


def four_kernel(bit, carried, last, flag_ref, own_ref, one_ref, two_ref, three_ref, *refs):
    group_ref, level_ref, next_ref = refs[-3:]
    width = next_ref.shape[0]
    flag = lambda at: jnp.broadcast_to(flag_ref[at : at + 1, :], (width, width)) == 1
    set_low, set_high = flag(bit), flag(bit + 1)
    held = (own_ref, one_ref, two_ref, three_ref)

    def placed(part):
        by_low = [jnp.where(set_low, held[at ^ 1][part], held[at][part]) for at in range(4)]
        return [jnp.where(set_high, by_low[at ^ 2], by_low[at]) for at in range(4)]

    trans, memory = placed(0), placed(1)
    joined = lambda at: jnp.concatenate([trans[at], memory[at]], axis=1)
    onto_low = product(trans[1], joined(0))
    onto_high = product(trans[3], joined(2))
    low_a, low_s = onto_low[:, :width], onto_low[:, width:] + memory[1]
    high_a, high_s = onto_high[:, :width], onto_high[:, width:] + memory[3]
    if last:
        group_ref[...] = product(high_a, low_s) + high_s
    else:
        onto = product(high_a, jnp.concatenate([low_a, low_s], axis=1))
        group_ref[0] = onto[:, :width]
        group_ref[1] = onto[:, width:] + high_s
    if carried:
        carry = refs[0][...]
        first = product(carry, jnp.concatenate([one_ref[0], one_ref[1]], axis=1))
        first_a, first_s = first[:, :width], first[:, width:]
    else:
        row = lax.broadcasted_iota(jnp.int32, (width, width), 0)
        col = lax.broadcasted_iota(jnp.int32, (width, width), 1)
        carry = jnp.where(row == col, 1.0, 0.0).astype(F32)
        first_a, first_s = one_ref[0], one_ref[1]
    level_ref[0] = jnp.where(set_low, first_s, 0.0)
    carry = jnp.where(set_low, first_a, carry)
    second = product(carry, jnp.concatenate([low_a, low_s], axis=1))
    level_ref[1] = jnp.where(set_high, second[:, width:], 0.0)
    carry = jnp.where(set_high, second[:, :width], carry)
    next_ref[...] = jnp.where(flag(bit + 2), carry, 0.0) if last else carry


def level_kernel(stages, single, carried_ref, local_ref, low_ref, high_ref, *refs):
    states = [ref[spot] for ref in refs[:stages] for spot in range(ref.shape[0])]
    carried = left_parts(carried_ref[...])
    weights = jnp.concatenate([low_ref[...], high_ref[...]], axis=0)
    mixed = weights[:, 2:3] * local_ref[...]
    for level, state in enumerate(states):
        mixed = mixed + weights[:, level + 3 : level + 4] * parts_dot(carried, right_parts(state))
    if single:
        carry_ref, mixed_ref, reach_ref = refs[stages:]
        level = len(states) + 3
        reach_ref[...] = weights[:, level : level + 1] * parts_dot(
            carried, right_parts(carry_ref[...])
        )
    else:
        (mixed_ref,) = refs[stages:]
    mixed_ref[...] = mixed


def mix_kernel(single, mixed_ref, gate_ref, gain_ref, *refs):
    mixed = mixed_ref[...]
    if single:
        mixed = mixed + product(refs[0][...], refs[1][...])
    outs = refs[2 if single else 0 :]
    scale = lax.rsqrt(jnp.mean(mixed * mixed, axis=1, keepdims=True) + 1e-05)
    normed = mixed * scale * gain_ref[...] * gate_ref[...]
    outs[0][...] = normed
    base = 0
    for out in outs[1:]:
        out[...] = normed[base : base + out.shape[0]]
        base += out.shape[0]


def block_product(pieces, weight, rows):
    parts = [halves(ref[rows, :]) for ref in pieces]
    high, low = (jnp.concatenate(part, axis=1) for part in zip(*parts))
    columns = weight.shape[1] // 2
    both = jnp.dot(high, weight, preferred_element_type=F32)
    rest = jnp.dot(low, weight[:, :columns], preferred_element_type=F32)
    return (both[:, :columns] + both[:, columns:]) + rest


def order_kernel(sources, index_ref, weight_ref, out_ref):
    depth = weight_ref.shape[0] // sources
    for source in range(sources):
        rows = pl.ds(pl.multiple_of(index_ref[source] * depth, depth), depth)
        out_ref[source * depth : (source + 1) * depth, :] = left_parts(weight_ref[rows, :])


def source_rows(first, pieces, weight_ref):
    depth = pieces[0].shape[1]
    return weight_ref[first * depth : (first + len(pieces)) * depth, :]


def row_blocks(rows):
    return [slice(base, base + CHUNK) for base in range(0, rows, CHUNK)]


def near_kernel(own_ref, near_ref, weight_ref, low_ref, high_ref):
    weight = source_rows(0, [own_ref, near_ref], weight_ref)
    half = low_ref.shape[0]
    for rows in row_blocks(half):
        low_ref[rows, :] = block_product([own_ref, near_ref], weight, rows)
        later = slice(half + rows.start, half + rows.stop)
        high_ref[rows, :] = block_product([own_ref, near_ref], weight, later)


def far_kernel(count, first, *refs):
    held, (weight_ref, total_ref, out_ref) = refs[:-3], refs[-3:]
    weight = source_rows(first, held[:count], weight_ref)
    base = 0
    for at in range(0, len(held), count):
        pieces = held[at : at + count]
        for rows in row_blocks(pieces[0].shape[0]):
            out = slice(base + rows.start, base + rows.stop)
            out_ref[out, :] = total_ref[out, :] + block_product(pieces, weight, rows)
        base += pieces[0].shape[0]


def flush_kernel(count, first, *refs):
    pieces = refs[:count]
    weight_ref, ready_ref, total_ref, out_ref, next_ref, sem = refs[count:]
    half = ready_ref.shape[0]
    copy = pltpu.make_async_copy(ready_ref, out_ref.at[:half, :], sem)
    copy.start()
    weight = source_rows(first, pieces, weight_ref)
    for rows in row_blocks(half):
        next_ref[rows, :] = total_ref[rows, :] + block_product(pieces, weight, rows)
    copy.wait()


def last_kernel(count, first, *refs):
    pieces = refs[:count]
    weight_ref, total_ref, begun_ref, out_ref, held, sems = refs[count:]
    half = total_ref.shape[0]
    copies = []
    weight = source_rows(first, pieces, weight_ref)
    for spot, rows in enumerate(row_blocks(half)):
        held[rows, :] = total_ref[rows, :] + block_product(pieces, weight, rows)
        out = slice(half + rows.start, half + rows.stop)
        copies.append(
            pltpu.make_async_copy(held.at[rows, :], out_ref.at[out, :], sems.at[spot])
        )
        copies[-1].start()
    for copy in copies:
        copy.wait()


def vmem_call(kernel, outs, scratch, cost, *args, any_in=(), any_out=(), aliases=()):
    spec = pl.BlockSpec(memory_space=pltpu.VMEM)
    small = pl.BlockSpec(memory_space=pltpu.SMEM)
    free = pl.BlockSpec(memory_space=pl.ANY)
    return pl.pallas_call(
        kernel,
        out_shape=outs,
        in_specs=[
            free if spot in any_in else small if arg.dtype == jnp.int32 and arg.ndim == 1 else spec
            for spot, arg in enumerate(args)
        ],
        out_specs=[free if spot in any_out else spec for spot in range(len(outs))]
        if isinstance(outs, list)
        else (free if any_out else spec),
        input_output_aliases=dict(aliases),
        scratch_shapes=scratch,
        compiler_params=pltpu.CompilerParams(vmem_limit_bytes=VMEM_GRANT),
        cost_estimate=pl.CostEstimate(flops=int(cost * 1e9), bytes_accessed=1 << 20, transcendentals=0),
    )(*args)


def to_sibling(value):
    count = lax.axis_size("head")
    return lax.ppermute(value, "head", [(source, source ^ 1) for source in range(count)])


def to_chips(value):
    count = lax.axis_size("head")
    return [
        lax.ppermute(
            value, "head", [(source, (source + 2 * step) % count) for source in range(count)]
        )
        for step in range(1, count // 2)
    ]


def after(value, *earlier):
    return lax.optimization_barrier((value, *earlier))


def shards(tokens, w_proj, w_mix, conv_w, rates, doc_start, norm_gain, w_out):
    tok_rows, depth = tokens.shape
    width = w_proj.shape[1] // 4
    state_columns, query_columns = 2 * width + CHUNK, 2 * width
    heads, me = lax.axis_size("head"), lax.axis_index("head")
    blocks, my_index = lax.axis_size("ctx"), lax.axis_index("ctx")
    remote = [(me + heads - 2 * step) % heads for step in range(1, heads // 2)]
    order = [me, me ^ 1] + remote + [index ^ 1 for index in remote]
    bits = blocks.bit_length() - 1
    index = jnp.stack(order + [my_index >> bit & 1 for bit in range(bits)]).astype(jnp.int32)
    count = heads - 2
    like = lambda *shape: jax.ShapeDtypeStruct(shape, F32)
    parts = lambda *shape: jax.ShapeDtypeStruct(shape, BF16)

    first = tok_rows // 2
    cut = first - RIM
    middle = tok_rows - CHUNK - RIM
    segments = (slice(cut, middle), slice(middle, tok_rows))
    late = [to_chips(tokens[rows]) for rows in segments]
    beside = to_sibling(tokens)
    early_rows, beside = after(tokens, beside)
    early = to_chips(early_rows[:cut])
    base_state, base_query, far_state, far_query, flags = vmem_call(
        base_kernel,
        [like(tok_rows, state_columns), like(tok_rows, query_columns),
         parts(count * depth, 2 * state_columns), parts(count * depth, 2 * query_columns),
         jax.ShapeDtypeStruct((bits, CHUNK), jnp.int32)],
        [pltpu.VMEM((heads, depth, 4 * width), F32),
         pltpu.VMEM((2 * depth, 2 * state_columns), BF16),
         pltpu.VMEM((2 * depth, 2 * query_columns), BF16),
         pltpu.SemaphoreType.DMA((heads,))],
        3, index, tokens, beside, w_mix.T, w_proj, any_in=(4,),
    )
    late, far_state = after(late, far_state)
    late_on = [[to_sibling(value) for value in values] for values in late]
    arrived = [value for pair in zip(late, late_on) for values in pair for value in values]
    late_state, late_query, rim = vmem_call(
        functools.partial(late_kernel, count, segments),
        [like(tok_rows - cut, state_columns), like(tok_rows - cut, query_columns),
         like(RIM, 3 * width)],
        [], 0.5, *arrived, base_state, base_query, far_state, far_query,
    )
    rim = lax.ppermute(rim, "ctx", [(source, source + 1) for source in range(blocks - 1)])
    docs = doc_start.reshape(tok_rows // CHUNK, CHUNK)
    rate = rates[:, None]

    def outs(rows):
        chunks = like(rows // CHUNK, 2, width, width)
        return [like(rows, width)] * 6 + [chunks, like(2, width, width)]

    later = vmem_call(
        functools.partial(later_kernel, first // CHUNK), outs(tok_rows - first), [], 0.5,
        late_state, conv_w, rate, docs,
    )
    early, pair_late, rim = after(early, later[7], rim)
    early_on = [to_sibling(value) for value in early]
    partial = vmem_call(
        functools.partial(partial_kernel, len(early)), like(cut, state_columns), [], 1,
        *early, base_state, far_state,
    )
    earlier = vmem_call(
        functools.partial(earlier_kernel, len(early), len(early)), outs(first),
        [pltpu.VMEM((first + RIM, state_columns), F32)], 5,
        *early_on, partial, far_state, rim, late_state, pair_late, conv_w, rate, docs,
    )

    pair = earlier[7]
    fields = vmem_call(
        functools.partial(query_kernel, count), [like(tok_rows, width)] * 3,
        [pltpu.VMEM((first + RIM, query_columns), F32)], 5,
        *early, *early_on, base_query, far_query, rim, late_query, conv_w,
        *earlier[:5], earlier[6], *later[:5], later[6],
    )
    own_weight = vmem_call(
        functools.partial(order_kernel, heads), parts(w_out.shape[0], 2 * w_out.shape[1]), [], 1,
        index, w_out,
    )
    carry = ()
    levels = []
    for bit in range(0, bits - 1, 2):
        others = [
            lax.ppermute(
                pair, "ctx", [(source, source ^ (mask << bit)) for source in range(blocks)]
            )
            for mask in (1, 2, 3)
        ]
        if not bit:
            others[0], *fields, own_weight = after(others[0], *fields, own_weight)
        last = bit + 2 >= bits - 1 and bits % 2
        group = [like(width, width)] if last else [like(2, width, width)]
        pair, level, *carry = vmem_call(
            functools.partial(four_kernel, bit, bool(carry), last),
            group + [like(2, width, width), like(width, width)], [], 1,
            flags, pair, *others, *carry,
        )
        levels.append(level)
    carried, local, gate = fields
    lone = bool(bits % 2)
    reach = blocks // 2
    if lone:
        other = lax.ppermute(
            pair if carry else pair[1],
            "ctx", [(source, source ^ reach) for source in range(blocks)],
        )
        if not carry:
            carry = [jnp.where(my_index >= reach, jnp.eye(width, dtype=F32), 0.0)]
    rows_shape = like(tok_rows, width)
    mixed, *reached = vmem_call(
        functools.partial(level_kernel, len(levels), lone), [rows_shape] * (2 if lone else 1), [], 1,
        carried, local, earlier[5], later[5], *levels, *(carry if lone else ()),
    )
    if lone:
        reached.append(other)
    half = tok_rows // 2
    normed, *lows, high = vmem_call(
        functools.partial(mix_kernel, lone),
        [rows_shape] + [like(half // 2, width)] * 2 + [like(half, width)], [], 1,
        mixed, gate, norm_gain[None, :], *reached,
    )
    columns = w_out.shape[1]
    near = to_sibling(normed)
    far_lows = [to_chips(low) for low in lows]
    high, near = after(high, near)
    far_high = to_chips(high)
    total_low, total_high = vmem_call(
        near_kernel, [like(half, columns)] * 2, [], 2, normed, near, own_weight
    )
    far_lows, total_low = after(far_lows, total_low)
    far_lows_on = [[to_sibling(value) for value in values] for values in far_lows]
    arrived = [value for pair in zip(far_lows, far_lows_on) for values in pair for value in values]
    total_low = vmem_call(
        functools.partial(far_kernel, count, 2), like(half, columns), [], 0.01,
        *arrived, own_weight, total_low,
    )
    far_high, total_low = after(far_high, total_low)
    far_high_on = [to_sibling(value) for value in far_high]
    whole = like(tok_rows, columns)
    begun, total_high = vmem_call(
        functools.partial(flush_kernel, len(far_high), 2), [whole, like(half, columns)],
        [pltpu.SemaphoreType.DMA], 1,
        *far_high, own_weight, total_low, total_high, any_out=(0,),
    )
    args = [*far_high_on, own_weight, total_high, begun]
    last = len(args) - 1
    return vmem_call(
        functools.partial(last_kernel, len(far_high), 2 + len(far_high)), whole,
        [pltpu.VMEM((half, columns), F32), pltpu.SemaphoreType.DMA((half // CHUNK,))], 1,
        *args, any_in=(last,), any_out=True, aliases=((last, 0),),
    )


def solution(mesh):
    placed = (
        P("ctx", "head"),
        P(None, "head"),
        P(None, "head"),
        P(None, "head"),
        P("head"),
        P("ctx"),
        P("head"),
        P(None, "head"),
    )
    return jax.shard_map(
        shards, mesh=mesh, in_specs=placed, out_specs=P("ctx", "head"), check_vma=False
    )
```

```python
import functools

import jax
import jax.numpy as jnp
from jax import lax
from jax.experimental import pallas as pl
from jax.experimental.pallas import tpu as pltpu
from jax.sharding import PartitionSpec as P

CHUNK = 128
RIM = 16
VMEM_GRANT = 16 << 20
F32 = jnp.float32
BF16 = jnp.bfloat16


def halves(value):
    high = value.astype(BF16)
    return high, (value - high.astype(F32)).astype(BF16)


def left_parts(value):
    return jnp.concatenate(halves(value), axis=1)


def right_parts(value):
    row = jnp.concatenate(halves(value), axis=1)
    return jnp.concatenate([row, row], axis=0)


def parts_dot(left, right):
    both = jnp.dot(left, right, preferred_element_type=F32)
    half = both.shape[1] // 2
    return both[:, :half] + both[:, half:]


def product(left, right):
    return parts_dot(left_parts(left), right_parts(right))


def softplus(value):
    return jnp.maximum(value, 0.0) + jnp.log1p(jnp.exp(-jnp.abs(value)))


def sigmoid(value):
    return 1.0 / (1.0 + jnp.exp(-value))


def unit_lower_inverse(lowers, row, col):
    size = lowers[0].shape[0]
    eye = jnp.where(row == col, 1.0, 0.0).astype(F32)
    inverses = [eye - jnp.where((row >> 1) == (col >> 1), lower, 0.0) for lower in lowers]
    lower_parts = [halves(lower) for lower in lowers]
    step = 1
    while 1 << step < size:
        off = ((row >> (step + 2)) == (col >> (step + 2))) & ((row >> step) > (col >> step))
        offs = [
            jnp.concatenate([jnp.where(off, part, jnp.zeros_like(part)) for part in parts], axis=1)
            for parts in lower_parts
        ]
        onto = [parts_dot(left, right_parts(inverse)) for left, inverse in zip(offs, inverses)]
        rights = [right_parts(value) for value in onto]
        squares = [parts_dot(left_parts(value), right) for value, right in zip(onto, rights)]
        firsts = [
            inverse - parts_dot(left_parts(inverse), right)
            for inverse, right in zip(inverses, rights)
        ]
        inverses = [first + product(first, square) for first, square in zip(firsts, squares)]
        step += 2
    return inverses


def add_products(total, pieces, weight_ref, first):
    columns = weight_ref.shape[1] // 2
    for spot, piece in enumerate(pieces):
        depth = piece.shape[1]
        rows = slice((first + spot) * depth, (first + spot + 1) * depth)
        high, low = halves(piece)
        both = jnp.dot(high, weight_ref[rows, :], preferred_element_type=F32)
        rest = jnp.dot(low, weight_ref[rows, :columns], preferred_element_type=F32)
        part = (both[:, :columns] + both[:, columns:]) + rest
        total = part if total is None else total + part
    return total


def stage_kernel(spans, tokens_ref, *refs):
    outs, sems = refs[:-1], refs[-1]
    copies = [
        pltpu.make_async_copy(tokens_ref.at[rows, :], out, sems.at[spot])
        for spot, (rows, out) in enumerate(zip(spans, outs))
    ]
    for copy in copies:
        copy.start()
    for copy in copies:
        copy.wait()


def base_kernel(
    index_ref, own_ref, beside_ref, mix_ref, proj_ref,
    state_ref, query_ref, far_state_ref, far_query_ref, flag_ref,
    held, near_state, near_query, sems,
):
    sources, depth, across = held.shape
    width = across // 4
    copies = []
    for source in range(sources):
        rows = pl.ds(pl.multiple_of(index_ref[source] * depth, depth), depth)
        copies.append(pltpu.make_async_copy(proj_ref.at[rows, :], held.at[source], sems.at[source]))
        copies[-1].start()
    for bit in range(flag_ref.shape[0]):
        flag_ref[bit : bit + 1, :] = jnp.broadcast_to(index_ref[sources + bit], (1, CHUNK))
    mixes = mix_ref.shape[0]

    def split(source, state_out, query_out, base):
        copies[source].wait()
        lanes = pl.ds(pl.multiple_of(index_ref[source] * depth, depth), depth)
        for begin in range(0, depth, CHUNK):
            rows = slice(begin, begin + CHUNK)
            out = slice(base + begin, base + begin + CHUNK)
            value = held[source, rows, :]
            mixing = mix_ref[:, lanes][:, rows]
            mixing = jnp.concatenate([mixing, jnp.zeros((CHUNK - mixes, CHUNK), F32)], axis=0)
            state = jnp.concatenate([value[:, width : 3 * width], jnp.transpose(mixing)], axis=1)
            query = jnp.concatenate([value[:, :width], value[:, 3 * width :]], axis=1)
            state_out[out, :] = left_parts(state)
            query_out[out, :] = left_parts(query)

    for source in range(2):
        split(source, near_state, near_query, source * depth)
    half = own_ref.shape[0] // 2
    for rows in (slice(0, half), slice(half, 2 * half)):
        pieces = [own_ref[rows, :], beside_ref[rows, :]]
        state_ref[rows, :] = add_products(None, pieces, near_state, 0)
        query_ref[rows, :] = add_products(None, pieces, near_query, 0)
    for source in range(2, sources):
        split(source, far_state_ref, far_query_ref, (source - 2) * depth)


def late_kernel(count, segments, *refs):
    begin = segments[0].start
    held, refs = refs[: count * len(segments)], refs[count * len(segments) :]
    base_state, base_query, far_state, far_query, state_ref, query_ref, rim_ref = refs
    width = base_query.shape[1] // 2
    for turn, rows in enumerate(segments):
        pieces = [ref[...] for ref in held[turn * count : (turn + 1) * count]]
        out = slice(rows.start - begin, rows.stop - begin)
        state_ref[out, :] = add_products(base_state[rows, :], pieces, far_state, 0)
        query_ref[out, :] = add_products(base_query[rows, :], pieces, far_query, 0)
    last = state_ref.shape[0] - RIM
    rim_ref[:, :width] = query_ref[last:, :width]
    rim_ref[:, width:] = state_ref[last:, : 2 * width]


def partial_kernel(count, *refs):
    base_state, far_state, out_ref = refs[count:]
    out_ref[...] = add_products(
        base_state[: out_ref.shape[0], :], [ref[...] for ref in refs[:count]], far_state, 0
    )


def convolve(raw, start, columns, conv_ref, taps_at):
    taps = conv_ref.shape[0]
    conv = 0.0
    for tap in range(taps):
        spot = start - taps + 1 + tap
        conv = conv + conv_ref[tap : tap + 1, taps_at] * raw[spot : spot + CHUNK, columns]
    return conv * sigmoid(conv)


def unit_rows(value):
    return value * lax.rsqrt(jnp.sum(value * value, axis=1, keepdims=True) + 1e-06)


def key_pass(raw, conv_ref, rate, doc_ref, first_chunk, outs, state):
    key_ref, x_ref, y_ref, grid_ref, gamma_ref, plus_ref, chunk_ref, pair_ref = outs
    width = key_ref.shape[1]
    chunks = key_ref.shape[0] // CHUNK
    row = lax.broadcasted_iota(jnp.int32, (CHUNK, CHUNK), 0)
    col = lax.broadcasted_iota(jnp.int32, (CHUNK, CHUNK), 1)
    lower = row >= col
    tri = jnp.where(lower, 1.0, 0.0).astype(F32)
    eye = jnp.where(row == col, 1.0, 0.0).astype(F32)
    keys, values, betas, grids, gammas, tails = [], [], [], [], [], []
    for part in range(chunks):
        start = RIM + part * CHUNK
        rows = slice(part * CHUNK, (part + 1) * CHUNK)
        middle, last = slice(width, 2 * width), slice(2 * width, 3 * width)
        keys.append(unit_rows(convolve(raw, start, slice(0, width), conv_ref, middle)))
        values.append(convolve(raw, start, middle, conv_ref, last))
        mixing = raw[start : start + CHUNK, last]
        plus = softplus(mixing)
        plus_ref[rows, :] = plus
        betas.append(sigmoid(mixing[:, 0:1]))
        spot = first_chunk + part
        docs = jnp.broadcast_to(doc_ref[spot : spot + 1, :].astype(F32), (CHUNK, CHUNK))
        docs = jnp.transpose(docs)
        steps = jnp.where(col == 1, -rate * plus, jnp.where(col == 0, docs, 0.0))
        sums = jnp.dot(tri, steps, precision=lax.Precision.HIGHEST, preferred_element_type=F32)
        across = jnp.transpose(sums)
        smooth, count = sums[:, 1:2], sums[:, 0:1]
        span = (smooth - across[1:2, :]) - 20.0 * (count - across[0:1, :])
        grids.append(jnp.exp(jnp.where(lower, span, -1e30)))
        gammas.append(jnp.exp(smooth - 20.0 * count))
        last = sums[CHUNK - 1 : CHUNK, :]
        tails.append(jnp.exp((last[:, 1:2] - smooth) - 20.0 * (last[:, 0:1] - count)))
        key_ref[rows, :] = keys[part]
        grid_ref[rows, :] = grids[part]
        gamma_ref[rows, :] = jnp.broadcast_to(gammas[part], (CHUNK, width))
    across_keys = [jnp.transpose(key) for key in keys]
    grams = [
        parts_dot(left_parts(key), right_parts(across)) for key, across in zip(keys, across_keys)
    ]
    lowers = [jnp.where(row > col, beta * gram, 0.0) for beta, gram in zip(betas, grams)]
    inverses = unit_lower_inverse(lowers, row, col)
    states = []
    if state is not None:
        later_keys = product(state[0], across_keys[-1])
    for part in range(chunks):
        rows = slice(part * CHUNK, (part + 1) * CHUNK)
        inverse, beta = inverses[part], betas[part]
        factor_x = product(inverse, beta * keys[part])
        factor_y = product(grids[part] * inverse, beta * values[part])
        x_ref[rows, :] = factor_x
        y_ref[rows, :] = factor_y
        factors = jnp.concatenate([factor_x, tails[part] * factor_y], axis=1)
        onto = product(across_keys[part], factors)
        if state is not None and part == chunks - 1:
            behind = product(later_keys, factors)
        trans = gammas[part][CHUNK - 1 : CHUNK, :] * (eye - onto[:, :width])
        states.append((trans, onto[:, width:]))
        chunk_ref[part, 0] = trans
        chunk_ref[part, 1] = onto[:, width:]
    if state is not None:
        decay = gammas[-1][CHUNK - 1 : CHUNK, :]
        states[-1] = (decay * (state[0] - behind[:, :width]), behind[:, width:] + state[1])
    while len(states) > 1:
        joined = [followed(*states[at : at + 2]) for at in range(0, len(states) - 1, 2)]
        states = joined + states[2 * len(joined) :]
    pair_ref[0] = states[0][0]
    pair_ref[1] = states[0][1]


def followed(first, second):
    width = first[0].shape[0]
    onto = product(second[0], jnp.concatenate(first, axis=1))
    return onto[:, :width], onto[:, width:] + second[1]


def later_kernel(first_chunk, raw_ref, conv_ref, rate_ref, doc_ref, *outs):
    key_pass(raw_ref, conv_ref, rate_ref[0, 0], doc_ref, first_chunk, outs, None)


def earlier_kernel(first, count, *refs):
    held, refs = refs[:count], refs[count:]
    part_ref, far_ref, rim_ref, next_ref, state_ref, conv_ref, rate_ref, doc_ref = refs[:8]
    outs, raw = refs[8:-1], refs[-1]
    rows, width = part_ref.shape[0], state_ref.shape[1]
    raw[RIM : RIM + rows, :] = add_products(
        part_ref[...], [ref[...] for ref in held], far_ref, first
    )
    raw[:RIM, : 2 * width] = rim_ref[:, width:]
    raw[RIM + rows :, :] = next_ref[:RIM, :]
    key_pass(raw, conv_ref, rate_ref[0, 0], doc_ref, 0, outs, (state_ref[0], state_ref[1]))


def query_kernel(count, *refs):
    held, refs = refs[:count], refs[count:]
    base_ref, far_ref, rim_ref, next_ref, conv_ref = refs[:5]
    fields = [(refs[5:11], 0), (refs[11:17], 1)]
    carried_ref, local_ref, gate_ref, raw = refs[17:]
    width = carried_ref.shape[1]
    rows = held[0].shape[0]
    raw[RIM : RIM + rows, :] = add_products(
        base_ref[:rows, :], [ref[...] for ref in held], far_ref, 0
    )
    raw[:RIM, :width] = rim_ref[:, :width]
    raw[RIM + rows :, :] = next_ref[:RIM, :]
    row = lax.broadcasted_iota(jnp.int32, (CHUNK, CHUNK), 0)
    col = lax.broadcasted_iota(jnp.int32, (CHUNK, CHUNK), 1)
    state = None
    base = 0
    for (key_ref, x_ref, y_ref, grid_ref, gamma_ref, chunk_ref), later in fields:
        source = next_ref if later else raw
        for part in range(key_ref.shape[0] // CHUNK):
            start = RIM + part * CHUNK
            rows = slice(part * CHUNK, (part + 1) * CHUNK)
            out = slice(base, base + CHUNK)
            base += CHUNK
            columns = slice(0, width)
            query = unit_rows(convolve(source, start, columns, conv_ref, columns))
            gate = source[start : start + CHUNK, width:]
            gate_ref[out, :] = gate * sigmoid(gate)
            overlap = product(query, jnp.transpose(key_ref[rows, :]))
            carried = gamma_ref[rows, :] * (
                query - product(jnp.where(row >= col, overlap, 0.0), x_ref[rows, :])
            )
            local = product(grid_ref[rows, :] * overlap, y_ref[rows, :])
            trans, memory = chunk_ref[part, 0], chunk_ref[part, 1]
            if state is None:
                state = (trans, memory)
            else:
                onto = product(
                    jnp.concatenate([trans, carried], axis=0), jnp.concatenate(state, axis=1)
                )
                carried = onto[CHUNK:, :width]
                local = local + onto[CHUNK:, width:]
                state = (onto[:CHUNK, :width], onto[:CHUNK, width:] + memory)
            carried_ref[out, :] = carried
            local_ref[out, :] = local


def four_kernel(bit, carried, last, flag_ref, own_ref, one_ref, two_ref, three_ref, *refs):
    group_ref, level_ref, next_ref = refs[-3:]
    width = next_ref.shape[0]
    flag = lambda at: jnp.broadcast_to(flag_ref[at : at + 1, :], (width, width)) == 1
    set_low, set_high = flag(bit), flag(bit + 1)
    held = (own_ref, one_ref, two_ref, three_ref)

    def placed(part):
        by_low = [jnp.where(set_low, held[at ^ 1][part], held[at][part]) for at in range(4)]
        return [jnp.where(set_high, by_low[at ^ 2], by_low[at]) for at in range(4)]

    trans, memory = placed(0), placed(1)
    joined = lambda at: jnp.concatenate([trans[at], memory[at]], axis=1)
    onto_low = product(trans[1], joined(0))
    onto_high = product(trans[3], joined(2))
    low_a, low_s = onto_low[:, :width], onto_low[:, width:] + memory[1]
    high_a, high_s = onto_high[:, :width], onto_high[:, width:] + memory[3]
    if last:
        group_ref[...] = product(high_a, low_s) + high_s
    else:
        onto = product(high_a, jnp.concatenate([low_a, low_s], axis=1))
        group_ref[0] = onto[:, :width]
        group_ref[1] = onto[:, width:] + high_s
    if carried:
        carry = refs[0][...]
        first = product(carry, jnp.concatenate([one_ref[0], one_ref[1]], axis=1))
        first_a, first_s = first[:, :width], first[:, width:]
    else:
        row = lax.broadcasted_iota(jnp.int32, (width, width), 0)
        col = lax.broadcasted_iota(jnp.int32, (width, width), 1)
        carry = jnp.where(row == col, 1.0, 0.0).astype(F32)
        first_a, first_s = one_ref[0], one_ref[1]
    level_ref[0] = jnp.where(set_low, first_s, 0.0)
    carry = jnp.where(set_low, first_a, carry)
    second = product(carry, jnp.concatenate([low_a, low_s], axis=1))
    level_ref[1] = jnp.where(set_high, second[:, width:], 0.0)
    carry = jnp.where(set_high, second[:, :width], carry)
    next_ref[...] = jnp.where(flag(bit + 2), carry, 0.0) if last else carry


def level_kernel(stages, single, carried_ref, local_ref, low_ref, high_ref, *refs):
    states = [ref[spot] for ref in refs[:stages] for spot in range(ref.shape[0])]
    carried = left_parts(carried_ref[...])
    weights = jnp.concatenate([low_ref[...], high_ref[...]], axis=0)
    mixed = weights[:, 2:3] * local_ref[...]
    for level, state in enumerate(states):
        mixed = mixed + weights[:, level + 3 : level + 4] * parts_dot(carried, right_parts(state))
    if single:
        carry_ref, mixed_ref, reach_ref = refs[stages:]
        level = len(states) + 3
        reach_ref[...] = weights[:, level : level + 1] * parts_dot(
            carried, right_parts(carry_ref[...])
        )
    else:
        (mixed_ref,) = refs[stages:]
    mixed_ref[...] = mixed


def mix_kernel(single, mixed_ref, gate_ref, gain_ref, *refs):
    mixed = mixed_ref[...]
    if single:
        mixed = mixed + product(refs[0][...], refs[1][...])
    outs = refs[2 if single else 0 :]
    scale = lax.rsqrt(jnp.mean(mixed * mixed, axis=1, keepdims=True) + 1e-05)
    normed = mixed * scale * gain_ref[...] * gate_ref[...]
    outs[0][...] = normed
    base = 0
    for out in outs[1:]:
        out[...] = normed[base : base + out.shape[0]]
        base += out.shape[0]


def block_product(pieces, weight, rows):
    parts = [halves(ref[rows, :]) for ref in pieces]
    high, low = (jnp.concatenate(part, axis=1) for part in zip(*parts))
    columns = weight.shape[1] // 2
    both = jnp.dot(high, weight, preferred_element_type=F32)
    rest = jnp.dot(low, weight[:, :columns], preferred_element_type=F32)
    return (both[:, :columns] + both[:, columns:]) + rest


def order_kernel(sources, index_ref, weight_ref, out_ref):
    depth = weight_ref.shape[0] // sources
    for source in range(sources):
        rows = pl.ds(pl.multiple_of(index_ref[source] * depth, depth), depth)
        out_ref[source * depth : (source + 1) * depth, :] = left_parts(weight_ref[rows, :])


def source_rows(first, pieces, weight_ref):
    depth = pieces[0].shape[1]
    return weight_ref[first * depth : (first + len(pieces)) * depth, :]


def row_blocks(rows):
    return [slice(base, base + CHUNK) for base in range(0, rows, CHUNK)]


def near_kernel(own_ref, near_ref, weight_ref, low_ref, high_ref):
    weight = source_rows(0, [own_ref, near_ref], weight_ref)
    half = low_ref.shape[0]
    for rows in row_blocks(half):
        low_ref[rows, :] = block_product([own_ref, near_ref], weight, rows)
        later = slice(half + rows.start, half + rows.stop)
        high_ref[rows, :] = block_product([own_ref, near_ref], weight, later)


def far_kernel(count, first, *refs):
    held, (weight_ref, total_ref, out_ref) = refs[:-3], refs[-3:]
    weight = source_rows(first, held[:count], weight_ref)
    base = 0
    for at in range(0, len(held), count):
        pieces = held[at : at + count]
        for rows in row_blocks(pieces[0].shape[0]):
            out = slice(base + rows.start, base + rows.stop)
            out_ref[out, :] = total_ref[out, :] + block_product(pieces, weight, rows)
        base += pieces[0].shape[0]


def flush_kernel(count, first, *refs):
    pieces = refs[:count]
    weight_ref, ready_ref, total_ref, out_ref, next_ref, sem = refs[count:]
    half = ready_ref.shape[0]
    copy = pltpu.make_async_copy(ready_ref, out_ref.at[:half, :], sem)
    copy.start()
    weight = source_rows(first, pieces, weight_ref)
    for rows in row_blocks(half):
        next_ref[rows, :] = total_ref[rows, :] + block_product(pieces, weight, rows)
    copy.wait()


def last_kernel(count, first, *refs):
    pieces = refs[:count]
    weight_ref, total_ref, begun_ref, out_ref, held, sems = refs[count:]
    half = total_ref.shape[0]
    copies = []
    weight = source_rows(first, pieces, weight_ref)
    for spot, rows in enumerate(row_blocks(half)):
        held[rows, :] = total_ref[rows, :] + block_product(pieces, weight, rows)
        out = slice(half + rows.start, half + rows.stop)
        copies.append(
            pltpu.make_async_copy(held.at[rows, :], out_ref.at[out, :], sems.at[spot])
        )
        copies[-1].start()
    for copy in copies:
        copy.wait()


def vmem_call(kernel, outs, scratch, cost, *args, any_in=(), any_out=(), aliases=()):
    spec = pl.BlockSpec(memory_space=pltpu.VMEM)
    small = pl.BlockSpec(memory_space=pltpu.SMEM)
    free = pl.BlockSpec(memory_space=pl.ANY)
    return pl.pallas_call(
        kernel,
        out_shape=outs,
        in_specs=[
            free if spot in any_in else small if arg.dtype == jnp.int32 and arg.ndim == 1 else spec
            for spot, arg in enumerate(args)
        ],
        out_specs=[free if spot in any_out else spec for spot in range(len(outs))]
        if isinstance(outs, list)
        else (free if any_out else spec),
        input_output_aliases=dict(aliases),
        scratch_shapes=scratch,
        compiler_params=pltpu.CompilerParams(vmem_limit_bytes=VMEM_GRANT),
        cost_estimate=pl.CostEstimate(flops=int(cost * 1e9), bytes_accessed=1 << 20, transcendentals=0),
    )(*args)


def to_sibling(value):
    count = lax.axis_size("head")
    return lax.ppermute(value, "head", [(source, source ^ 1) for source in range(count)])


def to_chips(value):
    count = lax.axis_size("head")
    return [
        lax.ppermute(
            value, "head", [(source, (source + 2 * step) % count) for source in range(count)]
        )
        for step in range(1, count // 2)
    ]


def after(value, *earlier):
    return lax.optimization_barrier((value, *earlier))


def shards(tokens, w_proj, w_mix, conv_w, rates, doc_start, norm_gain, w_out):
    tok_rows, depth = tokens.shape
    width = w_proj.shape[1] // 4
    state_columns, query_columns = 2 * width + CHUNK, 2 * width
    heads, me = lax.axis_size("head"), lax.axis_index("head")
    blocks, my_index = lax.axis_size("ctx"), lax.axis_index("ctx")
    remote = [(me + heads - 2 * step) % heads for step in range(1, heads // 2)]
    order = [me, me ^ 1] + remote + [index ^ 1 for index in remote]
    bits = blocks.bit_length() - 1
    index = jnp.stack(order + [my_index >> bit & 1 for bit in range(bits)]).astype(jnp.int32)
    count = heads - 2
    like = lambda *shape: jax.ShapeDtypeStruct(shape, F32)
    parts = lambda *shape: jax.ShapeDtypeStruct(shape, BF16)

    first = tok_rows // 2
    cut = first - RIM
    middle = tok_rows - CHUNK - RIM
    segments = (slice(cut, middle), slice(middle, tok_rows))
    spans = (segments[1], segments[0], slice(0, cut), slice(0, tok_rows))
    tokens, index = after(tokens, index)
    last_rows, next_rows, early_rows, own = vmem_call(
        functools.partial(stage_kernel, spans),
        [like(rows.stop - rows.start, depth) for rows in spans],
        [pltpu.SemaphoreType.DMA((len(spans),))], 1, tokens, any_in=(0,),
    )
    late = [to_chips(next_rows), to_chips(last_rows)]
    beside = to_sibling(own)
    early_rows, beside = after(early_rows, beside)
    early = to_chips(early_rows)
    base_state, base_query, far_state, far_query, flags = vmem_call(
        base_kernel,
        [like(tok_rows, state_columns), like(tok_rows, query_columns),
         parts(count * depth, 2 * state_columns), parts(count * depth, 2 * query_columns),
         jax.ShapeDtypeStruct((bits, CHUNK), jnp.int32)],
        [pltpu.VMEM((heads, depth, 4 * width), F32),
         pltpu.VMEM((2 * depth, 2 * state_columns), BF16),
         pltpu.VMEM((2 * depth, 2 * query_columns), BF16),
         pltpu.SemaphoreType.DMA((heads,))],
        3, index, own, beside, w_mix.T, w_proj, any_in=(4,),
    )
    late, far_state = after(late, far_state)
    late_on = [[to_sibling(value) for value in values] for values in late]
    arrived = [value for pair in zip(late, late_on) for values in pair for value in values]
    late_state, late_query, rim = vmem_call(
        functools.partial(late_kernel, count, segments),
        [like(tok_rows - cut, state_columns), like(tok_rows - cut, query_columns),
         like(RIM, 3 * width)],
        [], 0.5, *arrived, base_state, base_query, far_state, far_query,
    )
    rim = lax.ppermute(rim, "ctx", [(source, source + 1) for source in range(blocks - 1)])
    docs = doc_start.reshape(tok_rows // CHUNK, CHUNK)
    rate = rates[:, None]

    def outs(rows):
        chunks = like(rows // CHUNK, 2, width, width)
        return [like(rows, width)] * 6 + [chunks, like(2, width, width)]

    later = vmem_call(
        functools.partial(later_kernel, first // CHUNK), outs(tok_rows - first), [], 0.5,
        late_state, conv_w, rate, docs,
    )
    early, pair_late, rim = after(early, later[7], rim)
    early_on = [to_sibling(value) for value in early]
    partial = vmem_call(
        functools.partial(partial_kernel, len(early)), like(cut, state_columns), [], 1,
        *early, base_state, far_state,
    )
    earlier = vmem_call(
        functools.partial(earlier_kernel, len(early), len(early)), outs(first),
        [pltpu.VMEM((first + RIM, state_columns), F32)], 5,
        *early_on, partial, far_state, rim, late_state, pair_late, conv_w, rate, docs,
    )

    pair = earlier[7]
    fields = vmem_call(
        functools.partial(query_kernel, count), [like(tok_rows, width)] * 3,
        [pltpu.VMEM((first + RIM, query_columns), F32)], 5,
        *early, *early_on, base_query, far_query, rim, late_query, conv_w,
        *earlier[:5], earlier[6], *later[:5], later[6],
    )
    own_weight = vmem_call(
        functools.partial(order_kernel, heads), parts(w_out.shape[0], 2 * w_out.shape[1]), [], 1,
        index, w_out,
    )
    carry = ()
    levels = []
    for bit in range(0, bits - 1, 2):
        others = [
            lax.ppermute(
                pair, "ctx", [(source, source ^ (mask << bit)) for source in range(blocks)]
            )
            for mask in (1, 2, 3)
        ]
        if not bit:
            others[0], *fields, own_weight = after(others[0], *fields, own_weight)
        last = bit + 2 >= bits - 1 and bits % 2
        group = [like(width, width)] if last else [like(2, width, width)]
        pair, level, *carry = vmem_call(
            functools.partial(four_kernel, bit, bool(carry), last),
            group + [like(2, width, width), like(width, width)], [], 1,
            flags, pair, *others, *carry,
        )
        levels.append(level)
    carried, local, gate = fields
    lone = bool(bits % 2)
    reach = blocks // 2
    if lone:
        other = lax.ppermute(
            pair if carry else pair[1],
            "ctx", [(source, source ^ reach) for source in range(blocks)],
        )
        if not carry:
            carry = [jnp.where(my_index >= reach, jnp.eye(width, dtype=F32), 0.0)]
    rows_shape = like(tok_rows, width)
    mixed, *reached = vmem_call(
        functools.partial(level_kernel, len(levels), lone), [rows_shape] * (2 if lone else 1), [], 1,
        carried, local, earlier[5], later[5], *levels, *(carry if lone else ()),
    )
    if lone:
        reached.append(other)
    half = tok_rows // 2
    normed, *lows, high = vmem_call(
        functools.partial(mix_kernel, lone),
        [rows_shape] + [like(half // 2, width)] * 2 + [like(half, width)], [], 1,
        mixed, gate, norm_gain[None, :], *reached,
    )
    columns = w_out.shape[1]
    near = to_sibling(normed)
    far_lows = [to_chips(low) for low in lows]
    high, near = after(high, near)
    far_high = to_chips(high)
    total_low, total_high = vmem_call(
        near_kernel, [like(half, columns)] * 2, [], 2, normed, near, own_weight
    )
    far_lows, total_low = after(far_lows, total_low)
    far_lows_on = [[to_sibling(value) for value in values] for values in far_lows]
    arrived = [value for pair in zip(far_lows, far_lows_on) for values in pair for value in values]
    total_low = vmem_call(
        functools.partial(far_kernel, count, 2), like(half, columns), [], 0.01,
        *arrived, own_weight, total_low,
    )
    far_high, total_low = after(far_high, total_low)
    far_high_on = [to_sibling(value) for value in far_high]
    whole = like(tok_rows, columns)
    begun, total_high = vmem_call(
        functools.partial(flush_kernel, len(far_high), 2), [whole, like(half, columns)],
        [pltpu.SemaphoreType.DMA], 1,
        *far_high, own_weight, total_low, total_high, any_out=(0,),
    )
    args = [*far_high_on, own_weight, total_high, begun]
    last = len(args) - 1
    return vmem_call(
        functools.partial(last_kernel, len(far_high), 2 + len(far_high)), whole,
        [pltpu.VMEM((half, columns), F32), pltpu.SemaphoreType.DMA((half // CHUNK,))], 1,
        *args, any_in=(last,), any_out=True, aliases=((last, 0),),
    )


def solution(mesh):
    placed = (
        P("ctx", "head"),
        P(None, "head"),
        P(None, "head"),
        P(None, "head"),
        P("head"),
        P("ctx"),
        P("head"),
        P(None, "head"),
    )
    return jax.shard_map(
        shards, mesh=mesh, in_specs=placed, out_specs=P("ctx", "head"), check_vma=False
    )
```

```python
import functools

import jax
import jax.numpy as jnp
from jax import lax
from jax.experimental import pallas as pl
from jax.experimental.pallas import tpu as pltpu
from jax.sharding import PartitionSpec as P

CHUNK = 128
RIM = 16
VMEM_GRANT = 16 << 20
STAGE_GRANT = 61 << 20
F32 = jnp.float32
BF16 = jnp.bfloat16


def halves(value):
    high = value.astype(BF16)
    return high, (value - high.astype(F32)).astype(BF16)


def left_parts(value):
    return jnp.concatenate(halves(value), axis=1)


def right_parts(value):
    row = jnp.concatenate(halves(value), axis=1)
    return jnp.concatenate([row, row], axis=0)


def parts_dot(left, right):
    both = jnp.dot(left, right, preferred_element_type=F32)
    half = both.shape[1] // 2
    return both[:, :half] + both[:, half:]


def product(left, right):
    return parts_dot(left_parts(left), right_parts(right))


def softplus(value):
    return jnp.maximum(value, 0.0) + jnp.log1p(jnp.exp(-jnp.abs(value)))


def sigmoid(value):
    return 1.0 / (1.0 + jnp.exp(-value))


def unit_lower_inverse(lowers, row, col):
    size = lowers[0].shape[0]
    eye = jnp.where(row == col, 1.0, 0.0).astype(F32)
    inverses = [eye - jnp.where((row >> 1) == (col >> 1), lower, 0.0) for lower in lowers]
    lower_parts = [halves(lower) for lower in lowers]
    step = 1
    while 1 << step < size:
        off = ((row >> (step + 2)) == (col >> (step + 2))) & ((row >> step) > (col >> step))
        offs = [
            jnp.concatenate([jnp.where(off, part, jnp.zeros_like(part)) for part in parts], axis=1)
            for parts in lower_parts
        ]
        onto = [parts_dot(left, right_parts(inverse)) for left, inverse in zip(offs, inverses)]
        rights = [right_parts(value) for value in onto]
        squares = [parts_dot(left_parts(value), right) for value, right in zip(onto, rights)]
        firsts = [
            inverse - parts_dot(left_parts(inverse), right)
            for inverse, right in zip(inverses, rights)
        ]
        inverses = [first + product(first, square) for first, square in zip(firsts, squares)]
        step += 2
    return inverses


def add_products(total, pieces, weight_ref, first):
    columns = weight_ref.shape[1] // 2
    for spot, piece in enumerate(pieces):
        depth = piece.shape[1]
        rows = slice((first + spot) * depth, (first + spot + 1) * depth)
        high, low = halves(piece)
        both = jnp.dot(high, weight_ref[rows, :], preferred_element_type=F32)
        rest = jnp.dot(low, weight_ref[rows, :columns], preferred_element_type=F32)
        part = (both[:, :columns] + both[:, columns:]) + rest
        total = part if total is None else total + part
    return total


def stage_kernel(spans, tokens_ref, *refs):
    outs, sems = refs[:-1], refs[-1]
    copies = [
        pltpu.make_async_copy(tokens_ref.at[rows, :], out, sems.at[spot])
        for spot, (rows, out) in enumerate(zip(spans, outs))
    ]
    for copy in copies:
        copy.start()
    for copy in copies:
        copy.wait()


def base_kernel(
    index_ref, own_ref, beside_ref, mix_ref, proj_ref,
    state_ref, query_ref, far_state_ref, far_query_ref, flag_ref,
    held, near_state, near_query, sems,
):
    sources, depth, across = held.shape
    width = across // 4
    copies = []
    for source in range(sources):
        rows = pl.ds(pl.multiple_of(index_ref[source] * depth, depth), depth)
        copies.append(pltpu.make_async_copy(proj_ref.at[rows, :], held.at[source], sems.at[source]))
        copies[-1].start()
    for bit in range(flag_ref.shape[0]):
        flag_ref[bit : bit + 1, :] = jnp.broadcast_to(index_ref[sources + bit], (1, CHUNK))
    mixes = mix_ref.shape[0]

    def split(source, state_out, query_out, base):
        copies[source].wait()
        lanes = pl.ds(pl.multiple_of(index_ref[source] * depth, depth), depth)
        for begin in range(0, depth, CHUNK):
            rows = slice(begin, begin + CHUNK)
            out = slice(base + begin, base + begin + CHUNK)
            value = held[source, rows, :]
            mixing = mix_ref[:, lanes][:, rows]
            mixing = jnp.concatenate([mixing, jnp.zeros((CHUNK - mixes, CHUNK), F32)], axis=0)
            state = jnp.concatenate([value[:, width : 3 * width], jnp.transpose(mixing)], axis=1)
            query = jnp.concatenate([value[:, :width], value[:, 3 * width :]], axis=1)
            state_out[out, :] = left_parts(state)
            query_out[out, :] = left_parts(query)

    for source in range(2):
        split(source, near_state, near_query, source * depth)
    half = own_ref.shape[0] // 2
    for rows in (slice(0, half), slice(half, 2 * half)):
        pieces = [own_ref[rows, :], beside_ref[rows, :]]
        state_ref[rows, :] = add_products(None, pieces, near_state, 0)
        query_ref[rows, :] = add_products(None, pieces, near_query, 0)
    for source in range(2, sources):
        split(source, far_state_ref, far_query_ref, (source - 2) * depth)


def late_kernel(count, segments, *refs):
    begin = segments[0].start
    held, refs = refs[: count * len(segments)], refs[count * len(segments) :]
    base_state, base_query, far_state, far_query, state_ref, query_ref, rim_ref = refs
    width = base_query.shape[1] // 2
    for turn, rows in enumerate(segments):
        pieces = [ref[...] for ref in held[turn * count : (turn + 1) * count]]
        out = slice(rows.start - begin, rows.stop - begin)
        state_ref[out, :] = add_products(base_state[rows, :], pieces, far_state, 0)
        query_ref[out, :] = add_products(base_query[rows, :], pieces, far_query, 0)
    last = state_ref.shape[0] - RIM
    rim_ref[:, :width] = query_ref[last:, :width]
    rim_ref[:, width:] = state_ref[last:, : 2 * width]


def partial_kernel(count, *refs):
    base_state, far_state, out_ref = refs[count:]
    out_ref[...] = add_products(
        base_state[: out_ref.shape[0], :], [ref[...] for ref in refs[:count]], far_state, 0
    )


def convolve(raw, start, columns, conv_ref, taps_at):
    taps = conv_ref.shape[0]
    conv = 0.0
    for tap in range(taps):
        spot = start - taps + 1 + tap
        conv = conv + conv_ref[tap : tap + 1, taps_at] * raw[spot : spot + CHUNK, columns]
    return conv * sigmoid(conv)


def unit_rows(value):
    return value * lax.rsqrt(jnp.sum(value * value, axis=1, keepdims=True) + 1e-06)


def key_pass(raw, conv_ref, rate, doc_ref, first_chunk, outs, state):
    key_ref, x_ref, y_ref, grid_ref, gamma_ref, plus_ref, chunk_ref, pair_ref = outs
    width = key_ref.shape[1]
    chunks = key_ref.shape[0] // CHUNK
    row = lax.broadcasted_iota(jnp.int32, (CHUNK, CHUNK), 0)
    col = lax.broadcasted_iota(jnp.int32, (CHUNK, CHUNK), 1)
    lower = row >= col
    tri = jnp.where(lower, 1.0, 0.0).astype(F32)
    eye = jnp.where(row == col, 1.0, 0.0).astype(F32)
    keys, values, betas, grids, gammas, tails = [], [], [], [], [], []
    for part in range(chunks):
        start = RIM + part * CHUNK
        rows = slice(part * CHUNK, (part + 1) * CHUNK)
        middle, last = slice(width, 2 * width), slice(2 * width, 3 * width)
        keys.append(unit_rows(convolve(raw, start, slice(0, width), conv_ref, middle)))
        values.append(convolve(raw, start, middle, conv_ref, last))
        mixing = raw[start : start + CHUNK, last]
        plus = softplus(mixing)
        plus_ref[rows, :] = plus
        betas.append(sigmoid(mixing[:, 0:1]))
        spot = first_chunk + part
        docs = jnp.broadcast_to(doc_ref[spot : spot + 1, :].astype(F32), (CHUNK, CHUNK))
        docs = jnp.transpose(docs)
        steps = jnp.where(col == 1, -rate * plus, jnp.where(col == 0, docs, 0.0))
        sums = jnp.dot(tri, steps, precision=lax.Precision.HIGHEST, preferred_element_type=F32)
        across = jnp.transpose(sums)
        smooth, count = sums[:, 1:2], sums[:, 0:1]
        span = (smooth - across[1:2, :]) - 20.0 * (count - across[0:1, :])
        grids.append(jnp.exp(jnp.where(lower, span, -1e30)))
        gammas.append(jnp.exp(smooth - 20.0 * count))
        last = sums[CHUNK - 1 : CHUNK, :]
        tails.append(jnp.exp((last[:, 1:2] - smooth) - 20.0 * (last[:, 0:1] - count)))
        key_ref[rows, :] = keys[part]
        grid_ref[rows, :] = grids[part]
        gamma_ref[rows, :] = jnp.broadcast_to(gammas[part], (CHUNK, width))
    across_keys = [jnp.transpose(key) for key in keys]
    grams = [
        parts_dot(left_parts(key), right_parts(across)) for key, across in zip(keys, across_keys)
    ]
    lowers = [jnp.where(row > col, beta * gram, 0.0) for beta, gram in zip(betas, grams)]
    inverses = unit_lower_inverse(lowers, row, col)
    states = []
    if state is not None:
        later_keys = product(state[0], across_keys[-1])
    for part in range(chunks):
        rows = slice(part * CHUNK, (part + 1) * CHUNK)
        inverse, beta = inverses[part], betas[part]
        factor_x = product(inverse, beta * keys[part])
        factor_y = product(grids[part] * inverse, beta * values[part])
        x_ref[rows, :] = factor_x
        y_ref[rows, :] = factor_y
        factors = jnp.concatenate([factor_x, tails[part] * factor_y], axis=1)
        onto = product(across_keys[part], factors)
        if state is not None and part == chunks - 1:
            behind = product(later_keys, factors)
        trans = gammas[part][CHUNK - 1 : CHUNK, :] * (eye - onto[:, :width])
        states.append((trans, onto[:, width:]))
        chunk_ref[part, 0] = trans
        chunk_ref[part, 1] = onto[:, width:]
    if state is not None:
        decay = gammas[-1][CHUNK - 1 : CHUNK, :]
        states[-1] = (decay * (state[0] - behind[:, :width]), behind[:, width:] + state[1])
    while len(states) > 1:
        joined = [followed(*states[at : at + 2]) for at in range(0, len(states) - 1, 2)]
        states = joined + states[2 * len(joined) :]
    pair_ref[0] = states[0][0]
    pair_ref[1] = states[0][1]


def followed(first, second):
    width = first[0].shape[0]
    onto = product(second[0], jnp.concatenate(first, axis=1))
    return onto[:, :width], onto[:, width:] + second[1]


def later_kernel(first_chunk, raw_ref, conv_ref, rate_ref, doc_ref, *outs):
    key_pass(raw_ref, conv_ref, rate_ref[0, 0], doc_ref, first_chunk, outs, None)


def earlier_kernel(first, count, *refs):
    held, refs = refs[:count], refs[count:]
    part_ref, far_ref, rim_ref, next_ref, state_ref, conv_ref, rate_ref, doc_ref = refs[:8]
    outs, raw = refs[8:-1], refs[-1]
    rows, width = part_ref.shape[0], state_ref.shape[1]
    raw[RIM : RIM + rows, :] = add_products(
        part_ref[...], [ref[...] for ref in held], far_ref, first
    )
    raw[:RIM, : 2 * width] = rim_ref[:, width:]
    raw[RIM + rows :, :] = next_ref[:RIM, :]
    key_pass(raw, conv_ref, rate_ref[0, 0], doc_ref, 0, outs, (state_ref[0], state_ref[1]))


def query_kernel(count, *refs):
    held, refs = refs[:count], refs[count:]
    base_ref, far_ref, rim_ref, next_ref, conv_ref = refs[:5]
    fields = [(refs[5:11], 0), (refs[11:17], 1)]
    carried_ref, local_ref, gate_ref, raw = refs[17:]
    width = carried_ref.shape[1]
    rows = held[0].shape[0]
    raw[RIM : RIM + rows, :] = add_products(
        base_ref[:rows, :], [ref[...] for ref in held], far_ref, 0
    )
    raw[:RIM, :width] = rim_ref[:, :width]
    raw[RIM + rows :, :] = next_ref[:RIM, :]
    row = lax.broadcasted_iota(jnp.int32, (CHUNK, CHUNK), 0)
    col = lax.broadcasted_iota(jnp.int32, (CHUNK, CHUNK), 1)
    state = None
    base = 0
    for (key_ref, x_ref, y_ref, grid_ref, gamma_ref, chunk_ref), later in fields:
        source = next_ref if later else raw
        for part in range(key_ref.shape[0] // CHUNK):
            start = RIM + part * CHUNK
            rows = slice(part * CHUNK, (part + 1) * CHUNK)
            out = slice(base, base + CHUNK)
            base += CHUNK
            columns = slice(0, width)
            query = unit_rows(convolve(source, start, columns, conv_ref, columns))
            gate = source[start : start + CHUNK, width:]
            gate_ref[out, :] = gate * sigmoid(gate)
            overlap = product(query, jnp.transpose(key_ref[rows, :]))
            carried = gamma_ref[rows, :] * (
                query - product(jnp.where(row >= col, overlap, 0.0), x_ref[rows, :])
            )
            local = product(grid_ref[rows, :] * overlap, y_ref[rows, :])
            trans, memory = chunk_ref[part, 0], chunk_ref[part, 1]
            if state is None:
                state = (trans, memory)
            else:
                onto = product(
                    jnp.concatenate([trans, carried], axis=0), jnp.concatenate(state, axis=1)
                )
                carried = onto[CHUNK:, :width]
                local = local + onto[CHUNK:, width:]
                state = (onto[:CHUNK, :width], onto[:CHUNK, width:] + memory)
            carried_ref[out, :] = carried
            local_ref[out, :] = local


def four_kernel(bit, carried, last, flag_ref, own_ref, one_ref, two_ref, three_ref, *refs):
    group_ref, level_ref, next_ref = refs[-3:]
    width = next_ref.shape[0]
    flag = lambda at: jnp.broadcast_to(flag_ref[at : at + 1, :], (width, width)) == 1
    set_low, set_high = flag(bit), flag(bit + 1)
    held = (own_ref, one_ref, two_ref, three_ref)

    def placed(part):
        by_low = [jnp.where(set_low, held[at ^ 1][part], held[at][part]) for at in range(4)]
        return [jnp.where(set_high, by_low[at ^ 2], by_low[at]) for at in range(4)]

    trans, memory = placed(0), placed(1)
    joined = lambda at: jnp.concatenate([trans[at], memory[at]], axis=1)
    onto_low = product(trans[1], joined(0))
    onto_high = product(trans[3], joined(2))
    low_a, low_s = onto_low[:, :width], onto_low[:, width:] + memory[1]
    high_a, high_s = onto_high[:, :width], onto_high[:, width:] + memory[3]
    if last:
        group_ref[...] = product(high_a, low_s) + high_s
    else:
        onto = product(high_a, jnp.concatenate([low_a, low_s], axis=1))
        group_ref[0] = onto[:, :width]
        group_ref[1] = onto[:, width:] + high_s
    if carried:
        carry = refs[0][...]
        first = product(carry, jnp.concatenate([one_ref[0], one_ref[1]], axis=1))
        first_a, first_s = first[:, :width], first[:, width:]
    else:
        row = lax.broadcasted_iota(jnp.int32, (width, width), 0)
        col = lax.broadcasted_iota(jnp.int32, (width, width), 1)
        carry = jnp.where(row == col, 1.0, 0.0).astype(F32)
        first_a, first_s = one_ref[0], one_ref[1]
    level_ref[0] = jnp.where(set_low, first_s, 0.0)
    carry = jnp.where(set_low, first_a, carry)
    second = product(carry, jnp.concatenate([low_a, low_s], axis=1))
    level_ref[1] = jnp.where(set_high, second[:, width:], 0.0)
    carry = jnp.where(set_high, second[:, :width], carry)
    next_ref[...] = jnp.where(flag(bit + 2), carry, 0.0) if last else carry


def level_kernel(stages, single, carried_ref, local_ref, low_ref, high_ref, *refs):
    states = [ref[spot] for ref in refs[:stages] for spot in range(ref.shape[0])]
    carried = left_parts(carried_ref[...])
    weights = jnp.concatenate([low_ref[...], high_ref[...]], axis=0)
    mixed = weights[:, 2:3] * local_ref[...]
    for level, state in enumerate(states):
        mixed = mixed + weights[:, level + 3 : level + 4] * parts_dot(carried, right_parts(state))
    if single:
        carry_ref, mixed_ref, reach_ref = refs[stages:]
        level = len(states) + 3
        reach_ref[...] = weights[:, level : level + 1] * parts_dot(
            carried, right_parts(carry_ref[...])
        )
    else:
        (mixed_ref,) = refs[stages:]
    mixed_ref[...] = mixed


def mix_kernel(single, mixed_ref, gate_ref, gain_ref, *refs):
    mixed = mixed_ref[...]
    if single:
        mixed = mixed + product(refs[0][...], refs[1][...])
    outs = refs[2 if single else 0 :]
    scale = lax.rsqrt(jnp.mean(mixed * mixed, axis=1, keepdims=True) + 1e-05)
    normed = mixed * scale * gain_ref[...] * gate_ref[...]
    outs[0][...] = normed
    base = 0
    for out in outs[1:]:
        out[...] = normed[base : base + out.shape[0]]
        base += out.shape[0]


def block_product(pieces, weight, rows):
    parts = [halves(ref[rows, :]) for ref in pieces]
    high, low = (jnp.concatenate(part, axis=1) for part in zip(*parts))
    columns = weight.shape[1] // 2
    both = jnp.dot(high, weight, preferred_element_type=F32)
    rest = jnp.dot(low, weight[:, :columns], preferred_element_type=F32)
    return (both[:, :columns] + both[:, columns:]) + rest


def order_kernel(sources, index_ref, weight_ref, out_ref):
    depth = weight_ref.shape[0] // sources
    for source in range(sources):
        rows = pl.ds(pl.multiple_of(index_ref[source] * depth, depth), depth)
        out_ref[source * depth : (source + 1) * depth, :] = left_parts(weight_ref[rows, :])


def source_rows(first, pieces, weight_ref):
    depth = pieces[0].shape[1]
    return weight_ref[first * depth : (first + len(pieces)) * depth, :]


def row_blocks(rows):
    return [slice(base, base + CHUNK) for base in range(0, rows, CHUNK)]


def near_kernel(own_ref, near_ref, weight_ref, low_ref, high_ref):
    weight = source_rows(0, [own_ref, near_ref], weight_ref)
    half = low_ref.shape[0]
    for rows in row_blocks(half):
        low_ref[rows, :] = block_product([own_ref, near_ref], weight, rows)
        later = slice(half + rows.start, half + rows.stop)
        high_ref[rows, :] = block_product([own_ref, near_ref], weight, later)


def far_kernel(count, first, *refs):
    held, (weight_ref, total_ref, out_ref) = refs[:-3], refs[-3:]
    weight = source_rows(first, held[:count], weight_ref)
    base = 0
    for at in range(0, len(held), count):
        pieces = held[at : at + count]
        for rows in row_blocks(pieces[0].shape[0]):
            out = slice(base + rows.start, base + rows.stop)
            out_ref[out, :] = total_ref[out, :] + block_product(pieces, weight, rows)
        base += pieces[0].shape[0]


def flush_kernel(count, first, *refs):
    pieces = refs[:count]
    weight_ref, ready_ref, total_ref, out_ref, next_ref, sem = refs[count:]
    half = ready_ref.shape[0]
    copy = pltpu.make_async_copy(ready_ref, out_ref.at[:half, :], sem)
    copy.start()
    weight = source_rows(first, pieces, weight_ref)
    for rows in row_blocks(half):
        next_ref[rows, :] = total_ref[rows, :] + block_product(pieces, weight, rows)
    copy.wait()


def last_kernel(count, first, *refs):
    pieces = refs[:count]
    weight_ref, total_ref, begun_ref, out_ref, held, sems = refs[count:]
    half = total_ref.shape[0]
    copies = []
    weight = source_rows(first, pieces, weight_ref)
    for spot, rows in enumerate(row_blocks(half)):
        held[rows, :] = total_ref[rows, :] + block_product(pieces, weight, rows)
        out = slice(half + rows.start, half + rows.stop)
        copies.append(
            pltpu.make_async_copy(held.at[rows, :], out_ref.at[out, :], sems.at[spot])
        )
        copies[-1].start()
    for copy in copies:
        copy.wait()


def vmem_call(kernel, outs, scratch, cost, *args, any_in=(), any_out=(), aliases=(), grant=VMEM_GRANT):
    spec = pl.BlockSpec(memory_space=pltpu.VMEM)
    small = pl.BlockSpec(memory_space=pltpu.SMEM)
    free = pl.BlockSpec(memory_space=pl.ANY)
    return pl.pallas_call(
        kernel,
        out_shape=outs,
        in_specs=[
            free if spot in any_in else small if arg.dtype == jnp.int32 and arg.ndim == 1 else spec
            for spot, arg in enumerate(args)
        ],
        out_specs=[free if spot in any_out else spec for spot in range(len(outs))]
        if isinstance(outs, list)
        else (free if any_out else spec),
        input_output_aliases=dict(aliases),
        scratch_shapes=scratch,
        compiler_params=pltpu.CompilerParams(vmem_limit_bytes=grant),
        cost_estimate=pl.CostEstimate(flops=int(cost * 1e9), bytes_accessed=1 << 20, transcendentals=0),
    )(*args)


def to_sibling(value):
    count = lax.axis_size("head")
    return lax.ppermute(value, "head", [(source, source ^ 1) for source in range(count)])


def to_chips(value):
    count = lax.axis_size("head")
    return [
        lax.ppermute(
            value, "head", [(source, (source + 2 * step) % count) for source in range(count)]
        )
        for step in range(1, count // 2)
    ]


def after(value, *earlier):
    return lax.optimization_barrier((value, *earlier))


def shards(tokens, w_proj, w_mix, conv_w, rates, doc_start, norm_gain, w_out):
    tok_rows, depth = tokens.shape
    width = w_proj.shape[1] // 4
    state_columns, query_columns = 2 * width + CHUNK, 2 * width
    heads, me = lax.axis_size("head"), lax.axis_index("head")
    blocks, my_index = lax.axis_size("ctx"), lax.axis_index("ctx")
    remote = [(me + heads - 2 * step) % heads for step in range(1, heads // 2)]
    order = [me, me ^ 1] + remote + [index ^ 1 for index in remote]
    bits = blocks.bit_length() - 1
    index = jnp.stack(order + [my_index >> bit & 1 for bit in range(bits)]).astype(jnp.int32)
    count = heads - 2
    like = lambda *shape: jax.ShapeDtypeStruct(shape, F32)
    parts = lambda *shape: jax.ShapeDtypeStruct(shape, BF16)

    first = tok_rows // 2
    cut = first - RIM
    middle = tok_rows - CHUNK - RIM
    segments = (slice(cut, middle), slice(middle, tok_rows))
    spans = (segments[1], segments[0], slice(0, cut), slice(0, tok_rows))
    tokens, index = after(tokens, index)
    last_rows, next_rows, early_rows, own = vmem_call(
        functools.partial(stage_kernel, spans),
        [like(rows.stop - rows.start, depth) for rows in spans],
        [pltpu.SemaphoreType.DMA((len(spans),))], 1, tokens, any_in=(0,), any_out=(0, 1, 2, 3), grant=STAGE_GRANT,
    )
    late = [to_chips(next_rows), to_chips(last_rows)]
    beside = to_sibling(own)
    early_rows, beside = after(early_rows, beside)
    early = to_chips(early_rows)
    base_state, base_query, far_state, far_query, flags = vmem_call(
        base_kernel,
        [like(tok_rows, state_columns), like(tok_rows, query_columns),
         parts(count * depth, 2 * state_columns), parts(count * depth, 2 * query_columns),
         jax.ShapeDtypeStruct((bits, CHUNK), jnp.int32)],
        [pltpu.VMEM((heads, depth, 4 * width), F32),
         pltpu.VMEM((2 * depth, 2 * state_columns), BF16),
         pltpu.VMEM((2 * depth, 2 * query_columns), BF16),
         pltpu.SemaphoreType.DMA((heads,))],
        3, index, tokens, beside, w_mix.T, w_proj, any_in=(4,),
    )
    late, far_state = after(late, far_state)
    late_on = [[to_sibling(value) for value in values] for values in late]
    arrived = [value for pair in zip(late, late_on) for values in pair for value in values]
    late_state, late_query, rim = vmem_call(
        functools.partial(late_kernel, count, segments),
        [like(tok_rows - cut, state_columns), like(tok_rows - cut, query_columns),
         like(RIM, 3 * width)],
        [], 0.5, *arrived, base_state, base_query, far_state, far_query,
    )
    rim = lax.ppermute(rim, "ctx", [(source, source + 1) for source in range(blocks - 1)])
    docs = doc_start.reshape(tok_rows // CHUNK, CHUNK)
    rate = rates[:, None]

    def outs(rows):
        chunks = like(rows // CHUNK, 2, width, width)
        return [like(rows, width)] * 6 + [chunks, like(2, width, width)]

    later = vmem_call(
        functools.partial(later_kernel, first // CHUNK), outs(tok_rows - first), [], 0.5,
        late_state, conv_w, rate, docs,
    )
    early, pair_late, rim = after(early, later[7], rim)
    early_on = [to_sibling(value) for value in early]
    partial = vmem_call(
        functools.partial(partial_kernel, len(early)), like(cut, state_columns), [], 1,
        *early, base_state, far_state,
    )
    earlier = vmem_call(
        functools.partial(earlier_kernel, len(early), len(early)), outs(first),
        [pltpu.VMEM((first + RIM, state_columns), F32)], 5,
        *early_on, partial, far_state, rim, late_state, pair_late, conv_w, rate, docs,
    )

    pair = earlier[7]
    fields = vmem_call(
        functools.partial(query_kernel, count), [like(tok_rows, width)] * 3,
        [pltpu.VMEM((first + RIM, query_columns), F32)], 5,
        *early, *early_on, base_query, far_query, rim, late_query, conv_w,
        *earlier[:5], earlier[6], *later[:5], later[6],
    )
    own_weight = vmem_call(
        functools.partial(order_kernel, heads), parts(w_out.shape[0], 2 * w_out.shape[1]), [], 1,
        index, w_out,
    )
    carry = ()
    levels = []
    for bit in range(0, bits - 1, 2):
        others = [
            lax.ppermute(
                pair, "ctx", [(source, source ^ (mask << bit)) for source in range(blocks)]
            )
            for mask in (1, 2, 3)
        ]
        if not bit:
            others[0], *fields, own_weight = after(others[0], *fields, own_weight)
        last = bit + 2 >= bits - 1 and bits % 2
        group = [like(width, width)] if last else [like(2, width, width)]
        pair, level, *carry = vmem_call(
            functools.partial(four_kernel, bit, bool(carry), last),
            group + [like(2, width, width), like(width, width)], [], 1,
            flags, pair, *others, *carry,
        )
        levels.append(level)
    carried, local, gate = fields
    lone = bool(bits % 2)
    reach = blocks // 2
    if lone:
        other = lax.ppermute(
            pair if carry else pair[1],
            "ctx", [(source, source ^ reach) for source in range(blocks)],
        )
        if not carry:
            carry = [jnp.where(my_index >= reach, jnp.eye(width, dtype=F32), 0.0)]
    rows_shape = like(tok_rows, width)
    mixed, *reached = vmem_call(
        functools.partial(level_kernel, len(levels), lone), [rows_shape] * (2 if lone else 1), [], 1,
        carried, local, earlier[5], later[5], *levels, *(carry if lone else ()),
    )
    if lone:
        reached.append(other)
    half = tok_rows // 2
    normed, *lows, high = vmem_call(
        functools.partial(mix_kernel, lone),
        [rows_shape] + [like(half // 2, width)] * 2 + [like(half, width)], [], 1,
        mixed, gate, norm_gain[None, :], *reached,
    )
    columns = w_out.shape[1]
    near = to_sibling(normed)
    far_lows = [to_chips(low) for low in lows]
    high, near = after(high, near)
    far_high = to_chips(high)
    total_low, total_high = vmem_call(
        near_kernel, [like(half, columns)] * 2, [], 2, normed, near, own_weight
    )
    far_lows, total_low = after(far_lows, total_low)
    far_lows_on = [[to_sibling(value) for value in values] for values in far_lows]
    arrived = [value for pair in zip(far_lows, far_lows_on) for values in pair for value in values]
    total_low = vmem_call(
        functools.partial(far_kernel, count, 2), like(half, columns), [], 0.01,
        *arrived, own_weight, total_low,
    )
    far_high, total_low = after(far_high, total_low)
    far_high_on = [to_sibling(value) for value in far_high]
    whole = like(tok_rows, columns)
    begun, total_high = vmem_call(
        functools.partial(flush_kernel, len(far_high), 2), [whole, like(half, columns)],
        [pltpu.SemaphoreType.DMA], 1,
        *far_high, own_weight, total_low, total_high, any_out=(0,),
    )
    args = [*far_high_on, own_weight, total_high, begun]
    last = len(args) - 1
    return vmem_call(
        functools.partial(last_kernel, len(far_high), 2 + len(far_high)), whole,
        [pltpu.VMEM((half, columns), F32), pltpu.SemaphoreType.DMA((half // CHUNK,))], 1,
        *args, any_in=(last,), any_out=True, aliases=((last, 0),),
    )


def solution(mesh):
    placed = (
        P("ctx", "head"),
        P(None, "head"),
        P(None, "head"),
        P(None, "head"),
        P("head"),
        P("ctx"),
        P("head"),
        P(None, "head"),
    )
    return jax.shard_map(
        shards, mesh=mesh, in_specs=placed, out_specs=P("ctx", "head"), check_vma=False
    )
```

```python
import functools

import jax
import jax.numpy as jnp
from jax import lax
from jax.experimental import pallas as pl
from jax.experimental.pallas import tpu as pltpu
from jax.sharding import PartitionSpec as P

CHUNK = 128
RIM = 16
VMEM_GRANT = 16 << 20
F32 = jnp.float32
BF16 = jnp.bfloat16


def halves(value):
    high = value.astype(BF16)
    return high, (value - high.astype(F32)).astype(BF16)


def left_parts(value):
    return jnp.concatenate(halves(value), axis=1)


def right_parts(value):
    row = jnp.concatenate(halves(value), axis=1)
    return jnp.concatenate([row, row], axis=0)


def parts_dot(left, right):
    both = jnp.dot(left, right, preferred_element_type=F32)
    half = both.shape[1] // 2
    return both[:, :half] + both[:, half:]


def product(left, right):
    return parts_dot(left_parts(left), right_parts(right))


def softplus(value):
    return jnp.maximum(value, 0.0) + jnp.log1p(jnp.exp(-jnp.abs(value)))


def sigmoid(value):
    return 1.0 / (1.0 + jnp.exp(-value))


def unit_lower_inverse(lowers, row, col):
    size = lowers[0].shape[0]
    eye = jnp.where(row == col, 1.0, 0.0).astype(F32)
    inverses = [eye - jnp.where((row >> 1) == (col >> 1), lower, 0.0) for lower in lowers]
    lower_parts = [halves(lower) for lower in lowers]
    step = 1
    while 1 << step < size:
        off = ((row >> (step + 2)) == (col >> (step + 2))) & ((row >> step) > (col >> step))
        offs = [
            jnp.concatenate([jnp.where(off, part, jnp.zeros_like(part)) for part in parts], axis=1)
            for parts in lower_parts
        ]
        onto = [parts_dot(left, right_parts(inverse)) for left, inverse in zip(offs, inverses)]
        rights = [right_parts(value) for value in onto]
        squares = [parts_dot(left_parts(value), right) for value, right in zip(onto, rights)]
        firsts = [
            inverse - parts_dot(left_parts(inverse), right)
            for inverse, right in zip(inverses, rights)
        ]
        inverses = [first + product(first, square) for first, square in zip(firsts, squares)]
        step += 2
    return inverses


def add_products(total, pieces, weight_ref, first):
    columns = weight_ref.shape[1] // 2
    for spot, piece in enumerate(pieces):
        depth = piece.shape[1]
        rows = slice((first + spot) * depth, (first + spot + 1) * depth)
        high, low = halves(piece)
        both = jnp.dot(high, weight_ref[rows, :], preferred_element_type=F32)
        rest = jnp.dot(low, weight_ref[rows, :columns], preferred_element_type=F32)
        part = (both[:, :columns] + both[:, columns:]) + rest
        total = part if total is None else total + part
    return total


def base_kernel(
    index_ref, own_ref, beside_ref, mix_ref, proj_ref,
    state_ref, query_ref, far_state_ref, far_query_ref, flag_ref,
    held, near_state, near_query, sems,
):
    sources, depth, across = held.shape
    width = across // 4
    copies = []
    for source in range(sources):
        rows = pl.ds(pl.multiple_of(index_ref[source] * depth, depth), depth)
        copies.append(pltpu.make_async_copy(proj_ref.at[rows, :], held.at[source], sems.at[source]))
        copies[-1].start()
    for bit in range(flag_ref.shape[0]):
        flag_ref[bit : bit + 1, :] = jnp.broadcast_to(index_ref[sources + bit], (1, CHUNK))
    mixes = mix_ref.shape[0]

    def split(source, state_out, query_out, base):
        copies[source].wait()
        lanes = pl.ds(pl.multiple_of(index_ref[source] * depth, depth), depth)
        for begin in range(0, depth, CHUNK):
            rows = slice(begin, begin + CHUNK)
            out = slice(base + begin, base + begin + CHUNK)
            value = held[source, rows, :]
            mixing = mix_ref[:, lanes][:, rows]
            mixing = jnp.concatenate([mixing, jnp.zeros((CHUNK - mixes, CHUNK), F32)], axis=0)
            state = jnp.concatenate([value[:, width : 3 * width], jnp.transpose(mixing)], axis=1)
            query = jnp.concatenate([value[:, :width], value[:, 3 * width :]], axis=1)
            state_out[out, :] = left_parts(state)
            query_out[out, :] = left_parts(query)

    for source in range(2):
        split(source, near_state, near_query, source * depth)
    half = own_ref.shape[0] // 2
    for rows in (slice(0, half), slice(half, 2 * half)):
        pieces = [own_ref[rows, :], beside_ref[rows, :]]
        state_ref[rows, :] = add_products(None, pieces, near_state, 0)
        query_ref[rows, :] = add_products(None, pieces, near_query, 0)
    for source in range(2, sources):
        split(source, far_state_ref, far_query_ref, (source - 2) * depth)


def late_kernel(count, segments, *refs):
    begin = segments[0].start
    held, refs = refs[: count * len(segments)], refs[count * len(segments) :]
    base_state, base_query, far_state, far_query, state_ref, query_ref, rim_ref = refs
    width = base_query.shape[1] // 2
    for turn, rows in enumerate(segments):
        pieces = [ref[...] for ref in held[turn * count : (turn + 1) * count]]
        out = slice(rows.start - begin, rows.stop - begin)
        state_ref[out, :] = add_products(base_state[rows, :], pieces, far_state, 0)
        query_ref[out, :] = add_products(base_query[rows, :], pieces, far_query, 0)
    last = state_ref.shape[0] - RIM
    rim_ref[:, :width] = query_ref[last:, :width]
    rim_ref[:, width:] = state_ref[last:, : 2 * width]


def partial_kernel(count, *refs):
    base_state, far_state, out_ref = refs[count:]
    out_ref[...] = add_products(
        base_state[: out_ref.shape[0], :], [ref[...] for ref in refs[:count]], far_state, 0
    )


def convolve(raw, start, columns, conv_ref, taps_at):
    taps = conv_ref.shape[0]
    conv = 0.0
    for tap in range(taps):
        spot = start - taps + 1 + tap
        conv = conv + conv_ref[tap : tap + 1, taps_at] * raw[spot : spot + CHUNK, columns]
    return conv * sigmoid(conv)


def unit_rows(value):
    return value * lax.rsqrt(jnp.sum(value * value, axis=1, keepdims=True) + 1e-06)


def key_pass(raw, conv_ref, rate, doc_ref, first_chunk, outs, state):
    key_ref, x_ref, y_ref, grid_ref, gamma_ref, plus_ref, chunk_ref, pair_ref = outs
    width = key_ref.shape[1]
    chunks = key_ref.shape[0] // CHUNK
    row = lax.broadcasted_iota(jnp.int32, (CHUNK, CHUNK), 0)
    col = lax.broadcasted_iota(jnp.int32, (CHUNK, CHUNK), 1)
    lower = row >= col
    tri = jnp.where(lower, 1.0, 0.0).astype(BF16)
    eye = jnp.where(row == col, 1.0, 0.0).astype(F32)
    keys, values, betas, grids, gammas, tails = [], [], [], [], [], []
    for part in range(chunks):
        start = RIM + part * CHUNK
        rows = slice(part * CHUNK, (part + 1) * CHUNK)
        middle, last = slice(width, 2 * width), slice(2 * width, 3 * width)
        keys.append(unit_rows(convolve(raw, start, slice(0, width), conv_ref, middle)))
        values.append(convolve(raw, start, middle, conv_ref, last))
        mixing = raw[start : start + CHUNK, last]
        plus = softplus(mixing)
        plus_ref[rows, :] = plus
        betas.append(sigmoid(mixing[:, 0:1]))
        spot = first_chunk + part
        docs = jnp.broadcast_to(doc_ref[spot : spot + 1, :].astype(F32), (CHUNK, CHUNK))
        docs = jnp.transpose(docs)
        smooth = -rate * plus[:, 1:2]
        high = smooth.astype(BF16).astype(F32)
        middle = (smooth - high).astype(BF16).astype(F32)
        rest = smooth - high - middle
        steps = jnp.where(col == 0, docs, jnp.where(col == 1, high, jnp.where(col == 2, middle, rest)))
        steps = jnp.where(col < 4, steps, 0.0).astype(BF16)
        sums = jnp.dot(tri, steps, preferred_element_type=F32)
        across = jnp.transpose(sums)
        across = jnp.concatenate([across[0:1, :], across[1:2, :] + (across[2:3, :] + across[3:4, :])], axis=0)
        count = sums[:, 0:1]
        smooth = sums[:, 1:2] + (sums[:, 2:3] + sums[:, 3:4])
        span = (smooth - across[1:2, :]) - 20.0 * (count - across[0:1, :])
        grids.append(jnp.exp(jnp.where(lower, span, -1e30)))
        gammas.append(jnp.exp(smooth - 20.0 * count))
        end = slice(CHUNK - 1, CHUNK)
        tails.append(jnp.exp((smooth[end] - smooth) - 20.0 * (count[end] - count)))
        key_ref[rows, :] = keys[part]
        grid_ref[rows, :] = grids[part]
        gamma_ref[rows, :] = jnp.broadcast_to(gammas[part], (CHUNK, width))
    across_keys = [jnp.transpose(key) for key in keys]
    grams = [
        parts_dot(left_parts(key), right_parts(across)) for key, across in zip(keys, across_keys)
    ]
    lowers = [jnp.where(row > col, beta * gram, 0.0) for beta, gram in zip(betas, grams)]
    inverses = unit_lower_inverse(lowers, row, col)
    states = []
    if state is not None:
        later_keys = product(state[0], across_keys[-1])
    for part in range(chunks):
        rows = slice(part * CHUNK, (part + 1) * CHUNK)
        inverse, beta = inverses[part], betas[part]
        factor_x = product(inverse, beta * keys[part])
        factor_y = product(grids[part] * inverse, beta * values[part])
        x_ref[rows, :] = factor_x
        y_ref[rows, :] = factor_y
        factors = jnp.concatenate([factor_x, tails[part] * factor_y], axis=1)
        onto = product(across_keys[part], factors)
        if state is not None and part == chunks - 1:
            behind = product(later_keys, factors)
        trans = gammas[part][CHUNK - 1 : CHUNK, :] * (eye - onto[:, :width])
        states.append((trans, onto[:, width:]))
        chunk_ref[part, 0] = trans
        chunk_ref[part, 1] = onto[:, width:]
    if state is not None:
        decay = gammas[-1][CHUNK - 1 : CHUNK, :]
        states[-1] = (decay * (state[0] - behind[:, :width]), behind[:, width:] + state[1])
    while len(states) > 1:
        joined = [followed(*states[at : at + 2]) for at in range(0, len(states) - 1, 2)]
        states = joined + states[2 * len(joined) :]
    pair_ref[0] = states[0][0]
    pair_ref[1] = states[0][1]


def followed(first, second):
    width = first[0].shape[0]
    onto = product(second[0], jnp.concatenate(first, axis=1))
    return onto[:, :width], onto[:, width:] + second[1]


def later_kernel(first_chunk, raw_ref, conv_ref, rate_ref, doc_ref, *outs):
    key_pass(raw_ref, conv_ref, rate_ref[0, 0], doc_ref, first_chunk, outs, None)


def earlier_kernel(first, count, *refs):
    held, refs = refs[:count], refs[count:]
    part_ref, far_ref, rim_ref, next_ref, state_ref, conv_ref, rate_ref, doc_ref = refs[:8]
    outs, raw = refs[8:-1], refs[-1]
    rows, width = part_ref.shape[0], state_ref.shape[1]
    raw[RIM : RIM + rows, :] = add_products(
        part_ref[...], [ref[...] for ref in held], far_ref, first
    )
    raw[:RIM, : 2 * width] = rim_ref[:, width:]
    raw[RIM + rows :, :] = next_ref[:RIM, :]
    key_pass(raw, conv_ref, rate_ref[0, 0], doc_ref, 0, outs, (state_ref[0], state_ref[1]))


def query_kernel(count, *refs):
    held, refs = refs[:count], refs[count:]
    base_ref, far_ref, rim_ref, next_ref, conv_ref = refs[:5]
    fields = [(refs[5:11], 0), (refs[11:17], 1)]
    carried_ref, local_ref, gate_ref, raw = refs[17:]
    width = carried_ref.shape[1]
    rows = held[0].shape[0]
    raw[RIM : RIM + rows, :] = add_products(
        base_ref[:rows, :], [ref[...] for ref in held], far_ref, 0
    )
    raw[:RIM, :width] = rim_ref[:, :width]
    raw[RIM + rows :, :] = next_ref[:RIM, :]
    row = lax.broadcasted_iota(jnp.int32, (CHUNK, CHUNK), 0)
    col = lax.broadcasted_iota(jnp.int32, (CHUNK, CHUNK), 1)
    state = None
    base = 0
    for (key_ref, x_ref, y_ref, grid_ref, gamma_ref, chunk_ref), later in fields:
        source = next_ref if later else raw
        for part in range(key_ref.shape[0] // CHUNK):
            start = RIM + part * CHUNK
            rows = slice(part * CHUNK, (part + 1) * CHUNK)
            out = slice(base, base + CHUNK)
            base += CHUNK
            columns = slice(0, width)
            query = unit_rows(convolve(source, start, columns, conv_ref, columns))
            gate = source[start : start + CHUNK, width:]
            gate_ref[out, :] = gate * sigmoid(gate)
            overlap = product(query, jnp.transpose(key_ref[rows, :]))
            carried = gamma_ref[rows, :] * (
                query - product(jnp.where(row >= col, overlap, 0.0), x_ref[rows, :])
            )
            local = product(grid_ref[rows, :] * overlap, y_ref[rows, :])
            trans, memory = chunk_ref[part, 0], chunk_ref[part, 1]
            if state is None:
                state = (trans, memory)
            else:
                onto = product(
                    jnp.concatenate([trans, carried], axis=0), jnp.concatenate(state, axis=1)
                )
                carried = onto[CHUNK:, :width]
                local = local + onto[CHUNK:, width:]
                state = (onto[:CHUNK, :width], onto[:CHUNK, width:] + memory)
            carried_ref[out, :] = carried
            local_ref[out, :] = local


def four_kernel(bit, carried, last, flag_ref, own_ref, one_ref, two_ref, three_ref, *refs):
    group_ref, level_ref, next_ref = refs[-3:]
    width = next_ref.shape[0]
    flag = lambda at: jnp.broadcast_to(flag_ref[at : at + 1, :], (width, width)) == 1
    set_low, set_high = flag(bit), flag(bit + 1)
    held = (own_ref, one_ref, two_ref, three_ref)

    def placed(part):
        by_low = [jnp.where(set_low, held[at ^ 1][part], held[at][part]) for at in range(4)]
        return [jnp.where(set_high, by_low[at ^ 2], by_low[at]) for at in range(4)]

    trans, memory = placed(0), placed(1)
    joined = lambda at: jnp.concatenate([trans[at], memory[at]], axis=1)
    onto_low = product(trans[1], joined(0))
    onto_high = product(trans[3], joined(2))
    low_a, low_s = onto_low[:, :width], onto_low[:, width:] + memory[1]
    high_a, high_s = onto_high[:, :width], onto_high[:, width:] + memory[3]
    if last:
        group_ref[...] = product(high_a, low_s) + high_s
    else:
        onto = product(high_a, jnp.concatenate([low_a, low_s], axis=1))
        group_ref[0] = onto[:, :width]
        group_ref[1] = onto[:, width:] + high_s
    if carried:
        carry = refs[0][...]
        first = product(carry, jnp.concatenate([one_ref[0], one_ref[1]], axis=1))
        first_a, first_s = first[:, :width], first[:, width:]
    else:
        row = lax.broadcasted_iota(jnp.int32, (width, width), 0)
        col = lax.broadcasted_iota(jnp.int32, (width, width), 1)
        carry = jnp.where(row == col, 1.0, 0.0).astype(F32)
        first_a, first_s = one_ref[0], one_ref[1]
    level_ref[0] = jnp.where(set_low, first_s, 0.0)
    carry = jnp.where(set_low, first_a, carry)
    second = product(carry, jnp.concatenate([low_a, low_s], axis=1))
    level_ref[1] = jnp.where(set_high, second[:, width:], 0.0)
    carry = jnp.where(set_high, second[:, :width], carry)
    next_ref[...] = jnp.where(flag(bit + 2), carry, 0.0) if last else carry


def level_kernel(stages, single, carried_ref, local_ref, low_ref, high_ref, *refs):
    states = [ref[spot] for ref in refs[:stages] for spot in range(ref.shape[0])]
    carried = left_parts(carried_ref[...])
    weights = jnp.concatenate([low_ref[...], high_ref[...]], axis=0)
    mixed = weights[:, 2:3] * local_ref[...]
    for level, state in enumerate(states):
        mixed = mixed + weights[:, level + 3 : level + 4] * parts_dot(carried, right_parts(state))
    if single:
        carry_ref, mixed_ref, reach_ref = refs[stages:]
        level = len(states) + 3
        reach_ref[...] = weights[:, level : level + 1] * parts_dot(
            carried, right_parts(carry_ref[...])
        )
    else:
        (mixed_ref,) = refs[stages:]
    mixed_ref[...] = mixed


def mix_kernel(single, mixed_ref, gate_ref, gain_ref, *refs):
    mixed = mixed_ref[...]
    if single:
        mixed = mixed + product(refs[0][...], refs[1][...])
    outs = refs[2 if single else 0 :]
    scale = lax.rsqrt(jnp.mean(mixed * mixed, axis=1, keepdims=True) + 1e-05)
    normed = mixed * scale * gain_ref[...] * gate_ref[...]
    outs[0][...] = normed
    base = 0
    for out in outs[1:]:
        out[...] = normed[base : base + out.shape[0]]
        base += out.shape[0]


def block_product(pieces, weight, rows):
    parts = [halves(ref[rows, :]) for ref in pieces]
    high, low = (jnp.concatenate(part, axis=1) for part in zip(*parts))
    columns = weight.shape[1] // 2
    both = jnp.dot(high, weight, preferred_element_type=F32)
    rest = jnp.dot(low, weight[:, :columns], preferred_element_type=F32)
    return (both[:, :columns] + both[:, columns:]) + rest


def order_kernel(sources, index_ref, weight_ref, out_ref):
    depth = weight_ref.shape[0] // sources
    for source in range(sources):
        rows = pl.ds(pl.multiple_of(index_ref[source] * depth, depth), depth)
        out_ref[source * depth : (source + 1) * depth, :] = left_parts(weight_ref[rows, :])


def source_rows(first, pieces, weight_ref):
    depth = pieces[0].shape[1]
    return weight_ref[first * depth : (first + len(pieces)) * depth, :]


def row_blocks(rows):
    return [slice(base, base + CHUNK) for base in range(0, rows, CHUNK)]


def near_kernel(own_ref, near_ref, weight_ref, low_ref, high_ref):
    weight = source_rows(0, [own_ref, near_ref], weight_ref)
    half = low_ref.shape[0]
    for rows in row_blocks(half):
        low_ref[rows, :] = block_product([own_ref, near_ref], weight, rows)
        later = slice(half + rows.start, half + rows.stop)
        high_ref[rows, :] = block_product([own_ref, near_ref], weight, later)


def far_kernel(count, first, *refs):
    held, (weight_ref, total_ref, out_ref) = refs[:-3], refs[-3:]
    weight = source_rows(first, held[:count], weight_ref)
    base = 0
    for at in range(0, len(held), count):
        pieces = held[at : at + count]
        for rows in row_blocks(pieces[0].shape[0]):
            out = slice(base + rows.start, base + rows.stop)
            out_ref[out, :] = total_ref[out, :] + block_product(pieces, weight, rows)
        base += pieces[0].shape[0]


def flush_kernel(count, first, *refs):
    pieces = refs[:count]
    weight_ref, ready_ref, total_ref, out_ref, next_ref, sem = refs[count:]
    half = ready_ref.shape[0]
    copy = pltpu.make_async_copy(ready_ref, out_ref.at[:half, :], sem)
    copy.start()
    weight = source_rows(first, pieces, weight_ref)
    for rows in row_blocks(half):
        next_ref[rows, :] = total_ref[rows, :] + block_product(pieces, weight, rows)
    copy.wait()


def last_kernel(count, first, *refs):
    pieces = refs[:count]
    weight_ref, total_ref, begun_ref, out_ref, held, sems = refs[count:]
    half = total_ref.shape[0]
    copies = []
    weight = source_rows(first, pieces, weight_ref)
    for spot, rows in enumerate(row_blocks(half)):
        held[rows, :] = total_ref[rows, :] + block_product(pieces, weight, rows)
        out = slice(half + rows.start, half + rows.stop)
        copies.append(
            pltpu.make_async_copy(held.at[rows, :], out_ref.at[out, :], sems.at[spot])
        )
        copies[-1].start()
    for copy in copies:
        copy.wait()


def vmem_call(kernel, outs, scratch, cost, *args, any_in=(), any_out=(), aliases=()):
    spec = pl.BlockSpec(memory_space=pltpu.VMEM)
    small = pl.BlockSpec(memory_space=pltpu.SMEM)
    free = pl.BlockSpec(memory_space=pl.ANY)
    return pl.pallas_call(
        kernel,
        out_shape=outs,
        in_specs=[
            free if spot in any_in else small if arg.dtype == jnp.int32 and arg.ndim == 1 else spec
            for spot, arg in enumerate(args)
        ],
        out_specs=[free if spot in any_out else spec for spot in range(len(outs))]
        if isinstance(outs, list)
        else (free if any_out else spec),
        input_output_aliases=dict(aliases),
        scratch_shapes=scratch,
        compiler_params=pltpu.CompilerParams(vmem_limit_bytes=VMEM_GRANT),
        cost_estimate=pl.CostEstimate(flops=int(cost * 1e9), bytes_accessed=1 << 20, transcendentals=0),
    )(*args)


def to_sibling(value):
    count = lax.axis_size("head")
    return lax.ppermute(value, "head", [(source, source ^ 1) for source in range(count)])


def to_chips(value):
    count = lax.axis_size("head")
    return [
        lax.ppermute(
            value, "head", [(source, (source + 2 * step) % count) for source in range(count)]
        )
        for step in range(1, count // 2)
    ]


def after(value, *earlier):
    return lax.optimization_barrier((value, *earlier))


def shards(tokens, w_proj, w_mix, conv_w, rates, doc_start, norm_gain, w_out):
    tok_rows, depth = tokens.shape
    width = w_proj.shape[1] // 4
    state_columns, query_columns = 2 * width + CHUNK, 2 * width
    heads, me = lax.axis_size("head"), lax.axis_index("head")
    blocks, my_index = lax.axis_size("ctx"), lax.axis_index("ctx")
    remote = [(me + heads - 2 * step) % heads for step in range(1, heads // 2)]
    order = [me, me ^ 1] + remote + [index ^ 1 for index in remote]
    bits = blocks.bit_length() - 1
    index = jnp.stack(order + [my_index >> bit & 1 for bit in range(bits)]).astype(jnp.int32)
    count = heads - 2
    like = lambda *shape: jax.ShapeDtypeStruct(shape, F32)
    parts = lambda *shape: jax.ShapeDtypeStruct(shape, BF16)

    first = tok_rows // 2
    cut = first - RIM
    middle = tok_rows - CHUNK - RIM
    segments = (slice(cut, middle), slice(middle, tok_rows))
    late = [to_chips(tokens[rows]) for rows in segments]
    beside = to_sibling(tokens)
    early_rows, beside = after(tokens, beside)
    early = to_chips(early_rows[:cut])
    base_state, base_query, far_state, far_query, flags = vmem_call(
        base_kernel,
        [like(tok_rows, state_columns), like(tok_rows, query_columns),
         parts(count * depth, 2 * state_columns), parts(count * depth, 2 * query_columns),
         jax.ShapeDtypeStruct((bits, CHUNK), jnp.int32)],
        [pltpu.VMEM((heads, depth, 4 * width), F32),
         pltpu.VMEM((2 * depth, 2 * state_columns), BF16),
         pltpu.VMEM((2 * depth, 2 * query_columns), BF16),
         pltpu.SemaphoreType.DMA((heads,))],
        3, index, tokens, beside, w_mix.T, w_proj, any_in=(4,),
    )
    late, far_state = after(late, far_state)
    late_on = [[to_sibling(value) for value in values] for values in late]
    arrived = [value for pair in zip(late, late_on) for values in pair for value in values]
    late_state, late_query, rim = vmem_call(
        functools.partial(late_kernel, count, segments),
        [like(tok_rows - cut, state_columns), like(tok_rows - cut, query_columns),
         like(RIM, 3 * width)],
        [], 0.5, *arrived, base_state, base_query, far_state, far_query,
    )
    rim = lax.ppermute(rim, "ctx", [(source, source + 1) for source in range(blocks - 1)])
    docs = doc_start.reshape(tok_rows // CHUNK, CHUNK)
    rate = rates[:, None]

    def outs(rows):
        chunks = like(rows // CHUNK, 2, width, width)
        return [like(rows, width)] * 6 + [chunks, like(2, width, width)]

    later = vmem_call(
        functools.partial(later_kernel, first // CHUNK), outs(tok_rows - first), [], 0.5,
        late_state, conv_w, rate, docs,
    )
    early, pair_late, rim = after(early, later[7], rim)
    early_on = [to_sibling(value) for value in early]
    partial = vmem_call(
        functools.partial(partial_kernel, len(early)), like(cut, state_columns), [], 1,
        *early, base_state, far_state,
    )
    earlier = vmem_call(
        functools.partial(earlier_kernel, len(early), len(early)), outs(first),
        [pltpu.VMEM((first + RIM, state_columns), F32)], 5,
        *early_on, partial, far_state, rim, late_state, pair_late, conv_w, rate, docs,
    )

    pair = earlier[7]
    fields = vmem_call(
        functools.partial(query_kernel, count), [like(tok_rows, width)] * 3,
        [pltpu.VMEM((first + RIM, query_columns), F32)], 5,
        *early, *early_on, base_query, far_query, rim, late_query, conv_w,
        *earlier[:5], earlier[6], *later[:5], later[6],
    )
    own_weight = vmem_call(
        functools.partial(order_kernel, heads), parts(w_out.shape[0], 2 * w_out.shape[1]), [], 1,
        index, w_out,
    )
    carry = ()
    levels = []
    for bit in range(0, bits - 1, 2):
        others = [
            lax.ppermute(
                pair, "ctx", [(source, source ^ (mask << bit)) for source in range(blocks)]
            )
            for mask in (1, 2, 3)
        ]
        if not bit:
            others[0], *fields, own_weight = after(others[0], *fields, own_weight)
        last = bit + 2 >= bits - 1 and bits % 2
        group = [like(width, width)] if last else [like(2, width, width)]
        pair, level, *carry = vmem_call(
            functools.partial(four_kernel, bit, bool(carry), last),
            group + [like(2, width, width), like(width, width)], [], 1,
            flags, pair, *others, *carry,
        )
        levels.append(level)
    carried, local, gate = fields
    lone = bool(bits % 2)
    reach = blocks // 2
    if lone:
        other = lax.ppermute(
            pair if carry else pair[1],
            "ctx", [(source, source ^ reach) for source in range(blocks)],
        )
        if not carry:
            carry = [jnp.where(my_index >= reach, jnp.eye(width, dtype=F32), 0.0)]
    rows_shape = like(tok_rows, width)
    mixed, *reached = vmem_call(
        functools.partial(level_kernel, len(levels), lone), [rows_shape] * (2 if lone else 1), [], 1,
        carried, local, earlier[5], later[5], *levels, *(carry if lone else ()),
    )
    if lone:
        reached.append(other)
    half = tok_rows // 2
    normed, *lows, high = vmem_call(
        functools.partial(mix_kernel, lone),
        [rows_shape] + [like(half // 2, width)] * 2 + [like(half, width)], [], 1,
        mixed, gate, norm_gain[None, :], *reached,
    )
    columns = w_out.shape[1]
    near = to_sibling(normed)
    far_lows = [to_chips(low) for low in lows]
    high, near = after(high, near)
    far_high = to_chips(high)
    total_low, total_high = vmem_call(
        near_kernel, [like(half, columns)] * 2, [], 2, normed, near, own_weight
    )
    far_lows, total_low = after(far_lows, total_low)
    far_lows_on = [[to_sibling(value) for value in values] for values in far_lows]
    arrived = [value for pair in zip(far_lows, far_lows_on) for values in pair for value in values]
    total_low = vmem_call(
        functools.partial(far_kernel, count, 2), like(half, columns), [], 0.01,
        *arrived, own_weight, total_low,
    )
    far_high, total_low = after(far_high, total_low)
    far_high_on = [to_sibling(value) for value in far_high]
    whole = like(tok_rows, columns)
    begun, total_high = vmem_call(
        functools.partial(flush_kernel, len(far_high), 2), [whole, like(half, columns)],
        [pltpu.SemaphoreType.DMA], 1,
        *far_high, own_weight, total_low, total_high, any_out=(0,),
    )
    args = [*far_high_on, own_weight, total_high, begun]
    last = len(args) - 1
    return vmem_call(
        functools.partial(last_kernel, len(far_high), 2 + len(far_high)), whole,
        [pltpu.VMEM((half, columns), F32), pltpu.SemaphoreType.DMA((half // CHUNK,))], 1,
        *args, any_in=(last,), any_out=True, aliases=((last, 0),),
    )


def solution(mesh):
    placed = (
        P("ctx", "head"),
        P(None, "head"),
        P(None, "head"),
        P(None, "head"),
        P("head"),
        P("ctx"),
        P("head"),
        P(None, "head"),
    )
    return jax.shard_map(
        shards, mesh=mesh, in_specs=placed, out_specs=P("ctx", "head"), check_vma=False
    )
```

```python
import functools

import jax
import jax.numpy as jnp
from jax import lax
from jax.experimental import pallas as pl
from jax.experimental.pallas import tpu as pltpu
from jax.sharding import PartitionSpec as P

CHUNK = 128
RIM = 16
VMEM_GRANT = 16 << 20
F32 = jnp.float32
BF16 = jnp.bfloat16


def halves(value):
    high = value.astype(BF16)
    return high, (value - high.astype(F32)).astype(BF16)


def left_parts(value):
    return jnp.concatenate(halves(value), axis=1)


def right_parts(value):
    row = jnp.concatenate(halves(value), axis=1)
    return jnp.concatenate([row, row], axis=0)


def parts_dot(left, right):
    both = jnp.dot(left, right, preferred_element_type=F32)
    half = both.shape[1] // 2
    return both[:, :half] + both[:, half:]


def product(left, right):
    return parts_dot(left_parts(left), right_parts(right))


def softplus(value):
    return jnp.maximum(value, 0.0) + jnp.log1p(jnp.exp(-jnp.abs(value)))


def sigmoid(value):
    return 1.0 / (1.0 + jnp.exp(-value))


def unit_lower_inverse(lowers, row, col):
    size = lowers[0].shape[0]
    eye = jnp.where(row == col, 1.0, 0.0).astype(F32)
    inverses = [eye - jnp.where((row >> 1) == (col >> 1), lower, 0.0) for lower in lowers]
    lower_parts = [halves(lower) for lower in lowers]
    step = 1
    while 1 << step < size:
        off = ((row >> (step + 2)) == (col >> (step + 2))) & ((row >> step) > (col >> step))
        offs = [
            jnp.concatenate([jnp.where(off, part, jnp.zeros_like(part)) for part in parts], axis=1)
            for parts in lower_parts
        ]
        if step == 1:
            pairs = [jnp.where((row >> 1) == (col >> 1), lower, 0.0) for lower in lowers]
            entries = [jnp.sum(pair, axis=0, keepdims=True) for pair in pairs]
            parts = [jnp.where(off, lower, 0.0) for lower in lowers]
            onto = [
                part - pltpu.roll(part, size - 1, 1) * entry for part, entry in zip(parts, entries)
            ]
        else:
            onto = [parts_dot(left, right_parts(inverse)) for left, inverse in zip(offs, inverses)]
        rights = [right_parts(value) for value in onto]
        squares = [parts_dot(left_parts(value), right) for value, right in zip(onto, rights)]
        firsts = [
            inverse - parts_dot(left_parts(inverse), right)
            for inverse, right in zip(inverses, rights)
        ]
        inverses = [first + product(first, square) for first, square in zip(firsts, squares)]
        step += 2
    return inverses


def add_products(total, pieces, weight_ref, first):
    columns = weight_ref.shape[1] // 2
    for spot, piece in enumerate(pieces):
        depth = piece.shape[1]
        rows = slice((first + spot) * depth, (first + spot + 1) * depth)
        high, low = halves(piece)
        both = jnp.dot(high, weight_ref[rows, :], preferred_element_type=F32)
        rest = jnp.dot(low, weight_ref[rows, :columns], preferred_element_type=F32)
        part = (both[:, :columns] + both[:, columns:]) + rest
        total = part if total is None else total + part
    return total


def base_kernel(
    index_ref, own_ref, beside_ref, mix_ref, proj_ref,
    state_ref, query_ref, far_state_ref, far_query_ref, flag_ref,
    held, near_state, near_query, sems,
):
    sources, depth, across = held.shape
    width = across // 4
    copies = []
    for source in range(sources):
        rows = pl.ds(pl.multiple_of(index_ref[source] * depth, depth), depth)
        copies.append(pltpu.make_async_copy(proj_ref.at[rows, :], held.at[source], sems.at[source]))
        copies[-1].start()
    for bit in range(flag_ref.shape[0]):
        flag_ref[bit : bit + 1, :] = jnp.broadcast_to(index_ref[sources + bit], (1, CHUNK))
    mixes = mix_ref.shape[0]

    def split(source, state_out, query_out, base):
        copies[source].wait()
        lanes = pl.ds(pl.multiple_of(index_ref[source] * depth, depth), depth)
        for begin in range(0, depth, CHUNK):
            rows = slice(begin, begin + CHUNK)
            out = slice(base + begin, base + begin + CHUNK)
            value = held[source, rows, :]
            mixing = mix_ref[:, lanes][:, rows]
            mixing = jnp.concatenate([mixing, jnp.zeros((CHUNK - mixes, CHUNK), F32)], axis=0)
            state = jnp.concatenate([value[:, width : 3 * width], jnp.transpose(mixing)], axis=1)
            query = jnp.concatenate([value[:, :width], value[:, 3 * width :]], axis=1)
            state_out[out, :] = left_parts(state)
            query_out[out, :] = left_parts(query)

    for source in range(2):
        split(source, near_state, near_query, source * depth)
    half = own_ref.shape[0] // 2
    for rows in (slice(0, half), slice(half, 2 * half)):
        pieces = [own_ref[rows, :], beside_ref[rows, :]]
        state_ref[rows, :] = add_products(None, pieces, near_state, 0)
        query_ref[rows, :] = add_products(None, pieces, near_query, 0)
    for source in range(2, sources):
        split(source, far_state_ref, far_query_ref, (source - 2) * depth)


def late_kernel(count, segments, *refs):
    begin = segments[0].start
    held, refs = refs[: count * len(segments)], refs[count * len(segments) :]
    base_state, base_query, far_state, far_query, state_ref, query_ref, rim_ref = refs
    width = base_query.shape[1] // 2
    for turn, rows in enumerate(segments):
        pieces = [ref[...] for ref in held[turn * count : (turn + 1) * count]]
        out = slice(rows.start - begin, rows.stop - begin)
        state_ref[out, :] = add_products(base_state[rows, :], pieces, far_state, 0)
        query_ref[out, :] = add_products(base_query[rows, :], pieces, far_query, 0)
    last = state_ref.shape[0] - RIM
    rim_ref[:, :width] = query_ref[last:, :width]
    rim_ref[:, width:] = state_ref[last:, : 2 * width]


def partial_kernel(count, *refs):
    base_state, far_state, out_ref = refs[count:]
    out_ref[...] = add_products(
        base_state[: out_ref.shape[0], :], [ref[...] for ref in refs[:count]], far_state, 0
    )


def convolve(raw, start, columns, conv_ref, taps_at):
    taps = conv_ref.shape[0]
    conv = 0.0
    for tap in range(taps):
        spot = start - taps + 1 + tap
        conv = conv + conv_ref[tap : tap + 1, taps_at] * raw[spot : spot + CHUNK, columns]
    return conv * sigmoid(conv)


def unit_rows(value):
    return value * lax.rsqrt(jnp.sum(value * value, axis=1, keepdims=True) + 1e-06)


def key_pass(raw, conv_ref, rate, doc_ref, first_chunk, outs, state):
    key_ref, x_ref, y_ref, grid_ref, gamma_ref, plus_ref, chunk_ref, pair_ref = outs
    width = key_ref.shape[1]
    chunks = key_ref.shape[0] // CHUNK
    row = lax.broadcasted_iota(jnp.int32, (CHUNK, CHUNK), 0)
    col = lax.broadcasted_iota(jnp.int32, (CHUNK, CHUNK), 1)
    lower = row >= col
    tri = jnp.where(lower, 1.0, 0.0).astype(BF16)
    eye = jnp.where(row == col, 1.0, 0.0).astype(F32)
    keys, values, betas, grids, gammas, tails = [], [], [], [], [], []
    for part in range(chunks):
        start = RIM + part * CHUNK
        rows = slice(part * CHUNK, (part + 1) * CHUNK)
        middle, last = slice(width, 2 * width), slice(2 * width, 3 * width)
        keys.append(unit_rows(convolve(raw, start, slice(0, width), conv_ref, middle)))
        values.append(convolve(raw, start, middle, conv_ref, last))
        mixing = raw[start : start + CHUNK, last]
        plus = softplus(mixing)
        plus_ref[rows, :] = plus
        betas.append(sigmoid(mixing[:, 0:1]))
        spot = first_chunk + part
        docs = jnp.broadcast_to(doc_ref[spot : spot + 1, :].astype(F32), (CHUNK, CHUNK))
        docs = jnp.transpose(docs)
        smooth = -rate * plus[:, 1:2]
        high = smooth.astype(BF16).astype(F32)
        middle = (smooth - high).astype(BF16).astype(F32)
        rest = smooth - high - middle
        steps = jnp.where(col == 0, docs, jnp.where(col == 1, high, jnp.where(col == 2, middle, rest)))
        steps = jnp.where(col < 4, steps, 0.0).astype(BF16)
        sums = jnp.dot(tri, steps, preferred_element_type=F32)
        across = jnp.transpose(sums)
        across = jnp.concatenate([across[0:1, :], across[1:2, :] + (across[2:3, :] + across[3:4, :])], axis=0)
        count = sums[:, 0:1]
        smooth = sums[:, 1:2] + (sums[:, 2:3] + sums[:, 3:4])
        span = (smooth - across[1:2, :]) - 20.0 * (count - across[0:1, :])
        grids.append(jnp.exp(jnp.where(lower, span, -1e30)))
        gammas.append(jnp.exp(smooth - 20.0 * count))
        end = slice(CHUNK - 1, CHUNK)
        tails.append(jnp.exp((smooth[end] - smooth) - 20.0 * (count[end] - count)))
        key_ref[rows, :] = keys[part]
        grid_ref[rows, :] = grids[part]
        gamma_ref[rows, :] = jnp.broadcast_to(gammas[part], (CHUNK, width))
    across_keys = [jnp.transpose(key) for key in keys]
    grams = [
        parts_dot(left_parts(key), right_parts(across)) for key, across in zip(keys, across_keys)
    ]
    lowers = [jnp.where(row > col, beta * gram, 0.0) for beta, gram in zip(betas, grams)]
    inverses = unit_lower_inverse(lowers, row, col)
    states = []
    if state is not None:
        later_keys = product(state[0], across_keys[-1])
    for part in range(chunks):
        rows = slice(part * CHUNK, (part + 1) * CHUNK)
        inverse, beta = inverses[part], betas[part]
        factor_x = product(inverse, beta * keys[part])
        factor_y = product(grids[part] * inverse, beta * values[part])
        x_ref[rows, :] = factor_x
        y_ref[rows, :] = factor_y
        factors = jnp.concatenate([factor_x, tails[part] * factor_y], axis=1)
        onto = product(across_keys[part], factors)
        if state is not None and part == chunks - 1:
            behind = product(later_keys, factors)
        trans = gammas[part][CHUNK - 1 : CHUNK, :] * (eye - onto[:, :width])
        states.append((trans, onto[:, width:]))
        chunk_ref[part, 0] = trans
        chunk_ref[part, 1] = onto[:, width:]
    if state is not None:
        decay = gammas[-1][CHUNK - 1 : CHUNK, :]
        states[-1] = (decay * (state[0] - behind[:, :width]), behind[:, width:] + state[1])
    while len(states) > 1:
        joined = [followed(*states[at : at + 2]) for at in range(0, len(states) - 1, 2)]
        states = joined + states[2 * len(joined) :]
    pair_ref[0] = states[0][0]
    pair_ref[1] = states[0][1]


def followed(first, second):
    width = first[0].shape[0]
    onto = product(second[0], jnp.concatenate(first, axis=1))
    return onto[:, :width], onto[:, width:] + second[1]


def later_kernel(first_chunk, raw_ref, conv_ref, rate_ref, doc_ref, *outs):
    key_pass(raw_ref, conv_ref, rate_ref[0, 0], doc_ref, first_chunk, outs, None)


def earlier_kernel(first, count, *refs):
    held, refs = refs[:count], refs[count:]
    part_ref, far_ref, rim_ref, next_ref, state_ref, conv_ref, rate_ref, doc_ref = refs[:8]
    outs, raw = refs[8:-1], refs[-1]
    rows, width = part_ref.shape[0], state_ref.shape[1]
    raw[RIM : RIM + rows, :] = add_products(
        part_ref[...], [ref[...] for ref in held], far_ref, first
    )
    raw[:RIM, : 2 * width] = rim_ref[:, width:]
    raw[RIM + rows :, :] = next_ref[:RIM, :]
    key_pass(raw, conv_ref, rate_ref[0, 0], doc_ref, 0, outs, (state_ref[0], state_ref[1]))


def query_kernel(count, *refs):
    held, refs = refs[:count], refs[count:]
    base_ref, far_ref, rim_ref, next_ref, conv_ref = refs[:5]
    fields = [(refs[5:11], 0), (refs[11:17], 1)]
    carried_ref, local_ref, gate_ref, raw = refs[17:]
    width = carried_ref.shape[1]
    rows = held[0].shape[0]
    raw[RIM : RIM + rows, :] = add_products(
        base_ref[:rows, :], [ref[...] for ref in held], far_ref, 0
    )
    raw[:RIM, :width] = rim_ref[:, :width]
    raw[RIM + rows :, :] = next_ref[:RIM, :]
    row = lax.broadcasted_iota(jnp.int32, (CHUNK, CHUNK), 0)
    col = lax.broadcasted_iota(jnp.int32, (CHUNK, CHUNK), 1)
    state = None
    base = 0
    for (key_ref, x_ref, y_ref, grid_ref, gamma_ref, chunk_ref), later in fields:
        source = next_ref if later else raw
        for part in range(key_ref.shape[0] // CHUNK):
            start = RIM + part * CHUNK
            rows = slice(part * CHUNK, (part + 1) * CHUNK)
            out = slice(base, base + CHUNK)
            base += CHUNK
            columns = slice(0, width)
            query = unit_rows(convolve(source, start, columns, conv_ref, columns))
            gate = source[start : start + CHUNK, width:]
            gate_ref[out, :] = gate * sigmoid(gate)
            overlap = product(query, jnp.transpose(key_ref[rows, :]))
            carried = gamma_ref[rows, :] * (
                query - product(jnp.where(row >= col, overlap, 0.0), x_ref[rows, :])
            )
            local = product(grid_ref[rows, :] * overlap, y_ref[rows, :])
            trans, memory = chunk_ref[part, 0], chunk_ref[part, 1]
            if state is None:
                state = (trans, memory)
            else:
                onto = product(
                    jnp.concatenate([trans, carried], axis=0), jnp.concatenate(state, axis=1)
                )
                carried = onto[CHUNK:, :width]
                local = local + onto[CHUNK:, width:]
                state = (onto[:CHUNK, :width], onto[:CHUNK, width:] + memory)
            carried_ref[out, :] = carried
            local_ref[out, :] = local


def four_kernel(bit, carried, last, flag_ref, own_ref, one_ref, two_ref, three_ref, *refs):
    group_ref, level_ref, next_ref = refs[-3:]
    width = next_ref.shape[0]
    flag = lambda at: jnp.broadcast_to(flag_ref[at : at + 1, :], (width, width)) == 1
    set_low, set_high = flag(bit), flag(bit + 1)
    held = (own_ref, one_ref, two_ref, three_ref)

    def placed(part):
        by_low = [jnp.where(set_low, held[at ^ 1][part], held[at][part]) for at in range(4)]
        return [jnp.where(set_high, by_low[at ^ 2], by_low[at]) for at in range(4)]

    trans, memory = placed(0), placed(1)
    joined = lambda at: jnp.concatenate([trans[at], memory[at]], axis=1)
    onto_low = product(trans[1], joined(0))
    onto_high = product(trans[3], joined(2))
    low_a, low_s = onto_low[:, :width], onto_low[:, width:] + memory[1]
    high_a, high_s = onto_high[:, :width], onto_high[:, width:] + memory[3]
    if last:
        group_ref[...] = product(high_a, low_s) + high_s
    else:
        onto = product(high_a, jnp.concatenate([low_a, low_s], axis=1))
        group_ref[0] = onto[:, :width]
        group_ref[1] = onto[:, width:] + high_s
    if carried:
        carry = refs[0][...]
        first = product(carry, jnp.concatenate([one_ref[0], one_ref[1]], axis=1))
        first_a, first_s = first[:, :width], first[:, width:]
    else:
        row = lax.broadcasted_iota(jnp.int32, (width, width), 0)
        col = lax.broadcasted_iota(jnp.int32, (width, width), 1)
        carry = jnp.where(row == col, 1.0, 0.0).astype(F32)
        first_a, first_s = one_ref[0], one_ref[1]
    level_ref[0] = jnp.where(set_low, first_s, 0.0)
    carry = jnp.where(set_low, first_a, carry)
    second = product(carry, jnp.concatenate([low_a, low_s], axis=1))
    level_ref[1] = jnp.where(set_high, second[:, width:], 0.0)
    carry = jnp.where(set_high, second[:, :width], carry)
    next_ref[...] = jnp.where(flag(bit + 2), carry, 0.0) if last else carry


def level_kernel(stages, single, carried_ref, local_ref, low_ref, high_ref, *refs):
    states = [ref[spot] for ref in refs[:stages] for spot in range(ref.shape[0])]
    carried = left_parts(carried_ref[...])
    weights = jnp.concatenate([low_ref[...], high_ref[...]], axis=0)
    mixed = weights[:, 2:3] * local_ref[...]
    for level, state in enumerate(states):
        mixed = mixed + weights[:, level + 3 : level + 4] * parts_dot(carried, right_parts(state))
    if single:
        carry_ref, mixed_ref, reach_ref = refs[stages:]
        level = len(states) + 3
        reach_ref[...] = weights[:, level : level + 1] * parts_dot(
            carried, right_parts(carry_ref[...])
        )
    else:
        (mixed_ref,) = refs[stages:]
    mixed_ref[...] = mixed


def mix_kernel(single, mixed_ref, gate_ref, gain_ref, *refs):
    mixed = mixed_ref[...]
    if single:
        mixed = mixed + product(refs[0][...], refs[1][...])
    outs = refs[2 if single else 0 :]
    scale = lax.rsqrt(jnp.mean(mixed * mixed, axis=1, keepdims=True) + 1e-05)
    normed = mixed * scale * gain_ref[...] * gate_ref[...]
    outs[0][...] = normed
    base = 0
    for out in outs[1:]:
        out[...] = normed[base : base + out.shape[0]]
        base += out.shape[0]


def block_product(pieces, weight, rows):
    parts = [halves(ref[rows, :]) for ref in pieces]
    high, low = (jnp.concatenate(part, axis=1) for part in zip(*parts))
    columns = weight.shape[1] // 2
    both = jnp.dot(high, weight, preferred_element_type=F32)
    rest = jnp.dot(low, weight[:, :columns], preferred_element_type=F32)
    return (both[:, :columns] + both[:, columns:]) + rest


def order_kernel(sources, index_ref, weight_ref, out_ref):
    depth = weight_ref.shape[0] // sources
    for source in range(sources):
        rows = pl.ds(pl.multiple_of(index_ref[source] * depth, depth), depth)
        out_ref[source * depth : (source + 1) * depth, :] = left_parts(weight_ref[rows, :])


def source_rows(first, pieces, weight_ref):
    depth = pieces[0].shape[1]
    return weight_ref[first * depth : (first + len(pieces)) * depth, :]


def row_blocks(rows):
    return [slice(base, base + CHUNK) for base in range(0, rows, CHUNK)]


def near_kernel(own_ref, near_ref, weight_ref, low_ref, high_ref):
    weight = source_rows(0, [own_ref, near_ref], weight_ref)
    half = low_ref.shape[0]
    for rows in row_blocks(half):
        low_ref[rows, :] = block_product([own_ref, near_ref], weight, rows)
        later = slice(half + rows.start, half + rows.stop)
        high_ref[rows, :] = block_product([own_ref, near_ref], weight, later)


def far_kernel(count, first, *refs):
    held, (weight_ref, total_ref, out_ref) = refs[:-3], refs[-3:]
    weight = source_rows(first, held[:count], weight_ref)
    base = 0
    for at in range(0, len(held), count):
        pieces = held[at : at + count]
        for rows in row_blocks(pieces[0].shape[0]):
            out = slice(base + rows.start, base + rows.stop)
            out_ref[out, :] = total_ref[out, :] + block_product(pieces, weight, rows)
        base += pieces[0].shape[0]


def flush_kernel(count, first, *refs):
    pieces = refs[:count]
    weight_ref, ready_ref, total_ref, out_ref, next_ref, sem = refs[count:]
    half = ready_ref.shape[0]
    copy = pltpu.make_async_copy(ready_ref, out_ref.at[:half, :], sem)
    copy.start()
    weight = source_rows(first, pieces, weight_ref)
    for rows in row_blocks(half):
        next_ref[rows, :] = total_ref[rows, :] + block_product(pieces, weight, rows)
    copy.wait()


def last_kernel(count, first, *refs):
    pieces = refs[:count]
    weight_ref, total_ref, begun_ref, out_ref, held, sems = refs[count:]
    half = total_ref.shape[0]
    copies = []
    weight = source_rows(first, pieces, weight_ref)
    for spot, rows in enumerate(row_blocks(half)):
        held[rows, :] = total_ref[rows, :] + block_product(pieces, weight, rows)
        out = slice(half + rows.start, half + rows.stop)
        copies.append(
            pltpu.make_async_copy(held.at[rows, :], out_ref.at[out, :], sems.at[spot])
        )
        copies[-1].start()
    for copy in copies:
        copy.wait()


def vmem_call(kernel, outs, scratch, cost, *args, any_in=(), any_out=(), aliases=()):
    spec = pl.BlockSpec(memory_space=pltpu.VMEM)
    small = pl.BlockSpec(memory_space=pltpu.SMEM)
    free = pl.BlockSpec(memory_space=pl.ANY)
    return pl.pallas_call(
        kernel,
        out_shape=outs,
        in_specs=[
            free if spot in any_in else small if arg.dtype == jnp.int32 and arg.ndim == 1 else spec
            for spot, arg in enumerate(args)
        ],
        out_specs=[free if spot in any_out else spec for spot in range(len(outs))]
        if isinstance(outs, list)
        else (free if any_out else spec),
        input_output_aliases=dict(aliases),
        scratch_shapes=scratch,
        compiler_params=pltpu.CompilerParams(vmem_limit_bytes=VMEM_GRANT),
        cost_estimate=pl.CostEstimate(flops=int(cost * 1e9), bytes_accessed=1 << 20, transcendentals=0),
    )(*args)


def to_sibling(value):
    count = lax.axis_size("head")
    return lax.ppermute(value, "head", [(source, source ^ 1) for source in range(count)])


def to_chips(value):
    count = lax.axis_size("head")
    return [
        lax.ppermute(
            value, "head", [(source, (source + 2 * step) % count) for source in range(count)]
        )
        for step in range(1, count // 2)
    ]


def after(value, *earlier):
    return lax.optimization_barrier((value, *earlier))


def shards(tokens, w_proj, w_mix, conv_w, rates, doc_start, norm_gain, w_out):
    tok_rows, depth = tokens.shape
    width = w_proj.shape[1] // 4
    state_columns, query_columns = 2 * width + CHUNK, 2 * width
    heads, me = lax.axis_size("head"), lax.axis_index("head")
    blocks, my_index = lax.axis_size("ctx"), lax.axis_index("ctx")
    remote = [(me + heads - 2 * step) % heads for step in range(1, heads // 2)]
    order = [me, me ^ 1] + remote + [index ^ 1 for index in remote]
    bits = blocks.bit_length() - 1
    index = jnp.stack(order + [my_index >> bit & 1 for bit in range(bits)]).astype(jnp.int32)
    count = heads - 2
    like = lambda *shape: jax.ShapeDtypeStruct(shape, F32)
    parts = lambda *shape: jax.ShapeDtypeStruct(shape, BF16)

    first = tok_rows // 2
    cut = first - RIM
    middle = tok_rows - CHUNK - RIM
    segments = (slice(cut, middle), slice(middle, tok_rows))
    late = [to_chips(tokens[rows]) for rows in segments]
    beside = to_sibling(tokens)
    early_rows, beside = after(tokens, beside)
    early = to_chips(early_rows[:cut])
    base_state, base_query, far_state, far_query, flags = vmem_call(
        base_kernel,
        [like(tok_rows, state_columns), like(tok_rows, query_columns),
         parts(count * depth, 2 * state_columns), parts(count * depth, 2 * query_columns),
         jax.ShapeDtypeStruct((bits, CHUNK), jnp.int32)],
        [pltpu.VMEM((heads, depth, 4 * width), F32),
         pltpu.VMEM((2 * depth, 2 * state_columns), BF16),
         pltpu.VMEM((2 * depth, 2 * query_columns), BF16),
         pltpu.SemaphoreType.DMA((heads,))],
        3, index, tokens, beside, w_mix.T, w_proj, any_in=(4,),
    )
    late, far_state = after(late, far_state)
    late_on = [[to_sibling(value) for value in values] for values in late]
    arrived = [value for pair in zip(late, late_on) for values in pair for value in values]
    late_state, late_query, rim = vmem_call(
        functools.partial(late_kernel, count, segments),
        [like(tok_rows - cut, state_columns), like(tok_rows - cut, query_columns),
         like(RIM, 3 * width)],
        [], 0.5, *arrived, base_state, base_query, far_state, far_query,
    )
    rim = lax.ppermute(rim, "ctx", [(source, source + 1) for source in range(blocks - 1)])
    docs = doc_start.reshape(tok_rows // CHUNK, CHUNK)
    rate = rates[:, None]

    def outs(rows):
        chunks = like(rows // CHUNK, 2, width, width)
        return [like(rows, width)] * 6 + [chunks, like(2, width, width)]

    later = vmem_call(
        functools.partial(later_kernel, first // CHUNK), outs(tok_rows - first), [], 0.5,
        late_state, conv_w, rate, docs,
    )
    early, pair_late, rim = after(early, later[7], rim)
    early_on = [to_sibling(value) for value in early]
    partial = vmem_call(
        functools.partial(partial_kernel, len(early)), like(cut, state_columns), [], 1,
        *early, base_state, far_state,
    )
    earlier = vmem_call(
        functools.partial(earlier_kernel, len(early), len(early)), outs(first),
        [pltpu.VMEM((first + RIM, state_columns), F32)], 5,
        *early_on, partial, far_state, rim, late_state, pair_late, conv_w, rate, docs,
    )

    pair = earlier[7]
    fields = vmem_call(
        functools.partial(query_kernel, count), [like(tok_rows, width)] * 3,
        [pltpu.VMEM((first + RIM, query_columns), F32)], 5,
        *early, *early_on, base_query, far_query, rim, late_query, conv_w,
        *earlier[:5], earlier[6], *later[:5], later[6],
    )
    own_weight = vmem_call(
        functools.partial(order_kernel, heads), parts(w_out.shape[0], 2 * w_out.shape[1]), [], 1,
        index, w_out,
    )
    carry = ()
    levels = []
    for bit in range(0, bits - 1, 2):
        others = [
            lax.ppermute(
                pair, "ctx", [(source, source ^ (mask << bit)) for source in range(blocks)]
            )
            for mask in (1, 2, 3)
        ]
        if not bit:
            others[0], *fields, own_weight = after(others[0], *fields, own_weight)
        last = bit + 2 >= bits - 1 and bits % 2
        group = [like(width, width)] if last else [like(2, width, width)]
        pair, level, *carry = vmem_call(
            functools.partial(four_kernel, bit, bool(carry), last),
            group + [like(2, width, width), like(width, width)], [], 1,
            flags, pair, *others, *carry,
        )
        levels.append(level)
    carried, local, gate = fields
    lone = bool(bits % 2)
    reach = blocks // 2
    if lone:
        other = lax.ppermute(
            pair if carry else pair[1],
            "ctx", [(source, source ^ reach) for source in range(blocks)],
        )
        if not carry:
            carry = [jnp.where(my_index >= reach, jnp.eye(width, dtype=F32), 0.0)]
    rows_shape = like(tok_rows, width)
    mixed, *reached = vmem_call(
        functools.partial(level_kernel, len(levels), lone), [rows_shape] * (2 if lone else 1), [], 1,
        carried, local, earlier[5], later[5], *levels, *(carry if lone else ()),
    )
    if lone:
        reached.append(other)
    half = tok_rows // 2
    normed, *lows, high = vmem_call(
        functools.partial(mix_kernel, lone),
        [rows_shape] + [like(half // 2, width)] * 2 + [like(half, width)], [], 1,
        mixed, gate, norm_gain[None, :], *reached,
    )
    columns = w_out.shape[1]
    near = to_sibling(normed)
    far_lows = [to_chips(low) for low in lows]
    high, near = after(high, near)
    far_high = to_chips(high)
    total_low, total_high = vmem_call(
        near_kernel, [like(half, columns)] * 2, [], 2, normed, near, own_weight
    )
    far_lows, total_low = after(far_lows, total_low)
    far_lows_on = [[to_sibling(value) for value in values] for values in far_lows]
    arrived = [value for pair in zip(far_lows, far_lows_on) for values in pair for value in values]
    total_low = vmem_call(
        functools.partial(far_kernel, count, 2), like(half, columns), [], 0.01,
        *arrived, own_weight, total_low,
    )
    far_high, total_low = after(far_high, total_low)
    far_high_on = [to_sibling(value) for value in far_high]
    whole = like(tok_rows, columns)
    begun, total_high = vmem_call(
        functools.partial(flush_kernel, len(far_high), 2), [whole, like(half, columns)],
        [pltpu.SemaphoreType.DMA], 1,
        *far_high, own_weight, total_low, total_high, any_out=(0,),
    )
    args = [*far_high_on, own_weight, total_high, begun]
    last = len(args) - 1
    return vmem_call(
        functools.partial(last_kernel, len(far_high), 2 + len(far_high)), whole,
        [pltpu.VMEM((half, columns), F32), pltpu.SemaphoreType.DMA((half // CHUNK,))], 1,
        *args, any_in=(last,), any_out=True, aliases=((last, 0),),
    )


def solution(mesh):
    placed = (
        P("ctx", "head"),
        P(None, "head"),
        P(None, "head"),
        P(None, "head"),
        P("head"),
        P("ctx"),
        P("head"),
        P(None, "head"),
    )
    return jax.shard_map(
        shards, mesh=mesh, in_specs=placed, out_specs=P("ctx", "head"), check_vma=False
    )
```

```python
import functools

import jax
import jax.numpy as jnp
from jax import lax
from jax.experimental import pallas as pl
from jax.experimental.pallas import tpu as pltpu
from jax.sharding import PartitionSpec as P

CHUNK = 128
RIM = 16
VMEM_GRANT = 16 << 20
F32 = jnp.float32
BF16 = jnp.bfloat16


def halves(value):
    high = value.astype(BF16)
    return high, (value - high.astype(F32)).astype(BF16)


def left_parts(value):
    return jnp.concatenate(halves(value), axis=1)


def right_parts(value):
    row = jnp.concatenate(halves(value), axis=1)
    return jnp.concatenate([row, row], axis=0)


def parts_dot(left, right):
    both = jnp.dot(left, right, preferred_element_type=F32)
    half = both.shape[1] // 2
    return both[:, :half] + both[:, half:]


def product(left, right):
    return parts_dot(left_parts(left), right_parts(right))


def softplus(value):
    return jnp.maximum(value, 0.0) + jnp.log1p(jnp.exp(-jnp.abs(value)))


def sigmoid(value):
    return 1.0 / (1.0 + jnp.exp(-value))


def unit_lower_inverse(lowers, row, col):
    size = lowers[0].shape[0]
    eye = jnp.where(row == col, 1.0, 0.0).astype(F32)
    inverses = [eye - jnp.where((row >> 1) == (col >> 1), lower, 0.0) for lower in lowers]
    lower_parts = [halves(lower) for lower in lowers]
    step = 1
    while 1 << step < size:
        off = ((row >> (step + 2)) == (col >> (step + 2))) & ((row >> step) > (col >> step))
        offs = [
            jnp.concatenate([jnp.where(off, part, jnp.zeros_like(part)) for part in parts], axis=1)
            for parts in lower_parts
        ]
        if step == 1:
            pairs = [jnp.where((row >> 1) == (col >> 1), lower, 0.0) for lower in lowers]
            entries = [jnp.sum(pair, axis=0, keepdims=True) for pair in pairs]
            parts = [jnp.where(off, lower, 0.0) for lower in lowers]
            onto = [
                part - pltpu.roll(part, size - 1, 1) * entry for part, entry in zip(parts, entries)
            ]
        else:
            onto = [parts_dot(left, right_parts(inverse)) for left, inverse in zip(offs, inverses)]
        rights = [right_parts(value) for value in onto]
        squares = [parts_dot(left_parts(value), right) for value, right in zip(onto, rights)]
        if step == 1:
            columns = [jnp.sum(pair, axis=1, keepdims=True) for pair in pairs]
            firsts = [
                inverse - value + column * pltpu.roll(value, 1, 0)
                for inverse, value, column in zip(inverses, onto, columns)
            ]
        else:
            firsts = [
                inverse - parts_dot(left_parts(inverse), right)
                for inverse, right in zip(inverses, rights)
            ]
        inverses = [first + product(first, square) for first, square in zip(firsts, squares)]
        step += 2
    return inverses


def add_products(total, pieces, weight_ref, first):
    columns = weight_ref.shape[1] // 2
    for spot, piece in enumerate(pieces):
        depth = piece.shape[1]
        rows = slice((first + spot) * depth, (first + spot + 1) * depth)
        high, low = halves(piece)
        both = jnp.dot(high, weight_ref[rows, :], preferred_element_type=F32)
        rest = jnp.dot(low, weight_ref[rows, :columns], preferred_element_type=F32)
        part = (both[:, :columns] + both[:, columns:]) + rest
        total = part if total is None else total + part
    return total


def base_kernel(
    index_ref, own_ref, beside_ref, mix_ref, proj_ref,
    state_ref, query_ref, far_state_ref, far_query_ref, flag_ref,
    held, near_state, near_query, sems,
):
    sources, depth, across = held.shape
    width = across // 4
    copies = []
    for source in range(sources):
        rows = pl.ds(pl.multiple_of(index_ref[source] * depth, depth), depth)
        copies.append(pltpu.make_async_copy(proj_ref.at[rows, :], held.at[source], sems.at[source]))
        copies[-1].start()
    for bit in range(flag_ref.shape[0]):
        flag_ref[bit : bit + 1, :] = jnp.broadcast_to(index_ref[sources + bit], (1, CHUNK))
    mixes = mix_ref.shape[0]

    def split(source, state_out, query_out, base):
        copies[source].wait()
        lanes = pl.ds(pl.multiple_of(index_ref[source] * depth, depth), depth)
        for begin in range(0, depth, CHUNK):
            rows = slice(begin, begin + CHUNK)
            out = slice(base + begin, base + begin + CHUNK)
            value = held[source, rows, :]
            mixing = mix_ref[:, lanes][:, rows]
            mixing = jnp.concatenate([mixing, jnp.zeros((CHUNK - mixes, CHUNK), F32)], axis=0)
            state = jnp.concatenate([value[:, width : 3 * width], jnp.transpose(mixing)], axis=1)
            query = jnp.concatenate([value[:, :width], value[:, 3 * width :]], axis=1)
            state_out[out, :] = left_parts(state)
            query_out[out, :] = left_parts(query)

    for source in range(2):
        split(source, near_state, near_query, source * depth)
    half = own_ref.shape[0] // 2
    for rows in (slice(0, half), slice(half, 2 * half)):
        pieces = [own_ref[rows, :], beside_ref[rows, :]]
        state_ref[rows, :] = add_products(None, pieces, near_state, 0)
        query_ref[rows, :] = add_products(None, pieces, near_query, 0)
    for source in range(2, sources):
        split(source, far_state_ref, far_query_ref, (source - 2) * depth)


def late_kernel(count, segments, *refs):
    begin = segments[0].start
    held, refs = refs[: count * len(segments)], refs[count * len(segments) :]
    base_state, base_query, far_state, far_query, state_ref, query_ref, rim_ref = refs
    width = base_query.shape[1] // 2
    for turn, rows in enumerate(segments):
        pieces = [ref[...] for ref in held[turn * count : (turn + 1) * count]]
        out = slice(rows.start - begin, rows.stop - begin)
        state_ref[out, :] = add_products(base_state[rows, :], pieces, far_state, 0)
        query_ref[out, :] = add_products(base_query[rows, :], pieces, far_query, 0)
    last = state_ref.shape[0] - RIM
    rim_ref[:, :width] = query_ref[last:, :width]
    rim_ref[:, width:] = state_ref[last:, : 2 * width]


def partial_kernel(count, *refs):
    base_state, far_state, out_ref = refs[count:]
    out_ref[...] = add_products(
        base_state[: out_ref.shape[0], :], [ref[...] for ref in refs[:count]], far_state, 0
    )


def convolve(raw, start, columns, conv_ref, taps_at):
    taps = conv_ref.shape[0]
    conv = 0.0
    for tap in range(taps):
        spot = start - taps + 1 + tap
        conv = conv + conv_ref[tap : tap + 1, taps_at] * raw[spot : spot + CHUNK, columns]
    return conv * sigmoid(conv)


def unit_rows(value):
    return value * lax.rsqrt(jnp.sum(value * value, axis=1, keepdims=True) + 1e-06)


def key_pass(raw, conv_ref, rate, doc_ref, first_chunk, outs, state):
    key_ref, x_ref, y_ref, grid_ref, gamma_ref, plus_ref, chunk_ref, pair_ref = outs
    width = key_ref.shape[1]
    chunks = key_ref.shape[0] // CHUNK
    row = lax.broadcasted_iota(jnp.int32, (CHUNK, CHUNK), 0)
    col = lax.broadcasted_iota(jnp.int32, (CHUNK, CHUNK), 1)
    lower = row >= col
    tri = jnp.where(lower, 1.0, 0.0).astype(BF16)
    eye = jnp.where(row == col, 1.0, 0.0).astype(F32)
    keys, values, betas, grids, gammas, tails = [], [], [], [], [], []
    for part in range(chunks):
        start = RIM + part * CHUNK
        rows = slice(part * CHUNK, (part + 1) * CHUNK)
        middle, last = slice(width, 2 * width), slice(2 * width, 3 * width)
        keys.append(unit_rows(convolve(raw, start, slice(0, width), conv_ref, middle)))
        values.append(convolve(raw, start, middle, conv_ref, last))
        mixing = raw[start : start + CHUNK, last]
        plus = softplus(mixing)
        plus_ref[rows, :] = plus
        betas.append(sigmoid(mixing[:, 0:1]))
        spot = first_chunk + part
        docs = jnp.broadcast_to(doc_ref[spot : spot + 1, :].astype(F32), (CHUNK, CHUNK))
        docs = jnp.transpose(docs)
        smooth = -rate * plus[:, 1:2]
        high = smooth.astype(BF16).astype(F32)
        middle = (smooth - high).astype(BF16).astype(F32)
        rest = smooth - high - middle
        steps = jnp.where(col == 0, docs, jnp.where(col == 1, high, jnp.where(col == 2, middle, rest)))
        steps = jnp.where(col < 4, steps, 0.0).astype(BF16)
        sums = jnp.dot(tri, steps, preferred_element_type=F32)
        across = jnp.transpose(sums)
        across = jnp.concatenate([across[0:1, :], across[1:2, :] + (across[2:3, :] + across[3:4, :])], axis=0)
        count = sums[:, 0:1]
        smooth = sums[:, 1:2] + (sums[:, 2:3] + sums[:, 3:4])
        span = (smooth - across[1:2, :]) - 20.0 * (count - across[0:1, :])
        grids.append(jnp.exp(jnp.where(lower, span, -1e30)))
        gammas.append(jnp.exp(smooth - 20.0 * count))
        end = slice(CHUNK - 1, CHUNK)
        tails.append(jnp.exp((smooth[end] - smooth) - 20.0 * (count[end] - count)))
        key_ref[rows, :] = keys[part]
        grid_ref[rows, :] = grids[part]
        gamma_ref[rows, :] = jnp.broadcast_to(gammas[part], (CHUNK, width))
    across_keys = [jnp.transpose(key) for key in keys]
    grams = [
        parts_dot(left_parts(key), right_parts(across)) for key, across in zip(keys, across_keys)
    ]
    lowers = [jnp.where(row > col, beta * gram, 0.0) for beta, gram in zip(betas, grams)]
    inverses = unit_lower_inverse(lowers, row, col)
    states = []
    if state is not None:
        later_keys = product(state[0], across_keys[-1])
    for part in range(chunks):
        rows = slice(part * CHUNK, (part + 1) * CHUNK)
        inverse, beta = inverses[part], betas[part]
        factor_x = product(inverse, beta * keys[part])
        factor_y = product(grids[part] * inverse, beta * values[part])
        x_ref[rows, :] = factor_x
        y_ref[rows, :] = factor_y
        factors = jnp.concatenate([factor_x, tails[part] * factor_y], axis=1)
        onto = product(across_keys[part], factors)
        if state is not None and part == chunks - 1:
            behind = product(later_keys, factors)
        trans = gammas[part][CHUNK - 1 : CHUNK, :] * (eye - onto[:, :width])
        states.append((trans, onto[:, width:]))
        chunk_ref[part, 0] = trans
        chunk_ref[part, 1] = onto[:, width:]
    if state is not None:
        decay = gammas[-1][CHUNK - 1 : CHUNK, :]
        states[-1] = (decay * (state[0] - behind[:, :width]), behind[:, width:] + state[1])
    while len(states) > 1:
        joined = [followed(*states[at : at + 2]) for at in range(0, len(states) - 1, 2)]
        states = joined + states[2 * len(joined) :]
    pair_ref[0] = states[0][0]
    pair_ref[1] = states[0][1]


def followed(first, second):
    width = first[0].shape[0]
    onto = product(second[0], jnp.concatenate(first, axis=1))
    return onto[:, :width], onto[:, width:] + second[1]


def later_kernel(first_chunk, raw_ref, conv_ref, rate_ref, doc_ref, *outs):
    key_pass(raw_ref, conv_ref, rate_ref[0, 0], doc_ref, first_chunk, outs, None)


def earlier_kernel(first, count, *refs):
    held, refs = refs[:count], refs[count:]
    part_ref, far_ref, rim_ref, next_ref, state_ref, conv_ref, rate_ref, doc_ref = refs[:8]
    outs, raw = refs[8:-1], refs[-1]
    rows, width = part_ref.shape[0], state_ref.shape[1]
    raw[RIM : RIM + rows, :] = add_products(
        part_ref[...], [ref[...] for ref in held], far_ref, first
    )
    raw[:RIM, : 2 * width] = rim_ref[:, width:]
    raw[RIM + rows :, :] = next_ref[:RIM, :]
    key_pass(raw, conv_ref, rate_ref[0, 0], doc_ref, 0, outs, (state_ref[0], state_ref[1]))


def query_kernel(count, *refs):
    held, refs = refs[:count], refs[count:]
    base_ref, far_ref, rim_ref, next_ref, conv_ref = refs[:5]
    fields = [(refs[5:11], 0), (refs[11:17], 1)]
    carried_ref, local_ref, gate_ref, raw = refs[17:]
    width = carried_ref.shape[1]
    rows = held[0].shape[0]
    raw[RIM : RIM + rows, :] = add_products(
        base_ref[:rows, :], [ref[...] for ref in held], far_ref, 0
    )
    raw[:RIM, :width] = rim_ref[:, :width]
    raw[RIM + rows :, :] = next_ref[:RIM, :]
    row = lax.broadcasted_iota(jnp.int32, (CHUNK, CHUNK), 0)
    col = lax.broadcasted_iota(jnp.int32, (CHUNK, CHUNK), 1)
    state = None
    base = 0
    for (key_ref, x_ref, y_ref, grid_ref, gamma_ref, chunk_ref), later in fields:
        source = next_ref if later else raw
        for part in range(key_ref.shape[0] // CHUNK):
            start = RIM + part * CHUNK
            rows = slice(part * CHUNK, (part + 1) * CHUNK)
            out = slice(base, base + CHUNK)
            base += CHUNK
            columns = slice(0, width)
            query = unit_rows(convolve(source, start, columns, conv_ref, columns))
            gate = source[start : start + CHUNK, width:]
            gate_ref[out, :] = gate * sigmoid(gate)
            overlap = product(query, jnp.transpose(key_ref[rows, :]))
            carried = gamma_ref[rows, :] * (
                query - product(jnp.where(row >= col, overlap, 0.0), x_ref[rows, :])
            )
            local = product(grid_ref[rows, :] * overlap, y_ref[rows, :])
            trans, memory = chunk_ref[part, 0], chunk_ref[part, 1]
            if state is None:
                state = (trans, memory)
            else:
                onto = product(
                    jnp.concatenate([trans, carried], axis=0), jnp.concatenate(state, axis=1)
                )
                carried = onto[CHUNK:, :width]
                local = local + onto[CHUNK:, width:]
                state = (onto[:CHUNK, :width], onto[:CHUNK, width:] + memory)
            carried_ref[out, :] = carried
            local_ref[out, :] = local


def four_kernel(bit, carried, last, flag_ref, own_ref, one_ref, two_ref, three_ref, *refs):
    group_ref, level_ref, next_ref = refs[-3:]
    width = next_ref.shape[0]
    flag = lambda at: jnp.broadcast_to(flag_ref[at : at + 1, :], (width, width)) == 1
    set_low, set_high = flag(bit), flag(bit + 1)
    held = (own_ref, one_ref, two_ref, three_ref)

    def placed(part):
        by_low = [jnp.where(set_low, held[at ^ 1][part], held[at][part]) for at in range(4)]
        return [jnp.where(set_high, by_low[at ^ 2], by_low[at]) for at in range(4)]

    trans, memory = placed(0), placed(1)
    joined = lambda at: jnp.concatenate([trans[at], memory[at]], axis=1)
    onto_low = product(trans[1], joined(0))
    onto_high = product(trans[3], joined(2))
    low_a, low_s = onto_low[:, :width], onto_low[:, width:] + memory[1]
    high_a, high_s = onto_high[:, :width], onto_high[:, width:] + memory[3]
    if last:
        group_ref[...] = product(high_a, low_s) + high_s
    else:
        onto = product(high_a, jnp.concatenate([low_a, low_s], axis=1))
        group_ref[0] = onto[:, :width]
        group_ref[1] = onto[:, width:] + high_s
    if carried:
        carry = refs[0][...]
        first = product(carry, jnp.concatenate([one_ref[0], one_ref[1]], axis=1))
        first_a, first_s = first[:, :width], first[:, width:]
    else:
        row = lax.broadcasted_iota(jnp.int32, (width, width), 0)
        col = lax.broadcasted_iota(jnp.int32, (width, width), 1)
        carry = jnp.where(row == col, 1.0, 0.0).astype(F32)
        first_a, first_s = one_ref[0], one_ref[1]
    level_ref[0] = jnp.where(set_low, first_s, 0.0)
    carry = jnp.where(set_low, first_a, carry)
    second = product(carry, jnp.concatenate([low_a, low_s], axis=1))
    level_ref[1] = jnp.where(set_high, second[:, width:], 0.0)
    carry = jnp.where(set_high, second[:, :width], carry)
    next_ref[...] = jnp.where(flag(bit + 2), carry, 0.0) if last else carry


def level_kernel(stages, single, carried_ref, local_ref, low_ref, high_ref, *refs):
    states = [ref[spot] for ref in refs[:stages] for spot in range(ref.shape[0])]
    carried = left_parts(carried_ref[...])
    weights = jnp.concatenate([low_ref[...], high_ref[...]], axis=0)
    mixed = weights[:, 2:3] * local_ref[...]
    for level, state in enumerate(states):
        mixed = mixed + weights[:, level + 3 : level + 4] * parts_dot(carried, right_parts(state))
    if single:
        carry_ref, mixed_ref, reach_ref = refs[stages:]
        level = len(states) + 3
        reach_ref[...] = weights[:, level : level + 1] * parts_dot(
            carried, right_parts(carry_ref[...])
        )
    else:
        (mixed_ref,) = refs[stages:]
    mixed_ref[...] = mixed


def mix_kernel(single, mixed_ref, gate_ref, gain_ref, *refs):
    mixed = mixed_ref[...]
    if single:
        mixed = mixed + product(refs[0][...], refs[1][...])
    outs = refs[2 if single else 0 :]
    scale = lax.rsqrt(jnp.mean(mixed * mixed, axis=1, keepdims=True) + 1e-05)
    normed = mixed * scale * gain_ref[...] * gate_ref[...]
    outs[0][...] = normed
    base = 0
    for out in outs[1:]:
        out[...] = normed[base : base + out.shape[0]]
        base += out.shape[0]


def block_product(pieces, weight, rows):
    parts = [halves(ref[rows, :]) for ref in pieces]
    high, low = (jnp.concatenate(part, axis=1) for part in zip(*parts))
    columns = weight.shape[1] // 2
    both = jnp.dot(high, weight, preferred_element_type=F32)
    rest = jnp.dot(low, weight[:, :columns], preferred_element_type=F32)
    return (both[:, :columns] + both[:, columns:]) + rest


def order_kernel(sources, index_ref, weight_ref, out_ref):
    depth = weight_ref.shape[0] // sources
    for source in range(sources):
        rows = pl.ds(pl.multiple_of(index_ref[source] * depth, depth), depth)
        out_ref[source * depth : (source + 1) * depth, :] = left_parts(weight_ref[rows, :])


def source_rows(first, pieces, weight_ref):
    depth = pieces[0].shape[1]
    return weight_ref[first * depth : (first + len(pieces)) * depth, :]


def row_blocks(rows):
    return [slice(base, base + CHUNK) for base in range(0, rows, CHUNK)]


def near_kernel(own_ref, near_ref, weight_ref, low_ref, high_ref):
    weight = source_rows(0, [own_ref, near_ref], weight_ref)
    half = low_ref.shape[0]
    for rows in row_blocks(half):
        low_ref[rows, :] = block_product([own_ref, near_ref], weight, rows)
        later = slice(half + rows.start, half + rows.stop)
        high_ref[rows, :] = block_product([own_ref, near_ref], weight, later)


def far_kernel(count, first, *refs):
    held, (weight_ref, total_ref, out_ref) = refs[:-3], refs[-3:]
    weight = source_rows(first, held[:count], weight_ref)
    base = 0
    for at in range(0, len(held), count):
        pieces = held[at : at + count]
        for rows in row_blocks(pieces[0].shape[0]):
            out = slice(base + rows.start, base + rows.stop)
            out_ref[out, :] = total_ref[out, :] + block_product(pieces, weight, rows)
        base += pieces[0].shape[0]


def flush_kernel(count, first, *refs):
    pieces = refs[:count]
    weight_ref, ready_ref, total_ref, out_ref, next_ref, sem = refs[count:]
    half = ready_ref.shape[0]
    copy = pltpu.make_async_copy(ready_ref, out_ref.at[:half, :], sem)
    copy.start()
    weight = source_rows(first, pieces, weight_ref)
    for rows in row_blocks(half):
        next_ref[rows, :] = total_ref[rows, :] + block_product(pieces, weight, rows)
    copy.wait()


def last_kernel(count, first, *refs):
    pieces = refs[:count]
    weight_ref, total_ref, begun_ref, out_ref, held, sems = refs[count:]
    half = total_ref.shape[0]
    copies = []
    weight = source_rows(first, pieces, weight_ref)
    for spot, rows in enumerate(row_blocks(half)):
        held[rows, :] = total_ref[rows, :] + block_product(pieces, weight, rows)
        out = slice(half + rows.start, half + rows.stop)
        copies.append(
            pltpu.make_async_copy(held.at[rows, :], out_ref.at[out, :], sems.at[spot])
        )
        copies[-1].start()
    for copy in copies:
        copy.wait()


def vmem_call(kernel, outs, scratch, cost, *args, any_in=(), any_out=(), aliases=()):
    spec = pl.BlockSpec(memory_space=pltpu.VMEM)
    small = pl.BlockSpec(memory_space=pltpu.SMEM)
    free = pl.BlockSpec(memory_space=pl.ANY)
    return pl.pallas_call(
        kernel,
        out_shape=outs,
        in_specs=[
            free if spot in any_in else small if arg.dtype == jnp.int32 and arg.ndim == 1 else spec
            for spot, arg in enumerate(args)
        ],
        out_specs=[free if spot in any_out else spec for spot in range(len(outs))]
        if isinstance(outs, list)
        else (free if any_out else spec),
        input_output_aliases=dict(aliases),
        scratch_shapes=scratch,
        compiler_params=pltpu.CompilerParams(vmem_limit_bytes=VMEM_GRANT),
        cost_estimate=pl.CostEstimate(flops=int(cost * 1e9), bytes_accessed=1 << 20, transcendentals=0),
    )(*args)


def to_sibling(value):
    count = lax.axis_size("head")
    return lax.ppermute(value, "head", [(source, source ^ 1) for source in range(count)])


def to_chips(value):
    count = lax.axis_size("head")
    return [
        lax.ppermute(
            value, "head", [(source, (source + 2 * step) % count) for source in range(count)]
        )
        for step in range(1, count // 2)
    ]


def after(value, *earlier):
    return lax.optimization_barrier((value, *earlier))


def shards(tokens, w_proj, w_mix, conv_w, rates, doc_start, norm_gain, w_out):
    tok_rows, depth = tokens.shape
    width = w_proj.shape[1] // 4
    state_columns, query_columns = 2 * width + CHUNK, 2 * width
    heads, me = lax.axis_size("head"), lax.axis_index("head")
    blocks, my_index = lax.axis_size("ctx"), lax.axis_index("ctx")
    remote = [(me + heads - 2 * step) % heads for step in range(1, heads // 2)]
    order = [me, me ^ 1] + remote + [index ^ 1 for index in remote]
    bits = blocks.bit_length() - 1
    index = jnp.stack(order + [my_index >> bit & 1 for bit in range(bits)]).astype(jnp.int32)
    count = heads - 2
    like = lambda *shape: jax.ShapeDtypeStruct(shape, F32)
    parts = lambda *shape: jax.ShapeDtypeStruct(shape, BF16)

    first = tok_rows // 2
    cut = first - RIM
    middle = tok_rows - CHUNK - RIM
    segments = (slice(cut, middle), slice(middle, tok_rows))
    late = [to_chips(tokens[rows]) for rows in segments]
    beside = to_sibling(tokens)
    early_rows, beside = after(tokens, beside)
    early = to_chips(early_rows[:cut])
    base_state, base_query, far_state, far_query, flags = vmem_call(
        base_kernel,
        [like(tok_rows, state_columns), like(tok_rows, query_columns),
         parts(count * depth, 2 * state_columns), parts(count * depth, 2 * query_columns),
         jax.ShapeDtypeStruct((bits, CHUNK), jnp.int32)],
        [pltpu.VMEM((heads, depth, 4 * width), F32),
         pltpu.VMEM((2 * depth, 2 * state_columns), BF16),
         pltpu.VMEM((2 * depth, 2 * query_columns), BF16),
         pltpu.SemaphoreType.DMA((heads,))],
        3, index, tokens, beside, w_mix.T, w_proj, any_in=(4,),
    )
    late, far_state = after(late, far_state)
    late_on = [[to_sibling(value) for value in values] for values in late]
    arrived = [value for pair in zip(late, late_on) for values in pair for value in values]
    late_state, late_query, rim = vmem_call(
        functools.partial(late_kernel, count, segments),
        [like(tok_rows - cut, state_columns), like(tok_rows - cut, query_columns),
         like(RIM, 3 * width)],
        [], 0.5, *arrived, base_state, base_query, far_state, far_query,
    )
    rim = lax.ppermute(rim, "ctx", [(source, source + 1) for source in range(blocks - 1)])
    docs = doc_start.reshape(tok_rows // CHUNK, CHUNK)
    rate = rates[:, None]

    def outs(rows):
        chunks = like(rows // CHUNK, 2, width, width)
        return [like(rows, width)] * 6 + [chunks, like(2, width, width)]

    later = vmem_call(
        functools.partial(later_kernel, first // CHUNK), outs(tok_rows - first), [], 0.5,
        late_state, conv_w, rate, docs,
    )
    early, pair_late, rim = after(early, later[7], rim)
    early_on = [to_sibling(value) for value in early]
    partial = vmem_call(
        functools.partial(partial_kernel, len(early)), like(cut, state_columns), [], 1,
        *early, base_state, far_state,
    )
    earlier = vmem_call(
        functools.partial(earlier_kernel, len(early), len(early)), outs(first),
        [pltpu.VMEM((first + RIM, state_columns), F32)], 5,
        *early_on, partial, far_state, rim, late_state, pair_late, conv_w, rate, docs,
    )

    pair = earlier[7]
    fields = vmem_call(
        functools.partial(query_kernel, count), [like(tok_rows, width)] * 3,
        [pltpu.VMEM((first + RIM, query_columns), F32)], 5,
        *early, *early_on, base_query, far_query, rim, late_query, conv_w,
        *earlier[:5], earlier[6], *later[:5], later[6],
    )
    own_weight = vmem_call(
        functools.partial(order_kernel, heads), parts(w_out.shape[0], 2 * w_out.shape[1]), [], 1,
        index, w_out,
    )
    carry = ()
    levels = []
    for bit in range(0, bits - 1, 2):
        others = [
            lax.ppermute(
                pair, "ctx", [(source, source ^ (mask << bit)) for source in range(blocks)]
            )
            for mask in (1, 2, 3)
        ]
        if not bit:
            others[0], *fields, own_weight = after(others[0], *fields, own_weight)
        last = bit + 2 >= bits - 1 and bits % 2
        group = [like(width, width)] if last else [like(2, width, width)]
        pair, level, *carry = vmem_call(
            functools.partial(four_kernel, bit, bool(carry), last),
            group + [like(2, width, width), like(width, width)], [], 1,
            flags, pair, *others, *carry,
        )
        levels.append(level)
    carried, local, gate = fields
    lone = bool(bits % 2)
    reach = blocks // 2
    if lone:
        other = lax.ppermute(
            pair if carry else pair[1],
            "ctx", [(source, source ^ reach) for source in range(blocks)],
        )
        if not carry:
            carry = [jnp.where(my_index >= reach, jnp.eye(width, dtype=F32), 0.0)]
    rows_shape = like(tok_rows, width)
    mixed, *reached = vmem_call(
        functools.partial(level_kernel, len(levels), lone), [rows_shape] * (2 if lone else 1), [], 1,
        carried, local, earlier[5], later[5], *levels, *(carry if lone else ()),
    )
    if lone:
        reached.append(other)
    half = tok_rows // 2
    normed, *lows, high = vmem_call(
        functools.partial(mix_kernel, lone),
        [rows_shape] + [like(half // 2, width)] * 2 + [like(half, width)], [], 1,
        mixed, gate, norm_gain[None, :], *reached,
    )
    columns = w_out.shape[1]
    near = to_sibling(normed)
    far_lows = [to_chips(low) for low in lows]
    high, near = after(high, near)
    far_high = to_chips(high)
    total_low, total_high = vmem_call(
        near_kernel, [like(half, columns)] * 2, [], 2, normed, near, own_weight
    )
    far_lows, total_low = after(far_lows, total_low)
    far_lows_on = [[to_sibling(value) for value in values] for values in far_lows]
    arrived = [value for pair in zip(far_lows, far_lows_on) for values in pair for value in values]
    total_low = vmem_call(
        functools.partial(far_kernel, count, 2), like(half, columns), [], 0.01,
        *arrived, own_weight, total_low,
    )
    far_high, total_low = after(far_high, total_low)
    far_high_on = [to_sibling(value) for value in far_high]
    whole = like(tok_rows, columns)
    begun, total_high = vmem_call(
        functools.partial(flush_kernel, len(far_high), 2), [whole, like(half, columns)],
        [pltpu.SemaphoreType.DMA], 1,
        *far_high, own_weight, total_low, total_high, any_out=(0,),
    )
    args = [*far_high_on, own_weight, total_high, begun]
    last = len(args) - 1
    return vmem_call(
        functools.partial(last_kernel, len(far_high), 2 + len(far_high)), whole,
        [pltpu.VMEM((half, columns), F32), pltpu.SemaphoreType.DMA((half // CHUNK,))], 1,
        *args, any_in=(last,), any_out=True, aliases=((last, 0),),
    )


def solution(mesh):
    placed = (
        P("ctx", "head"),
        P(None, "head"),
        P(None, "head"),
        P(None, "head"),
        P("head"),
        P("ctx"),
        P("head"),
        P(None, "head"),
    )
    return jax.shard_map(
        shards, mesh=mesh, in_specs=placed, out_specs=P("ctx", "head"), check_vma=False
    )
```
